32 devices in a mesh: fsdp: 8 (over z, core), sp: 4 (over y, x).
Axes of the slice: x: 2, y: 2, z: 4, core: 2. Of those that a mesh axis runs over, the one named last changes fastest.
Arguments:
- tokens: bfloat16 [8192, 2048], P(('fsdp', 'sp')), may hold values from -6 to 6
- w_attn: bfloat16 [2048, 8192], P(('fsdp', 'sp'))
- norm_gains: bfloat16 [2048, 4], P(('fsdp', 'sp')), may hold values from 0.25 to 1.75
- w_expert: bfloat16 [2048, 16, 3072], P('fsdp', 'sp')
- gate_weights: float32 [8192, 8], P(('fsdp', 'sp')), may hold values from 0.06 to 0.25
- routes: int32 [8192, 8], P(('fsdp', 'sp')), may hold values from 0 to 15, all different within a row; in each aligned block of 256 rows (0 to 255, 256 to 511, ...) at most 136 rows name the same one
- segment: int32 [8192], P('fsdp'), may hold values from 0 to 2, as said below
- valid_mask: int32 [8192], P(('fsdp', 'sp')), may hold values from 0 to 1, as said below
- teacher: bfloat16 [8192, 2048], P(('fsdp', 'sp')), may hold values from -6 to 6
- cotangent: bfloat16 [8192, 2048], P(('fsdp', 'sp')), may hold values from -6 to 6
Outputs:
- output: bfloat16 [8192, 2048], P(('fsdp', 'sp'))
- loss: float32 [], replicated
- grad_tokens: float32 [8192, 2048], P(('fsdp', 'sp'))
- grad_attn: float32 [2048, 8192], P(('fsdp', 'sp'))
- grad_gains: float32 [2048, 4], P(('fsdp', 'sp'))
- grad_expert: float32 [2048, 16, 3072], P('fsdp', 'sp')
The draws below stay inside these ranges and needn't reach their ends.
Inputs may be any that keep to these rules, and one draw needn't show every extreme that they name: `routes`: each row names 8 different experts; among the 256 tokens of one device no expert is named more than 136 times. `segment`: ids never fall within a sequence of 1024 tokens. `valid_mask`: at least one token is valid.
All inputs are finite; a program needn't handle non-finite values.
Results may differ from the reference program's by a relative error of at most 0.017.
Values may be sent and summed in bfloat16 or wider, within the bound.
No kernel may reach another device: no remote copies, remote signals or barrier semaphores. Data moves between devices by JAX's collectives and lax.ppermute only.
A program may use at most 448 MiB of HBM per device.

```python
import math
import jax
import jax.numpy as jnp
import numpy as np
from jax import lax

D = 2048
H = 16
HD = 128
FF = 1024
TOP = 8
SEQ = 1024
TOK_DEV = 256
TOKENS = 8192
EXPERTS = 16
CAP = 136
N_FSDP = 8
N_SP = 4


def draw_w_attn(key, part):
    key = jax.random.fold_in(key, 11)
    drawn = jax.random.normal(key, (D, 4 * D), jnp.float32)
    columns = jnp.arange(4 * D)
    factor = jnp.where(columns < 3 * D, 1.0, 6.0) * D ** (-0.5)
    return (drawn * factor[None, :]).astype(jnp.bfloat16)


def draw_w_expert(key, part):
    key = jax.random.fold_in(key, 12)
    drawn = jax.random.normal(key, (D, EXPERTS, 3 * FF), jnp.float32)
    columns = jnp.arange(3 * FF)
    factor = jnp.where(columns < 2 * FF, D ** (-0.5), 4.0 * FF ** (-0.5))
    return (drawn * factor[None, None, :]).astype(jnp.bfloat16)


def draw_segment(key, part):
    key = jax.random.fold_in(key, 13)
    first_key, second_key = jax.random.split(key)
    first_end = jax.random.randint(first_key, (N_FSDP,), 1, TOK_DEV)
    last_start = SEQ - jax.random.randint(second_key, (N_FSDP,), 1, TOK_DEV)
    position = jnp.arange(SEQ)
    ids = (position[None, :] >= first_end[:, None]).astype(jnp.int32) + (position[None, :] >= last_start[:, None]).astype(jnp.int32)
    return ids.reshape(-1).astype(jnp.int32)


def draw_valid_mask(key, part):
    key = jax.random.fold_in(key, 14)
    position = jnp.arange(TOKENS)
    threshold = 250 + 500 * position // TOKENS
    drawn = jax.random.randint(key, (TOKENS,), 0, 1000)
    chosen = (drawn < threshold) | (position == TOKENS - 1)
    return chosen.astype(jnp.int32)


def steps_of(rng, shape, cuts, low, top_value):
    factor_of, own = 1.0, jax.random.fold_in(rng, 6)
    for dim, parts in cuts:
        steps = jnp.exp(jax.random.uniform(jax.random.fold_in(own, dim), (parts,), jnp.float32, low / len(cuts), top_value / len(cuts)))
        factor_of = factor_of * jnp.repeat(steps, shape[dim] // parts).reshape([-1 if axis == dim else 1 for axis in range(len(shape))])
    return factor_of


def deal_out(rng, own, number, rows, count, top, limit, skew):
    order = jax.random.permutation(rng, count)
    heavy_load, ordinary = load_shares(count, rows * top, limit, skew, True), load_shares(count, rows * top, limit, skew, False)
    places = jnp.arange(count)

    def named(tallies, turn):
        used = int((tallies > 0).sum())
        fixed = max(1, used // 4)
        moved = fixed + (places - fixed + turn * (used - fixed)) % max(1, count - fixed)
        return jnp.zeros((count,), jnp.int32).at[order[jnp.where(places < fixed, places, moved)]].set(jnp.asarray(tallies, jnp.int32))

    tallies = jnp.where(number % 4 == 0, named(heavy_load, number // 4), named(ordinary, number - number // 4 - 1))
    mixed = jax.random.permutation(jax.random.fold_in(own, 3), count)
    source_of, receiver = mixed[0:count // 2 * 2:2], mixed[1:count // 2 * 2:2]
    margin = jnp.minimum(tallies[source_of] - 1, limit - tallies[receiver]) // 2
    margin = jnp.where((source_of == order[0]) | (receiver == order[0]) | (tallies[receiver] == 0), 0, jnp.maximum(margin, 0))
    moved = jax.random.randint(jax.random.fold_in(own, 4), (count // 2,), 0, 1 << 20) % (margin + 1)
    tallies = tallies.at[source_of].add(-moved).at[receiver].add(moved)
    members = jnp.searchsorted(jnp.cumsum(tallies), jnp.arange(rows * top), side="right").astype(jnp.int32)
    table = members.reshape(top, rows).T
    table = table[jax.random.permutation(jax.random.fold_in(own, 1), rows)]
    turn = jax.random.randint(jax.random.fold_in(own, 2), (rows, 1), 0, top)
    return jnp.take_along_axis(table, (jnp.arange(top)[None, :] + turn) % top, axis=1)


def load_shares(number_of, total, reach, slope, full):
    portions = [(1 << 20) // math.isqrt(grade ** slope) + 1 for grade in range(1, number_of + 1)]
    largest = reach if full else min(reach, max(-(-total // number_of), total * portions[0] // sum(portions)))
    least = 1 if total - largest >= number_of - 1 else 0
    holding, surplus = [largest] + [least] * (number_of - 1), total - largest - least * (number_of - 1)
    while surplus > 0:
        movable = [i for i in range(1, number_of) if holding[i] < largest] or [i for i in range(1, number_of) if holding[i] < reach]
        mass, budget = sum([portions[i] for i in movable]), surplus
        for i in movable:
            more = min(reach - holding[i], max(1, budget * portions[i] // mass), surplus)
            holding[i] = holding[i] + more
            surplus = surplus - more
    return np.array(holding)


def noise(stream_key, shape, deviation, most, cuts=(), dtype=jnp.bfloat16):
    gain = steps_of(stream_key, shape, cuts, -0.22, 0.18) if cuts else 1.0
    entries = jax.random.normal(stream_key, shape, jnp.float32) * deviation * gain
    return jnp.minimum(jnp.maximum(entries, -most), most).astype(dtype)


def setup_inputs(seed: int = 0) -> dict:
    arg_keys = jax.random.split(jax.random.key(seed), 11)
    tokens = noise(arg_keys[0], (TOKENS, D), 1.0, 6.0, ((0, 32),))
    w_attn = draw_w_attn(jax.random.fold_in(arg_keys[10], 71), 0)
    norm_gains = jnp.clip(1.0 + 0.15 * jax.random.normal(arg_keys[2], (D, 4), jnp.float32), 0.25, 1.75).astype(jnp.bfloat16)
    w_expert = draw_w_expert(jax.random.fold_in(arg_keys[10], 71), 0)
    gate_weights = jnp.clip(jnp.exp(math.log(0.25) - 1.4271164 * jax.random.uniform(arg_keys[4], (TOKENS, TOP), jnp.float32) ** steps_of(arg_keys[4], (TOKENS, TOP), ((0, 32),), -0.2, 0.2)), 0.06, 0.25)
    routes_keys = jax.random.split(jax.random.fold_in(arg_keys[5], 1), TOKENS // TOK_DEV)
    routes_turns = jax.random.permutation(jax.random.fold_in(arg_keys[5], 3), TOKENS // TOK_DEV)
    routes = jax.vmap(lambda own, number: deal_out(jax.random.fold_in(arg_keys[5], 2), own, number, TOK_DEV, EXPERTS, TOP, CAP, 1))(routes_keys, routes_turns).reshape((TOKENS, TOP))
    segment = draw_segment(jax.random.fold_in(arg_keys[10], 71), 0)
    valid_mask = draw_valid_mask(jax.random.fold_in(arg_keys[10], 71), 0)
    teacher = noise(arg_keys[8], (TOKENS, D), 1.0, 6.0, ((0, 32),))
    cotangent = noise(arg_keys[9], (TOKENS, D), 1.0, 6.0, ((0, 32),))
    return dict(tokens=tokens, w_attn=w_attn, norm_gains=norm_gains, w_expert=w_expert, gate_weights=gate_weights, routes=routes, segment=segment, valid_mask=valid_mask, teacher=teacher, cotangent=cotangent)


epsilon = 1e-05
highest = lax.Precision.HIGHEST

@jax.custom_vjp
def low(v):
    return lax.optimization_barrier(v.astype(jnp.bfloat16)).astype(jnp.float32)

@jax.custom_vjp
def low_back(v):
    return v

def low_keep(v):
    return (low(v), None)

def low_pass(kept, grad):
    return (grad,)

def back_keep(v):
    return (v, None)

def back_low(kept, grad):
    return (low(grad),)
low.defvjp(low_keep, low_pass)
low_back.defvjp(back_keep, back_low)

def matmul_hi(left, right):
    return jnp.dot(left, right, precision=highest, preferred_element_type=jnp.float32)

def rms_norm(values, gain_vec):
    return values * lax.rsqrt(lax.optimization_barrier(jnp.mean(values * values, axis=-1, keepdims=True)) + epsilon) * gain_vec

def rope_tables():
    position = jnp.arange(SEQ).astype(jnp.float32)
    inverse = 10000.0 ** (-(jnp.arange(HD // 2).astype(jnp.float32) * 2.0 / HD))
    angles = position[:, None] * inverse[None, :]
    cosine = jnp.concatenate([jnp.cos(angles), jnp.cos(angles)], axis=-1)
    sine_table = jnp.concatenate([jnp.sin(angles), jnp.sin(angles)], axis=-1)
    return (cosine[:, None, :], sine_table[:, None, :])

def rotate_half(values):
    half_size = values.shape[-1] // 2
    return jnp.concatenate([-values[..., half_size:], values[..., :half_size]], axis=-1)

def attend(query, keyed, valued, segment):
    scores = jnp.einsum('qhd,khd->hqk', query, keyed, precision=highest) * HD ** (-0.5)
    scores = low_back(scores)
    places = jnp.arange(SEQ).astype(jnp.int32)
    allowed = (segment[:, None] == segment[None, :]) & (places[:, None] >= places[None, :])
    scores = jnp.where(allowed[None], scores, -1e+30)
    row_top = lax.optimization_barrier(jnp.max(scores, axis=-1, keepdims=True))
    exp_scores = jnp.exp(scores - row_top)
    weights = low(exp_scores / lax.optimization_barrier(jnp.sum(exp_scores, axis=-1, keepdims=True)))
    return jnp.einsum('hqk,khd->qhd', weights, valued, precision=highest)

def block_layer(inputs, w_attn, norm_gains, expert_stack, gate_weights, routes, segment, cosine, sine_table):
    normed_in = low(rms_norm(inputs, norm_gains[:, 0]))
    proj = low_back(matmul_hi(normed_in, w_attn[:, :3 * D]))
    query = rms_norm(proj[:, :D], norm_gains[:, 2]).reshape(SEQ, H, HD)
    keyed = rms_norm(proj[:, D:2 * D], norm_gains[:, 3]).reshape(SEQ, H, HD)
    query = low_back(low(query * cosine + rotate_half(query) * sine_table))
    keyed = low_back(low(keyed * cosine + rotate_half(keyed) * sine_table))
    valued = low_back(low(proj[:, 2 * D:3 * D].reshape(SEQ, H, HD)))
    attn_vals = low_back(low(attend(query, keyed, valued, segment).reshape(SEQ, D)))
    residual = inputs + low_back(matmul_hi(attn_vals, w_attn[:, 3 * D:].T))
    normed_mid = low(rms_norm(residual, norm_gains[:, 1]))
    route_flat = routes.reshape(N_SP, TOK_DEV * TOP).astype(jnp.int32)
    onehot = (route_flat[:, :, None] == jnp.arange(EXPERTS).astype(jnp.int32)[None, None, :]).astype(jnp.int32)
    slot_place = (lax.optimization_barrier(jnp.sum(jnp.cumsum(onehot, axis=1) * onehot, axis=-1)) - 1).astype(jnp.int32)
    block_base = jnp.arange(N_SP).astype(jnp.int32)[:, None]
    slot_index = (route_flat * (N_SP * CAP) + block_base * CAP + slot_place).reshape(-1).astype(jnp.int32)
    token_of = (jnp.arange(SEQ * TOP) // TOP).astype(jnp.int32)
    routed_rows = normed_mid[token_of]
    buffer = jnp.zeros((EXPERTS * N_SP * CAP, D), jnp.float32).at[slot_index].set(routed_rows)
    buffer = low_back(buffer).reshape(EXPERTS, N_SP * CAP, D)

    def run_expert(pieces):
        rows_in, weight = pieces
        gate_up = low_back(matmul_hi(rows_in, weight[:, :2 * FF]))
        activated = low(jax.nn.silu(gate_up[:, :FF]) * gate_up[:, FF:])
        return low_back(low(matmul_hi(activated, weight[:, 2 * FF:].T)))
    outputs = lax.map(jax.checkpoint(run_expert), (buffer, expert_stack))
    gathered_back = outputs.reshape(EXPERTS * N_SP * CAP, D)[slot_index].reshape(SEQ, TOP, D)
    expert_sum = low_back(lax.optimization_barrier(jnp.sum(gate_weights[:, :, None] * gathered_back, axis=1)))
    return residual + expert_sum

def reference(tokens, w_attn, norm_gains, w_expert, gate_weights, routes, segment, valid_mask, teacher, cotangent):
    cosine, sine_table = rope_tables()
    valid_f = valid_mask.astype(jnp.float32)
    valid_count = jnp.sum(valid_f)
    teacher_f = teacher.astype(jnp.float32)

    def objective(inputs, attn_weight, gain_weight, expert_weight):
        expert_stack = jnp.transpose(expert_weight, (1, 0, 2))

        def per_sequence(pieces):
            return block_layer(pieces[0], attn_weight, gain_weight, expert_stack, pieces[1], pieces[2], pieces[3], cosine, sine_table)
        outputs = lax.map(jax.checkpoint(per_sequence), (inputs.reshape(N_FSDP, SEQ, D), gate_weights.reshape(N_FSDP, SEQ, TOP), routes.reshape(N_FSDP, SEQ, TOP), segment.reshape(N_FSDP, SEQ)))
        outputs = outputs.reshape(TOKENS, D)
        difference = outputs - teacher_f
        loss_value = jnp.sum(valid_f[:, None] * difference * difference) / (valid_count * D)
        return (outputs, loss_value)
    (outputs, loss_value), pullback = jax.vjp(objective, tokens.astype(jnp.float32), w_attn.astype(jnp.float32), norm_gains.astype(jnp.float32), w_expert.astype(jnp.float32))
    grads = pullback((cotangent.astype(jnp.float32), jnp.ones((), jnp.float32)))
    return (outputs.astype(jnp.bfloat16), loss_value, grads[0], grads[1], grads[2], grads[3])
```

```python
import jax
import jax.numpy as jnp
from jax import lax
from jax.sharding import Mesh, PartitionSpec as P

H = 16
HD = 128
TOP = 8
CORES = 2
PAD = 128

epsilon = 1e-05
masked = -1e30
f32 = jnp.float32
bf16 = jnp.bfloat16


def swap(pieces, axis):
    if pieces.shape[0] == 1:
        return pieces
    return lax.all_to_all(pieces, axis, split_axis=0, concat_axis=0, tiled=True)


def collect(block, axis):
    size = lax.axis_size(axis)
    return swap(jnp.broadcast_to(block[None], (size,) + block.shape), axis)


def rms_factor(values):
    return lax.rsqrt(jnp.mean(values * values, axis=-1, keepdims=True) + epsilon)


def norm_back(values, gain_vec, grad_in):
    factor = rms_factor(values)
    normed = values * factor
    gain_grad = jnp.sum(grad_in * normed, axis=0)
    inner = grad_in * gain_vec
    grad = factor * (inner - normed * jnp.mean(inner * normed, axis=-1, keepdims=True))
    return grad, gain_grad


def rope_tables(rows):
    inverse = 10000.0 ** (-(jnp.arange(HD // 2).astype(f32) * 2.0 / HD))
    angles = jnp.arange(rows).astype(f32)[:, None] * inverse[None, :]
    cosine = jnp.concatenate([jnp.cos(angles), jnp.cos(angles)], axis=-1)
    sine = jnp.concatenate([jnp.sin(angles), jnp.sin(angles)], axis=-1)
    return cosine[:, None, :], sine[:, None, :]


def rotate_half(values):
    half = values.shape[-1] // 2
    return jnp.concatenate([-values[..., half:], values[..., :half]], axis=-1)


def rotate_back(values):
    half = values.shape[-1] // 2
    return jnp.concatenate([values[..., half:], -values[..., :half]], axis=-1)


def block_scores(query, keyed, segment, block_index, rows, scale):
    start = block_index * rows
    q_block = lax.dynamic_slice_in_dim(query, start, rows, 0)
    q_segment = lax.dynamic_slice_in_dim(segment, start, rows, 0)
    q_places = start + jnp.arange(rows)
    k_places = jnp.arange(keyed.shape[0])
    allowed = (q_segment[:, None] == segment[None, :]) & (q_places[:, None] >= k_places[None, :])
    scores = jnp.einsum("qhd,khd->hqk", q_block, keyed, preferred_element_type=f32) * scale
    return q_block, jnp.where(allowed[None], scores, masked)


def attend_forward(query, keyed, valued, segment, rows, scale):
    blocks = keyed.shape[0] // rows

    def one_block(block_index):
        q_block, scores = block_scores(query, keyed, segment, block_index, rows, scale)
        row_top = jnp.max(scores, axis=-1, keepdims=True)
        exp_scores = jnp.exp(scores - row_top)
        row_total = jnp.sum(exp_scores, axis=-1, keepdims=True)
        weights = (exp_scores / row_total).astype(bf16)
        out = jnp.einsum("hqk,khd->qhd", weights, valued, preferred_element_type=f32)
        return out.astype(bf16), (row_top + jnp.log(row_total))[..., 0]

    outputs, log_total = lax.map(one_block, jnp.arange(blocks))
    return outputs.reshape(keyed.shape[0], -1), log_total


def attend_backward(query, keyed, valued, segment, log_total, grad_heads, rows, scale):
    blocks = keyed.shape[0] // rows

    def one_block(carry, pieces):
        grad_k, grad_v = carry
        block_index, block_total = pieces
        q_block, scores = block_scores(query, keyed, segment, block_index, rows, scale)
        probs = jnp.exp(scores - block_total[:, :, None])
        grad_block = lax.dynamic_slice_in_dim(grad_heads, block_index * rows, rows, 0)
        grad_v = grad_v + jnp.einsum(
            "hqk,qhd->khd", probs.astype(bf16), grad_block, preferred_element_type=f32
        )
        grad_probs = jnp.einsum("qhd,khd->hqk", grad_block, valued, preferred_element_type=f32)
        inner = jnp.sum(probs * grad_probs, axis=-1, keepdims=True)
        grad_scores = (probs * (grad_probs - inner)).astype(bf16)
        grad_q = jnp.einsum("hqk,khd->qhd", grad_scores, keyed, preferred_element_type=f32) * scale
        grad_k = (
            grad_k
            + jnp.einsum("hqk,qhd->khd", grad_scores, q_block, preferred_element_type=f32) * scale
        )
        return (grad_k, grad_v), grad_q

    initial = jnp.zeros(keyed.shape, f32)
    (grad_k, grad_v), grad_q = lax.scan(
        one_block, (initial, initial), (jnp.arange(blocks), log_total)
    )
    return grad_q.reshape(keyed.shape), grad_k, grad_v


def dot(spec, left, right):
    return jnp.einsum(spec, left, right, preferred_element_type=f32)


def shards(
    tokens,
    w_attn,
    norm_gains,
    w_expert,
    gate_weights,
    routes,
    segment,
    valid_mask,
    teacher,
    cotangent,
):
    outer, planes, seqs = lax.axis_size("o"), lax.axis_size("z"), lax.axis_size("s")
    plane, rank = lax.axis_index("z"), lax.axis_index("s")
    own, width = tokens.shape
    rows_dev = w_attn.shape[0]
    seq = own * seqs
    heads = H // seqs
    cols = heads * HD
    hidden = w_expert.shape[2] // 3
    part = w_expert.shape[0]
    capacity = own * TOP * 17 // (16 * planes * seqs)
    scale = HD ** (-0.5)
    block_rows = min(512, seq)

    def to_inner(v):
        lead = v.shape[:-1]
        v = v.reshape(lead + (outer, planes, CORES, part))
        return jnp.swapaxes(v, -3, -2).reshape(lead + (width,))

    def to_outer(v):
        lead = v.shape[:-1]
        v = v.reshape(lead + (outer, CORES, planes, part))
        return jnp.swapaxes(v, -3, -2).reshape(lead + (width,))

    def gather_rows(block):
        return collect(collect(collect(block, "z"), "c"), "o").reshape((-1,) + block.shape[1:])

    count = jnp.sum(valid_mask).astype(jnp.int32)
    digits = jnp.stack([count // 128, count % 128]).astype(bf16)
    extra = jnp.concatenate(
        [
            norm_gains,
            jnp.broadcast_to(digits[None], (rows_dev, 2)),
            jnp.zeros((rows_dev, PAD - 6), bf16),
        ],
        axis=1,
    )
    packed = jnp.concatenate(
        [
            w_attn.reshape(rows_dev, 4, seqs, cols).transpose(2, 0, 1, 3).reshape(
                seqs, rows_dev, 4 * cols
            ),
            jnp.broadcast_to(extra[None], (seqs, rows_dev, PAD)),
        ],
        axis=2,
    )
    mine = swap(packed, "s").reshape(part, 4 * cols + PAD)
    weights = gather_rows(mine)
    w_qkv = weights[:, : 3 * cols]
    w_out = weights[:, 3 * cols : 4 * cols]
    side = weights[:, 4 * cols : 4 * cols + 6].astype(f32).T
    gain_in, gain_mid = side[0], side[1]
    gain_q = lax.dynamic_slice_in_dim(to_outer(side[2]), rank * cols, cols, 0)
    gain_k = lax.dynamic_slice_in_dim(to_outer(side[3]), rank * cols, cols, 0)
    total_count = jnp.sum(side[4, ::rows_dev]) * 128.0 + jnp.sum(side[5, ::rows_dev])

    expert_parts = []
    for i in range(3):
        chunk = w_expert[:, :, i * hidden : (i + 1) * hidden].transpose(1, 0, 2)
        chunk = swap(chunk, "z").reshape(planes * part, hidden)
        chunk = lax.all_gather(chunk, ("s", "o", "c"), axis=0, tiled=True)
        expert_parts.append(chunk.reshape(seqs, width, hidden))
    w_gate, w_up, w_down = expert_parts

    routed = collect(
        jnp.concatenate([routes.astype(f32), gate_weights.astype(f32)], axis=1), "z"
    )
    route_all, gate_all = routed[..., :TOP].astype(jnp.int32), routed[..., TOP:]
    expert_ids = jnp.arange(seqs) * planes + plane
    match = route_all[:, :, None, :] == expert_ids[None, None, :, None]
    used = jnp.any(match, axis=-1)
    gate_of = jnp.sum(jnp.where(match, gate_all[:, :, None, :], 0.0), axis=-1)
    before = (jnp.arange(own)[:, None] > jnp.arange(own)[None, :]).astype(bf16)
    place = dot("tu,buk->btk", before, used.astype(bf16)).astype(jnp.int32)
    place = jnp.where(used, place, -1)
    taken = place.transpose(0, 2, 1)[:, :, None, :] == jnp.arange(capacity)[None, None, :, None]
    choose = taken.astype(bf16)
    gate_slot = jnp.sum(jnp.where(taken, gate_of.transpose(0, 2, 1)[:, :, None, :], 0.0), axis=-1)
    gate_slot = gate_slot.transpose(1, 0, 2).reshape(seqs, planes * capacity, 1)

    def dispatch(rows_in):
        spread = dot("bkjt,btd->kbjd", choose, rows_in)
        return spread.reshape(seqs, planes * capacity, width)

    def combine(rows_out):
        rows_out = rows_out.reshape(seqs, planes, capacity, width)
        partial = dot("bkjt,kbjd->btd", choose, rows_out).astype(bf16)
        return jnp.sum(swap(partial, "z").astype(f32), axis=0)

    inputs = to_inner(tokens)
    seq_tokens = to_inner(collect(tokens, "s").reshape(seq, width)).astype(f32)
    normed_in = (seq_tokens * rms_factor(seq_tokens) * gain_in).astype(bf16)
    inputs = inputs.astype(f32)
    projected = jnp.dot(normed_in, w_qkv, preferred_element_type=f32)
    query_raw = projected[:, :cols]
    key_raw = projected[:, cols : 2 * cols]
    valued = projected[:, 2 * cols :].astype(bf16).reshape(seq, heads, HD)

    def over_heads(first, second):
        pair = jnp.stack([jnp.sum(first, axis=-1), jnp.sum(second, axis=-1)])
        pair = jnp.sum(collect(pair, "s"), axis=0) / width
        return pair[0][:, None], pair[1][:, None]

    q_mean, k_mean = over_heads(query_raw * query_raw, key_raw * key_raw)
    q_factor, k_factor = lax.rsqrt(q_mean + epsilon), lax.rsqrt(k_mean + epsilon)
    cosine, sine = rope_tables(seq)

    def rope(raw, factor, gain):
        cube = (raw * factor * gain).reshape(seq, heads, HD)
        return (cube * cosine + rotate_half(cube) * sine).astype(bf16)

    query, keyed = rope(query_raw, q_factor, gain_q), rope(key_raw, k_factor, gain_k)
    attended, log_total = attend_forward(query, keyed, valued, segment, block_rows, scale)
    attn_out = dot("tc,dc->td", attended, w_out).astype(bf16)
    attn_out = jnp.sum(swap(attn_out.reshape(seqs, own, width), "s").astype(f32), axis=0)
    residual = inputs + attn_out

    normed_mid = (residual * rms_factor(residual) * gain_mid).astype(bf16)
    rows_in = dispatch(collect(normed_mid, "z")).astype(bf16)
    gate_pre = dot("krd,kdf->krf", rows_in, w_gate)
    up_pre = dot("krd,kdf->krf", rows_in, w_up)
    activated = (jax.nn.silu(gate_pre) * up_pre).astype(bf16)
    expert_out = (dot("krf,kdf->krd", activated, w_down) * gate_slot).astype(bf16)
    final_out = residual + combine(expert_out)

    valid_f = valid_mask.astype(f32)[:, None]
    difference = final_out - to_inner(teacher).astype(f32)
    squared = jnp.sum(valid_f * difference * difference)
    for axis in ("z", "s", "c", "o"):
        squared = jnp.sum(collect(jnp.broadcast_to(squared, (1, PAD)), axis)[:, 0, 0])
    loss_value = squared / (total_count * width)
    grad_out = (
        to_inner(cotangent).astype(f32) + 2.0 / (total_count * width) * valid_f * difference
    )

    grad_rows = dispatch(collect(grad_out.astype(bf16), "z"))
    grad_rows = (grad_rows * gate_slot).astype(bf16)

    def scatter_expert(grad):
        grad = grad.astype(bf16).reshape(seqs * width, hidden)
        grad = lax.psum_scatter(grad, ("s", "o", "c"), scatter_dimension=0, tiled=True)
        return swap(grad.reshape(planes, part, hidden), "z").astype(f32).transpose(1, 0, 2)

    grad_down = scatter_expert(dot("krd,krf->kdf", grad_rows, activated))
    grad_act = dot("krd,kdf->krf", grad_rows, w_down)
    sigmoid = jax.nn.sigmoid(gate_pre)
    grad_gate = (grad_act * up_pre * sigmoid * (1.0 + gate_pre * (1.0 - sigmoid))).astype(bf16)
    grad_up = (grad_act * gate_pre * sigmoid).astype(bf16)
    back_rows = dot("krf,kdf->krd", grad_gate, w_gate) + dot("krf,kdf->krd", grad_up, w_up)
    grad_mid = combine(back_rows.astype(bf16))
    grad_w_gate = scatter_expert(dot("krd,krf->kdf", rows_in, grad_gate))
    grad_w_up = scatter_expert(dot("krd,krf->kdf", rows_in, grad_up))
    grad_expert = jnp.concatenate([grad_w_gate, grad_w_up, grad_down], axis=2)

    grad_resid_norm, gain_mid_grad = norm_back(residual, gain_mid, grad_mid)
    grad_resid = grad_out + grad_resid_norm

    grad_attn_out = collect(grad_resid.astype(bf16), "s").reshape(seq, width)
    grad_w_out = dot("td,tc->dc", grad_attn_out, attended)
    grad_heads = jnp.dot(grad_attn_out, w_out, preferred_element_type=f32).astype(bf16)
    grad_q, grad_k, grad_v = attend_backward(
        query,
        keyed,
        valued,
        segment,
        log_total,
        grad_heads.reshape(seq, heads, HD),
        block_rows,
        scale,
    )

    def unrotate(grad):
        grad = grad.astype(bf16).astype(f32)
        return (grad * cosine + rotate_back(grad * sine)).reshape(seq, cols)

    grad_q, grad_k = unrotate(grad_q), unrotate(grad_k)
    q_normed, k_normed = query_raw * q_factor, key_raw * k_factor
    gain_q_grad = jnp.sum(grad_q * q_normed, axis=0)
    gain_k_grad = jnp.sum(grad_k * k_normed, axis=0)
    grad_q, grad_k = grad_q * gain_q, grad_k * gain_k
    q_inner, k_inner = over_heads(grad_q * q_normed, grad_k * k_normed)
    grad_q = q_factor * (grad_q - q_normed * q_inner)
    grad_k = k_factor * (grad_k - k_normed * k_inner)
    grad_proj = jnp.concatenate(
        [grad_q.astype(bf16), grad_k.astype(bf16), grad_v.reshape(seq, cols).astype(bf16)], axis=1
    )
    grad_w_qkv = dot("td,tc->dc", normed_in, grad_proj)
    grad_normed = dot("tc,dc->td", grad_proj, w_qkv).astype(bf16)
    grad_normed = jnp.sum(swap(grad_normed.reshape(seqs, own, width), "s").astype(f32), axis=0)
    grad_in_norm, gain_in_grad = norm_back(inputs, gain_in, grad_normed)
    grad_tokens = to_outer(grad_resid + grad_in_norm)

    def widen(local):
        full = jnp.zeros((width,), f32)
        return to_inner(lax.dynamic_update_slice_in_dim(full, local, rank * cols, 0))

    gains = jnp.stack(
        [gain_in_grad, gain_mid_grad, widen(gain_q_grad), widen(gain_k_grad)], axis=1
    )
    high = gains.astype(bf16)
    low = (gains - high.astype(f32)).astype(bf16)
    term = jnp.concatenate(
        [
            grad_w_qkv.astype(bf16),
            grad_w_out.astype(bf16),
            high,
            low,
            jnp.zeros((width, PAD - 8), bf16),
        ],
        axis=1,
    )
    term = lax.psum_scatter(term, ("o", "c", "z"), scatter_dimension=0, tiled=True)
    term = swap(term.reshape(seqs, rows_dev, 4 * cols + PAD), "s").astype(f32)
    grad_attn = (
        term[:, :, : 4 * cols]
        .reshape(seqs, rows_dev, 4, cols)
        .transpose(1, 2, 0, 3)
        .reshape(rows_dev, 4 * width)
    )
    gain_term = jnp.sum(term[:, :, 4 * cols : 4 * cols + 8], axis=0)
    grad_gains = gain_term[:, :4] + gain_term[:, 4:]
    return (
        to_outer(final_out).astype(bf16),
        loss_value,
        grad_tokens,
        grad_attn,
        grad_gains,
        grad_expert,
    )


def solution(mesh):
    fsdp, seqs = mesh.shape["fsdp"], mesh.shape["sp"]

    def whole(*arrays):
        planes = arrays[3].shape[1] // seqs
        outer = fsdp // (planes * CORES)
        inner = Mesh(mesh.devices.reshape(outer, planes, CORES, seqs), ("o", "z", "c", "s"))
        every = ("o", "z", "c", "s")
        rows = P(every, None)
        experts = P(("o", "z", "c"), "s", None)
        return jax.shard_map(
            shards,
            mesh=inner,
            in_specs=(
                rows,
                rows,
                rows,
                experts,
                rows,
                rows,
                P(("o", "z", "c")),
                P(every),
                rows,
                rows,
            ),
            out_specs=(rows, P(), rows, rows, rows, experts),
            check_vma=False,
        )(*arrays)

    return whole
```

```python
import jax
import jax.numpy as jnp
from jax import lax
from jax.sharding import Mesh, PartitionSpec as P

H = 16
HD = 128
TOP = 8
CORES = 2
PAD = 128

epsilon = 1e-05
masked = -1e30
f32 = jnp.float32
bf16 = jnp.bfloat16


def send(block, axis, step):
    size = lax.axis_size(axis)
    return lax.ppermute(block, axis, [(i, i ^ step) for i in range(size)])


def gather_near(block, axis):
    return [block] + [send(block, axis, k) for k in range(1, lax.axis_size(axis))]


def in_order(blocks, axis, start=0):
    rank = lax.axis_index(axis)
    if len(blocks) == 1:
        return blocks[0][None]
    stacked = jnp.zeros((len(blocks),) + blocks[0].shape, blocks[0].dtype)
    for k, block in enumerate(blocks):
        stacked = lax.dynamic_update_index_in_dim(stacked, block, (rank ^ k) + start, 0)
    return stacked


def collect(block, axis):
    return in_order(gather_near(block, axis), axis)


def exchange(piece_for, axis, start=0):
    rank, size = lax.axis_index(axis) + start, lax.axis_size(axis)
    return [piece_for(rank)] + [send(piece_for(rank ^ k), axis, k) for k in range(1, size)]


def exchange_sum(pieces, axis):
    got = exchange(lambda i: lax.dynamic_index_in_dim(pieces, i, 0, keepdims=False), axis)
    return sum(piece.astype(f32) for piece in got)


def token(*values):
    firsts = [value[(slice(0, 1),) * value.ndim].reshape(()).astype(f32) for value in values]
    total = sum(firsts)
    return (total != total).astype(jnp.int32)


def after(value, *others):
    return value + token(*others).astype(value.dtype)


def rms_factor(values):
    return lax.rsqrt(jnp.mean(values * values, axis=-1, keepdims=True) + epsilon)


def norm_back(values, gain_vec, grad_in):
    factor = rms_factor(values)
    normed = values * factor
    gain_grad = jnp.sum(grad_in * normed, axis=0)
    inner = grad_in * gain_vec
    grad = factor * (inner - normed * jnp.mean(inner * normed, axis=-1, keepdims=True))
    return grad, gain_grad


def rope_tables(rows):
    inverse = 10000.0 ** (-(jnp.arange(HD // 2).astype(f32) * 2.0 / HD))
    angles = jnp.arange(rows).astype(f32)[:, None] * inverse[None, :]
    cosine = jnp.concatenate([jnp.cos(angles), jnp.cos(angles)], axis=-1)
    sine = jnp.concatenate([jnp.sin(angles), jnp.sin(angles)], axis=-1)
    return cosine[:, None, :], sine[:, None, :]


def rotate_half(values):
    half = values.shape[-1] // 2
    return jnp.concatenate([-values[..., half:], values[..., :half]], axis=-1)


def rotate_back(values):
    half = values.shape[-1] // 2
    return jnp.concatenate([values[..., half:], -values[..., :half]], axis=-1)


def block_scores(query, keyed, segment, block_index, rows, scale):
    start = block_index * rows
    q_block = lax.dynamic_slice_in_dim(query, start, rows, 0)
    q_segment = lax.dynamic_slice_in_dim(segment, start, rows, 0)
    q_places = start + jnp.arange(rows)
    k_places = jnp.arange(keyed.shape[0])
    allowed = (q_segment[:, None] == segment[None, :]) & (q_places[:, None] >= k_places[None, :])
    scores = jnp.einsum("qhd,khd->hqk", q_block, keyed, preferred_element_type=f32) * scale
    return q_block, jnp.where(allowed[None], scores, masked)


def attend_forward(query, keyed, valued, segment, rows, scale):
    blocks = keyed.shape[0] // rows

    def one_block(block_index):
        q_block, scores = block_scores(query, keyed, segment, block_index, rows, scale)
        row_top = jnp.max(scores, axis=-1, keepdims=True)
        exp_scores = jnp.exp(scores - row_top)
        row_total = jnp.sum(exp_scores, axis=-1, keepdims=True)
        weights = (exp_scores / row_total).astype(bf16)
        out = jnp.einsum("hqk,khd->qhd", weights, valued, preferred_element_type=f32)
        return out.astype(bf16), (row_top + jnp.log(row_total))[..., 0]

    outputs, log_total = lax.map(one_block, jnp.arange(blocks))
    return outputs.reshape(keyed.shape[0], -1), log_total


def attend_backward(query, keyed, valued, segment, log_total, grad_heads, rows, scale):
    blocks = keyed.shape[0] // rows

    def one_block(carry, pieces):
        grad_k, grad_v = carry
        block_index, block_total = pieces
        q_block, scores = block_scores(query, keyed, segment, block_index, rows, scale)
        probs = jnp.exp(scores - block_total[:, :, None])
        grad_block = lax.dynamic_slice_in_dim(grad_heads, block_index * rows, rows, 0)
        grad_v = grad_v + jnp.einsum(
            "hqk,qhd->khd", probs.astype(bf16), grad_block, preferred_element_type=f32
        )
        grad_probs = jnp.einsum("qhd,khd->hqk", grad_block, valued, preferred_element_type=f32)
        inner = jnp.sum(probs * grad_probs, axis=-1, keepdims=True)
        grad_scores = (probs * (grad_probs - inner)).astype(bf16)
        grad_q = jnp.einsum("hqk,khd->qhd", grad_scores, keyed, preferred_element_type=f32) * scale
        grad_k = (
            grad_k
            + jnp.einsum("hqk,qhd->khd", grad_scores, q_block, preferred_element_type=f32) * scale
        )
        return (grad_k, grad_v), grad_q

    initial = jnp.zeros(keyed.shape, f32)
    (grad_k, grad_v), grad_q = lax.scan(
        one_block, (initial, initial), (jnp.arange(blocks), log_total)
    )
    return grad_q.reshape(keyed.shape), grad_k, grad_v


def dot(spec, left, right):
    return jnp.einsum(spec, left, right, preferred_element_type=f32)


def shards(
    tokens,
    w_attn,
    norm_gains,
    w_expert,
    gate_weights,
    routes,
    segment,
    valid_mask,
    teacher,
    cotangent,
):
    outer, planes, seqs = lax.axis_size("o"), lax.axis_size("z"), lax.axis_size("s")
    plane, rank = lax.axis_index("z"), lax.axis_index("s")
    own, width = tokens.shape
    rows_dev = w_attn.shape[0]
    seq = own * seqs
    heads = H // seqs
    cols = heads * HD
    hidden = w_expert.shape[2] // 3
    part = w_expert.shape[0]
    capacity = own * TOP * 17 // (16 * planes * seqs)
    scale = HD ** (-0.5)
    block_rows = min(512, seq)

    def to_inner(v):
        lead = v.shape[:-1]
        v = v.reshape(lead + (outer, planes, CORES, part))
        return jnp.swapaxes(v, -3, -2).reshape(lead + (width,))

    def to_outer(v):
        lead = v.shape[:-1]
        v = v.reshape(lead + (outer, CORES, planes, part))
        return jnp.swapaxes(v, -3, -2).reshape(lead + (width,))

    def gather_rows(block):
        return collect(collect(collect(block, "z"), "c"), "o").reshape((-1,) + block.shape[1:])

    def gather_sum(value):
        for axis in ("z", "s", "c", "o"):
            value = sum(gather_near(jnp.broadcast_to(value, (8, PAD)), axis))[0, 0]
        return value

    by_expert = w_expert.transpose(1, 0, 2)

    def expert_chunk(i, start=0):
        def piece_for(owner):
            return lax.dynamic_slice(by_expert, (owner, 0, i * hidden), (1, part, hidden))[0]

        return exchange(piece_for, "z", start)

    def gather_plane(blocks, start=0):
        chunk = in_order(blocks, "z", start).reshape(planes * part, hidden)
        chunk = lax.all_gather(chunk, ("s", "o", "c"), axis=0, tiled=True)
        return chunk.reshape(seqs, width, hidden)

    gate_blocks = expert_chunk(0)
    w_gate = gather_plane(gate_blocks)

    count = jnp.sum(valid_mask).astype(jnp.int32)
    digits = jnp.stack([count // 128, count % 128]).astype(bf16)
    extra = jnp.concatenate(
        [
            norm_gains,
            jnp.broadcast_to(digits[None], (rows_dev, 2)),
            jnp.zeros((rows_dev, PAD - 6), bf16),
        ],
        axis=1,
    )

    def columns_of(owner):
        picked = [
            lax.dynamic_slice_in_dim(w_attn, i * width + owner * cols, cols, 1) for i in range(4)
        ]
        return jnp.concatenate(picked + [extra], axis=1)

    mine = in_order(exchange(columns_of, "s"), "s", token(*gate_blocks))
    mine = mine.reshape(part, 4 * cols + PAD)
    w_in = gather_rows(jnp.concatenate([mine[:, : 3 * cols], mine[:, 4 * cols :]], axis=1))
    w_out = gather_rows(after(mine[:, 3 * cols : 4 * cols], w_in))
    side = w_in[:, 3 * cols : 3 * cols + 6].astype(f32).T
    gain_in, gain_mid = side[0], side[1]
    gain_q = lax.dynamic_slice_in_dim(to_outer(side[2]), rank * cols, cols, 0)
    gain_k = lax.dynamic_slice_in_dim(to_outer(side[3]), rank * cols, cols, 0)
    total_count = jnp.sum(side[4, ::rows_dev]) * 128.0 + jnp.sum(side[5, ::rows_dev])

    up_blocks = expert_chunk(1, token(w_in))

    routed = jnp.stack(
        gather_near(jnp.concatenate([routes.astype(f32), gate_weights], axis=1), "z")
    )
    route_all, gate_all = routed[..., :TOP].astype(jnp.int32), routed[..., TOP:]
    expert_ids = jnp.arange(seqs) * planes + plane
    match = route_all[:, :, None, :] == expert_ids[None, None, :, None]
    used = jnp.any(match, axis=-1)
    gate_of = jnp.sum(jnp.where(match, gate_all[:, :, None, :], 0.0), axis=-1)
    before = (jnp.arange(own)[:, None] > jnp.arange(own)[None, :]).astype(bf16)
    place = dot("tu,buk->btk", before, used.astype(bf16)).astype(jnp.int32)
    place = jnp.where(used, place, -1)
    taken = place.transpose(0, 2, 1)[:, :, None, :] == jnp.arange(capacity)[None, None, :, None]
    choose = taken.astype(bf16)
    gate_slot = jnp.sum(jnp.where(taken, gate_of.transpose(0, 2, 1)[:, :, None, :], 0.0), axis=-1)
    gate_slot = gate_slot.transpose(1, 0, 2).reshape(seqs, planes * capacity, 1)

    def dispatch(rows_in):
        spread = dot("bkjt,btd->kbjd", choose, rows_in)
        return spread.reshape(seqs, planes * capacity, width)

    def combine(rows_out, *others):
        rows_out = rows_out.reshape(seqs, planes, capacity, width)
        partial = dot("bkjt,kbjd->btd", choose, rows_out).astype(bf16)
        got = [partial[0]] + [send(partial[k], "z", k) for k in range(1, planes)]
        if others:
            got[0] = after(got[0], *others)
        return sum(piece.astype(f32) for piece in got)

    inputs = to_inner(tokens)
    seq_tokens = collect(inputs, "s").reshape(seq, width).astype(f32)
    normed_in = (seq_tokens * rms_factor(seq_tokens) * gain_in).astype(bf16)
    inputs = inputs.astype(f32)
    projected = jnp.dot(normed_in, w_in, preferred_element_type=f32)
    query_raw = projected[:, :cols]
    key_raw = projected[:, cols : 2 * cols]
    valued = projected[:, 2 * cols : 3 * cols].astype(bf16).reshape(seq, heads, HD)

    def over_heads(first, second):
        pair = jnp.stack([jnp.sum(first, axis=-1), jnp.sum(second, axis=-1)])
        pair = sum(gather_near(pair, "s")) / width
        return pair[0][:, None], pair[1][:, None]

    q_mean, k_mean = over_heads(query_raw * query_raw, key_raw * key_raw)
    q_factor, k_factor = lax.rsqrt(q_mean + epsilon), lax.rsqrt(k_mean + epsilon)
    cosine, sine = rope_tables(seq)

    def rope(raw, factor, gain):
        cube = (raw * factor * gain).reshape(seq, heads, HD)
        return (cube * cosine + rotate_half(cube) * sine).astype(bf16)

    query, keyed = rope(query_raw, q_factor, gain_q), rope(key_raw, k_factor, gain_k)
    query = after(query, w_gate)
    attended, log_total = attend_forward(query, keyed, valued, segment, block_rows, scale)
    attended = after(attended, *up_blocks)
    w_up = gather_plane(up_blocks, token(attended))
    down_blocks = expert_chunk(2, token(attended))
    attn_out = dot("tc,dc->td", attended, w_out).astype(bf16)
    residual = inputs + exchange_sum(attn_out.reshape(seqs, own, width), "s")

    residual = after(residual, *down_blocks)
    w_down = gather_plane(down_blocks, token(residual))

    normed_mid = (residual * rms_factor(residual) * gain_mid).astype(bf16)
    rows_in = dispatch(after(jnp.stack(gather_near(normed_mid, "z")), w_up)).astype(bf16)
    gate_pre = dot("krd,kdf->krf", rows_in, w_gate)
    up_pre = dot("krd,kdf->krf", rows_in, w_up)
    activated = (jax.nn.silu(gate_pre) * up_pre).astype(bf16)
    expert_out = (dot("krf,kdf->krd", activated, w_down) * gate_slot).astype(bf16)
    final_out = residual + combine(expert_out)

    valid_f = valid_mask.astype(f32)[:, None]
    difference = final_out - to_inner(teacher).astype(f32)
    squared = jnp.sum(valid_f * difference * difference)
    squared = gather_sum(squared)
    loss_value = squared / (total_count * width)
    grad_out = (
        to_inner(cotangent).astype(f32) + 2.0 / (total_count * width) * valid_f * difference
    )

    grad_rows = dispatch(jnp.stack(gather_near(grad_out.astype(bf16), "z")))
    grad_rows = (grad_rows * gate_slot).astype(bf16)

    def scatter_expert(grad):
        grad = grad.reshape(seqs * width, hidden)
        grad = lax.psum_scatter(grad, ("s", "o", "c"), scatter_dimension=0, tiled=True)
        return grad.reshape(planes, part, hidden)

    def to_owners(grad, start=0):
        def piece_for(owner):
            return lax.dynamic_index_in_dim(grad, owner, 0, keepdims=False)

        return exchange(piece_for, "z", start)

    grad_w_down = scatter_expert(dot("krd,krf->kdf", grad_rows, activated).astype(bf16))
    grad_act = dot("krd,kdf->krf", grad_rows, w_down)
    sigmoid = jax.nn.sigmoid(gate_pre)
    grad_gate = (grad_act * up_pre * sigmoid * (1.0 + gate_pre * (1.0 - sigmoid))).astype(bf16)
    grad_up = (grad_act * gate_pre * sigmoid).astype(bf16)
    back_rows = dot("krf,kdf->krd", grad_gate, w_gate) + dot("krf,kdf->krd", grad_up, w_up)
    grad_w_gate = dot("krd,krf->kdf", rows_in, grad_gate).astype(bf16)
    grad_w_up = dot("krd,krf->kdf", rows_in, grad_up).astype(bf16)
    grad_mid = combine(back_rows.astype(bf16), grad_w_gate, grad_w_up)
    grad_w_gate, grad_w_up = scatter_expert(grad_w_gate), scatter_expert(grad_w_up)
    down_part = to_owners(grad_w_down, token(grad_mid))
    gate_part = to_owners(grad_w_gate)
    up_part = to_owners(grad_w_up)

    grad_resid_norm, gain_mid_grad = norm_back(residual, gain_mid, grad_mid)
    grad_resid = grad_out + grad_resid_norm

    def scatter_rows(grad):
        grad = grad.astype(bf16)
        return lax.psum_scatter(grad, ("o", "c", "z"), scatter_dimension=0, tiled=True)

    grad_attn_out = collect(grad_resid.astype(bf16), "s").reshape(seq, width)
    grad_w_out = scatter_rows(dot("td,tc->dc", grad_attn_out, attended))
    grad_attn_out = after(grad_attn_out, *down_part)
    grad_heads = jnp.dot(grad_attn_out, w_out, preferred_element_type=f32).astype(bf16)
    grad_q, grad_k, grad_v = attend_backward(
        query,
        keyed,
        valued,
        segment,
        log_total,
        grad_heads.reshape(seq, heads, HD),
        block_rows,
        scale,
    )

    def unrotate(grad):
        grad = grad.astype(bf16).astype(f32)
        return (grad * cosine + rotate_back(grad * sine)).reshape(seq, cols)

    down_part = in_order(down_part, "z", token(grad_q))
    grad_q = after(grad_q, *gate_part)
    grad_q, grad_k = unrotate(grad_q), unrotate(grad_k)
    q_normed, k_normed = query_raw * q_factor, key_raw * k_factor
    gain_q_grad = jnp.sum(grad_q * q_normed, axis=0)
    gain_k_grad = jnp.sum(grad_k * k_normed, axis=0)
    grad_q, grad_k = grad_q * gain_q, grad_k * gain_k
    q_inner, k_inner = over_heads(grad_q * q_normed, grad_k * k_normed)
    grad_q = q_factor * (grad_q - q_normed * q_inner)
    grad_k = k_factor * (grad_k - k_normed * k_inner)
    grad_proj = jnp.concatenate(
        [grad_q.astype(bf16), grad_k.astype(bf16), grad_v.reshape(seq, cols).astype(bf16)], axis=1
    )
    gate_part = in_order(gate_part, "z", token(grad_proj))
    grad_padded = jnp.concatenate([grad_proj, jnp.zeros((seq, PAD), bf16)], axis=1)
    grad_normed = dot("tc,dc->td", grad_padded, w_in).astype(bf16)
    grad_normed = exchange_sum(grad_normed.reshape(seqs, own, width), "s")
    grad_w_qkv = scatter_rows(
        dot("td,tc->dc", normed_in, grad_proj)
    )
    grad_in_norm, gain_in_grad = norm_back(inputs, gain_in, grad_normed)
    grad_tokens = to_outer(grad_resid + grad_in_norm)

    def widen(local):
        full = jnp.zeros((width,), f32)
        return to_inner(lax.dynamic_update_slice_in_dim(full, local, rank * cols, 0))

    gains = jnp.stack([gain_in_grad, gain_mid_grad, widen(gain_q_grad), widen(gain_k_grad)])
    for axis in ("z", "c", "s", "o"):
        gains = sum(gather_near(gains, axis))
    row = (lax.axis_index(("o", "c", "z")) * seqs + rank) * rows_dev
    grad_gains = lax.dynamic_slice_in_dim(gains, row, rows_dev, 1).T

    def own_rows(grad):
        grad = grad.reshape(seqs, rows_dev, grad.shape[1])
        got = exchange(lambda i: lax.dynamic_index_in_dim(grad, i, 0, keepdims=False), "s")
        return in_order(got, "s").astype(f32)

    qkv_rows, out_rows = own_rows(grad_w_qkv), own_rows(grad_w_out)
    grad_attn = jnp.concatenate(
        [qkv_rows[s, :, i * cols : (i + 1) * cols] for i in range(3) for s in range(seqs)]
        + [out_rows[s] for s in range(seqs)],
        axis=1,
    )
    up_part = in_order(up_part, "z")
    grad_expert = jnp.concatenate([gate_part, up_part, down_part], axis=2)
    grad_expert = grad_expert.astype(f32).transpose(1, 0, 2)
    return (
        to_outer(final_out).astype(bf16),
        loss_value,
        grad_tokens,
        grad_attn,
        grad_gains,
        grad_expert,
    )


def solution(mesh):
    fsdp, seqs = mesh.shape["fsdp"], mesh.shape["sp"]

    def whole(*arrays):
        planes = arrays[3].shape[1] // seqs
        outer = fsdp // (planes * CORES)
        inner = Mesh(mesh.devices.reshape(outer, planes, CORES, seqs), ("o", "z", "c", "s"))
        every = ("o", "z", "c", "s")
        rows = P(every, None)
        experts = P(("o", "z", "c"), "s", None)
        return jax.shard_map(
            shards,
            mesh=inner,
            in_specs=(
                rows,
                rows,
                rows,
                experts,
                rows,
                rows,
                P(("o", "z", "c")),
                P(every),
                rows,
                rows,
            ),
            out_specs=(rows, P(), rows, rows, rows, experts),
            check_vma=False,
        )(*arrays)

    return whole
```

```python
import jax
import jax.numpy as jnp
from jax import lax
from jax.sharding import Mesh, PartitionSpec as P

H = 16
HD = 128
TOP = 8
CORES = 2
PAD = 128

epsilon = 1e-05
masked = -1e30
f32 = jnp.float32
bf16 = jnp.bfloat16


def send(block, axis, step):
    size = lax.axis_size(axis)
    return lax.ppermute(block, axis, [(i, i ^ step) for i in range(size)])


def gather_near(block, axis):
    return [block] + [send(block, axis, k) for k in range(1, lax.axis_size(axis))]


def in_order(blocks, axis, start=0):
    rank = lax.axis_index(axis)
    if len(blocks) == 1:
        return blocks[0][None]
    stacked = jnp.zeros((len(blocks),) + blocks[0].shape, blocks[0].dtype)
    for k, block in enumerate(blocks):
        stacked = lax.dynamic_update_index_in_dim(stacked, block, (rank ^ k) + start, 0)
    return stacked


def collect(block, axis):
    return in_order(gather_near(block, axis), axis)


def exchange(piece_for, axis, start=0):
    rank, size = lax.axis_index(axis) + start, lax.axis_size(axis)
    return [piece_for(rank)] + [send(piece_for(rank ^ k), axis, k) for k in range(1, size)]


def exchange_sum(pieces, axis):
    got = exchange(lambda i: lax.dynamic_index_in_dim(pieces, i, 0, keepdims=False), axis)
    return sum(piece.astype(f32) for piece in got)


def token(*values):
    firsts = [value[(slice(0, 1),) * value.ndim].reshape(()).astype(f32) for value in values]
    total = sum(firsts)
    return (total != total).astype(jnp.int32)


def after(value, *others):
    return value + token(*others).astype(value.dtype)


def rms_factor(values):
    return lax.rsqrt(jnp.mean(values * values, axis=-1, keepdims=True) + epsilon)


def norm_back(values, gain_vec, grad_in):
    factor = rms_factor(values)
    normed = values * factor
    gain_grad = jnp.sum(grad_in * normed, axis=0)
    inner = grad_in * gain_vec
    grad = factor * (inner - normed * jnp.mean(inner * normed, axis=-1, keepdims=True))
    return grad, gain_grad


def rope_tables(rows):
    inverse = 10000.0 ** (-(jnp.arange(HD // 2).astype(f32) * 2.0 / HD))
    angles = jnp.arange(rows).astype(f32)[:, None] * inverse[None, :]
    cosine = jnp.concatenate([jnp.cos(angles), jnp.cos(angles)], axis=-1)
    sine = jnp.concatenate([jnp.sin(angles), jnp.sin(angles)], axis=-1)
    return cosine[:, None, :], sine[:, None, :]


def rotate_half(values):
    half = values.shape[-1] // 2
    return jnp.concatenate([-values[..., half:], values[..., :half]], axis=-1)


def rotate_back(values):
    half = values.shape[-1] // 2
    return jnp.concatenate([values[..., half:], -values[..., :half]], axis=-1)


def block_scores(query, keyed, segment, block_index, rows, scale):
    start = block_index * rows
    q_block = lax.dynamic_slice_in_dim(query, start, rows, 0)
    q_segment = lax.dynamic_slice_in_dim(segment, start, rows, 0)
    q_places = start + jnp.arange(rows)
    k_places = jnp.arange(keyed.shape[0])
    allowed = (q_segment[:, None] == segment[None, :]) & (q_places[:, None] >= k_places[None, :])
    scores = jnp.einsum("qhd,khd->hqk", q_block, keyed, preferred_element_type=f32) * scale
    return q_block, jnp.where(allowed[None], scores, masked)


def attend_forward(query, keyed, valued, segment, rows, scale):
    blocks = keyed.shape[0] // rows

    def one_block(block_index):
        q_block, scores = block_scores(query, keyed, segment, block_index, rows, scale)
        row_top = jnp.max(scores, axis=-1, keepdims=True)
        exp_scores = jnp.exp(scores - row_top)
        row_total = jnp.sum(exp_scores, axis=-1, keepdims=True)
        weights = (exp_scores / row_total).astype(bf16)
        out = jnp.einsum("hqk,khd->qhd", weights, valued, preferred_element_type=f32)
        return out.astype(bf16), (row_top + jnp.log(row_total))[..., 0]

    outputs, log_total = lax.map(one_block, jnp.arange(blocks))
    return outputs.reshape(keyed.shape[0], -1), log_total


def attend_backward(query, keyed, valued, segment, log_total, grad_heads, rows, scale):
    blocks = keyed.shape[0] // rows

    def one_block(carry, pieces):
        grad_k, grad_v = carry
        block_index, block_total = pieces
        q_block, scores = block_scores(query, keyed, segment, block_index, rows, scale)
        probs = jnp.exp(scores - block_total[:, :, None])
        grad_block = lax.dynamic_slice_in_dim(grad_heads, block_index * rows, rows, 0)
        grad_v = grad_v + jnp.einsum(
            "hqk,qhd->khd", probs.astype(bf16), grad_block, preferred_element_type=f32
        )
        grad_probs = jnp.einsum("qhd,khd->hqk", grad_block, valued, preferred_element_type=f32)
        inner = jnp.sum(probs * grad_probs, axis=-1, keepdims=True)
        grad_scores = (probs * (grad_probs - inner)).astype(bf16)
        grad_q = jnp.einsum("hqk,khd->qhd", grad_scores, keyed, preferred_element_type=f32) * scale
        grad_k = (
            grad_k
            + jnp.einsum("hqk,qhd->khd", grad_scores, q_block, preferred_element_type=f32) * scale
        )
        return (grad_k, grad_v), grad_q

    initial = jnp.zeros(keyed.shape, f32)
    (grad_k, grad_v), grad_q = lax.scan(
        one_block, (initial, initial), (jnp.arange(blocks), log_total)
    )
    return grad_q.reshape(keyed.shape), grad_k, grad_v


def dot(spec, left, right):
    return jnp.einsum(spec, left, right, preferred_element_type=f32)


def shards(
    tokens,
    w_attn,
    norm_gains,
    w_expert,
    gate_weights,
    routes,
    segment,
    valid_mask,
    teacher,
    cotangent,
):
    outer, planes, seqs = lax.axis_size("o"), lax.axis_size("z"), lax.axis_size("s")
    plane, rank = lax.axis_index("z"), lax.axis_index("s")
    own, width = tokens.shape
    rows_dev = w_attn.shape[0]
    seq = own * seqs
    heads = H // seqs
    cols = heads * HD
    hidden = w_expert.shape[2] // 3
    part = w_expert.shape[0]
    capacity = own * TOP * 17 // (16 * planes * seqs)
    scale = HD ** (-0.5)
    block_rows = min(512, seq)

    def to_inner(v):
        lead = v.shape[:-1]
        v = v.reshape(lead + (outer * planes, CORES, part))
        return jnp.swapaxes(v, -3, -2).reshape(lead + (width,))

    def to_outer(v):
        lead = v.shape[:-1]
        v = v.reshape(lead + (CORES, outer * planes, part))
        return jnp.swapaxes(v, -3, -2).reshape(lead + (width,))

    first_core = lax.axis_index("c") == 0

    def halves(v):
        low, high = v[..., : width // 2], v[..., width // 2 :]
        return jnp.where(first_core, low, high), jnp.where(first_core, high, low)

    def whole_of(mine, other, axis):
        low, high = jnp.where(first_core, mine, other), jnp.where(first_core, other, mine)
        return jnp.concatenate([low, high], axis=axis)

    def stack_rows(blocks, start=0):
        rows = in_order(blocks, "z", start)
        return collect(rows, "o").reshape((width // 2,) + rows.shape[2:])

    def sum_rows(grad):
        count = grad.shape[1]
        grad = exchange_sum(grad.reshape(CORES, width // 2, count), "c").astype(bf16)
        if outer > 1:
            grad = exchange_sum(grad.reshape(outer, planes * part, count), "o").astype(bf16)
        return exchange_sum(grad.reshape(planes, part, count), "z")

    def gather_sum(value):
        for axis in ("z", "s", "c", "o"):
            value = sum(gather_near(jnp.broadcast_to(value, (8, PAD)), axis))[0, 0]
        return value

    by_expert = w_expert.transpose(1, 0, 2)

    def expert_chunk(i, start=0):
        def piece_for(owner):
            return lax.dynamic_slice(by_expert, (owner, 0, i * hidden), (1, part, hidden))[0]

        return exchange(piece_for, "z", start)

    def gather_plane(ready):
        chunk = ready.reshape(planes * part, hidden)
        chunk = lax.all_gather(chunk, ("s", "c", "o"), axis=0, tiled=True)
        return chunk.reshape(seqs, width, hidden)

    count = jnp.sum(valid_mask).astype(jnp.int32)
    digits = jnp.stack([count // 128, count % 128]).astype(bf16)
    extra = jnp.concatenate(
        [
            norm_gains,
            jnp.broadcast_to(digits[None], (rows_dev, 2)),
            jnp.zeros((rows_dev, PAD - 6), bf16),
        ],
        axis=1,
    )

    def columns_of(owner):
        picked = [
            lax.dynamic_slice_in_dim(w_attn, i * width + owner * cols, cols, 1) for i in range(4)
        ]
        return jnp.concatenate(picked[:3] + [extra] + picked[3:], axis=1)

    mine_blocks = exchange(columns_of, "s")
    gate_blocks = expert_chunk(0)
    inputs = to_inner(tokens)
    token_blocks = gather_near(inputs, "s")
    inputs = inputs.astype(f32)

    mine = in_order(mine_blocks, "s").reshape(part, 4 * cols + PAD)
    in_blocks = gather_near(mine[:, : 3 * cols + PAD], "z")
    gate_ready = in_order(gate_blocks, "z", token(mine))
    w_gate = gather_plane(gate_ready)
    seq_tokens = in_order(token_blocks, "s", token(gate_ready)).reshape(seq, width).astype(f32)
    seq_factor = rms_factor(seq_tokens)
    w_in = stack_rows(in_blocks, token(seq_factor))
    w_in_other = send(w_in, "c", 1)
    up_blocks = expert_chunk(1, token(w_in))

    side = whole_of(w_in[:, 3 * cols :], w_in_other[:, 3 * cols :], 0)[:, :6].astype(f32).T
    gain_in, gain_mid = side[0], side[1]
    gain_q = lax.dynamic_slice_in_dim(to_outer(side[2]), rank * cols, cols, 0)
    gain_k = lax.dynamic_slice_in_dim(to_outer(side[3]), rank * cols, cols, 0)
    total_count = jnp.sum(side[4, ::rows_dev]) * 128.0 + jnp.sum(side[5, ::rows_dev])

    routed = jnp.stack(
        gather_near(jnp.concatenate([routes.astype(f32), gate_weights], axis=1), "z")
    )
    route_all, gate_all = routed[..., :TOP].astype(jnp.int32), routed[..., TOP:]
    expert_ids = jnp.arange(seqs) * planes + plane
    match = route_all[:, :, None, :] == expert_ids[None, None, :, None]
    used = jnp.any(match, axis=-1)
    gate_of = jnp.sum(jnp.where(match, gate_all[:, :, None, :], 0.0), axis=-1)
    before = (jnp.arange(own)[:, None] > jnp.arange(own)[None, :]).astype(bf16)
    place = dot("tu,buk->btk", before, used.astype(bf16)).astype(jnp.int32)
    place = jnp.where(used, place, -1)
    taken = place.transpose(0, 2, 1)[:, :, None, :] == jnp.arange(capacity)[None, None, :, None]
    choose = taken.astype(bf16)
    gate_slot = jnp.sum(jnp.where(taken, gate_of.transpose(0, 2, 1)[:, :, None, :], 0.0), axis=-1)
    gate_slot = gate_slot.transpose(1, 0, 2).reshape(seqs, planes * capacity, 1)

    def dispatch(rows_in):
        spread = dot("bkjt,btd->kbjd", choose, rows_in)
        return spread.reshape(seqs, planes * capacity, width)

    def combine_rows(rows_out):
        rows_out = rows_out.reshape(seqs, planes, capacity, width)
        return dot("bkjt,kbjd->btd", choose, rows_out).astype(bf16)

    def send_back(partial, *others):
        got = [partial[0]] + [send(partial[k], "z", k) for k in range(1, planes)]
        if others:
            got[0] = after(got[0], *others)
        return sum(piece.astype(f32) for piece in got)

    normed_in = (seq_tokens * seq_factor * gain_in).astype(bf16)
    normed_mine, normed_other = halves(normed_in)
    projected = jnp.dot(normed_mine, w_in, preferred_element_type=f32) + jnp.dot(
        normed_other, w_in_other, preferred_element_type=f32
    )
    query_raw = projected[:, :cols]
    key_raw = projected[:, cols : 2 * cols]
    valued = projected[:, 2 * cols : 3 * cols].astype(bf16).reshape(seq, heads, HD)

    def over_heads(first, second):
        pair = jnp.stack([jnp.sum(first, axis=-1), jnp.sum(second, axis=-1)])
        pair = sum(gather_near(pair, "s")) / width
        return pair[0][:, None], pair[1][:, None]

    q_mean, k_mean = over_heads(query_raw * query_raw, key_raw * key_raw)
    q_factor, k_factor = lax.rsqrt(q_mean + epsilon), lax.rsqrt(k_mean + epsilon)
    cosine, sine = rope_tables(seq)

    def rope(raw, factor, gain):
        cube = (raw * factor * gain).reshape(seq, heads, HD)
        return (cube * cosine + rotate_half(cube) * sine).astype(bf16)

    query, keyed = rope(query_raw, q_factor, gain_q), rope(key_raw, k_factor, gain_k)
    query = after(query, w_gate)
    up_ready = in_order(up_blocks, "z", token(keyed))
    keyed = after(keyed, up_ready)
    w_up = gather_plane(up_ready)
    out_blocks = gather_near(after(mine[:, 3 * cols + PAD :], up_ready), "z")
    attended, log_total = attend_forward(query, keyed, valued, segment, block_rows, scale)
    w_out = collect(stack_rows(out_blocks, token(attended)), "c").reshape(width, cols)
    down_blocks = expert_chunk(2, token(attended))
    attn_out = dot("tc,dc->td", attended, w_out).astype(bf16)
    residual = inputs + exchange_sum(attn_out.reshape(seqs, own, width), "s")
    down_ready = in_order(down_blocks, "z", token(residual))
    residual = after(residual, down_ready)
    w_down = gather_plane(down_ready)

    normed_mid = (residual * rms_factor(residual) * gain_mid).astype(bf16)
    rows_in = dispatch(after(jnp.stack(gather_near(normed_mid, "z")), w_up)).astype(bf16)
    gate_pre = dot("krd,kdf->krf", rows_in, w_gate)
    up_pre = dot("krd,kdf->krf", rows_in, w_up)
    activated = (jax.nn.silu(gate_pre) * up_pre).astype(bf16)
    expert_out = (dot("krf,kdf->krd", activated, w_down) * gate_slot).astype(bf16)
    final_out = residual + send_back(combine_rows(expert_out))

    valid_f = valid_mask.astype(f32)[:, None]
    difference = final_out - to_inner(teacher).astype(f32)
    squared = jnp.sum(valid_f * difference * difference)
    squared = gather_sum(squared)
    loss_value = squared / (total_count * width)
    grad_out = (
        to_inner(cotangent).astype(f32) + 2.0 / (total_count * width) * valid_f * difference
    )

    grad_rows = dispatch(jnp.stack(gather_near(grad_out.astype(bf16), "z")))
    grad_rows = (grad_rows * gate_slot).astype(bf16)

    def scatter_expert(grad):
        grad = grad.reshape(seqs * width, hidden)
        grad = lax.psum_scatter(grad, ("s", "c", "o"), scatter_dimension=0, tiled=True)
        return grad.reshape(planes, part, hidden)

    def to_owners(grad, start=0):
        def piece_for(owner):
            return lax.dynamic_index_in_dim(grad, owner, 0, keepdims=False)

        return exchange(piece_for, "z", start)

    grad_w_down = scatter_expert(dot("krd,krf->kdf", grad_rows, activated).astype(bf16))
    grad_act = dot("krd,kdf->krf", grad_rows, w_down)
    sigmoid = jax.nn.sigmoid(gate_pre)
    grad_gate = (grad_act * up_pre * sigmoid * (1.0 + gate_pre * (1.0 - sigmoid))).astype(bf16)
    grad_up = (grad_act * gate_pre * sigmoid).astype(bf16)
    back_rows = dot("krf,kdf->krd", grad_gate, w_gate) + dot("krf,kdf->krd", grad_up, w_up)
    back_rows = combine_rows(back_rows.astype(bf16))
    grad_gate, grad_up = after(grad_gate, back_rows), after(grad_up, back_rows)
    grad_w_gate = dot("krd,krf->kdf", rows_in, grad_gate).astype(bf16)
    grad_w_up = dot("krd,krf->kdf", rows_in, grad_up).astype(bf16)
    grad_mid = send_back(back_rows, grad_w_gate, grad_w_up)
    grad_w_gate, grad_w_up = scatter_expert(grad_w_gate), scatter_expert(grad_w_up)
    down_blocks = to_owners(grad_w_down, token(grad_mid))
    gate_blocks = to_owners(grad_w_gate)
    grad_resid_norm, gain_mid_grad = norm_back(residual, gain_mid, grad_mid)
    grad_resid = grad_out + grad_resid_norm

    grad_attn_out = collect(grad_resid.astype(bf16), "s").reshape(seq, width)
    grad_w_out = sum_rows(dot("td,tc->dc", grad_attn_out, attended).astype(bf16))
    grad_heads = jnp.dot(grad_attn_out, w_out, preferred_element_type=f32).astype(bf16)
    grad_q, grad_k, grad_v = attend_backward(
        query,
        keyed,
        valued,
        segment,
        log_total,
        grad_heads.reshape(seq, heads, HD),
        block_rows,
        scale,
    )

    def unrotate(grad):
        grad = grad.astype(bf16).astype(f32)
        return (grad * cosine + rotate_back(grad * sine)).reshape(seq, cols)

    down_ready = in_order(down_blocks, "z", token(grad_q))
    grad_q = after(grad_q, down_ready)
    grad_q, grad_k = unrotate(grad_q), unrotate(grad_k)
    q_normed, k_normed = query_raw * q_factor, key_raw * k_factor
    gain_q_grad = jnp.sum(grad_q * q_normed, axis=0)
    gain_k_grad = jnp.sum(grad_k * k_normed, axis=0)
    grad_q, grad_k = grad_q * gain_q, grad_k * gain_k
    q_inner, k_inner = over_heads(grad_q * q_normed, grad_k * k_normed)
    grad_q = q_factor * (grad_q - q_normed * q_inner)
    grad_k = k_factor * (grad_k - k_normed * k_inner)
    grad_proj = jnp.concatenate(
        [grad_q.astype(bf16), grad_k.astype(bf16), grad_v.reshape(seq, cols).astype(bf16)], axis=1
    )
    grad_padded = jnp.concatenate([grad_proj, jnp.zeros((seq, PAD), bf16)], axis=1)

    def back_half(weight):
        grad = dot("tc,dc->td", grad_padded, weight).astype(bf16)
        return exchange_sum(grad.reshape(seqs, own, width // 2), "s")

    grad_normed = whole_of(back_half(w_in), back_half(w_in_other), 1)
    grad_w_qkv = dot("td,tc->dc", normed_in, grad_proj).astype(bf16)
    gate_ready = in_order(gate_blocks, "z", token(grad_w_qkv))
    grad_w_qkv = sum_rows(grad_w_qkv)
    up_blocks = to_owners(grad_w_up, token(grad_w_qkv))
    grad_in_norm, gain_in_grad = norm_back(inputs, gain_in, grad_normed)
    grad_tokens = to_outer(grad_resid + grad_in_norm)

    def widen(local):
        full = jnp.zeros((width,), f32)
        return to_inner(lax.dynamic_update_slice_in_dim(full, local, rank * cols, 0))

    gains = jnp.stack([gain_in_grad, gain_mid_grad, widen(gain_q_grad), widen(gain_k_grad)])
    for axis in ("z", "c", "s", "o"):
        gains = sum(gather_near(gains, axis))
    row = (lax.axis_index(("c", "o", "z")) * seqs + rank) * rows_dev
    grad_gains = lax.dynamic_slice_in_dim(gains, row, rows_dev, 1).T

    def own_rows(grad):
        grad = grad.astype(bf16).reshape(seqs, rows_dev, grad.shape[1])
        got = exchange(lambda i: lax.dynamic_index_in_dim(grad, i, 0, keepdims=False), "s")
        return in_order(got, "s").astype(f32)

    qkv_rows, out_rows = own_rows(grad_w_qkv), own_rows(grad_w_out)
    grad_attn = jnp.concatenate(
        [qkv_rows[s, :, i * cols : (i + 1) * cols] for i in range(3) for s in range(seqs)]
        + [out_rows[s] for s in range(seqs)],
        axis=1,
    )
    up_ready = in_order(up_blocks, "z")
    grad_expert = jnp.concatenate([gate_ready, up_ready, down_ready], axis=2)
    grad_expert = grad_expert.astype(f32).transpose(1, 0, 2)
    return (
        to_outer(final_out).astype(bf16),
        loss_value,
        grad_tokens,
        grad_attn,
        grad_gains,
        grad_expert,
    )


def solution(mesh):
    fsdp, seqs = mesh.shape["fsdp"], mesh.shape["sp"]

    def whole(*arrays):
        planes = arrays[3].shape[1] // seqs
        outer = fsdp // (planes * CORES)
        inner = Mesh(mesh.devices.reshape(outer, planes, CORES, seqs), ("o", "z", "c", "s"))
        every = ("o", "z", "c", "s")
        rows = P(every, None)
        experts = P(("o", "z", "c"), "s", None)
        return jax.shard_map(
            shards,
            mesh=inner,
            in_specs=(
                rows,
                rows,
                rows,
                experts,
                rows,
                rows,
                P(("o", "z", "c")),
                P(every),
                rows,
                rows,
            ),
            out_specs=(rows, P(), rows, rows, rows, experts),
            check_vma=False,
        )(*arrays)

    return whole
```

```python
import functools

import jax
import jax.numpy as jnp
from jax import lax
from jax.experimental import pallas as pl
from jax.experimental.pallas import tpu as pltpu
from jax.sharding import Mesh, PartitionSpec as P

H = 16
HD = 128
TOP = 8
CORES = 2
PAD = 128

epsilon = 1e-05
masked = -1e30
f32 = jnp.float32
bf16 = jnp.bfloat16


def send(block, axis, step):
    size = lax.axis_size(axis)
    return lax.ppermute(block, axis, [(i, i ^ step) for i in range(size)])


def gather_near(block, axis):
    return [block] + [send(block, axis, k) for k in range(1, lax.axis_size(axis))]


def in_order(blocks, axis, start=0):
    rank = lax.axis_index(axis)
    if len(blocks) == 1:
        return blocks[0][None]
    stacked = jnp.zeros((len(blocks),) + blocks[0].shape, blocks[0].dtype)
    for k, block in enumerate(blocks):
        stacked = lax.dynamic_update_index_in_dim(stacked, block, (rank ^ k) + start, 0)
    return stacked


def collect(block, axis):
    return in_order(gather_near(block, axis), axis)


def exchange(piece_for, axis, start=0):
    rank, size = lax.axis_index(axis) + start, lax.axis_size(axis)
    return [piece_for(rank)] + [send(piece_for(rank ^ k), axis, k) for k in range(1, size)]


def exchange_sum(pieces, axis):
    got = exchange(lambda i: lax.dynamic_index_in_dim(pieces, i, 0, keepdims=False), axis)
    return sum(piece.astype(f32) for piece in got)


def token(*values):
    firsts = [value[(slice(0, 1),) * value.ndim].reshape(()).astype(f32) for value in values]
    total = sum(firsts)
    return (total != total).astype(jnp.int32)


def after(value, *others):
    return value + token(*others).astype(value.dtype)


def rms_factor(values):
    return lax.rsqrt(jnp.mean(values * values, axis=-1, keepdims=True) + epsilon)


def norm_back(values, gain_vec, grad_in):
    factor = rms_factor(values)
    normed = values * factor
    gain_grad = jnp.sum(grad_in * normed, axis=0)
    inner = grad_in * gain_vec
    grad = factor * (inner - normed * jnp.mean(inner * normed, axis=-1, keepdims=True))
    return grad, gain_grad


def rope_tables(rows):
    inverse = 10000.0 ** (-(jnp.arange(HD // 2).astype(f32) * 2.0 / HD))
    angles = jnp.arange(rows).astype(f32)[:, None] * inverse[None, :]
    cosine = jnp.concatenate([jnp.cos(angles), jnp.cos(angles)], axis=-1)
    sine = jnp.concatenate([-jnp.sin(angles), jnp.sin(angles)], axis=-1)
    return cosine, sine


def mm(left, right, dims):
    return lax.dot_general(left, right, (dims, ((), ())), preferred_element_type=f32)


def masked_scores(query, keyed, seg_col, seg_row, first, scale):
    scores = mm(query, keyed, ((1,), (1,))) * scale
    rows = first + lax.broadcasted_iota(jnp.int32, scores.shape, 0)
    allowed = (rows >= lax.broadcasted_iota(jnp.int32, scores.shape, 1)) & (seg_col == seg_row)
    return jnp.where(allowed, scores, masked)


def attend_kernel(
    block,
    q_raw,
    k_raw,
    v_raw,
    q_mean,
    k_mean,
    gain_q,
    gain_k,
    cosine,
    sine,
    seg_col,
    seg_row,
    out,
    q_out,
    k_out,
    v_out,
    log_total,
):
    def rope(raw, mean, gain):
        values = raw[...] * lax.rsqrt(mean[...] + epsilon) * gain[...]
        turned = pltpu.roll(values, HD // 2, 1)
        return (values * cosine[...] + turned * sine[...]).astype(bf16)

    q_out[...] = rope(q_raw, q_mean, gain_q)
    k_out[...] = rope(k_raw, k_mean, gain_k)
    v_out[...] = v_raw[...].astype(bf16)
    for first in range(0, out.shape[0], block):
        last = first + block
        scores = masked_scores(
            q_out[first:last],
            k_out[:last],
            seg_col[first:last],
            seg_row[:, :last],
            first,
            HD**-0.5,
        )
        top = jnp.max(scores, axis=-1, keepdims=True)
        exps = jnp.exp(scores - top)
        total = jnp.sum(exps, axis=-1, keepdims=True)
        weights = (exps * (1.0 / total)).astype(bf16)
        out[first:last] = mm(weights, v_out[:last], ((1,), (0,))).astype(bf16)
        log_total[0, first:last] = top + jnp.log(total)


def attend_back_kernel(
    block,
    q_raw,
    k_raw,
    q_mean,
    k_mean,
    gain_q,
    gain_k,
    cosine,
    sine,
    seg_col,
    seg_row,
    query,
    keyed,
    valued,
    grad,
    log_total,
    grad_q,
    grad_k,
    grad_v,
    q_inner,
    k_inner,
    gain_q_grad,
    gain_k_grad,
    sum_q,
    sum_k,
    sum_v,
):
    scale = HD**-0.5
    sum_k[...] = jnp.zeros_like(sum_k)
    sum_v[...] = jnp.zeros_like(sum_v)
    for first in range(0, query.shape[0], block):
        last = first + block
        q_block, g_block = query[first:last], grad[first:last]
        scores = masked_scores(
            q_block, keyed[:last], seg_col[first:last], seg_row[:, :last], first, scale
        )
        probs = jnp.exp(scores - log_total[0, first:last])
        sum_v[:last] += mm(probs.astype(bf16), g_block, ((0,), (0,)))
        grad_probs = mm(g_block, valued[:last], ((1,), (1,)))
        inner = jnp.sum(probs * grad_probs, axis=-1, keepdims=True)
        grad_scores = (probs * (grad_probs - inner)).astype(bf16)
        sum_q[first:last] = mm(grad_scores, keyed[:last], ((1,), (0,))) * scale
        sum_k[:last] += mm(grad_scores, q_block, ((0,), (0,))) * scale
    grad_v[...] = sum_v[...].astype(bf16)

    def undo(total, raw, mean, gain, inner_out, gain_out, grad_out):
        low = total[...].astype(bf16).astype(f32)
        back = low * cosine[...] + pltpu.roll(low * sine[...], HD // 2, 1)
        normed = raw[...] * lax.rsqrt(mean[...] + epsilon)
        gain_out[...] = jnp.sum(back * normed, axis=0, keepdims=True)
        back = back * gain[...]
        grad_out[...] = back
        inner = jnp.sum(back * normed, axis=-1, keepdims=True)

        @pl.when(pl.program_id(0) == 0)
        def _():
            inner_out[...] = inner

        @pl.when(pl.program_id(0) > 0)
        def _():
            inner_out[...] += inner

    undo(sum_q, q_raw, q_mean, gain_q, q_inner, gain_q_grad, grad_q)
    undo(sum_k, k_raw, k_mean, gain_k, k_inner, gain_k_grad, grad_k)


def head_specs(seq, heads):
    column = pl.BlockSpec((seq, 1), lambda h: (0, 0))
    gain = pl.BlockSpec((1, HD), lambda h: (0, h))
    table = pl.BlockSpec((seq, HD), lambda h: (0, 0))
    return [column, column, gain, gain, table, table, column, pl.BlockSpec((1, seq), lambda h: (0, 0))]


def raw_spec(seq, heads, which):
    return pl.BlockSpec((seq, HD), lambda h: (0, which * heads + h))


def attend(projected, shared, heads):
    seq = projected.shape[0]
    block = min(256, seq)
    head = pl.BlockSpec((seq, HD), lambda h: (0, h))
    low = jax.ShapeDtypeStruct((seq, heads * HD), bf16)
    return pl.pallas_call(
        functools.partial(attend_kernel, block),
        grid=(heads,),
        in_specs=[raw_spec(seq, heads, i) for i in range(3)] + head_specs(seq, heads),
        out_specs=[head] * 4 + [pl.BlockSpec((1, seq, 1), lambda h: (h, 0, 0))],
        out_shape=[low] * 4 + [jax.ShapeDtypeStruct((heads, seq, 1), f32)],
        compiler_params=pltpu.CompilerParams(vmem_limit_bytes=48 * 2**20),
        cost_estimate=pl.CostEstimate(
            flops=heads * seq * seq * HD * 4,
            bytes_accessed=heads * seq * HD * 24,
            transcendentals=heads * seq * seq,
        ),
    )(projected, projected, projected, *shared)


def attend_back(projected, shared, query, keyed, valued, grad, log_total, heads):
    seq = projected.shape[0]
    block = min(256, seq)
    head = pl.BlockSpec((seq, HD), lambda h: (0, h))
    column = pl.BlockSpec((seq, 1), lambda h: (0, 0))
    gain = pl.BlockSpec((1, HD), lambda h: (0, h))
    wide = jax.ShapeDtypeStruct((seq, heads * HD), f32)
    return pl.pallas_call(
        functools.partial(attend_back_kernel, block),
        grid=(heads,),
        in_specs=[raw_spec(seq, heads, i) for i in range(2)]
        + head_specs(seq, heads)
        + [head] * 4
        + [pl.BlockSpec((1, seq, 1), lambda h: (h, 0, 0))],
        out_specs=[head] * 3 + [column] * 2 + [gain] * 2,
        out_shape=[wide, wide, jax.ShapeDtypeStruct((seq, heads * HD), bf16)]
        + [jax.ShapeDtypeStruct((seq, 1), f32)] * 2
        + [jax.ShapeDtypeStruct((1, heads * HD), f32)] * 2,
        scratch_shapes=[pltpu.VMEM((seq, HD), f32)] * 3,
        compiler_params=pltpu.CompilerParams(vmem_limit_bytes=48 * 2**20),
        cost_estimate=pl.CostEstimate(
            flops=heads * seq * seq * HD * 10,
            bytes_accessed=heads * seq * HD * 36,
            transcendentals=heads * seq * seq,
        ),
    )(projected, projected, *shared, query, keyed, valued, grad, log_total)


def dot(spec, left, right):
    return jnp.einsum(spec, left, right, preferred_element_type=f32)


def shards(
    tokens,
    w_attn,
    norm_gains,
    w_expert,
    gate_weights,
    routes,
    segment,
    valid_mask,
    teacher,
    cotangent,
):
    outer, planes, seqs = lax.axis_size("o"), lax.axis_size("z"), lax.axis_size("s")
    plane, rank = lax.axis_index("z"), lax.axis_index("s")
    own, width = tokens.shape
    rows_dev = w_attn.shape[0]
    seq = own * seqs
    heads = H // seqs
    cols = heads * HD
    hidden = w_expert.shape[2] // 3
    part = w_expert.shape[0]
    capacity = own * TOP * 17 // (16 * planes * seqs)
    scale = HD ** (-0.5)

    def to_inner(v):
        lead = v.shape[:-1]
        v = v.reshape(lead + (outer * planes, CORES, part))
        return jnp.swapaxes(v, -3, -2).reshape(lead + (width,))

    def to_outer(v):
        lead = v.shape[:-1]
        v = v.reshape(lead + (CORES, outer * planes, part))
        return jnp.swapaxes(v, -3, -2).reshape(lead + (width,))

    first_core = lax.axis_index("c") == 0

    def halves(v):
        low, high = v[..., : width // 2], v[..., width // 2 :]
        return jnp.where(first_core, low, high), jnp.where(first_core, high, low)

    def whole_of(mine, other, axis):
        low, high = jnp.where(first_core, mine, other), jnp.where(first_core, other, mine)
        return jnp.concatenate([low, high], axis=axis)

    def stack_rows(blocks, start=0):
        rows = in_order(blocks, "z", start)
        return collect(rows, "o").reshape((width // 2,) + rows.shape[2:])

    def sum_rows(grad):
        count = grad.shape[1]
        grad = exchange_sum(grad.reshape(CORES, width // 2, count), "c").astype(bf16)
        if outer > 1:
            grad = exchange_sum(grad.reshape(outer, planes * part, count), "o").astype(bf16)
        return exchange_sum(grad.reshape(planes, part, count), "z")

    def gather_sum(value):
        for axis in ("z", "s", "c", "o"):
            value = sum(gather_near(jnp.broadcast_to(value, (8, PAD)), axis))[0, 0]
        return value

    by_expert = w_expert.transpose(1, 0, 2)

    def expert_chunk(i, start=0):
        def piece_for(owner):
            return lax.dynamic_slice(by_expert, (owner, 0, i * hidden), (1, part, hidden))[0]

        return exchange(piece_for, "z", start)

    def gather_plane(ready):
        chunk = ready.reshape(planes * part, hidden)
        chunk = lax.all_gather(chunk, ("s", "c", "o"), axis=0, tiled=True)
        return chunk.reshape(seqs, width, hidden)

    count = jnp.sum(valid_mask).astype(jnp.int32)
    digits = jnp.stack([count // 128, count % 128]).astype(bf16)
    extra = jnp.concatenate(
        [
            norm_gains,
            jnp.broadcast_to(digits[None], (rows_dev, 2)),
            jnp.zeros((rows_dev, PAD - 6), bf16),
        ],
        axis=1,
    )

    def columns_of(owner):
        picked = [
            lax.dynamic_slice_in_dim(w_attn, i * width + owner * cols, cols, 1) for i in range(4)
        ]
        return jnp.concatenate(picked[:3] + [extra] + picked[3:], axis=1)

    mine_blocks = exchange(columns_of, "s")
    gate_blocks = expert_chunk(0)
    inputs = to_inner(tokens)
    token_blocks = gather_near(inputs, "s")
    inputs = inputs.astype(f32)

    mine = in_order(mine_blocks, "s").reshape(part, 4 * cols + PAD)
    in_blocks = gather_near(mine[:, : 3 * cols + PAD], "z")
    gate_ready = in_order(gate_blocks, "z", token(mine))
    w_gate = gather_plane(gate_ready)
    seq_tokens = in_order(token_blocks, "s", token(gate_ready)).reshape(seq, width).astype(f32)
    seq_factor = rms_factor(seq_tokens)
    w_in = stack_rows(in_blocks, token(seq_factor))
    w_in_other = send(w_in, "c", 1)
    up_blocks = expert_chunk(1, token(w_in))

    side = whole_of(w_in[:, 3 * cols :], w_in_other[:, 3 * cols :], 0)[:, :6].astype(f32).T
    gain_in, gain_mid = side[0], side[1]
    gain_q = lax.dynamic_slice_in_dim(to_outer(side[2]), rank * cols, cols, 0)
    gain_k = lax.dynamic_slice_in_dim(to_outer(side[3]), rank * cols, cols, 0)
    total_count = jnp.sum(side[4, ::rows_dev]) * 128.0 + jnp.sum(side[5, ::rows_dev])

    routed = jnp.stack(
        gather_near(jnp.concatenate([routes.astype(f32), gate_weights], axis=1), "z")
    )
    route_all, gate_all = routed[..., :TOP].astype(jnp.int32), routed[..., TOP:]
    expert_ids = jnp.arange(seqs) * planes + plane
    match = route_all[:, :, None, :] == expert_ids[None, None, :, None]
    used = jnp.any(match, axis=-1)
    gate_of = jnp.sum(jnp.where(match, gate_all[:, :, None, :], 0.0), axis=-1)
    before = (jnp.arange(own)[:, None] > jnp.arange(own)[None, :]).astype(bf16)
    place = dot("tu,buk->btk", before, used.astype(bf16)).astype(jnp.int32)
    place = jnp.where(used, place, -1)
    taken = place.transpose(0, 2, 1)[:, :, None, :] == jnp.arange(capacity)[None, None, :, None]
    choose = taken.astype(bf16)
    gate_slot = jnp.sum(jnp.where(taken, gate_of.transpose(0, 2, 1)[:, :, None, :], 0.0), axis=-1)
    gate_slot = gate_slot.transpose(1, 0, 2)

    groups = [[k for k in range(planes) if k % 2 == odd] for odd in range(2)]
    slots = capacity * planes // 2

    def pick(table, group, axis):
        return jnp.concatenate([lax.slice_in_dim(table, k, k + 1, axis=axis) for k in group], axis)

    chosen = [pick(choose, group, 0) for group in groups]
    weight_of = [pick(gate_slot, group, 1).reshape(seqs, slots, 1) for group in groups]

    def dispatch(i, blocks):
        spread = dot("bkjt,btd->kbjd", chosen[i], blocks)
        return spread.reshape(seqs, slots, width)

    def combine(i, rows_out):
        rows_out = rows_out.reshape(seqs, planes // 2, capacity, width)
        return dot("bkjt,kbjd->btd", chosen[i], rows_out).astype(bf16)

    def through_planes(block, work):
        near = [block] + [None] * (planes - 1)
        for k in groups[0][1:]:
            near[k] = send(block, "z", k)
        later = after(block, *[near[k] for k in groups[0][1:]])
        for k in groups[1]:
            near[k] = send(later, "z", k)
        first = work(0, jnp.stack([near[k] for k in groups[0]]))[0]
        got = [first[0]] + [send(first[i], "z", k) for i, k in enumerate(groups[0]) if k]
        second, halfway = work(1, after(jnp.stack([near[k] for k in groups[1]]), first[0]))
        base = after(total(got), halfway)
        second = after(second, base)
        return second, [base] + [send(second[i], "z", k) for i, k in enumerate(groups[1])]

    def total(pieces):
        return sum(piece.astype(f32) for piece in pieces)

    normed_in = (seq_tokens * seq_factor * gain_in).astype(bf16)
    normed_mine, normed_other = halves(normed_in)
    projected = jnp.dot(normed_mine, w_in, preferred_element_type=f32) + jnp.dot(
        normed_other, w_in_other, preferred_element_type=f32
    )
    query_raw = projected[:, :cols]
    key_raw = projected[:, cols : 2 * cols]

    def over_heads(first, second):
        pair = sum(gather_near(jnp.stack([first, second]), "s")) / width
        return pair[0][:, None], pair[1][:, None]

    q_mean, k_mean = over_heads(
        jnp.sum(query_raw * query_raw, axis=-1), jnp.sum(key_raw * key_raw, axis=-1)
    )
    up_ready = in_order(up_blocks, "z", token(projected))
    w_up = gather_plane(up_ready)
    out_blocks = gather_near(after(mine[:, 3 * cols + PAD :], up_ready), "z")
    cosine, sine = rope_tables(seq)
    shared = [
        after(q_mean, up_ready, w_gate),
        k_mean,
        gain_q[None],
        gain_k[None],
        cosine,
        sine,
        segment[:, None],
        segment[None],
    ]
    attended, query, keyed, valued, log_total = attend(projected, shared, heads)
    w_out = collect(stack_rows(out_blocks, token(attended)), "c").reshape(width, cols)
    down_blocks = expert_chunk(2, token(attended))
    attn_out = dot("tc,dc->td", attended, w_out).astype(bf16)
    residual = inputs + exchange_sum(attn_out.reshape(seqs, own, width), "s")
    down_ready = in_order(down_blocks, "z", token(residual))
    residual = after(residual, down_ready)
    w_down = gather_plane(down_ready)

    normed_mid = (residual * rms_factor(residual) * gain_mid).astype(bf16)
    kept = [None, None]

    def forward(i, blocks):
        rows_in = dispatch(i, blocks).astype(bf16)
        gate_pre = dot("krd,kdf->krf", rows_in, w_gate)
        up_pre = dot("krd,kdf->krf", rows_in, w_up)
        activated = (jax.nn.silu(gate_pre) * up_pre).astype(bf16)
        kept[i] = (rows_in, gate_pre, up_pre, activated)
        out = dot("krf,kdf->krd", activated, w_down) * weight_of[i]
        return combine(i, out.astype(bf16)), activated

    final_out = residual + total(through_planes(normed_mid, forward)[1])

    w_out_near = gather_near(after(w_out, kept[1][3]), "s")
    valid_f = valid_mask.astype(f32)[:, None]
    difference = final_out - to_inner(teacher).astype(f32)
    squared = jnp.sum(valid_f * difference * difference)
    squared = gather_sum(squared)
    loss_value = squared / (total_count * width)
    grad_out = (
        to_inner(cotangent).astype(f32) + 2.0 / (total_count * width) * valid_f * difference
    )

    def scatter_expert(grad):
        grad = grad.reshape(seqs * width, hidden)
        grad = lax.psum_scatter(grad, ("s", "c", "o"), scatter_dimension=0, tiled=True)
        return grad.reshape(planes, part, hidden)

    def to_owners(grad, start=0):
        def piece_for(owner):
            return lax.dynamic_index_in_dim(grad, owner, 0, keepdims=False)

        return exchange(piece_for, "z", start)

    grads = [None, None]

    def backward(i, blocks):
        gate_pre, up_pre = kept[i][1:3]
        grad_rows = (dispatch(i, blocks) * weight_of[i]).astype(bf16)
        grad_act = dot("krd,kdf->krf", grad_rows, w_down)
        sigmoid = jax.nn.sigmoid(gate_pre)
        grad_gate = grad_act * up_pre * sigmoid * (1.0 + gate_pre * (1.0 - sigmoid))
        grad_gate, grad_up = grad_gate.astype(bf16), (grad_act * gate_pre * sigmoid).astype(bf16)
        back = dot("krf,kdf->krd", grad_gate, w_gate) + dot("krf,kdf->krd", grad_up, w_up)
        grads[i] = (grad_rows, grad_gate, grad_up)
        return combine(i, back.astype(bf16)), grad_gate

    back_last, back_pieces = through_planes(grad_out.astype(bf16), backward)

    def both(table, which):
        return jnp.concatenate([table[0][which], table[1][which]], axis=1)

    rows_in, activated = both(kept, 0), both(kept, 3)
    grad_w_down = dot("krd,krf->kdf", both(grads, 0), activated).astype(bf16)
    grad_w_gate = dot("krd,krf->kdf", rows_in, after(both(grads, 1), back_last)).astype(bf16)
    grad_w_up = dot("krd,krf->kdf", rows_in, after(both(grads, 2), back_last)).astype(bf16)
    back_pieces[0] = after(back_pieces[0], grad_w_down, grad_w_gate)
    grad_mid = total(back_pieces)
    up_done = grad_w_up
    grad_w_down, grad_w_gate, grad_w_up = [
        scatter_expert(grad) for grad in (grad_w_down, grad_w_gate, grad_w_up)
    ]
    down_blocks = to_owners(grad_w_down, token(grad_mid))
    gate_blocks = to_owners(grad_w_gate)
    grad_resid_norm, gain_mid_grad = norm_back(residual, gain_mid, grad_mid)
    grad_resid = grad_out + grad_resid_norm

    grad_low = grad_resid.astype(bf16)
    head_blocks = [
        send(jnp.dot(grad_low, w_out_near[k], preferred_element_type=f32).astype(bf16), "s", k)
        if k
        else jnp.dot(grad_low, w_out, preferred_element_type=f32).astype(bf16)
        for k in range(seqs)
    ]
    grad_heads = in_order(head_blocks, "s", token(up_done)).reshape(seq, cols)
    low_blocks = gather_near(after(grad_low, head_blocks[-1]), "s")
    grad_q, grad_k, grad_v, q_inner, k_inner, gain_q_grad, gain_k_grad = attend_back(
        projected, shared, query, keyed, valued, grad_heads, log_total, heads
    )
    down_ready = in_order(down_blocks, "z", token(grad_q))
    grad_attn_out = in_order(low_blocks, "s", token(grad_q)).reshape(seq, width)
    grad_w_out = dot("td,tc->dc", grad_attn_out, attended).astype(bf16)
    q_inner = after(q_inner, down_ready, grad_w_out)
    grad_w_out = sum_rows(grad_w_out)
    q_inner, k_inner = over_heads(q_inner[:, 0], k_inner[:, 0])

    def norm_grad(grad, raw, mean, inner):
        factor = lax.rsqrt(mean + epsilon)
        return (factor * (grad - raw * factor * inner)).astype(bf16)

    grad_proj = jnp.concatenate(
        [
            norm_grad(grad_q, query_raw, q_mean, q_inner),
            norm_grad(grad_k, key_raw, k_mean, k_inner),
            grad_v,
        ],
        axis=1,
    )
    grad_padded = jnp.concatenate([grad_proj, jnp.zeros((seq, PAD), bf16)], axis=1)

    def back_half(weight):
        grad = dot("tc,dc->td", grad_padded, weight).astype(bf16)
        return exchange_sum(grad.reshape(seqs, own, width // 2), "s")

    grad_normed = whole_of(back_half(w_in), back_half(w_in_other), 1)
    grad_w_qkv = dot("td,tc->dc", normed_in, grad_proj).astype(bf16)
    gate_ready = in_order(gate_blocks, "z", token(grad_w_qkv))
    grad_w_qkv = sum_rows(grad_w_qkv)
    up_blocks = to_owners(grad_w_up, token(grad_w_qkv))
    grad_in_norm, gain_in_grad = norm_back(inputs, gain_in, grad_normed)
    grad_tokens = to_outer(grad_resid + grad_in_norm)

    def widen(local):
        full = jnp.zeros((width,), f32)
        return to_inner(lax.dynamic_update_slice_in_dim(full, local, rank * cols, 0))

    gains = jnp.stack([gain_in_grad, gain_mid_grad, widen(gain_q_grad[0]), widen(gain_k_grad[0])])
    for axis in ("z", "c", "s", "o"):
        gains = sum(gather_near(gains, axis))
    row = (lax.axis_index(("c", "o", "z")) * seqs + rank) * rows_dev
    grad_gains = lax.dynamic_slice_in_dim(gains, row, rows_dev, 1).T

    def own_rows(grad):
        grad = grad.astype(bf16).reshape(seqs, rows_dev, grad.shape[1])
        got = exchange(lambda i: lax.dynamic_index_in_dim(grad, i, 0, keepdims=False), "s")
        return in_order(got, "s").astype(f32)

    qkv_rows, out_rows = own_rows(grad_w_qkv), own_rows(grad_w_out)
    grad_attn = jnp.concatenate(
        [qkv_rows[s, :, i * cols : (i + 1) * cols] for i in range(3) for s in range(seqs)]
        + [out_rows[s] for s in range(seqs)],
        axis=1,
    )
    up_ready = in_order(up_blocks, "z")
    grad_expert = jnp.concatenate([gate_ready, up_ready, down_ready], axis=2)
    grad_expert = grad_expert.astype(f32).transpose(1, 0, 2)
    return (
        to_outer(final_out).astype(bf16),
        loss_value,
        grad_tokens,
        grad_attn,
        grad_gains,
        grad_expert,
    )


def solution(mesh):
    fsdp, seqs = mesh.shape["fsdp"], mesh.shape["sp"]

    def whole(*arrays):
        planes = arrays[3].shape[1] // seqs
        outer = fsdp // (planes * CORES)
        inner = Mesh(mesh.devices.reshape(outer, planes, CORES, seqs), ("o", "z", "c", "s"))
        every = ("o", "z", "c", "s")
        rows = P(every, None)
        experts = P(("o", "z", "c"), "s", None)
        return jax.shard_map(
            shards,
            mesh=inner,
            in_specs=(
                rows,
                rows,
                rows,
                experts,
                rows,
                rows,
                P(("o", "z", "c")),
                P(every),
                rows,
                rows,
            ),
            out_specs=(rows, P(), rows, rows, rows, experts),
            check_vma=False,
        )(*arrays)

    return whole
```

```python
import functools

import jax
import jax.numpy as jnp
from jax import lax
from jax.experimental import pallas as pl
from jax.experimental.pallas import tpu as pltpu
from jax.sharding import Mesh, PartitionSpec as P

H = 16
HD = 128
TOP = 8
CORES = 2
PAD = 128

epsilon = 1e-05
masked = -1e30
f32 = jnp.float32
bf16 = jnp.bfloat16


def send(block, axis, step):
    size = lax.axis_size(axis)
    return lax.ppermute(block, axis, [(i, i ^ step) for i in range(size)])


def gather_near(block, axis):
    return [block] + [send(block, axis, k) for k in range(1, lax.axis_size(axis))]


def in_order(blocks, axis, start=0):
    rank = lax.axis_index(axis)
    if len(blocks) == 1:
        return blocks[0][None]
    stacked = jnp.zeros((len(blocks),) + blocks[0].shape, blocks[0].dtype)
    for k, block in enumerate(blocks):
        stacked = lax.dynamic_update_index_in_dim(stacked, block, (rank ^ k) + start, 0)
    return stacked


def collect(block, axis):
    return in_order(gather_near(block, axis), axis)


def exchange(piece_for, axis, start=0):
    rank, size = lax.axis_index(axis) + start, lax.axis_size(axis)
    return [piece_for(rank)] + [send(piece_for(rank ^ k), axis, k) for k in range(1, size)]


def exchange_sum(pieces, axis):
    got = exchange(lambda i: lax.dynamic_index_in_dim(pieces, i, 0, keepdims=False), axis)
    return sum(piece.astype(f32) for piece in got)


def token(*values):
    firsts = [value[(slice(0, 1),) * value.ndim].reshape(()).astype(f32) for value in values]
    total = sum(firsts)
    return (total != total).astype(jnp.int32)


def after(value, *others):
    return value + token(*others).astype(value.dtype)


def rms_factor(values):
    return lax.rsqrt(jnp.mean(values * values, axis=-1, keepdims=True) + epsilon)


def norm_back(values, gain_vec, grad_in):
    factor = rms_factor(values)
    normed = values * factor
    gain_grad = jnp.sum(grad_in * normed, axis=0)
    inner = grad_in * gain_vec
    grad = factor * (inner - normed * jnp.mean(inner * normed, axis=-1, keepdims=True))
    return grad, gain_grad


def rope_tables(rows):
    inverse = 10000.0 ** (-(jnp.arange(HD // 2).astype(f32) * 2.0 / HD))
    angles = jnp.arange(rows).astype(f32)[:, None] * inverse[None, :]
    cosine = jnp.concatenate([jnp.cos(angles), jnp.cos(angles)], axis=-1)
    sine = jnp.concatenate([-jnp.sin(angles), jnp.sin(angles)], axis=-1)
    return cosine, sine


def mm(left, right, dims):
    return lax.dot_general(left, right, (dims, ((), ())), preferred_element_type=f32)


def masked_scores(query, keyed, seg_col, seg_row, first, scale):
    scores = mm(query, keyed, ((1,), (1,))) * scale
    rows = first + lax.broadcasted_iota(jnp.int32, scores.shape, 0)
    allowed = (rows >= lax.broadcasted_iota(jnp.int32, scores.shape, 1)) & (seg_col == seg_row)
    return jnp.where(allowed, scores, masked)


def attend_kernel(
    block,
    q_raw,
    k_raw,
    v_raw,
    q_mean,
    k_mean,
    gain_q,
    gain_k,
    cosine,
    sine,
    seg_col,
    seg_row,
    out,
    q_out,
    k_out,
    v_out,
    log_total,
):
    def rope(raw, mean, gain):
        values = raw[...] * lax.rsqrt(mean[...] + epsilon) * gain[...]
        turned = pltpu.roll(values, HD // 2, 1)
        return (values * cosine[...] + turned * sine[...]).astype(bf16)

    q_out[...] = rope(q_raw, q_mean, gain_q)
    k_out[...] = rope(k_raw, k_mean, gain_k)
    v_out[...] = v_raw[...].astype(bf16)
    for first in range(0, out.shape[0], block):
        last = first + block
        scores = masked_scores(
            q_out[first:last],
            k_out[:last],
            seg_col[first:last],
            seg_row[:, :last],
            first,
            HD**-0.5,
        )
        top = jnp.max(scores, axis=-1, keepdims=True)
        exps = jnp.exp(scores - top)
        total = jnp.sum(exps, axis=-1, keepdims=True)
        weights = (exps * (1.0 / total)).astype(bf16)
        out[first:last] = mm(weights, v_out[:last], ((1,), (0,))).astype(bf16)
        log_total[0, first:last] = top + jnp.log(total)


def attend_back_kernel(
    block,
    q_raw,
    k_raw,
    q_mean,
    k_mean,
    gain_q,
    gain_k,
    cosine,
    sine,
    seg_col,
    seg_row,
    query,
    keyed,
    valued,
    grad,
    log_total,
    grad_q,
    grad_k,
    grad_v,
    q_inner,
    k_inner,
    gain_q_grad,
    gain_k_grad,
    sum_q,
    sum_k,
    sum_v,
):
    scale = HD**-0.5
    sum_k[...] = jnp.zeros_like(sum_k)
    sum_v[...] = jnp.zeros_like(sum_v)
    for first in range(0, query.shape[0], block):
        last = first + block
        q_block, g_block = query[first:last], grad[first:last]
        scores = masked_scores(
            q_block, keyed[:last], seg_col[first:last], seg_row[:, :last], first, scale
        )
        probs = jnp.exp(scores - log_total[0, first:last])
        sum_v[:last] += mm(probs.astype(bf16), g_block, ((0,), (0,)))
        grad_probs = mm(g_block, valued[:last], ((1,), (1,)))
        inner = jnp.sum(probs * grad_probs, axis=-1, keepdims=True)
        grad_scores = (probs * (grad_probs - inner)).astype(bf16)
        sum_q[first:last] = mm(grad_scores, keyed[:last], ((1,), (0,))) * scale
        sum_k[:last] += mm(grad_scores, q_block, ((0,), (0,))) * scale
    grad_v[...] = sum_v[...].astype(bf16)

    def undo(total, raw, mean, gain, inner_out, gain_out, grad_out):
        low = total[...].astype(bf16).astype(f32)
        back = low * cosine[...] + pltpu.roll(low * sine[...], HD // 2, 1)
        normed = raw[...] * lax.rsqrt(mean[...] + epsilon)
        gain_out[...] = jnp.sum(back * normed, axis=0, keepdims=True)
        back = back * gain[...]
        grad_out[...] = back
        inner = jnp.sum(back * normed, axis=-1, keepdims=True)

        @pl.when(pl.program_id(0) == 0)
        def _():
            inner_out[...] = inner

        @pl.when(pl.program_id(0) > 0)
        def _():
            inner_out[...] += inner

    undo(sum_q, q_raw, q_mean, gain_q, q_inner, gain_q_grad, grad_q)
    undo(sum_k, k_raw, k_mean, gain_k, k_inner, gain_k_grad, grad_k)


def head_specs(seq, heads):
    column = pl.BlockSpec((seq, 1), lambda h: (0, 0))
    gain = pl.BlockSpec((1, HD), lambda h: (0, h))
    table = pl.BlockSpec((seq, HD), lambda h: (0, 0))
    return [column, column, gain, gain, table, table, column, pl.BlockSpec((1, seq), lambda h: (0, 0))]


def raw_spec(seq, heads, which):
    return pl.BlockSpec((seq, HD), lambda h: (0, which * heads + h))


def attend(projected, shared, heads):
    seq = projected.shape[0]
    block = min(256, seq)
    head = pl.BlockSpec((seq, HD), lambda h: (0, h))
    low = jax.ShapeDtypeStruct((seq, heads * HD), bf16)
    return pl.pallas_call(
        functools.partial(attend_kernel, block),
        grid=(heads,),
        in_specs=[raw_spec(seq, heads, i) for i in range(3)] + head_specs(seq, heads),
        out_specs=[head] * 4 + [pl.BlockSpec((1, seq, 1), lambda h: (h, 0, 0))],
        out_shape=[low] * 4 + [jax.ShapeDtypeStruct((heads, seq, 1), f32)],
        compiler_params=pltpu.CompilerParams(vmem_limit_bytes=48 * 2**20),
        cost_estimate=pl.CostEstimate(flops=10**6, bytes_accessed=10**5, transcendentals=0),
    )(projected, projected, projected, *shared)


def attend_back(projected, shared, query, keyed, valued, grad, log_total, heads):
    seq = projected.shape[0]
    block = min(256, seq)
    head = pl.BlockSpec((seq, HD), lambda h: (0, h))
    column = pl.BlockSpec((seq, 1), lambda h: (0, 0))
    gain = pl.BlockSpec((1, HD), lambda h: (0, h))
    wide = jax.ShapeDtypeStruct((seq, heads * HD), f32)
    return pl.pallas_call(
        functools.partial(attend_back_kernel, block),
        grid=(heads,),
        in_specs=[raw_spec(seq, heads, i) for i in range(2)]
        + head_specs(seq, heads)
        + [head] * 4
        + [pl.BlockSpec((1, seq, 1), lambda h: (h, 0, 0))],
        out_specs=[head] * 3 + [column] * 2 + [gain] * 2,
        out_shape=[wide, wide, jax.ShapeDtypeStruct((seq, heads * HD), bf16)]
        + [jax.ShapeDtypeStruct((seq, 1), f32)] * 2
        + [jax.ShapeDtypeStruct((1, heads * HD), f32)] * 2,
        scratch_shapes=[pltpu.VMEM((seq, HD), f32)] * 3,
        compiler_params=pltpu.CompilerParams(vmem_limit_bytes=48 * 2**20),
        cost_estimate=pl.CostEstimate(flops=10**6, bytes_accessed=10**5, transcendentals=0),
    )(projected, projected, *shared, query, keyed, valued, grad, log_total)


def slot_choice(place, slots):
    return lax.broadcasted_iota(jnp.int32, (slots, place.shape[1]), 0) == place


def slot_weight(place, gate, slots):
    return jnp.sum(jnp.where(slot_choice(place, slots), gate, 0.0), axis=1, keepdims=True)


def expert_kernel(count, slots, place, gate, *refs):
    blocks, (w_gate, w_up, w_down), refs = refs[:count], refs[count : count + 3], refs[count + 3 :]
    rows, activated, gate_pre, up_pre = refs[-6 - count : -2 - count]
    partial, (sum_out, sum_tokens) = refs[-2 - count : -2], refs[-2:]
    expert, chunk = pl.program_id(0), pl.program_id(1)

    def spans():
        return [(b, slice(b * slots, (b + 1) * slots)) for b in range(count)]

    @pl.when(chunk == 0)
    def _():
        for b, span in spans():
            choice = slot_choice(place[0, b], slots).astype(bf16)
            rows[0, 0, span] = mm(choice, blocks[b][...], ((1,), (0,))).astype(bf16)

    rows_in = rows[0, 0]
    g = mm(rows_in, w_gate[0], ((1,), (0,)))
    u = mm(rows_in, w_up[0], ((1,), (0,)))
    m = (g * jax.nn.sigmoid(g) * u).astype(bf16)
    gate_pre[0], up_pre[0], activated[0, 0] = g.astype(bf16), u.astype(bf16), m
    term = mm(m, w_down[0], ((1,), (1,)))

    @pl.when(chunk == 0)
    def _():
        sum_out[...] = term

    @pl.when(chunk > 0)
    def _():
        sum_out[...] += term

    @pl.when(chunk == pl.num_programs(1) - 1)
    def _():
        for b, span in spans():
            weight = slot_weight(place[0, b], gate[0, b], slots)
            out = (sum_out[span] * weight).astype(bf16)
            back = mm(slot_choice(place[0, b], slots).astype(bf16), out, ((0,), (0,)))
            add_tokens(expert, b, back, sum_tokens, partial)


def add_tokens(expert, b, back, sum_tokens, partial):
    @pl.when(expert == 0)
    def _():
        sum_tokens[b] = back

    @pl.when(expert > 0)
    def _():
        sum_tokens[b] += back

    @pl.when(expert == pl.num_programs(0) - 1)
    def _():
        partial[b][...] = sum_tokens[b].astype(bf16)


def expert_back_kernel(count, slots, place, gate, *refs):
    blocks, (w_gate, w_up, w_down) = refs[:count], refs[count : count + 3]
    gate_pre, up_pre = refs[count + 3 : count + 5]
    grad_rows, grad_gate, grad_up = refs[-5 - count : -2 - count]
    partial, (sum_rows, sum_tokens) = refs[-2 - count : -2], refs[-2:]
    expert, chunk = pl.program_id(0), pl.program_id(1)

    def spans():
        return [(b, slice(b * slots, (b + 1) * slots)) for b in range(count)]

    @pl.when(chunk == 0)
    def _():
        for b, span in spans():
            choice = slot_choice(place[0, b], slots).astype(bf16)
            weight = slot_weight(place[0, b], gate[0, b], slots)
            picked = mm(choice, blocks[b][...], ((1,), (0,)))
            grad_rows[0, 0, span] = (picked * weight).astype(bf16)

    grad_act = mm(grad_rows[0, 0], w_down[0], ((1,), (0,)))
    g, u = gate_pre[0].astype(f32), up_pre[0].astype(f32)
    sigmoid = jax.nn.sigmoid(g)
    dg = (grad_act * u * sigmoid * (1.0 + g * (1.0 - sigmoid))).astype(bf16)
    du = (grad_act * g * sigmoid).astype(bf16)
    grad_gate[0, 0], grad_up[0, 0] = dg, du
    term = mm(dg, w_gate[0], ((1,), (1,))) + mm(du, w_up[0], ((1,), (1,)))

    @pl.when(chunk == 0)
    def _():
        sum_rows[...] = term

    @pl.when(chunk > 0)
    def _():
        sum_rows[...] += term

    @pl.when(chunk == pl.num_programs(1) - 1)
    def _():
        for b, span in spans():
            out = sum_rows[span].astype(bf16)
            back = mm(slot_choice(place[0, b], slots).astype(bf16), out, ((0,), (0,)))
            add_tokens(expert, b, back, sum_tokens, partial)


def run_experts(kernel, group, slots, place, gate, blocks, weights, saved, narrow, prior):
    experts, width, hidden = weights[0].shape
    count, (own, _) = len(blocks), blocks[0].shape
    rows = count * slots
    step = min(256, hidden)
    table = pl.BlockSpec((1, count, 1, own), lambda e, f: (e, group, 0, 0))
    tokens = pl.BlockSpec((own, width), lambda e, f: (0, 0))
    weight = pl.BlockSpec((1, width, step), lambda e, f: (e, 0, f))
    local = pl.BlockSpec((1, rows, step), lambda e, f: (e, 0, f))
    shared_specs = [pl.BlockSpec((1, 1, rows, width), lambda e, f: (e, group, 0, 0))] + [
        pl.BlockSpec((1, 1, rows, step), lambda e, f: (e, group, 0, f))
    ] * narrow
    shared_shapes = [jax.ShapeDtypeStruct((experts, 2, rows, width), bf16)] + [
        jax.ShapeDtypeStruct((experts, 2, rows, hidden), bf16)
    ] * narrow
    local_out = 0 if saved else 2
    first = 2 + count + 3 + len(saved)
    return pl.pallas_call(
        functools.partial(kernel, count, slots),
        grid=(experts, hidden // step),
        in_specs=[table, table]
        + [tokens] * count
        + [weight] * 3
        + [local] * len(saved)
        + [pl.BlockSpec(memory_space=pl.ANY)] * len(prior),
        out_specs=shared_specs + [local] * local_out + [tokens] * count,
        out_shape=shared_shapes
        + [jax.ShapeDtypeStruct((experts, rows, hidden), bf16)] * local_out
        + [jax.ShapeDtypeStruct((own, width), bf16)] * count,
        scratch_shapes=[pltpu.VMEM((rows, width), f32), pltpu.VMEM((count, own, width), f32)],
        input_output_aliases={first + i: i for i in range(len(prior))},
        compiler_params=pltpu.CompilerParams(vmem_limit_bytes=56 * 2**20),
        cost_estimate=pl.CostEstimate(
            flops=experts * rows * width * hidden * 6,
            bytes_accessed=experts * width * hidden * 8,
            transcendentals=experts * rows * hidden,
        ),
    )(place, gate, *blocks, *weights, *saved, *prior)


def dot(spec, left, right):
    return jnp.einsum(spec, left, right, preferred_element_type=f32)


def shards(
    tokens,
    w_attn,
    norm_gains,
    w_expert,
    gate_weights,
    routes,
    segment,
    valid_mask,
    teacher,
    cotangent,
):
    outer, planes, seqs = lax.axis_size("o"), lax.axis_size("z"), lax.axis_size("s")
    plane, rank = lax.axis_index("z"), lax.axis_index("s")
    own, width = tokens.shape
    rows_dev = w_attn.shape[0]
    seq = own * seqs
    heads = H // seqs
    cols = heads * HD
    hidden = w_expert.shape[2] // 3
    part = w_expert.shape[0]
    capacity = own * TOP * 17 // (16 * planes * seqs)
    scale = HD ** (-0.5)

    def to_inner(v):
        lead = v.shape[:-1]
        v = v.reshape(lead + (outer * planes, CORES, part))
        return jnp.swapaxes(v, -3, -2).reshape(lead + (width,))

    def to_outer(v):
        lead = v.shape[:-1]
        v = v.reshape(lead + (CORES, outer * planes, part))
        return jnp.swapaxes(v, -3, -2).reshape(lead + (width,))

    first_core = lax.axis_index("c") == 0

    def halves(v):
        low, high = v[..., : width // 2], v[..., width // 2 :]
        return jnp.where(first_core, low, high), jnp.where(first_core, high, low)

    def whole_of(mine, other, axis):
        low, high = jnp.where(first_core, mine, other), jnp.where(first_core, other, mine)
        return jnp.concatenate([low, high], axis=axis)

    def stack_rows(blocks, start=0):
        rows = in_order(blocks, "z", start)
        return collect(rows, "o").reshape((width // 2,) + rows.shape[2:])

    def sum_rows(grad):
        count = grad.shape[1]
        grad = exchange_sum(grad.reshape(CORES, width // 2, count), "c").astype(bf16)
        if outer > 1:
            grad = exchange_sum(grad.reshape(outer, planes * part, count), "o").astype(bf16)
        return exchange_sum(grad.reshape(planes, part, count), "z")

    def gather_sum(value):
        for axis in ("z", "s", "c", "o"):
            value = sum(gather_near(jnp.broadcast_to(value, (8, PAD)), axis))[0, 0]
        return value

    by_expert = w_expert.transpose(1, 0, 2)

    def expert_chunk(i, start=0):
        def piece_for(owner):
            return lax.dynamic_slice(by_expert, (owner, 0, i * hidden), (1, part, hidden))[0]

        return exchange(piece_for, "z", start)

    def gather_plane(ready):
        chunk = ready.reshape(planes * part, hidden)
        chunk = lax.all_gather(chunk, ("s", "c", "o"), axis=0, tiled=True)
        return chunk.reshape(seqs, width, hidden)

    count = jnp.sum(valid_mask).astype(jnp.int32)
    digits = jnp.stack([count // 128, count % 128]).astype(bf16)
    extra = jnp.concatenate(
        [
            norm_gains,
            jnp.broadcast_to(digits[None], (rows_dev, 2)),
            jnp.zeros((rows_dev, PAD - 6), bf16),
        ],
        axis=1,
    )

    def columns_of(owner):
        picked = [
            lax.dynamic_slice_in_dim(w_attn, i * width + owner * cols, cols, 1) for i in range(4)
        ]
        return jnp.concatenate(picked[:3] + [extra] + picked[3:], axis=1)

    mine_blocks = exchange(columns_of, "s")
    gate_blocks = expert_chunk(0)
    inputs = to_inner(tokens)
    token_blocks = gather_near(inputs, "s")
    inputs = inputs.astype(f32)

    mine = in_order(mine_blocks, "s").reshape(part, 4 * cols + PAD)
    in_blocks = gather_near(mine[:, : 3 * cols + PAD], "z")
    gate_ready = in_order(gate_blocks, "z", token(mine))
    w_gate = gather_plane(gate_ready)
    seq_tokens = in_order(token_blocks, "s", token(gate_ready)).reshape(seq, width).astype(f32)
    seq_factor = rms_factor(seq_tokens)
    w_in = stack_rows(in_blocks, token(seq_factor))
    w_in_other = send(w_in, "c", 1)
    up_blocks = expert_chunk(1, token(w_in))

    side = whole_of(w_in[:, 3 * cols :], w_in_other[:, 3 * cols :], 0)[:, :6].astype(f32).T
    gain_in, gain_mid = side[0], side[1]
    gain_q = lax.dynamic_slice_in_dim(to_outer(side[2]), rank * cols, cols, 0)
    gain_k = lax.dynamic_slice_in_dim(to_outer(side[3]), rank * cols, cols, 0)
    total_count = jnp.sum(side[4, ::rows_dev]) * 128.0 + jnp.sum(side[5, ::rows_dev])

    routed = jnp.stack(
        gather_near(jnp.concatenate([routes.astype(f32), gate_weights], axis=1), "z")
    )
    route_all, gate_all = routed[..., :TOP].astype(jnp.int32), routed[..., TOP:]
    expert_ids = jnp.arange(seqs) * planes + plane
    match = route_all[:, :, None, :] == expert_ids[None, None, :, None]
    used = jnp.any(match, axis=-1)
    gate_of = jnp.sum(jnp.where(match, gate_all[:, :, None, :], 0.0), axis=-1)
    before = (jnp.arange(own)[:, None] > jnp.arange(own)[None, :]).astype(bf16)
    place = dot("tu,buk->btk", before, used.astype(bf16)).astype(jnp.int32)
    place = jnp.where(used, place, -1)
    slots = -(-capacity // 16) * 16
    place = place.transpose(2, 0, 1)[:, :, None, :]
    gate_of = gate_of.transpose(2, 0, 1)[:, :, None, :]

    groups = [[k for k in range(planes) if k % 2 == odd] for odd in range(2)]

    def by_group(table):
        return jnp.concatenate([table[:, k : k + 1] for group in groups for k in group], axis=1)

    place, gate_of = by_group(place), by_group(gate_of)

    def through_planes(block, work):
        near = [block] + [None] * (planes - 1)
        for k in groups[0][1:]:
            near[k] = send(block, "z", k)
        later = after(block, *[near[k] for k in groups[0][1:]])
        for k in groups[1]:
            near[k] = send(later, "z", k)
        first = work(0, [near[k] for k in groups[0]])
        got = [first[0]] + [send(first[i], "z", k) for i, k in enumerate(groups[0]) if k]
        blocks = [near[k] for k in groups[1]]
        blocks[0] = after(blocks[0], first[0])
        second = work(1, blocks)
        base = after(total(got), second[0])
        second = [after(part, base) for part in second]
        return second[0], [base] + [send(second[i], "z", k) for i, k in enumerate(groups[1])]

    def total(pieces):
        return sum(piece.astype(f32) for piece in pieces)

    normed_in = (seq_tokens * seq_factor * gain_in).astype(bf16)
    normed_mine, normed_other = halves(normed_in)
    projected = jnp.dot(normed_mine, w_in, preferred_element_type=f32) + jnp.dot(
        normed_other, w_in_other, preferred_element_type=f32
    )
    query_raw = projected[:, :cols]
    key_raw = projected[:, cols : 2 * cols]

    def over_heads(first, second, *others):
        pairs = gather_near(jnp.stack([first, second]), "s")
        if others:
            pairs[0] = after(pairs[0], *others)
        pair = sum(pairs) / width
        return pair[0][:, None], pair[1][:, None]

    q_mean, k_mean = over_heads(
        jnp.sum(query_raw * query_raw, axis=-1), jnp.sum(key_raw * key_raw, axis=-1)
    )
    up_ready = in_order(up_blocks, "z", token(projected))
    w_up = gather_plane(up_ready)
    out_blocks = gather_near(after(mine[:, 3 * cols + PAD :], up_ready), "z")
    cosine, sine = rope_tables(seq)
    shared = [
        after(q_mean, up_ready, w_gate),
        k_mean,
        gain_q[None],
        gain_k[None],
        cosine,
        sine,
        segment[:, None],
        segment[None],
    ]
    attended, query, keyed, valued, log_total = attend(projected, shared, heads)
    w_out = collect(stack_rows(out_blocks, token(attended)), "c").reshape(width, cols)
    down_blocks = expert_chunk(2, token(attended))
    attn_out = dot("tc,dc->td", attended, w_out).astype(bf16)
    residual = inputs + exchange_sum(attn_out.reshape(seqs, own, width), "s")
    down_ready = in_order(down_blocks, "z", token(residual))
    residual = after(residual, down_ready)
    w_down = gather_plane(down_ready)

    normed_mid = (residual * rms_factor(residual) * gain_mid).astype(bf16)
    expert_weights = (w_gate, w_up, w_down)
    pres, kept = [], [()]

    def forward(i, blocks):
        rows_in, activated, gate_pre, up_pre, *partial = run_experts(
            expert_kernel, i, slots, place, gate_of, blocks, expert_weights, (), 1, kept[0]
        )
        pres.append((gate_pre, up_pre))
        kept[0] = (rows_in, activated)
        return partial

    final_out = residual + total(through_planes(normed_mid, forward)[1])
    rows_in, activated = [v.reshape(seqs, -1, v.shape[-1]) for v in kept[0]]

    w_out_all = lax.all_gather(after(w_out, w_up), "s", axis=0)
    valid_f = valid_mask.astype(f32)[:, None]
    difference = final_out - to_inner(teacher).astype(f32)
    squared = jnp.sum(valid_f * difference * difference)
    squared = gather_sum(squared)
    loss_value = squared / (total_count * width)
    grad_out = (
        to_inner(cotangent).astype(f32) + 2.0 / (total_count * width) * valid_f * difference
    )

    def scatter_expert(grad):
        grad = grad.reshape(seqs * width, hidden)
        grad = lax.psum_scatter(grad, ("s", "c", "o"), scatter_dimension=0, tiled=True)
        return grad.reshape(planes, part, hidden)

    def to_owners(grad, start=0):
        def piece_for(owner):
            return lax.dynamic_index_in_dim(grad, owner, 0, keepdims=False)

        return exchange(piece_for, "z", start)

    grads = [()]

    def backward(i, blocks):
        *shared_grads, first, last = run_experts(
            expert_back_kernel,
            i,
            slots,
            place,
            gate_of,
            blocks,
            expert_weights,
            pres[i],
            2,
            grads[0],
        )
        grads[0] = shared_grads
        return first, last

    back_last, back_pieces = through_planes(grad_out.astype(bf16), backward)
    grad_rows, grad_gate, grad_up = [v.reshape(seqs, -1, v.shape[-1]) for v in grads[0]]
    grad_w_down = dot("krd,krf->kdf", grad_rows, after(activated, back_last)).astype(bf16)
    back_pieces[0] = after(back_pieces[0], grad_w_down)
    grad_mid = total(back_pieces)
    grad_w_gate = dot("krd,krf->kdf", rows_in, after(grad_gate, grad_mid)).astype(bf16)
    grad_resid_norm, gain_mid_grad = norm_back(residual, gain_mid, grad_mid)
    grad_resid = grad_out + grad_resid_norm

    grad_low = grad_resid.astype(bf16)
    grad_heads = dot("td,sdc->stc", grad_low, w_out_all).astype(bf16)
    head_blocks = exchange(
        lambda i: lax.dynamic_index_in_dim(grad_heads, i, 0, keepdims=False), "s"
    )
    grad_heads = in_order(head_blocks, "s", token(grad_w_gate)).reshape(seq, cols)
    grad_w_up = dot("krd,krf->kdf", rows_in, after(grad_up, grad_heads)).astype(bf16)
    up_done = grad_w_up
    grad_w_down, grad_w_gate, grad_w_up = [
        scatter_expert(grad) for grad in (grad_w_down, grad_w_gate, grad_w_up)
    ]
    down_blocks, gate_blocks = to_owners(grad_w_down), to_owners(grad_w_gate)
    low_blocks = gather_near(grad_low, "s")
    grad_q, grad_k, grad_v, q_inner, k_inner, gain_q_grad, gain_k_grad = attend_back(
        projected, shared, query, keyed, valued, grad_heads, log_total, heads
    )
    grad_attn_out = in_order(low_blocks, "s", token(grad_q)).reshape(seq, width)
    grad_w_out = sum_rows(dot("td,tc->dc", grad_attn_out, attended).astype(bf16))
    q_inner, k_inner = over_heads(q_inner[:, 0], k_inner[:, 0], up_done)

    def norm_grad(grad, raw, mean, inner):
        factor = lax.rsqrt(mean + epsilon)
        return (factor * (grad - raw * factor * inner)).astype(bf16)

    grad_proj = jnp.concatenate(
        [
            norm_grad(grad_q, query_raw, q_mean, q_inner),
            norm_grad(grad_k, key_raw, k_mean, k_inner),
            grad_v,
        ],
        axis=1,
    )
    grad_padded = jnp.concatenate([grad_proj, jnp.zeros((seq, PAD), bf16)], axis=1)

    def back_half(weight):
        grad = dot("tc,dc->td", grad_padded, weight).astype(bf16)
        return exchange_sum(grad.reshape(seqs, own, width // 2), "s")

    grad_normed = whole_of(back_half(w_in), back_half(w_in_other), 1)
    grad_w_qkv = dot("td,tc->dc", normed_in, grad_proj).astype(bf16)
    down_ready = in_order(down_blocks, "z", token(grad_w_qkv))
    grad_w_qkv = sum_rows(grad_w_qkv)
    gate_ready = in_order(gate_blocks, "z", token(grad_w_qkv))
    up_blocks = to_owners(grad_w_up, token(down_ready, gate_ready))
    grad_in_norm, gain_in_grad = norm_back(inputs, gain_in, grad_normed)
    grad_tokens = to_outer(grad_resid + grad_in_norm)

    def widen(local):
        full = jnp.zeros((width,), f32)
        return to_inner(lax.dynamic_update_slice_in_dim(full, local, rank * cols, 0))

    gains = jnp.stack([gain_in_grad, gain_mid_grad, widen(gain_q_grad[0]), widen(gain_k_grad[0])])
    for axis in ("z", "c", "s", "o"):
        gains = sum(gather_near(gains, axis))
    row = (lax.axis_index(("c", "o", "z")) * seqs + rank) * rows_dev
    grad_gains = lax.dynamic_slice_in_dim(gains, row, rows_dev, 1).T

    def own_rows(grad):
        grad = grad.astype(bf16).reshape(seqs, rows_dev, grad.shape[1])
        got = exchange(lambda i: lax.dynamic_index_in_dim(grad, i, 0, keepdims=False), "s")
        return in_order(got, "s").astype(f32)

    qkv_rows, out_rows = own_rows(grad_w_qkv), own_rows(grad_w_out)
    grad_attn = jnp.concatenate(
        [qkv_rows[s, :, i * cols : (i + 1) * cols] for i in range(3) for s in range(seqs)]
        + [out_rows[s] for s in range(seqs)],
        axis=1,
    )
    up_ready = in_order(up_blocks, "z")
    grad_expert = jnp.concatenate([gate_ready, up_ready, down_ready], axis=2)
    grad_expert = grad_expert.astype(f32).transpose(1, 0, 2)
    return (
        to_outer(final_out).astype(bf16),
        loss_value,
        grad_tokens,
        grad_attn,
        grad_gains,
        grad_expert,
    )


def solution(mesh):
    fsdp, seqs = mesh.shape["fsdp"], mesh.shape["sp"]

    def whole(*arrays):
        planes = arrays[3].shape[1] // seqs
        outer = fsdp // (planes * CORES)
        inner = Mesh(mesh.devices.reshape(outer, planes, CORES, seqs), ("o", "z", "c", "s"))
        every = ("o", "z", "c", "s")
        rows = P(every, None)
        experts = P(("o", "z", "c"), "s", None)
        return jax.shard_map(
            shards,
            mesh=inner,
            in_specs=(
                rows,
                rows,
                rows,
                experts,
                rows,
                rows,
                P(("o", "z", "c")),
                P(every),
                rows,
                rows,
            ),
            out_specs=(rows, P(), rows, rows, rows, experts),
            check_vma=False,
        )(*arrays)

    return whole
```

```python
import functools

import jax
import jax.numpy as jnp
from jax import lax
from jax.experimental import pallas as pl
from jax.experimental.pallas import tpu as pltpu
from jax.sharding import Mesh, PartitionSpec as P

H = 16
HD = 128
TOP = 8
CORES = 2
PAD = 128

epsilon = 1e-05
masked = -1e30
f32 = jnp.float32
bf16 = jnp.bfloat16


def send(block, axis, step):
    size = lax.axis_size(axis)
    return lax.ppermute(block, axis, [(i, i ^ step) for i in range(size)])


def gather_near(block, axis):
    return [block] + [send(block, axis, k) for k in range(1, lax.axis_size(axis))]


def in_order(blocks, axis, start=0):
    rank = lax.axis_index(axis)
    if len(blocks) == 1:
        return blocks[0][None]
    stacked = jnp.zeros((len(blocks),) + blocks[0].shape, blocks[0].dtype)
    for k, block in enumerate(blocks):
        stacked = lax.dynamic_update_index_in_dim(stacked, block, (rank ^ k) + start, 0)
    return stacked


def collect(block, axis):
    return in_order(gather_near(block, axis), axis)


def exchange(piece_for, axis, start=0):
    rank, size = lax.axis_index(axis) + start, lax.axis_size(axis)
    return [piece_for(rank)] + [send(piece_for(rank ^ k), axis, k) for k in range(1, size)]


def exchange_sum(pieces, axis):
    got = exchange(lambda i: lax.dynamic_index_in_dim(pieces, i, 0, keepdims=False), axis)
    return sum(piece.astype(f32) for piece in got)


def token(*values):
    firsts = [value[(slice(0, 1),) * value.ndim].reshape(()).astype(f32) for value in values]
    total = sum(firsts)
    return (total != total).astype(jnp.int32)


def after(value, *others):
    return value + token(*others).astype(value.dtype)


def rms_factor(values):
    return lax.rsqrt(jnp.mean(values * values, axis=-1, keepdims=True) + epsilon)


def norm_back(values, gain_vec, grad_in):
    factor = rms_factor(values)
    normed = values * factor
    gain_grad = jnp.sum(grad_in * normed, axis=0)
    inner = grad_in * gain_vec
    grad = factor * (inner - normed * jnp.mean(inner * normed, axis=-1, keepdims=True))
    return grad, gain_grad


def rope_tables(rows):
    inverse = 10000.0 ** (-(jnp.arange(HD // 2).astype(f32) * 2.0 / HD))
    angles = jnp.arange(rows).astype(f32)[:, None] * inverse[None, :]
    cosine = jnp.concatenate([jnp.cos(angles), jnp.cos(angles)], axis=-1)
    sine = jnp.concatenate([-jnp.sin(angles), jnp.sin(angles)], axis=-1)
    return cosine, sine


def mm(left, right, dims):
    return lax.dot_general(left, right, (dims, ((), ())), preferred_element_type=f32)


def masked_scores(query, keyed, seg_col, seg_row, first, scale):
    scores = mm(query, keyed, ((1,), (1,))) * scale
    rows = first + lax.broadcasted_iota(jnp.int32, scores.shape, 0)
    allowed = (rows >= lax.broadcasted_iota(jnp.int32, scores.shape, 1)) & (seg_col == seg_row)
    return jnp.where(allowed, scores, masked)


def attend_kernel(
    block,
    q_raw,
    k_raw,
    v_raw,
    q_mean,
    k_mean,
    gain_q,
    gain_k,
    cosine,
    sine,
    seg_col,
    seg_row,
    out,
    q_out,
    k_out,
    v_out,
    log_total,
):
    def rope(raw, mean, gain):
        values = raw[...] * lax.rsqrt(mean[...] + epsilon) * gain[...]
        turned = pltpu.roll(values, HD // 2, 1)
        return (values * cosine[...] + turned * sine[...]).astype(bf16)

    q_out[...] = rope(q_raw, q_mean, gain_q)
    k_out[...] = rope(k_raw, k_mean, gain_k)
    v_out[...] = v_raw[...].astype(bf16)
    for first in range(0, out.shape[0], block):
        last = first + block
        scores = masked_scores(
            q_out[first:last],
            k_out[:last],
            seg_col[first:last],
            seg_row[:, :last],
            first,
            HD**-0.5,
        )
        top = jnp.max(scores, axis=-1, keepdims=True)
        exps = jnp.exp(scores - top)
        total = jnp.sum(exps, axis=-1, keepdims=True)
        weights = (exps * (1.0 / total)).astype(bf16)
        out[first:last] = mm(weights, v_out[:last], ((1,), (0,))).astype(bf16)
        log_total[0, first:last] = top + jnp.log(total)


def attend_back_kernel(
    block,
    q_raw,
    k_raw,
    q_mean,
    k_mean,
    gain_q,
    gain_k,
    cosine,
    sine,
    seg_col,
    seg_row,
    query,
    keyed,
    valued,
    grad,
    log_total,
    grad_q,
    grad_k,
    grad_v,
    q_inner,
    k_inner,
    gain_q_grad,
    gain_k_grad,
    sum_q,
    sum_k,
    sum_v,
):
    scale = HD**-0.5
    sum_k[...] = jnp.zeros_like(sum_k)
    sum_v[...] = jnp.zeros_like(sum_v)
    for first in range(0, query.shape[0], block):
        last = first + block
        q_block, g_block = query[first:last], grad[first:last]
        scores = masked_scores(
            q_block, keyed[:last], seg_col[first:last], seg_row[:, :last], first, scale
        )
        probs = jnp.exp(scores - log_total[0, first:last])
        sum_v[:last] += mm(probs.astype(bf16), g_block, ((0,), (0,)))
        grad_probs = mm(g_block, valued[:last], ((1,), (1,)))
        inner = jnp.sum(probs * grad_probs, axis=-1, keepdims=True)
        grad_scores = (probs * (grad_probs - inner)).astype(bf16)
        sum_q[first:last] = mm(grad_scores, keyed[:last], ((1,), (0,))) * scale
        sum_k[:last] += mm(grad_scores, q_block, ((0,), (0,))) * scale
    grad_v[...] = sum_v[...].astype(bf16)

    def undo(total, raw, mean, gain, inner_out, gain_out, grad_out):
        low = total[...].astype(bf16).astype(f32)
        back = low * cosine[...] + pltpu.roll(low * sine[...], HD // 2, 1)
        normed = raw[...] * lax.rsqrt(mean[...] + epsilon)
        gain_out[...] = jnp.sum(back * normed, axis=0, keepdims=True)
        back = back * gain[...]
        grad_out[...] = back
        inner = jnp.sum(back * normed, axis=-1, keepdims=True)

        @pl.when(pl.program_id(0) == 0)
        def _():
            inner_out[...] = inner

        @pl.when(pl.program_id(0) > 0)
        def _():
            inner_out[...] += inner

    undo(sum_q, q_raw, q_mean, gain_q, q_inner, gain_q_grad, grad_q)
    undo(sum_k, k_raw, k_mean, gain_k, k_inner, gain_k_grad, grad_k)


def head_specs(seq, heads):
    column = pl.BlockSpec((seq, 1), lambda h: (0, 0))
    gain = pl.BlockSpec((1, HD), lambda h: (0, h))
    table = pl.BlockSpec((seq, HD), lambda h: (0, 0))
    return [column, column, gain, gain, table, table, column, pl.BlockSpec((1, seq), lambda h: (0, 0))]


def raw_spec(seq, heads, which):
    return pl.BlockSpec((seq, HD), lambda h: (0, which * heads + h))


def attend(projected, shared, heads):
    seq = projected.shape[0]
    block = min(256, seq)
    head = pl.BlockSpec((seq, HD), lambda h: (0, h))
    low = jax.ShapeDtypeStruct((seq, heads * HD), bf16)
    return pl.pallas_call(
        functools.partial(attend_kernel, block),
        grid=(heads,),
        in_specs=[raw_spec(seq, heads, i) for i in range(3)] + head_specs(seq, heads),
        out_specs=[head] * 4 + [pl.BlockSpec((1, seq, 1), lambda h: (h, 0, 0))],
        out_shape=[low] * 4 + [jax.ShapeDtypeStruct((heads, seq, 1), f32)],
        compiler_params=pltpu.CompilerParams(vmem_limit_bytes=48 * 2**20),
        cost_estimate=pl.CostEstimate(flops=10**6, bytes_accessed=10**5, transcendentals=0),
    )(projected, projected, projected, *shared)


def attend_back(projected, shared, query, keyed, valued, grad, log_total, heads):
    seq = projected.shape[0]
    block = min(256, seq)
    head = pl.BlockSpec((seq, HD), lambda h: (0, h))
    column = pl.BlockSpec((seq, 1), lambda h: (0, 0))
    gain = pl.BlockSpec((1, HD), lambda h: (0, h))
    wide = jax.ShapeDtypeStruct((seq, heads * HD), f32)
    return pl.pallas_call(
        functools.partial(attend_back_kernel, block),
        grid=(heads,),
        in_specs=[raw_spec(seq, heads, i) for i in range(2)]
        + head_specs(seq, heads)
        + [head] * 4
        + [pl.BlockSpec((1, seq, 1), lambda h: (h, 0, 0))],
        out_specs=[head] * 3 + [column] * 2 + [gain] * 2,
        out_shape=[wide, wide, jax.ShapeDtypeStruct((seq, heads * HD), bf16)]
        + [jax.ShapeDtypeStruct((seq, 1), f32)] * 2
        + [jax.ShapeDtypeStruct((1, heads * HD), f32)] * 2,
        scratch_shapes=[pltpu.VMEM((seq, HD), f32)] * 3,
        compiler_params=pltpu.CompilerParams(vmem_limit_bytes=48 * 2**20),
        cost_estimate=pl.CostEstimate(flops=10**6, bytes_accessed=10**5, transcendentals=0),
    )(projected, projected, *shared, query, keyed, valued, grad, log_total)


def slot_choice(place, slots):
    return lax.broadcasted_iota(jnp.int32, (slots, place.shape[1]), 0) == place


def slot_weight(place, gate, slots):
    return jnp.sum(jnp.where(slot_choice(place, slots), gate, 0.0), axis=1, keepdims=True)


def spans_of(count, slots):
    return [(b, slice(b * slots, (b + 1) * slots)) for b in range(count)]


def add_tokens(place, b, slots, out, sum_tokens, partial):
    expert = pl.program_id(0)
    back = mm(slot_choice(place[0, b], slots).astype(bf16), out, ((0,), (0,)))

    @pl.when(expert == 0)
    def _():
        sum_tokens[b] = back

    @pl.when(expert > 0)
    def _():
        sum_tokens[b] += back

    @pl.when(expert == pl.num_programs(0) - 1)
    def _():
        partial[b][...] = sum_tokens[b].astype(bf16)


def hidden_kernel(count, slots, place, *refs):
    blocks, w_gate, w_up = refs[:count], refs[count], refs[count + 1]
    rows, activated, gate_pre, up_pre = refs[-4:]
    for b, span in spans_of(count, slots):
        choice = slot_choice(place[0, b], slots).astype(bf16)
        rows[0, 0, span] = mm(choice, blocks[b][...], ((1,), (0,))).astype(bf16)
    rows_in = rows[0, 0]
    g = mm(rows_in, w_gate[0], ((1,), (0,)))
    u = mm(rows_in, w_up[0], ((1,), (0,)))
    gate_pre[0], up_pre[0] = g.astype(bf16), u.astype(bf16)
    activated[0, 0] = (g * jax.nn.sigmoid(g) * u).astype(bf16)


def out_kernel(count, slots, place, gate, activated, w_down, *refs):
    partial, sum_tokens = refs[:-1], refs[-1]
    result = mm(activated[0, 0], w_down[0], ((1,), (1,)))
    for b, span in spans_of(count, slots):
        out = (result[span] * slot_weight(place[0, b], gate[0, b], slots)).astype(bf16)
        add_tokens(place, b, slots, out, sum_tokens, partial)


def expert_back_kernel(count, slots, place, gate, *refs):
    blocks, (w_gate, w_up, w_down) = refs[:count], refs[count : count + 3]
    gate_pre, up_pre = refs[count + 3 : count + 5]
    grad_rows, grad_gate, grad_up = refs[-4 - count : -1 - count]
    partial, sum_tokens = refs[-1 - count : -1], refs[-1]
    for b, span in spans_of(count, slots):
        choice = slot_choice(place[0, b], slots).astype(bf16)
        weight = slot_weight(place[0, b], gate[0, b], slots)
        picked = mm(choice, blocks[b][...], ((1,), (0,)))
        grad_rows[0, 0, span] = (picked * weight).astype(bf16)
    grad_act = mm(grad_rows[0, 0], w_down[0], ((1,), (0,)))
    g, u = gate_pre[0].astype(f32), up_pre[0].astype(f32)
    sigmoid = jax.nn.sigmoid(g)
    dg = (grad_act * u * sigmoid * (1.0 + g * (1.0 - sigmoid))).astype(bf16)
    du = (grad_act * g * sigmoid).astype(bf16)
    grad_gate[0, 0], grad_up[0, 0] = dg, du
    result = mm(dg, w_gate[0], ((1,), (1,))) + mm(du, w_up[0], ((1,), (1,)))
    result = result.astype(bf16)
    for b, span in spans_of(count, slots):
        add_tokens(place, b, slots, result[span], sum_tokens, partial)


class Experts:
    def __init__(self, group, slots, place, gate, blocks, weights):
        self.group, self.slots, self.place, self.gate = group, slots, place, gate
        self.experts, self.width, self.hidden = weights[0].shape
        self.count, self.own = len(blocks), blocks[0].shape[0]
        self.rows = self.count * slots
        group_of = lambda e: (e, group, 0, 0)
        self.table = pl.BlockSpec((1, self.count, 1, self.own), group_of)
        self.tokens = pl.BlockSpec((self.own, self.width), lambda e: (0, 0))
        self.weight = pl.BlockSpec((1, self.width, self.hidden), lambda e: (e, 0, 0))
        self.local = pl.BlockSpec((1, self.rows, self.hidden), lambda e: (e, 0, 0))
        self.wide = pl.BlockSpec((1, 1, self.rows, self.width), group_of)
        self.narrow = pl.BlockSpec((1, 1, self.rows, self.hidden), group_of)
        self.sums = pltpu.VMEM((self.count, self.own, self.width), f32)

    def shape(self, spec):
        rows, experts = self.rows, self.experts
        shapes = [
            (self.tokens, (self.own, self.width)),
            (self.local, (experts, rows, self.hidden)),
            (self.wide, (experts, 2, rows, self.width)),
            (self.narrow, (experts, 2, rows, self.hidden)),
        ]
        [shape] = [shape for known, shape in shapes if known is spec]
        return jax.ShapeDtypeStruct(shape, bf16)

    def run(self, kernel, ins, outs, scratch, prior=()):
        specs = [spec for spec, _ in ins] + [pl.BlockSpec(memory_space=pl.ANY)] * len(prior)
        return pl.pallas_call(
            functools.partial(kernel, self.count, self.slots),
            grid=(self.experts,),
            in_specs=specs,
            out_specs=outs,
            out_shape=[self.shape(spec) for spec in outs],
            scratch_shapes=scratch,
            input_output_aliases={len(ins) + i: i for i in range(len(prior))},
            compiler_params=pltpu.CompilerParams(vmem_limit_bytes=58 * 2**20),
            cost_estimate=pl.CostEstimate(
                flops=self.experts * self.rows * self.width * self.hidden * 4,
                bytes_accessed=self.experts * self.width * self.hidden * 6,
                transcendentals=self.experts * self.rows * self.hidden,
            ),
        )(*[array for _, array in ins], *prior)

    def to_hidden(self, blocks, w_gate, w_up, prior):
        ins = [(self.table, self.place)] + [(self.tokens, block) for block in blocks]
        ins += [(self.weight, w_gate), (self.weight, w_up)]
        outs = [self.wide, self.narrow, self.local, self.local]
        return self.run(hidden_kernel, ins, outs, [], prior)

    def to_tokens(self, activated, w_down):
        ins = [(self.table, self.place), (self.table, self.gate)]
        ins += [(self.narrow, activated), (self.weight, w_down)]
        return self.run(out_kernel, ins, [self.tokens] * self.count, [self.sums])

    def backward(self, blocks, weights, pres, prior):
        ins = [(self.table, self.place), (self.table, self.gate)]
        ins += [(self.tokens, block) for block in blocks]
        ins += [(self.weight, weight) for weight in weights]
        ins += [(self.local, pre) for pre in pres]
        outs = [self.wide, self.narrow, self.narrow] + [self.tokens] * self.count
        return self.run(expert_back_kernel, ins, outs, [self.sums], prior)


def dot(spec, left, right):
    return jnp.einsum(spec, left, right, preferred_element_type=f32)


def shards(
    tokens,
    w_attn,
    norm_gains,
    w_expert,
    gate_weights,
    routes,
    segment,
    valid_mask,
    teacher,
    cotangent,
):
    outer, planes, seqs = lax.axis_size("o"), lax.axis_size("z"), lax.axis_size("s")
    plane, rank = lax.axis_index("z"), lax.axis_index("s")
    own, width = tokens.shape
    rows_dev = w_attn.shape[0]
    seq = own * seqs
    heads = H // seqs
    cols = heads * HD
    hidden = w_expert.shape[2] // 3
    part = w_expert.shape[0]
    capacity = own * TOP * 17 // (16 * planes * seqs)
    scale = HD ** (-0.5)

    def to_inner(v):
        lead = v.shape[:-1]
        v = v.reshape(lead + (outer * planes, CORES, part))
        return jnp.swapaxes(v, -3, -2).reshape(lead + (width,))

    def to_outer(v):
        lead = v.shape[:-1]
        v = v.reshape(lead + (CORES, outer * planes, part))
        return jnp.swapaxes(v, -3, -2).reshape(lead + (width,))

    first_core = lax.axis_index("c") == 0

    def halves(v):
        low, high = v[..., : width // 2], v[..., width // 2 :]
        return jnp.where(first_core, low, high), jnp.where(first_core, high, low)

    def whole_of(mine, other, axis):
        low, high = jnp.where(first_core, mine, other), jnp.where(first_core, other, mine)
        return jnp.concatenate([low, high], axis=axis)

    def stack_rows(blocks, start=0):
        rows = in_order(blocks, "z", start)
        return collect(rows, "o").reshape((width // 2,) + rows.shape[2:])

    def sum_rows(grad, *others):
        count = grad.shape[1]
        grad = exchange_sum(grad.reshape(CORES, width // 2, count), "c").astype(bf16)
        if outer > 1:
            grad = exchange_sum(grad.reshape(outer, planes * part, count), "o").astype(bf16)
        if others:
            grad = after(grad, *others)
        return exchange_sum(grad.reshape(planes, part, count), "z")

    def gather_sum(value):
        for axis in ("z", "s", "c", "o"):
            value = sum(gather_near(jnp.broadcast_to(value, (8, PAD)), axis))[0, 0]
        return value

    by_expert = w_expert.transpose(1, 0, 2)

    def expert_chunk(i, start=0):
        def piece_for(owner):
            return lax.dynamic_slice(by_expert, (owner, 0, i * hidden), (1, part, hidden))[0]

        return exchange(piece_for, "z", start)

    def gather_plane(ready):
        chunk = ready.reshape(planes * part, hidden)
        chunk = lax.all_gather(chunk, ("s", "c", "o"), axis=0, tiled=True)
        return chunk.reshape(seqs, width, hidden)

    count = jnp.sum(valid_mask).astype(jnp.int32)
    digits = jnp.stack([count // 128, count % 128]).astype(bf16)
    extra = jnp.concatenate(
        [
            norm_gains,
            jnp.broadcast_to(digits[None], (rows_dev, 2)),
            jnp.zeros((rows_dev, PAD - 6), bf16),
        ],
        axis=1,
    )

    def columns_of(owner):
        picked = [
            lax.dynamic_slice_in_dim(w_attn, i * width + owner * cols, cols, 1) for i in range(4)
        ]
        return jnp.concatenate(picked[:3] + [extra] + picked[3:], axis=1)

    mine_blocks = exchange(columns_of, "s")
    gate_blocks = expert_chunk(0)
    inputs = to_inner(tokens)
    token_blocks = gather_near(inputs, "s")
    inputs = inputs.astype(f32)

    mine = in_order(mine_blocks, "s").reshape(part, 4 * cols + PAD)
    seq_tokens = in_order(token_blocks, "s", token(mine)).reshape(seq, width)
    gate_ready = in_order(gate_blocks, "z", token(seq_tokens))
    w_gate = gather_plane(gate_ready)
    in_blocks = gather_near(after(mine[:, : 3 * cols + PAD], gate_ready), "z")
    seq_tokens = seq_tokens.astype(f32)
    seq_factor = rms_factor(seq_tokens)
    w_in = stack_rows(in_blocks, token(seq_factor))
    w_in_other = send(w_in, "c", 1)
    up_blocks = expert_chunk(1, token(w_in))

    side = whole_of(w_in[:, 3 * cols :], w_in_other[:, 3 * cols :], 0)[:, :6].astype(f32).T
    gain_in, gain_mid = side[0], side[1]
    gain_q = lax.dynamic_slice_in_dim(to_outer(side[2]), rank * cols, cols, 0)
    gain_k = lax.dynamic_slice_in_dim(to_outer(side[3]), rank * cols, cols, 0)
    total_count = jnp.sum(side[4, ::rows_dev]) * 128.0 + jnp.sum(side[5, ::rows_dev])

    routed = jnp.stack(
        gather_near(jnp.concatenate([routes.astype(f32), gate_weights], axis=1), "z")
    )
    route_all, gate_all = routed[..., :TOP].astype(jnp.int32), routed[..., TOP:]
    expert_ids = jnp.arange(seqs) * planes + plane
    match = route_all[:, :, None, :] == expert_ids[None, None, :, None]
    used = jnp.any(match, axis=-1)
    gate_of = jnp.sum(jnp.where(match, gate_all[:, :, None, :], 0.0), axis=-1)
    before = (jnp.arange(own)[:, None] > jnp.arange(own)[None, :]).astype(bf16)
    place = dot("tu,buk->btk", before, used.astype(bf16)).astype(jnp.int32)
    place = jnp.where(used, place, -1)
    slots = -(-capacity // 16) * 16
    place = place.transpose(2, 0, 1)[:, :, None, :]
    gate_of = gate_of.transpose(2, 0, 1)[:, :, None, :]

    groups = [[k for k in range(planes) if k % 2 == odd] for odd in range(2)]

    def by_group(table):
        return jnp.concatenate([table[:, k : k + 1] for group in groups for k in group], axis=1)

    place, gate_of = by_group(place), by_group(gate_of)

    def near_planes(block):
        near = [block] + [None] * (planes - 1)
        for k in groups[0][1:]:
            near[k] = send(block, "z", k)
        later = after(block, *[near[k] for k in groups[0][1:]])
        for k in groups[1]:
            near[k] = send(later, "z", k)
        return [[near[k] for k in group] for group in groups]

    def send_back(first, second):
        got = [first[0]] + [send(first[i], "z", k) for i, k in enumerate(groups[0]) if k]
        base = after(total(got), second[0])
        second = [after(part, base) for part in second]
        return second[0], [base] + [send(second[i], "z", k) for i, k in enumerate(groups[1])]

    def total(pieces):
        return sum(piece.astype(f32) for piece in pieces)

    normed_in = (seq_tokens * seq_factor * gain_in).astype(bf16)
    normed_mine, normed_other = halves(normed_in)
    projected = jnp.dot(normed_mine, w_in, preferred_element_type=f32) + jnp.dot(
        normed_other, w_in_other, preferred_element_type=f32
    )
    query_raw = projected[:, :cols]
    key_raw = projected[:, cols : 2 * cols]

    def over_heads(first, second, *others):
        pairs = gather_near(jnp.stack([first, second]), "s")
        if others:
            pairs[0] = after(pairs[0], *others)
        pair = sum(pairs) / width
        return pair[0][:, None], pair[1][:, None]

    q_mean, k_mean = over_heads(
        jnp.sum(query_raw * query_raw, axis=-1), jnp.sum(key_raw * key_raw, axis=-1)
    )
    up_ready = in_order(up_blocks, "z", token(projected))
    w_up = gather_plane(up_ready)
    out_blocks = gather_near(after(mine[:, 3 * cols + PAD :], up_ready), "z")
    out_rows = stack_rows(out_blocks, token(q_mean))
    cosine, sine = rope_tables(seq)
    shared = [
        after(q_mean, up_ready, w_gate, out_rows, place),
        k_mean,
        gain_q[None],
        gain_k[None],
        cosine,
        sine,
        segment[:, None],
        segment[None],
    ]
    attended, query, keyed, valued, log_total = attend(projected, shared, heads)
    w_out = collect(out_rows, "c").reshape(width, cols)
    down_blocks = expert_chunk(2, token(attended))
    attn_out = dot("tc,dc->td", attended, w_out).astype(bf16)
    residual = inputs + exchange_sum(attn_out.reshape(seqs, own, width), "s")
    down_ready = in_order(down_blocks, "z", token(residual))
    residual = after(residual, down_ready)
    w_down = gather_plane(down_ready)

    normed_mid = (residual * rms_factor(residual) * gain_mid).astype(bf16)
    expert_weights = (w_gate, w_up, w_down)
    blocks = near_planes(normed_mid)
    work = [Experts(i, slots, place, gate_of, blocks[i], expert_weights) for i in range(2)]
    rows_in, activated, *pres = work[0].to_hidden(blocks[0], w_gate, w_up, ())
    pres = [pres]
    blocks[1][0] = after(blocks[1][0], pres[0][0])
    rows_in, activated, *last = work[1].to_hidden(
        blocks[1], w_gate, w_up, (rows_in, activated)
    )
    pres.append(last)
    partial = [group.to_tokens(activated, w_down) for group in work]
    final_out = residual + total(send_back(*partial)[1])
    rows_in, activated = [v.reshape(seqs, -1, v.shape[-1]) for v in (rows_in, activated)]

    w_out_all = lax.all_gather(after(w_out, w_up), "s", axis=0)
    valid_f = valid_mask.astype(f32)[:, None]
    difference = final_out - to_inner(teacher).astype(f32)
    squared = jnp.sum(valid_f * difference * difference)
    squared = gather_sum(squared)
    loss_value = squared / (total_count * width)
    grad_out = (
        to_inner(cotangent).astype(f32) + 2.0 / (total_count * width) * valid_f * difference
    )

    def scatter_expert(grad):
        grad = grad.reshape(seqs * width, hidden)
        grad = lax.psum_scatter(grad, ("s", "c", "o"), scatter_dimension=0, tiled=True)
        return grad.reshape(planes, part, hidden)

    def to_owners(grad, start=0):
        def piece_for(owner):
            return lax.dynamic_index_in_dim(grad, owner, 0, keepdims=False)

        return exchange(piece_for, "z", start)

    blocks = near_planes(grad_out.astype(bf16))
    *grads, first, last = work[0].backward(blocks[0], expert_weights, pres[0], ())
    partial = [(first, last)]
    blocks[1][0] = after(blocks[1][0], first)
    *grads, first, last = work[1].backward(blocks[1], expert_weights, pres[1], grads)
    partial.append((first, last))
    back_last, back_pieces = send_back(*partial)
    grad_rows, grad_gate, grad_up = [v.reshape(seqs, -1, v.shape[-1]) for v in grads]
    grad_w_down = dot("krd,krf->kdf", grad_rows, after(activated, back_last)).astype(bf16)
    back_pieces[0] = after(back_pieces[0], grad_w_down)
    grad_mid = total(back_pieces)
    grad_w_gate = dot("krd,krf->kdf", rows_in, after(grad_gate, grad_mid)).astype(bf16)
    grad_resid_norm, gain_mid_grad = norm_back(residual, gain_mid, grad_mid)
    grad_resid = grad_out + grad_resid_norm

    grad_low = grad_resid.astype(bf16)
    grad_heads = dot("td,sdc->stc", grad_low, w_out_all).astype(bf16)
    head_blocks = exchange(
        lambda i: lax.dynamic_index_in_dim(grad_heads, i, 0, keepdims=False), "s"
    )
    grad_heads = in_order(head_blocks, "s", token(grad_w_gate)).reshape(seq, cols)
    low_blocks = gather_near(grad_low, "s")
    grad_attn_out = in_order(low_blocks, "s", token(grad_w_gate)).reshape(seq, width)
    grad_w_up = dot("krd,krf->kdf", rows_in, after(grad_up, grad_heads, grad_attn_out))
    grad_w_up = grad_w_up.astype(bf16)
    up_done = grad_w_up
    grad_w_down, grad_w_gate, grad_w_up = [
        scatter_expert(grad) for grad in (grad_w_down, grad_w_gate, grad_w_up)
    ]
    down_blocks, gate_blocks = to_owners(grad_w_down), to_owners(grad_w_gate)
    down_ready = in_order(down_blocks, "z", token(up_done))
    grad_heads = after(grad_heads, down_ready)
    grad_q, grad_k, grad_v, q_inner, k_inner, gain_q_grad, gain_k_grad = attend_back(
        projected, shared, query, keyed, valued, grad_heads, log_total, heads
    )
    grad_w_out = sum_rows(dot("td,tc->dc", grad_attn_out, attended).astype(bf16))
    q_inner, k_inner = over_heads(q_inner[:, 0], k_inner[:, 0], up_done)

    def norm_grad(grad, raw, mean, inner):
        factor = lax.rsqrt(mean + epsilon)
        return (factor * (grad - raw * factor * inner)).astype(bf16)

    grad_proj = jnp.concatenate(
        [
            norm_grad(grad_q, query_raw, q_mean, q_inner),
            norm_grad(grad_k, key_raw, k_mean, k_inner),
            grad_v,
        ],
        axis=1,
    )
    grad_padded = jnp.concatenate([grad_proj, jnp.zeros((seq, PAD), bf16)], axis=1)

    def back_half(weight):
        grad = dot("tc,dc->td", grad_padded, weight).astype(bf16)
        return exchange_sum(grad.reshape(seqs, own, width // 2), "s")

    grad_normed = whole_of(back_half(w_in), back_half(w_in_other), 1)
    grad_w_qkv = dot("td,tc->dc", normed_in, grad_proj).astype(bf16)
    gate_ready = in_order(gate_blocks, "z", token(grad_w_qkv))
    grad_w_qkv = sum_rows(grad_w_qkv, gate_ready)
    up_blocks = to_owners(grad_w_up, token(grad_w_qkv))
    grad_in_norm, gain_in_grad = norm_back(inputs, gain_in, grad_normed)
    grad_tokens = to_outer(grad_resid + grad_in_norm)

    def widen(local):
        full = jnp.zeros((width,), f32)
        return to_inner(lax.dynamic_update_slice_in_dim(full, local, rank * cols, 0))

    gains = jnp.stack([gain_in_grad, gain_mid_grad, widen(gain_q_grad[0]), widen(gain_k_grad[0])])
    for axis in ("z", "c", "s", "o"):
        gains = sum(gather_near(gains, axis))
    row = (lax.axis_index(("c", "o", "z")) * seqs + rank) * rows_dev
    grad_gains = lax.dynamic_slice_in_dim(gains, row, rows_dev, 1).T

    def own_rows(grad):
        grad = grad.astype(bf16).reshape(seqs, rows_dev, grad.shape[1])
        got = exchange(lambda i: lax.dynamic_index_in_dim(grad, i, 0, keepdims=False), "s")
        return in_order(got, "s").astype(f32)

    qkv_part, out_part = own_rows(grad_w_qkv), own_rows(grad_w_out)
    grad_attn = jnp.concatenate(
        [qkv_part[s, :, i * cols : (i + 1) * cols] for i in range(3) for s in range(seqs)]
        + [out_part[s] for s in range(seqs)],
        axis=1,
    )
    up_ready = in_order(up_blocks, "z")
    grad_expert = jnp.concatenate([gate_ready, up_ready, down_ready], axis=2)
    grad_expert = grad_expert.astype(f32).transpose(1, 0, 2)
    return (
        to_outer(final_out).astype(bf16),
        loss_value,
        grad_tokens,
        grad_attn,
        grad_gains,
        grad_expert,
    )


def solution(mesh):
    fsdp, seqs = mesh.shape["fsdp"], mesh.shape["sp"]

    def whole(*arrays):
        planes = arrays[3].shape[1] // seqs
        outer = fsdp // (planes * CORES)
        inner = Mesh(mesh.devices.reshape(outer, planes, CORES, seqs), ("o", "z", "c", "s"))
        every = ("o", "z", "c", "s")
        rows = P(every, None)
        experts = P(("o", "z", "c"), "s", None)
        return jax.shard_map(
            shards,
            mesh=inner,
            in_specs=(
                rows,
                rows,
                rows,
                experts,
                rows,
                rows,
                P(("o", "z", "c")),
                P(every),
                rows,
                rows,
            ),
            out_specs=(rows, P(), rows, rows, rows, experts),
            check_vma=False,
        )(*arrays)

    return whole
```

```python
import functools

import jax
import jax.numpy as jnp
from jax import lax
from jax.experimental import pallas as pl
from jax.experimental.pallas import tpu as pltpu
from jax.sharding import Mesh, PartitionSpec as P

H = 16
HD = 128
TOP = 8
CORES = 2
PAD = 128

epsilon = 1e-05
masked = -1e30
f32 = jnp.float32
bf16 = jnp.bfloat16


def send(block, axis, step):
    size = lax.axis_size(axis)
    return lax.ppermute(block, axis, [(i, i ^ step) for i in range(size)])


def gather_near(block, axis):
    return [block] + [send(block, axis, k) for k in range(1, lax.axis_size(axis))]


def in_order(blocks, axis, start=0):
    rank = lax.axis_index(axis)
    if len(blocks) == 1:
        return blocks[0][None]
    stacked = jnp.zeros((len(blocks),) + blocks[0].shape, blocks[0].dtype)
    for k, block in enumerate(blocks):
        stacked = lax.dynamic_update_index_in_dim(stacked, block, (rank ^ k) + start, 0)
    return stacked


def collect(block, axis):
    return in_order(gather_near(block, axis), axis)


def exchange(piece_for, axis, start=0):
    rank, size = lax.axis_index(axis) + start, lax.axis_size(axis)
    return [piece_for(rank)] + [send(piece_for(rank ^ k), axis, k) for k in range(1, size)]


def exchange_sum(pieces, axis):
    got = exchange(lambda i: lax.dynamic_index_in_dim(pieces, i, 0, keepdims=False), axis)
    return sum(piece.astype(f32) for piece in got)


def token(*values):
    firsts = [value[(slice(0, 1),) * value.ndim].reshape(()).astype(f32) for value in values]
    total = sum(firsts)
    return (total != total).astype(jnp.int32)


def together(work, *operands):
    shapes = jax.eval_shape(work, *operands)

    def nothing(*_):
        return jax.tree.map(lambda leaf: jnp.zeros(leaf.shape, leaf.dtype), shapes)

    return lax.cond(token(jax.tree.leaves(operands)[0]) == 0, work, nothing, *operands)


def after(value, *others):
    return value + token(*others).astype(value.dtype)


def rms_factor(values):
    return lax.rsqrt(jnp.mean(values * values, axis=-1, keepdims=True) + epsilon)


def norm_back(values, gain_vec, grad_in):
    factor = rms_factor(values)
    normed = values * factor
    gain_grad = jnp.sum(grad_in * normed, axis=0)
    inner = grad_in * gain_vec
    grad = factor * (inner - normed * jnp.mean(inner * normed, axis=-1, keepdims=True))
    return grad, gain_grad


def rope_tables(rows):
    inverse = 10000.0 ** (-(jnp.arange(HD // 2).astype(f32) * 2.0 / HD))
    angles = jnp.arange(rows).astype(f32)[:, None] * inverse[None, :]
    cosine = jnp.concatenate([jnp.cos(angles), jnp.cos(angles)], axis=-1)
    sine = jnp.concatenate([-jnp.sin(angles), jnp.sin(angles)], axis=-1)
    return cosine, sine


def mm(left, right, dims):
    return lax.dot_general(left, right, (dims, ((), ())), preferred_element_type=f32)


def masked_scores(query, keyed, seg_col, seg_row, first, scale):
    scores = mm(query, keyed, ((1,), (1,))) * scale
    rows = first + lax.broadcasted_iota(jnp.int32, scores.shape, 0)
    allowed = (rows >= lax.broadcasted_iota(jnp.int32, scores.shape, 1)) & (seg_col == seg_row)
    return jnp.where(allowed, scores, masked)


def attend_kernel(
    block,
    q_raw,
    k_raw,
    v_raw,
    q_mean,
    k_mean,
    gain_q,
    gain_k,
    cosine,
    sine,
    seg_col,
    seg_row,
    out,
    q_out,
    k_out,
    v_out,
    log_total,
):
    def rope(raw, mean, gain):
        values = raw[...] * lax.rsqrt(mean[...] + epsilon) * gain[...]
        turned = pltpu.roll(values, HD // 2, 1)
        return (values * cosine[...] + turned * sine[...]).astype(bf16)

    q_out[...] = rope(q_raw, q_mean, gain_q)
    k_out[...] = rope(k_raw, k_mean, gain_k)
    v_out[...] = v_raw[...].astype(bf16)
    for first in range(0, out.shape[0], block):
        last = first + block
        scores = masked_scores(
            q_out[first:last],
            k_out[:last],
            seg_col[first:last],
            seg_row[:, :last],
            first,
            HD**-0.5,
        )
        top = jnp.max(scores, axis=-1, keepdims=True)
        exps = jnp.exp(scores - top)
        total = jnp.sum(exps, axis=-1, keepdims=True)
        weights = (exps * (1.0 / total)).astype(bf16)
        out[first:last] = mm(weights, v_out[:last], ((1,), (0,))).astype(bf16)
        log_total[0, first:last] = top + jnp.log(total)


def attend_back_kernel(
    block,
    q_raw,
    k_raw,
    q_mean,
    k_mean,
    gain_q,
    gain_k,
    cosine,
    sine,
    seg_col,
    seg_row,
    query,
    keyed,
    valued,
    grad,
    log_total,
    grad_q,
    grad_k,
    grad_v,
    q_inner,
    k_inner,
    gain_q_grad,
    gain_k_grad,
    sum_q,
    sum_k,
    sum_v,
):
    scale = HD**-0.5
    sum_k[...] = jnp.zeros_like(sum_k)
    sum_v[...] = jnp.zeros_like(sum_v)
    for first in range(0, query.shape[0], block):
        last = first + block
        q_block, g_block = query[first:last], grad[first:last]
        scores = masked_scores(
            q_block, keyed[:last], seg_col[first:last], seg_row[:, :last], first, scale
        )
        probs = jnp.exp(scores - log_total[0, first:last])
        sum_v[:last] += mm(probs.astype(bf16), g_block, ((0,), (0,)))
        grad_probs = mm(g_block, valued[:last], ((1,), (1,)))
        inner = jnp.sum(probs * grad_probs, axis=-1, keepdims=True)
        grad_scores = (probs * (grad_probs - inner)).astype(bf16)
        sum_q[first:last] = mm(grad_scores, keyed[:last], ((1,), (0,))) * scale
        sum_k[:last] += mm(grad_scores, q_block, ((0,), (0,))) * scale
    grad_v[...] = sum_v[...].astype(bf16)

    def undo(total, raw, mean, gain, inner_out, gain_out, grad_out):
        low = total[...].astype(bf16).astype(f32)
        back = low * cosine[...] + pltpu.roll(low * sine[...], HD // 2, 1)
        normed = raw[...] * lax.rsqrt(mean[...] + epsilon)
        gain_out[...] = jnp.sum(back * normed, axis=0, keepdims=True)
        back = back * gain[...]
        grad_out[...] = back
        inner = jnp.sum(back * normed, axis=-1, keepdims=True)

        @pl.when(pl.program_id(0) == 0)
        def _():
            inner_out[...] = inner

        @pl.when(pl.program_id(0) > 0)
        def _():
            inner_out[...] += inner

    undo(sum_q, q_raw, q_mean, gain_q, q_inner, gain_q_grad, grad_q)
    undo(sum_k, k_raw, k_mean, gain_k, k_inner, gain_k_grad, grad_k)


def head_specs(seq, heads):
    column = pl.BlockSpec((seq, 1), lambda h: (0, 0))
    gain = pl.BlockSpec((1, HD), lambda h: (0, h))
    table = pl.BlockSpec((seq, HD), lambda h: (0, 0))
    return [column, column, gain, gain, table, table, column, pl.BlockSpec((1, seq), lambda h: (0, 0))]


def raw_spec(seq, heads, which):
    return pl.BlockSpec((seq, HD), lambda h: (0, which * heads + h))


def attend(projected, shared, heads):
    seq = projected.shape[0]
    block = min(256, seq)
    head = pl.BlockSpec((seq, HD), lambda h: (0, h))
    low = jax.ShapeDtypeStruct((seq, heads * HD), bf16)
    return pl.pallas_call(
        functools.partial(attend_kernel, block),
        grid=(heads,),
        in_specs=[raw_spec(seq, heads, i) for i in range(3)] + head_specs(seq, heads),
        out_specs=[head] * 4 + [pl.BlockSpec((1, seq, 1), lambda h: (h, 0, 0))],
        out_shape=[low] * 4 + [jax.ShapeDtypeStruct((heads, seq, 1), f32)],
        compiler_params=pltpu.CompilerParams(vmem_limit_bytes=48 * 2**20),
        cost_estimate=pl.CostEstimate(flops=10**6, bytes_accessed=10**5, transcendentals=0),
    )(projected, projected, projected, *shared)


def attend_back(projected, shared, query, keyed, valued, grad, log_total, heads):
    seq = projected.shape[0]
    block = min(256, seq)
    head = pl.BlockSpec((seq, HD), lambda h: (0, h))
    column = pl.BlockSpec((seq, 1), lambda h: (0, 0))
    gain = pl.BlockSpec((1, HD), lambda h: (0, h))
    wide = jax.ShapeDtypeStruct((seq, heads * HD), f32)
    return pl.pallas_call(
        functools.partial(attend_back_kernel, block),
        grid=(heads,),
        in_specs=[raw_spec(seq, heads, i) for i in range(2)]
        + head_specs(seq, heads)
        + [head] * 4
        + [pl.BlockSpec((1, seq, 1), lambda h: (h, 0, 0))],
        out_specs=[head] * 3 + [column] * 2 + [gain] * 2,
        out_shape=[wide, wide, jax.ShapeDtypeStruct((seq, heads * HD), bf16)]
        + [jax.ShapeDtypeStruct((seq, 1), f32)] * 2
        + [jax.ShapeDtypeStruct((1, heads * HD), f32)] * 2,
        scratch_shapes=[pltpu.VMEM((seq, HD), f32)] * 3,
        compiler_params=pltpu.CompilerParams(vmem_limit_bytes=48 * 2**20),
        cost_estimate=pl.CostEstimate(flops=10**6, bytes_accessed=10**5, transcendentals=0),
    )(projected, projected, *shared, query, keyed, valued, grad, log_total)


def slot_choice(place, slots):
    return lax.broadcasted_iota(jnp.int32, (slots, place.shape[1]), 0) == place


def slot_weight(place, gate, slots):
    return jnp.sum(jnp.where(slot_choice(place, slots), gate, 0.0), axis=1, keepdims=True)


def spans_of(count, slots):
    return [(b, slice(b * slots, (b + 1) * slots)) for b in range(count)]


def add_tokens(place, b, slots, out, sum_tokens, partial):
    expert = pl.program_id(0)
    back = mm(slot_choice(place[0, b], slots).astype(bf16), out, ((0,), (0,)))

    @pl.when(expert == 0)
    def _():
        sum_tokens[b] = back

    @pl.when(expert > 0)
    def _():
        sum_tokens[b] += back

    @pl.when(expert == pl.num_programs(0) - 1)
    def _():
        partial[b][...] = sum_tokens[b].astype(bf16)


def hidden_kernel(count, slots, place, *refs):
    blocks, w_gate, w_up = refs[:count], refs[count], refs[count + 1]
    rows, activated, gate_pre, up_pre = refs[-4:]
    for b, span in spans_of(count, slots):
        choice = slot_choice(place[0, b], slots).astype(bf16)
        rows[0, 0, span] = mm(choice, blocks[b][...], ((1,), (0,))).astype(bf16)
    rows_in = rows[0, 0]
    g = mm(rows_in, w_gate[0], ((1,), (0,)))
    u = mm(rows_in, w_up[0], ((1,), (0,)))
    gate_pre[0], up_pre[0] = g.astype(bf16), u.astype(bf16)
    activated[0, 0] = (g * jax.nn.sigmoid(g) * u).astype(bf16)


def out_kernel(count, slots, place, gate, activated, w_down, *refs):
    partial, sum_tokens = refs[:-1], refs[-1]
    result = mm(activated[0, 0], w_down[0], ((1,), (1,)))
    for b, span in spans_of(count, slots):
        out = (result[span] * slot_weight(place[0, b], gate[0, b], slots)).astype(bf16)
        add_tokens(place, b, slots, out, sum_tokens, partial)


def expert_back_kernel(count, slots, place, gate, *refs):
    blocks, (w_gate, w_up, w_down) = refs[:count], refs[count : count + 3]
    gate_pre, up_pre = refs[count + 3 : count + 5]
    grad_rows, grad_gate, grad_up = refs[-4 - count : -1 - count]
    partial, sum_tokens = refs[-1 - count : -1], refs[-1]
    for b, span in spans_of(count, slots):
        choice = slot_choice(place[0, b], slots).astype(bf16)
        weight = slot_weight(place[0, b], gate[0, b], slots)
        picked = mm(choice, blocks[b][...], ((1,), (0,)))
        grad_rows[0, 0, span] = (picked * weight).astype(bf16)
    grad_act = mm(grad_rows[0, 0], w_down[0], ((1,), (0,)))
    g, u = gate_pre[0].astype(f32), up_pre[0].astype(f32)
    sigmoid = jax.nn.sigmoid(g)
    dg = (grad_act * u * sigmoid * (1.0 + g * (1.0 - sigmoid))).astype(bf16)
    du = (grad_act * g * sigmoid).astype(bf16)
    grad_gate[0, 0], grad_up[0, 0] = dg, du
    result = mm(dg, w_gate[0], ((1,), (1,))) + mm(du, w_up[0], ((1,), (1,)))
    result = result.astype(bf16)
    for b, span in spans_of(count, slots):
        add_tokens(place, b, slots, result[span], sum_tokens, partial)


class Experts:
    def __init__(self, group, slots, place, gate, blocks, weights):
        self.group, self.slots, self.place, self.gate = group, slots, place, gate
        self.experts, self.width, self.hidden = weights[0].shape
        self.count, self.own = len(blocks), blocks[0].shape[0]
        self.rows = self.count * slots
        group_of = lambda e: (e, group, 0, 0)
        self.table = pl.BlockSpec((1, self.count, 1, self.own), group_of)
        self.tokens = pl.BlockSpec((self.own, self.width), lambda e: (0, 0))
        self.weight = pl.BlockSpec((1, self.width, self.hidden), lambda e: (e, 0, 0))
        self.local = pl.BlockSpec((1, self.rows, self.hidden), lambda e: (e, 0, 0))
        self.wide = pl.BlockSpec((1, 1, self.rows, self.width), group_of)
        self.narrow = pl.BlockSpec((1, 1, self.rows, self.hidden), group_of)
        self.sums = pltpu.VMEM((self.count, self.own, self.width), f32)

    def shape(self, spec):
        rows, experts = self.rows, self.experts
        shapes = [
            (self.tokens, (self.own, self.width)),
            (self.local, (experts, rows, self.hidden)),
            (self.wide, (experts, 2, rows, self.width)),
            (self.narrow, (experts, 2, rows, self.hidden)),
        ]
        [shape] = [shape for known, shape in shapes if known is spec]
        return jax.ShapeDtypeStruct(shape, bf16)

    def run(self, kernel, ins, outs, scratch, prior=()):
        specs = [spec for spec, _ in ins] + [pl.BlockSpec(memory_space=pl.ANY)] * len(prior)
        return pl.pallas_call(
            functools.partial(kernel, self.count, self.slots),
            grid=(self.experts,),
            in_specs=specs,
            out_specs=outs,
            out_shape=[self.shape(spec) for spec in outs],
            scratch_shapes=scratch,
            input_output_aliases={len(ins) + i: i for i in range(len(prior))},
            compiler_params=pltpu.CompilerParams(vmem_limit_bytes=58 * 2**20),
            cost_estimate=pl.CostEstimate(
                flops=self.experts * self.rows * self.width * self.hidden * 4,
                bytes_accessed=self.experts * self.width * self.hidden * 6,
                transcendentals=self.experts * self.rows * self.hidden,
            ),
        )(*[array for _, array in ins], *prior)

    def to_hidden(self, blocks, w_gate, w_up, prior):
        ins = [(self.table, self.place)] + [(self.tokens, block) for block in blocks]
        ins += [(self.weight, w_gate), (self.weight, w_up)]
        outs = [self.wide, self.narrow, self.local, self.local]
        return self.run(hidden_kernel, ins, outs, [], prior)

    def to_tokens(self, activated, w_down):
        ins = [(self.table, self.place), (self.table, self.gate)]
        ins += [(self.narrow, activated), (self.weight, w_down)]
        return self.run(out_kernel, ins, [self.tokens] * self.count, [self.sums])

    def backward(self, blocks, weights, pres, prior):
        ins = [(self.table, self.place), (self.table, self.gate)]
        ins += [(self.tokens, block) for block in blocks]
        ins += [(self.weight, weight) for weight in weights]
        ins += [(self.local, pre) for pre in pres]
        outs = [self.wide, self.narrow, self.narrow] + [self.tokens] * self.count
        return self.run(expert_back_kernel, ins, outs, [self.sums], prior)


def dot(spec, left, right):
    return jnp.einsum(spec, left, right, preferred_element_type=f32)


def shards(
    tokens,
    w_attn,
    norm_gains,
    w_expert,
    gate_weights,
    routes,
    segment,
    valid_mask,
    teacher,
    cotangent,
):
    outer, planes, seqs = lax.axis_size("o"), lax.axis_size("z"), lax.axis_size("s")
    plane, rank = lax.axis_index("z"), lax.axis_index("s")
    own, width = tokens.shape
    rows_dev = w_attn.shape[0]
    seq = own * seqs
    heads = H // seqs
    cols = heads * HD
    hidden = w_expert.shape[2] // 3
    part = w_expert.shape[0]
    capacity = own * TOP * 17 // (16 * planes * seqs)
    scale = HD ** (-0.5)

    def to_inner(v):
        lead = v.shape[:-1]
        v = v.reshape(lead + (outer * planes, CORES, part))
        return jnp.swapaxes(v, -3, -2).reshape(lead + (width,))

    def to_outer(v):
        lead = v.shape[:-1]
        v = v.reshape(lead + (CORES, outer * planes, part))
        return jnp.swapaxes(v, -3, -2).reshape(lead + (width,))

    first_core = lax.axis_index("c") == 0

    def halves(v):
        low, high = v[..., : width // 2], v[..., width // 2 :]
        return jnp.where(first_core, low, high), jnp.where(first_core, high, low)

    def whole_of(mine, other, axis):
        low, high = jnp.where(first_core, mine, other), jnp.where(first_core, other, mine)
        return jnp.concatenate([low, high], axis=axis)

    def stack_rows(blocks, start=0):
        rows = in_order(blocks, "z", start)
        return collect(rows, "o").reshape((width // 2,) + rows.shape[2:])

    def sum_cores(grad):
        count = grad.shape[1]
        grad = exchange_sum(grad.reshape(CORES, width // 2, count), "c").astype(bf16)
        if outer > 1:
            grad = exchange_sum(grad.reshape(outer, planes * part, count), "o").astype(bf16)
        return grad.reshape(planes, part, count)

    def gather_sum(value):
        for axis in ("z", "s", "c", "o"):
            value = sum(gather_near(jnp.broadcast_to(value, (8, PAD)), axis))[0, 0]
        return value

    by_expert = w_expert.transpose(1, 0, 2)

    def expert_piece(i, owner):
        return lax.dynamic_slice(by_expert, (owner, 0, i * hidden), (1, part, hidden))[0]

    def gather_plane(ready):
        chunk = ready.reshape(planes * part, hidden)
        chunk = lax.all_gather(chunk, ("s", "c", "o"), axis=0, tiled=True)
        return chunk.reshape(seqs, width, hidden)

    count = jnp.sum(valid_mask).astype(jnp.int32)
    digits = jnp.stack([count // 128, count % 128]).astype(bf16)
    extra = jnp.concatenate(
        [
            norm_gains,
            jnp.broadcast_to(digits[None], (rows_dev, 2)),
            jnp.zeros((rows_dev, PAD - 6), bf16),
        ],
        axis=1,
    )

    def columns_of(owner):
        picked = [
            lax.dynamic_slice_in_dim(w_attn, i * width + owner * cols, cols, 1) for i in range(4)
        ]
        return jnp.concatenate(picked + [extra], axis=1)

    inputs = to_inner(tokens)

    def first_transfers(columns, experts, inputs):
        return (
            [columns[0]] + [send(columns[k], "s", k) for k in range(1, seqs)],
            [experts[0]] + [send(experts[k], "z", k) for k in range(1, planes)],
            gather_near(inputs, "s"),
        )

    mine_blocks, gate_blocks, token_blocks = together(
        first_transfers,
        [columns_of(rank ^ k) for k in range(seqs)],
        [expert_piece(0, plane ^ k) for k in range(planes)],
        inputs,
    )
    inputs = inputs.astype(f32)
    mine = in_order(mine_blocks, "s").reshape(part, 4 * cols + PAD)
    gate_ready = in_order(gate_blocks, "z")
    w_gate = gather_plane(gate_ready)
    in_blocks = gather_near(mine, "z")
    seq_tokens = in_order(token_blocks, "s").reshape(seq, width).astype(f32)
    seq_factor = rms_factor(seq_tokens)
    w_in = stack_rows(in_blocks, token(seq_factor))
    w_in_other = send(w_in, "c", 1)

    side = whole_of(w_in[:, 4 * cols :], w_in_other[:, 4 * cols :], 0)[:, :6].astype(f32).T
    gain_in, gain_mid = side[0], side[1]
    gain_q = lax.dynamic_slice_in_dim(to_outer(side[2]), rank * cols, cols, 0)
    gain_k = lax.dynamic_slice_in_dim(to_outer(side[3]), rank * cols, cols, 0)
    total_count = jnp.sum(side[4, ::rows_dev]) * 128.0 + jnp.sum(side[5, ::rows_dev])

    routed = jnp.stack(
        gather_near(jnp.concatenate([routes.astype(f32), gate_weights], axis=1), "z")
    )
    route_all, gate_all = routed[..., :TOP].astype(jnp.int32), routed[..., TOP:]
    expert_ids = jnp.arange(seqs) * planes + plane
    match = route_all[:, :, None, :] == expert_ids[None, None, :, None]
    used = jnp.any(match, axis=-1)
    gate_of = jnp.sum(jnp.where(match, gate_all[:, :, None, :], 0.0), axis=-1)
    before = (jnp.arange(own)[:, None] > jnp.arange(own)[None, :]).astype(bf16)
    place = dot("tu,buk->btk", before, used.astype(bf16)).astype(jnp.int32)
    place = jnp.where(used, place, -1)
    slots = -(-capacity // 16) * 16
    place = place.transpose(2, 0, 1)[:, :, None, :]
    gate_of = gate_of.transpose(2, 0, 1)[:, :, None, :]

    groups = [[k for k in range(planes) if k % 2 == odd] for odd in range(2)]

    def by_group(table):
        return jnp.concatenate([table[:, k : k + 1] for group in groups for k in group], axis=1)

    place, gate_of = by_group(place), by_group(gate_of)

    def near_planes(block):
        near = [block] + [None] * (planes - 1)
        for k in groups[0][1:]:
            near[k] = send(block, "z", k)
        later = after(block, *[near[k] for k in groups[0][1:]])
        for k in groups[1]:
            near[k] = send(later, "z", k)
        return [[near[k] for k in group] for group in groups]

    def send_back(first, second):
        got = [first[0]] + [send(first[i], "z", k) for i, k in enumerate(groups[0]) if k]
        base = after(total(got), second[0])
        second = [after(part, base) for part in second]
        return second[0], [base] + [send(second[i], "z", k) for i, k in enumerate(groups[1])]

    def total(pieces):
        return sum(piece.astype(f32) for piece in pieces)

    normed_in = (seq_tokens * seq_factor * gain_in).astype(bf16)
    normed_mine, normed_other = halves(normed_in)
    w_qkv, w_qkv_other = w_in[:, : 3 * cols], w_in_other[:, : 3 * cols]
    w_out = whole_of(w_in[:, 3 * cols : 4 * cols], w_in_other[:, 3 * cols : 4 * cols], 0)

    def project(experts, mine, other, weight, weight_other):
        got = [experts[0]] + [send(experts[k], "z", k) for k in range(1, planes)]
        projected = jnp.dot(mine, weight, preferred_element_type=f32) + jnp.dot(
            other, weight_other, preferred_element_type=f32
        )
        return got, projected

    up_blocks, projected = together(
        project,
        [expert_piece(1, (plane ^ k) + token(w_in)) for k in range(planes)],
        normed_mine,
        normed_other,
        w_qkv,
        w_qkv_other,
    )
    query_raw = projected[:, :cols]
    key_raw = projected[:, cols : 2 * cols]

    def over_heads(first, second, *others):
        pairs = gather_near(jnp.stack([first, second]), "s")
        if others:
            pairs[0] = after(pairs[0], *others)
        pair = sum(pairs) / width
        return pair[0][:, None], pair[1][:, None]

    q_mean, k_mean = over_heads(
        jnp.sum(query_raw * query_raw, axis=-1), jnp.sum(key_raw * key_raw, axis=-1)
    )
    up_ready = in_order(up_blocks, "z")
    w_up = gather_plane(up_ready)
    cosine, sine = rope_tables(seq)
    shared = [
        after(q_mean, up_ready, w_gate, place),
        k_mean,
        gain_q[None],
        gain_k[None],
        cosine,
        sine,
        segment[:, None],
        segment[None],
    ]
    attended, query, keyed, valued, log_total = attend(projected, shared, heads)
    attn_out = dot("tc,dc->td", attended, w_out).astype(bf16).reshape(seqs, own, width)

    def attention_back(parts, experts):
        return (
            [parts[0]] + [send(parts[k], "s", k) for k in range(1, seqs)],
            [experts[0]] + [send(experts[k], "z", k) for k in range(1, planes)],
        )

    got, down_blocks = together(
        attention_back,
        [lax.dynamic_index_in_dim(attn_out, rank ^ k, 0, keepdims=False) for k in range(seqs)],
        [expert_piece(2, (plane ^ k) + token(projected)) for k in range(planes)],
    )
    residual = inputs + sum(piece.astype(f32) for piece in got)
    down_ready = in_order(down_blocks, "z")
    w_down = gather_plane(down_ready)

    normed_mid = (residual * rms_factor(residual) * gain_mid).astype(bf16)
    expert_weights = (w_gate, w_up, w_down)
    blocks = near_planes(normed_mid)
    work = [Experts(i, slots, place, gate_of, blocks[i], expert_weights) for i in range(2)]
    rows_in, activated, *pres = work[0].to_hidden(blocks[0], w_gate, w_up, ())
    pres = [pres]
    blocks[1][0] = after(blocks[1][0], pres[0][0])
    rows_in, activated, *last = work[1].to_hidden(
        blocks[1], w_gate, w_up, (rows_in, activated)
    )
    pres.append(last)
    partial = [group.to_tokens(activated, w_down) for group in work]
    final_out = residual + total(send_back(*partial)[1])
    rows_in, activated = [v.reshape(seqs, -1, v.shape[-1]) for v in (rows_in, activated)]

    w_out_all = lax.all_gather(after(w_out, w_up), "s", axis=0)
    valid_f = valid_mask.astype(f32)[:, None]
    difference = final_out - to_inner(teacher).astype(f32)
    squared = jnp.sum(valid_f * difference * difference)
    squared = gather_sum(squared)
    loss_value = squared / (total_count * width)
    grad_out = (
        to_inner(cotangent).astype(f32) + 2.0 / (total_count * width) * valid_f * difference
    )

    def scatter_expert(grad):
        grad = grad.reshape(seqs * width, hidden)
        grad = lax.psum_scatter(grad, ("s", "c", "o"), scatter_dimension=0, tiled=True)
        return grad.reshape(planes, part, hidden)

    def to_owners(grad, start=0):
        def piece_for(owner):
            return lax.dynamic_index_in_dim(grad, owner, 0, keepdims=False)

        return exchange(piece_for, "z", start)

    blocks = near_planes(grad_out.astype(bf16))
    *grads, first, last = work[0].backward(blocks[0], expert_weights, pres[0], ())
    partial = [(first, last)]
    blocks[1][0] = after(blocks[1][0], first)
    *grads, first, last = work[1].backward(blocks[1], expert_weights, pres[1], grads)
    partial.append((first, last))
    back_last, back_pieces = send_back(*partial)
    grad_rows, grad_gate, grad_up = [v.reshape(seqs, -1, v.shape[-1]) for v in grads]
    grad_w_down = dot("krd,krf->kdf", grad_rows, activated).astype(bf16)
    back_pieces[0] = after(back_pieces[0], grad_w_down)
    grad_mid = total(back_pieces)
    grad_w_gate = dot("krd,krf->kdf", rows_in, after(grad_gate, grad_mid)).astype(bf16)
    grad_resid_norm, gain_mid_grad = norm_back(residual, gain_mid, grad_mid)
    grad_resid = grad_out + grad_resid_norm

    grad_low = grad_resid.astype(bf16)
    grad_heads = dot("td,sdc->stc", grad_low, w_out_all).astype(bf16)
    head_blocks = exchange(
        lambda i: lax.dynamic_index_in_dim(grad_heads, i, 0, keepdims=False), "s"
    )
    grad_heads = in_order(head_blocks, "s", token(grad_w_gate)).reshape(seq, cols)
    grad_w_down = scatter_expert(grad_w_down)
    grad_w_gate = scatter_expert(grad_w_gate)

    def attention_grads(experts, low, rows_in, grad_up, grad_heads, raw, *rest):
        moved = [experts[0]] + [send(experts[k], "z", k) for k in range(1, planes)]
        near = gather_near(low, "s")
        grad_w_up = dot("krd,krf->kdf", rows_in, grad_up).astype(bf16)
        *rest, log_total = rest
        query, keyed, valued, *shared = rest
        result = attend_back(
            raw, shared, query, keyed, valued, after(grad_heads, grad_w_up), log_total, heads
        )
        return moved, near, grad_w_up, result

    down_blocks, low_blocks, grad_w_up, result = together(
        attention_grads,
        [lax.dynamic_index_in_dim(grad_w_down, plane ^ k, 0, keepdims=False) for k in range(planes)],
        grad_low,
        rows_in,
        grad_up,
        grad_heads,
        projected,
        query,
        keyed,
        valued,
        *shared,
        log_total,
    )
    grad_q, grad_k, grad_v, q_inner, k_inner, gain_q_grad, gain_k_grad = result
    up_done = grad_w_up
    grad_w_up = scatter_expert(grad_w_up)
    grad_attn_out = in_order(low_blocks, "s").reshape(seq, width)
    grad_w_out = dot("td,tc->dc", grad_attn_out, attended).astype(bf16)
    q_inner, k_inner = over_heads(q_inner[:, 0], k_inner[:, 0], grad_w_out)

    def norm_grad(grad, raw, mean, inner):
        factor = lax.rsqrt(mean + epsilon)
        return (factor * (grad - raw * factor * inner)).astype(bf16)

    grad_proj = jnp.concatenate(
        [
            norm_grad(grad_q, query_raw, q_mean, q_inner),
            norm_grad(grad_k, key_raw, k_mean, k_inner),
            grad_v,
        ],
        axis=1,
    )

    def back_half(weight):
        grad = dot("tc,dc->td", grad_proj, weight).astype(bf16)
        return exchange_sum(grad.reshape(seqs, own, width // 2), "s")

    grad_normed = whole_of(back_half(w_qkv), back_half(w_qkv_other), 1)
    grad_w_qkv = dot("td,tc->dc", normed_in, grad_proj).astype(bf16)
    grad_w_qkv, grad_w_out = sum_cores(grad_w_qkv), sum_cores(grad_w_out)

    def row_transfers(qkv, out, experts):
        return [
            [parts[0]] + [send(parts[k], "z", k) for k in range(1, planes)]
            for parts in (qkv, out, experts)
        ]

    qkv_blocks, out_blocks, gate_blocks = together(
        row_transfers,
        *[
            [lax.dynamic_index_in_dim(grad, plane ^ k, 0, keepdims=False) for k in range(planes)]
            for grad in (grad_w_qkv, grad_w_out, grad_w_gate)
        ],
    )
    grad_w_qkv, grad_w_out = total(qkv_blocks), total(out_blocks)
    up_blocks = to_owners(grad_w_up, token(grad_w_qkv))
    down_ready, gate_ready = in_order(down_blocks, "z"), in_order(gate_blocks, "z")
    grad_in_norm, gain_in_grad = norm_back(inputs, gain_in, grad_normed)
    grad_tokens = to_outer(grad_resid + grad_in_norm)

    def widen(local):
        full = jnp.zeros((width,), f32)
        return to_inner(lax.dynamic_update_slice_in_dim(full, local, rank * cols, 0))

    gains = jnp.stack([gain_in_grad, gain_mid_grad, widen(gain_q_grad[0]), widen(gain_k_grad[0])])
    for axis in ("z", "c", "s", "o"):
        gains = sum(gather_near(gains, axis))
    row = (lax.axis_index(("c", "o", "z")) * seqs + rank) * rows_dev
    grad_gains = lax.dynamic_slice_in_dim(gains, row, rows_dev, 1).T

    def own_rows(grad):
        grad = grad.astype(bf16).reshape(seqs, rows_dev, grad.shape[1])
        got = exchange(lambda i: lax.dynamic_index_in_dim(grad, i, 0, keepdims=False), "s")
        return in_order(got, "s").astype(f32)

    qkv_part, out_part = own_rows(grad_w_qkv), own_rows(grad_w_out)
    grad_attn = jnp.concatenate(
        [qkv_part[s, :, i * cols : (i + 1) * cols] for i in range(3) for s in range(seqs)]
        + [out_part[s] for s in range(seqs)],
        axis=1,
    )
    up_ready = in_order(up_blocks, "z")
    grad_expert = jnp.concatenate([gate_ready, up_ready, down_ready], axis=2)
    grad_expert = grad_expert.astype(f32).transpose(1, 0, 2)
    return (
        to_outer(final_out).astype(bf16),
        loss_value,
        grad_tokens,
        grad_attn,
        grad_gains,
        grad_expert,
    )


def solution(mesh):
    fsdp, seqs = mesh.shape["fsdp"], mesh.shape["sp"]

    def whole(*arrays):
        planes = arrays[3].shape[1] // seqs
        outer = fsdp // (planes * CORES)
        inner = Mesh(mesh.devices.reshape(outer, planes, CORES, seqs), ("o", "z", "c", "s"))
        every = ("o", "z", "c", "s")
        rows = P(every, None)
        experts = P(("o", "z", "c"), "s", None)
        return jax.shard_map(
            shards,
            mesh=inner,
            in_specs=(
                rows,
                rows,
                rows,
                experts,
                rows,
                rows,
                P(("o", "z", "c")),
                P(every),
                rows,
                rows,
            ),
            out_specs=(rows, P(), rows, rows, rows, experts),
            check_vma=False,
        )(*arrays)

    return whole
```

```python
import functools

import jax
import jax.numpy as jnp
from jax import lax
from jax.experimental import pallas as pl
from jax.experimental.pallas import tpu as pltpu
from jax.sharding import Mesh, PartitionSpec as P

H = 16
HD = 128
TOP = 8
CORES = 2
PAD = 128

epsilon = 1e-05
masked = -1e30
f32 = jnp.float32
bf16 = jnp.bfloat16


def send(block, axis, step):
    size = lax.axis_size(axis)
    return lax.ppermute(block, axis, [(i, i ^ step) for i in range(size)])


def gather_near(block, axis):
    return [block] + [send(block, axis, k) for k in range(1, lax.axis_size(axis))]


def in_order(blocks, axis, start=0):
    rank = lax.axis_index(axis)
    if len(blocks) == 1:
        return blocks[0][None]
    stacked = jnp.zeros((len(blocks),) + blocks[0].shape, blocks[0].dtype)
    for k, block in enumerate(blocks):
        stacked = lax.dynamic_update_index_in_dim(stacked, block, (rank ^ k) + start, 0)
    return stacked


def collect(block, axis):
    return in_order(gather_near(block, axis), axis)


def exchange(piece_for, axis, start=0):
    rank, size = lax.axis_index(axis) + start, lax.axis_size(axis)
    return [piece_for(rank)] + [send(piece_for(rank ^ k), axis, k) for k in range(1, size)]


def swap(pieces, axis):
    return lax.all_to_all(pieces, axis, split_axis=0, concat_axis=0, tiled=True)


def exchange_by_rank(pieces, axis):
    return exchange(lambda i: lax.dynamic_index_in_dim(pieces, i, 0, keepdims=False), axis)


def exchange_sum(pieces, axis):
    got = exchange_by_rank(pieces, axis)
    return sum(piece.astype(f32) for piece in got)


def token(*values):
    firsts = [value[(slice(0, 1),) * value.ndim].reshape(()).astype(f32) for value in values]
    total = sum(firsts)
    return (total != total).astype(jnp.int32)


def after(value, *others):
    return value + token(*others).astype(value.dtype)


def rms_factor(values):
    return lax.rsqrt(jnp.mean(values * values, axis=-1, keepdims=True) + epsilon)


def norm_back(values, gain_vec, grad_in):
    factor = rms_factor(values)
    normed = values * factor
    gain_grad = jnp.sum(grad_in * normed, axis=0)
    inner = grad_in * gain_vec
    grad = factor * (inner - normed * jnp.mean(inner * normed, axis=-1, keepdims=True))
    return grad, gain_grad


def rope_tables(rows):
    inverse = 10000.0 ** (-(jnp.arange(HD // 2).astype(f32) * 2.0 / HD))
    angles = jnp.arange(rows).astype(f32)[:, None] * inverse[None, :]
    cosine = jnp.concatenate([jnp.cos(angles), jnp.cos(angles)], axis=-1)
    sine = jnp.concatenate([-jnp.sin(angles), jnp.sin(angles)], axis=-1)
    return cosine, sine


def mm(left, right, dims):
    return lax.dot_general(left, right, (dims, ((), ())), preferred_element_type=f32)


def masked_scores(query, keyed, seg_col, seg_row, first, scale):
    scores = mm(query, keyed, ((1,), (1,))) * scale
    rows = first + lax.broadcasted_iota(jnp.int32, scores.shape, 0)
    allowed = (rows >= lax.broadcasted_iota(jnp.int32, scores.shape, 1)) & (seg_col == seg_row)
    return jnp.where(allowed, scores, masked)


def attend_kernel(
    block,
    q_raw,
    k_raw,
    v_raw,
    q_mean,
    k_mean,
    gain_q,
    gain_k,
    cosine,
    sine,
    seg_col,
    seg_row,
    out,
    q_out,
    k_out,
    v_out,
    log_total,
):
    def rope(raw, mean, gain):
        values = raw[...] * lax.rsqrt(mean[...] + epsilon) * gain[...]
        turned = pltpu.roll(values, HD // 2, 1)
        return (values * cosine[...] + turned * sine[...]).astype(bf16)

    q_out[...] = rope(q_raw, q_mean, gain_q)
    k_out[...] = rope(k_raw, k_mean, gain_k)
    v_out[...] = v_raw[...].astype(bf16)
    for first in range(0, out.shape[0], block):
        last = first + block
        scores = masked_scores(
            q_out[first:last],
            k_out[:last],
            seg_col[first:last],
            seg_row[:, :last],
            first,
            HD**-0.5,
        )
        top = jnp.max(scores, axis=-1, keepdims=True)
        exps = jnp.exp(scores - top)
        total = jnp.sum(exps, axis=-1, keepdims=True)
        weights = (exps * (1.0 / total)).astype(bf16)
        out[first:last] = mm(weights, v_out[:last], ((1,), (0,))).astype(bf16)
        log_total[0, first:last] = top + jnp.log(total)


def attend_back_kernel(
    block,
    q_raw,
    k_raw,
    q_mean,
    k_mean,
    gain_q,
    gain_k,
    cosine,
    sine,
    seg_col,
    seg_row,
    query,
    keyed,
    valued,
    grad,
    log_total,
    grad_q,
    grad_k,
    grad_v,
    q_inner,
    k_inner,
    gain_q_grad,
    gain_k_grad,
    sum_q,
    sum_k,
    sum_v,
):
    scale = HD**-0.5
    sum_k[...] = jnp.zeros_like(sum_k)
    sum_v[...] = jnp.zeros_like(sum_v)
    for first in range(0, query.shape[0], block):
        last = first + block
        q_block, g_block = query[first:last], grad[first:last]
        scores = masked_scores(
            q_block, keyed[:last], seg_col[first:last], seg_row[:, :last], first, scale
        )
        probs = jnp.exp(scores - log_total[0, first:last])
        sum_v[:last] += mm(probs.astype(bf16), g_block, ((0,), (0,)))
        grad_probs = mm(g_block, valued[:last], ((1,), (1,)))
        inner = jnp.sum(probs * grad_probs, axis=-1, keepdims=True)
        grad_scores = (probs * (grad_probs - inner)).astype(bf16)
        sum_q[first:last] = mm(grad_scores, keyed[:last], ((1,), (0,))) * scale
        sum_k[:last] += mm(grad_scores, q_block, ((0,), (0,))) * scale
    grad_v[...] = sum_v[...].astype(bf16)

    def undo(total, raw, mean, gain, inner_out, gain_out, grad_out):
        low = total[...].astype(bf16).astype(f32)
        back = low * cosine[...] + pltpu.roll(low * sine[...], HD // 2, 1)
        normed = raw[...] * lax.rsqrt(mean[...] + epsilon)
        gain_out[...] = jnp.sum(back * normed, axis=0, keepdims=True)
        back = back * gain[...]
        grad_out[...] = back
        inner = jnp.sum(back * normed, axis=-1, keepdims=True)

        @pl.when(pl.program_id(0) == 0)
        def _():
            inner_out[...] = inner

        @pl.when(pl.program_id(0) > 0)
        def _():
            inner_out[...] += inner

    undo(sum_q, q_raw, q_mean, gain_q, q_inner, gain_q_grad, grad_q)
    undo(sum_k, k_raw, k_mean, gain_k, k_inner, gain_k_grad, grad_k)


def head_specs(seq, heads):
    column = pl.BlockSpec((seq, 1), lambda h: (0, 0))
    gain = pl.BlockSpec((1, HD), lambda h: (0, h))
    table = pl.BlockSpec((seq, HD), lambda h: (0, 0))
    return [column, column, gain, gain, table, table, column, pl.BlockSpec((1, seq), lambda h: (0, 0))]


def raw_spec(seq, heads, which):
    return pl.BlockSpec((seq, HD), lambda h: (0, which * heads + h))


def attend(projected, shared, heads):
    seq = projected.shape[0]
    block = min(256, seq)
    head = pl.BlockSpec((seq, HD), lambda h: (0, h))
    low = jax.ShapeDtypeStruct((seq, heads * HD), bf16)
    return pl.pallas_call(
        functools.partial(attend_kernel, block),
        grid=(heads,),
        in_specs=[raw_spec(seq, heads, i) for i in range(3)] + head_specs(seq, heads),
        out_specs=[head] * 4 + [pl.BlockSpec((1, seq, 1), lambda h: (h, 0, 0))],
        out_shape=[low] * 4 + [jax.ShapeDtypeStruct((heads, seq, 1), f32)],
        compiler_params=pltpu.CompilerParams(vmem_limit_bytes=48 * 2**20),
        cost_estimate=pl.CostEstimate(flops=10**6, bytes_accessed=10**5, transcendentals=0),
    )(projected, projected, projected, *shared)


def attend_back(projected, shared, query, keyed, valued, grad, log_total, heads):
    seq = projected.shape[0]
    block = min(256, seq)
    head = pl.BlockSpec((seq, HD), lambda h: (0, h))
    column = pl.BlockSpec((seq, 1), lambda h: (0, 0))
    gain = pl.BlockSpec((1, HD), lambda h: (0, h))
    wide = jax.ShapeDtypeStruct((seq, heads * HD), f32)
    return pl.pallas_call(
        functools.partial(attend_back_kernel, block),
        grid=(heads,),
        in_specs=[raw_spec(seq, heads, i) for i in range(2)]
        + head_specs(seq, heads)
        + [head] * 4
        + [pl.BlockSpec((1, seq, 1), lambda h: (h, 0, 0))],
        out_specs=[head] * 3 + [column] * 2 + [gain] * 2,
        out_shape=[wide, wide, jax.ShapeDtypeStruct((seq, heads * HD), bf16)]
        + [jax.ShapeDtypeStruct((seq, 1), f32)] * 2
        + [jax.ShapeDtypeStruct((1, heads * HD), f32)] * 2,
        scratch_shapes=[pltpu.VMEM((seq, HD), f32)] * 3,
        compiler_params=pltpu.CompilerParams(vmem_limit_bytes=48 * 2**20),
        cost_estimate=pl.CostEstimate(flops=10**6, bytes_accessed=10**5, transcendentals=0),
    )(projected, projected, *shared, query, keyed, valued, grad, log_total)


def slot_choice(place, slots):
    return lax.broadcasted_iota(jnp.int32, (slots, place.shape[1]), 0) == place


def slot_weight(place, gate, slots):
    return jnp.sum(jnp.where(slot_choice(place, slots), gate, 0.0), axis=1, keepdims=True)


def spans_of(count, slots):
    return [(b, slice(b * slots, (b + 1) * slots)) for b in range(count)]


def add_tokens(place, b, slots, out, sum_tokens, partial):
    expert = pl.program_id(0)
    back = mm(slot_choice(place[0, b], slots).astype(bf16), out, ((0,), (0,)))

    @pl.when(expert == 0)
    def _():
        sum_tokens[b] = back

    @pl.when(expert > 0)
    def _():
        sum_tokens[b] += back

    @pl.when(expert == pl.num_programs(0) - 1)
    def _():
        partial[b][...] = sum_tokens[b].astype(bf16)


def hidden_kernel(count, slots, place, *refs):
    blocks, w_gate, w_up = refs[:count], refs[count], refs[count + 1]
    rows, activated, gate_pre, up_pre = refs[-4:]
    for b, span in spans_of(count, slots):
        choice = slot_choice(place[0, b], slots).astype(bf16)
        rows[0, 0, span] = mm(choice, blocks[b][...], ((1,), (0,))).astype(bf16)
    rows_in = rows[0, 0]
    g = mm(rows_in, w_gate[0], ((1,), (0,)))
    u = mm(rows_in, w_up[0], ((1,), (0,)))
    gate_pre[0], up_pre[0] = g.astype(bf16), u.astype(bf16)
    activated[0, 0] = (g * jax.nn.sigmoid(g) * u).astype(bf16)


def out_kernel(count, slots, place, gate, activated, w_down, *refs):
    partial, sum_tokens = refs[:-1], refs[-1]
    result = mm(activated[0, 0], w_down[0], ((1,), (1,)))
    for b, span in spans_of(count, slots):
        out = (result[span] * slot_weight(place[0, b], gate[0, b], slots)).astype(bf16)
        add_tokens(place, b, slots, out, sum_tokens, partial)


def expert_back_kernel(count, slots, place, gate, *refs):
    blocks, (w_gate, w_up, w_down) = refs[:count], refs[count : count + 3]
    gate_pre, up_pre = refs[count + 3 : count + 5]
    grad_rows, grad_gate, grad_up = refs[-4 - count : -1 - count]
    partial, sum_tokens = refs[-1 - count : -1], refs[-1]
    for b, span in spans_of(count, slots):
        choice = slot_choice(place[0, b], slots).astype(bf16)
        weight = slot_weight(place[0, b], gate[0, b], slots)
        picked = mm(choice, blocks[b][...], ((1,), (0,)))
        grad_rows[0, 0, span] = (picked * weight).astype(bf16)
    grad_act = mm(grad_rows[0, 0], w_down[0], ((1,), (0,)))
    g, u = gate_pre[0].astype(f32), up_pre[0].astype(f32)
    sigmoid = jax.nn.sigmoid(g)
    dg = (grad_act * u * sigmoid * (1.0 + g * (1.0 - sigmoid))).astype(bf16)
    du = (grad_act * g * sigmoid).astype(bf16)
    grad_gate[0, 0], grad_up[0, 0] = dg, du
    result = mm(dg, w_gate[0], ((1,), (1,))) + mm(du, w_up[0], ((1,), (1,)))
    result = result.astype(bf16)
    for b, span in spans_of(count, slots):
        add_tokens(place, b, slots, result[span], sum_tokens, partial)


class Experts:
    def __init__(self, group, slots, place, gate, blocks, weights):
        self.group, self.slots, self.place, self.gate = group, slots, place, gate
        self.experts, self.width, self.hidden = weights[0].shape
        self.count, self.own = len(blocks), blocks[0].shape[0]
        self.rows = self.count * slots
        group_of = lambda e: (e, group, 0, 0)
        self.table = pl.BlockSpec((1, self.count, 1, self.own), group_of)
        self.tokens = pl.BlockSpec((self.own, self.width), lambda e: (0, 0))
        self.weight = pl.BlockSpec((1, self.width, self.hidden), lambda e: (e, 0, 0))
        self.local = pl.BlockSpec((1, self.rows, self.hidden), lambda e: (e, 0, 0))
        self.wide = pl.BlockSpec((1, 1, self.rows, self.width), group_of)
        self.narrow = pl.BlockSpec((1, 1, self.rows, self.hidden), group_of)
        self.sums = pltpu.VMEM((self.count, self.own, self.width), f32)

    def shape(self, spec):
        rows, experts = self.rows, self.experts
        shapes = [
            (self.tokens, (self.own, self.width)),
            (self.local, (experts, rows, self.hidden)),
            (self.wide, (experts, 2, rows, self.width)),
            (self.narrow, (experts, 2, rows, self.hidden)),
        ]
        [shape] = [shape for known, shape in shapes if known is spec]
        return jax.ShapeDtypeStruct(shape, bf16)

    def run(self, kernel, ins, outs, scratch, prior=()):
        specs = [spec for spec, _ in ins] + [pl.BlockSpec(memory_space=pl.ANY)] * len(prior)
        return pl.pallas_call(
            functools.partial(kernel, self.count, self.slots),
            grid=(self.experts,),
            in_specs=specs,
            out_specs=outs,
            out_shape=[self.shape(spec) for spec in outs],
            scratch_shapes=scratch,
            input_output_aliases={len(ins) + i: i for i in range(len(prior))},
            compiler_params=pltpu.CompilerParams(vmem_limit_bytes=58 * 2**20),
            cost_estimate=pl.CostEstimate(
                flops=self.experts * self.rows * self.width * self.hidden * 4,
                bytes_accessed=self.experts * self.width * self.hidden * 6,
                transcendentals=self.experts * self.rows * self.hidden,
            ),
        )(*[array for _, array in ins], *prior)

    def to_hidden(self, blocks, w_gate, w_up, prior):
        ins = [(self.table, self.place)] + [(self.tokens, block) for block in blocks]
        ins += [(self.weight, w_gate), (self.weight, w_up)]
        outs = [self.wide, self.narrow, self.local, self.local]
        return self.run(hidden_kernel, ins, outs, [], prior)

    def to_tokens(self, activated, w_down):
        ins = [(self.table, self.place), (self.table, self.gate)]
        ins += [(self.narrow, activated), (self.weight, w_down)]
        return self.run(out_kernel, ins, [self.tokens] * self.count, [self.sums])

    def backward(self, blocks, weights, pres, prior):
        ins = [(self.table, self.place), (self.table, self.gate)]
        ins += [(self.tokens, block) for block in blocks]
        ins += [(self.weight, weight) for weight in weights]
        ins += [(self.local, pre) for pre in pres]
        outs = [self.wide, self.narrow, self.narrow] + [self.tokens] * self.count
        return self.run(expert_back_kernel, ins, outs, [self.sums], prior)


def dot(spec, left, right):
    return jnp.einsum(spec, left, right, preferred_element_type=f32)


def shards(
    tokens,
    w_attn,
    norm_gains,
    w_expert,
    gate_weights,
    routes,
    segment,
    valid_mask,
    teacher,
    cotangent,
):
    outer, planes, seqs = lax.axis_size("o"), lax.axis_size("z"), lax.axis_size("s")
    plane, rank = lax.axis_index("z"), lax.axis_index("s")
    own, width = tokens.shape
    rows_dev = w_attn.shape[0]
    seq = own * seqs
    heads = H // seqs
    cols = heads * HD
    hidden = w_expert.shape[2] // 3
    part = w_expert.shape[0]
    capacity = own * TOP * 17 // (16 * planes * seqs)
    scale = HD ** (-0.5)

    def to_inner(v):
        lead = v.shape[:-1]
        v = v.reshape(lead + (outer * planes, CORES, part))
        return jnp.swapaxes(v, -3, -2).reshape(lead + (width,))

    def to_outer(v):
        lead = v.shape[:-1]
        v = v.reshape(lead + (CORES, outer * planes, part))
        return jnp.swapaxes(v, -3, -2).reshape(lead + (width,))

    first_core = lax.axis_index("c") == 0

    def halves(v):
        low, high = v[..., : width // 2], v[..., width // 2 :]
        return jnp.where(first_core, low, high), jnp.where(first_core, high, low)

    def whole_of(mine, other, axis):
        low, high = jnp.where(first_core, mine, other), jnp.where(first_core, other, mine)
        return jnp.concatenate([low, high], axis=axis)

    def stack_rows(blocks, start=0):
        rows = in_order(blocks, "z", start)
        return collect(rows, "o").reshape((width // 2,) + rows.shape[2:])

    def sum_cores(grad):
        count = grad.shape[1]
        grad = exchange_sum(grad.reshape(CORES, width // 2, count), "c")
        if outer > 1:
            grad = exchange_sum(grad.astype(bf16).reshape(outer, planes * part, count), "o")
        return grad

    def gather_sum(value):
        for axis in ("z", "s", "c", "o"):
            value = sum(gather_near(jnp.broadcast_to(value, (8, PAD)), axis))[0, 0]
        return value

    by_expert = w_expert.transpose(1, 0, 2)

    def expert_chunk(i, start=0):
        def piece_for(owner):
            return lax.dynamic_slice(by_expert, (owner, 0, i * hidden), (1, part, hidden))[0]

        return exchange(piece_for, "z", start)

    def gather_plane(ready):
        chunk = ready.reshape(planes * part, hidden)
        chunk = lax.all_gather(chunk, ("s", "c", "o"), axis=0, tiled=True)
        return chunk.reshape(seqs, width, hidden)

    count = jnp.sum(valid_mask).astype(jnp.int32)
    digits = jnp.stack([count // 128, count % 128]).astype(bf16)
    extra = jnp.concatenate(
        [
            norm_gains,
            jnp.broadcast_to(digits[None], (rows_dev, 2)),
            jnp.zeros((rows_dev, PAD - 6), bf16),
        ],
        axis=1,
    )

    inputs = to_inner(tokens)
    column_rows, extra_rows = rows_dev * 4 * cols // width, rows_dev * PAD // width
    extra = jnp.pad(extra.reshape(extra_rows, width), ((0, -extra_rows % 8), (0, 0)))

    def message_to(owner):
        picked = [
            lax.dynamic_slice_in_dim(w_attn, i * width + owner * cols, cols, 1) for i in range(4)
        ]
        picked = jnp.concatenate(picked, axis=1).reshape(column_rows, width)
        return jnp.concatenate([inputs, picked, extra], axis=0)

    messages = exchange(message_to, "s")
    gate_blocks = expert_chunk(0)
    last = own + column_rows
    columns = [
        jnp.concatenate(
            [
                message[own:last].reshape(rows_dev, 4 * cols),
                message[last : last + extra_rows].reshape(rows_dev, PAD),
            ],
            axis=1,
        )
        for message in messages
    ]
    mine = in_order(columns, "s").reshape(part, 4 * cols + PAD)
    seq_tokens = in_order([message[:own] for message in messages], "s")
    seq_tokens = seq_tokens.reshape(seq, width).astype(f32)
    inputs = inputs.astype(f32)
    gate_ready = in_order(gate_blocks, "z", token(mine))
    w_gate = gather_plane(gate_ready)
    in_blocks = gather_near(after(mine, gate_ready), "z")
    seq_factor = rms_factor(seq_tokens)
    w_in = stack_rows(in_blocks, token(seq_factor))
    w_in_other = send(w_in, "c", 1)
    up_blocks = expert_chunk(1, token(w_in))

    side = whole_of(w_in[:, 4 * cols :], w_in_other[:, 4 * cols :], 0)[:, :6].astype(f32).T
    gain_in, gain_mid = side[0], side[1]
    gain_q = lax.dynamic_slice_in_dim(to_outer(side[2]), rank * cols, cols, 0)
    gain_k = lax.dynamic_slice_in_dim(to_outer(side[3]), rank * cols, cols, 0)
    total_count = jnp.sum(side[4, ::rows_dev]) * 128.0 + jnp.sum(side[5, ::rows_dev])

    routed = jnp.stack(
        gather_near(jnp.concatenate([routes.astype(f32), gate_weights], axis=1), "z")
    )
    route_all, gate_all = routed[..., :TOP].astype(jnp.int32), routed[..., TOP:]
    expert_ids = jnp.arange(seqs) * planes + plane
    match = route_all[:, :, None, :] == expert_ids[None, None, :, None]
    used = jnp.any(match, axis=-1)
    gate_of = jnp.sum(jnp.where(match, gate_all[:, :, None, :], 0.0), axis=-1)
    before = (jnp.arange(own)[:, None] > jnp.arange(own)[None, :]).astype(bf16)
    place = dot("tu,buk->btk", before, used.astype(bf16)).astype(jnp.int32)
    place = jnp.where(used, place, -1)
    slots = -(-capacity // 16) * 16
    place = place.transpose(2, 0, 1)[:, :, None, :]
    gate_of = gate_of.transpose(2, 0, 1)[:, :, None, :]

    groups = [[k for k in range(planes) if k % 2 == odd] for odd in range(2)]

    def by_group(table):
        return jnp.concatenate([table[:, k : k + 1] for group in groups for k in group], axis=1)

    place, gate_of = by_group(place), by_group(gate_of)

    def near_planes(block):
        near = [block] + [None] * (planes - 1)
        for k in groups[0][1:]:
            near[k] = send(block, "z", k)
        later = after(block, *[near[k] for k in groups[0][1:]])
        for k in groups[1]:
            near[k] = send(later, "z", k)
        return [[near[k] for k in group] for group in groups]

    def send_back(first, second):
        got = [first[0]] + [send(first[i], "z", k) for i, k in enumerate(groups[0]) if k]
        base = after(total(got), second[0])
        second = [after(part, base) for part in second]
        return second[0], [base] + [send(second[i], "z", k) for i, k in enumerate(groups[1])]

    def total(pieces):
        return sum(piece.astype(f32) for piece in pieces)

    normed_in = (seq_tokens * seq_factor * gain_in).astype(bf16)
    normed_mine, normed_other = halves(normed_in)
    w_qkv, w_qkv_other = w_in[:, : 3 * cols], w_in_other[:, : 3 * cols]
    w_out = whole_of(w_in[:, 3 * cols : 4 * cols], w_in_other[:, 3 * cols : 4 * cols], 0)
    projected = jnp.dot(normed_mine, w_qkv, preferred_element_type=f32) + jnp.dot(
        normed_other, w_qkv_other, preferred_element_type=f32
    )
    query_raw = projected[:, :cols]
    key_raw = projected[:, cols : 2 * cols]

    def over_heads(first, second, *others):
        pairs = gather_near(jnp.stack([first, second]), "s")
        if others:
            pairs[0] = after(pairs[0], *others)
        pair = sum(pairs) / width
        return pair[0][:, None], pair[1][:, None]

    q_mean, k_mean = over_heads(
        jnp.sum(query_raw * query_raw, axis=-1), jnp.sum(key_raw * key_raw, axis=-1)
    )
    up_ready = in_order(up_blocks, "z", token(projected))
    w_up = gather_plane(up_ready)
    cosine, sine = rope_tables(seq)
    shared = [
        after(q_mean, up_ready, w_gate, place, w_out),
        k_mean,
        gain_q[None],
        gain_k[None],
        cosine,
        sine,
        segment[:, None],
        segment[None],
    ]
    attended, query, keyed, valued, log_total = attend(projected, shared, heads)
    down_blocks = expert_chunk(2, token(attended))
    attn_out = dot("tc,dc->td", attended, w_out).astype(bf16)
    got = exchange_sum(attn_out.reshape(seqs, own, width), "s")
    residual = inputs + got
    down_ready = in_order(down_blocks, "z", token(residual))
    residual = after(residual, down_ready)
    w_down = gather_plane(down_ready)

    normed_mid = (residual * rms_factor(residual) * gain_mid).astype(bf16)
    expert_weights = (w_gate, w_up, w_down)
    blocks = near_planes(normed_mid)
    work = [Experts(i, slots, place, gate_of, blocks[i], expert_weights) for i in range(2)]
    rows_in, activated, *pres = work[0].to_hidden(blocks[0], w_gate, w_up, ())
    first = work[0].to_tokens(activated, w_down)
    pres = [pres]
    blocks[1][0] = after(blocks[1][0], first[0])
    rows_in, activated, *last = work[1].to_hidden(
        blocks[1], w_gate, w_up, (rows_in, activated)
    )
    pres.append(last)
    second = work[1].to_tokens(activated, w_down)
    final_out = residual + total(send_back(first, second)[1])
    rows_in, activated = [v.reshape(seqs, -1, v.shape[-1]) for v in (rows_in, activated)]

    w_out_all = lax.all_gather(after(w_out, w_up), "s", axis=0)
    valid_f = valid_mask.astype(f32)[:, None]
    difference = final_out - to_inner(teacher).astype(f32)
    squared = jnp.sum(valid_f * difference * difference)
    squared = gather_sum(squared)
    loss_value = squared / (total_count * width)
    grad_out = (
        to_inner(cotangent).astype(f32) + 2.0 / (total_count * width) * valid_f * difference
    )

    def scatter_expert(grad):
        grad = grad.reshape(seqs * width, hidden)
        grad = lax.psum_scatter(grad, ("s", "c", "o"), scatter_dimension=0, tiled=True)
        return grad.reshape(planes, part, hidden)

    blocks = near_planes(grad_out.astype(bf16))
    *grads, first, last = work[0].backward(blocks[0], expert_weights, pres[0], ())
    partial = [(first, last)]
    blocks[1][0] = after(blocks[1][0], first)
    *grads, first, last = work[1].backward(blocks[1], expert_weights, pres[1], grads)
    partial.append((first, last))
    back_last, back_pieces = send_back(*partial)
    grad_rows, grad_gate, grad_up = [v.reshape(seqs, -1, v.shape[-1]) for v in grads]
    grad_w_down = dot("krd,krf->kdf", grad_rows, after(activated, back_last)).astype(bf16)
    back_pieces[0] = after(back_pieces[0], grad_w_down)
    grad_mid = total(back_pieces)
    grad_w_gate = dot("krd,krf->kdf", rows_in, after(grad_gate, grad_mid)).astype(bf16)
    grad_resid_norm, gain_mid_grad = norm_back(residual, gain_mid, grad_mid)
    grad_resid = grad_out + grad_resid_norm

    grad_low = grad_resid.astype(bf16)
    grad_heads = dot("td,sdc->stc", grad_low, w_out_all).astype(bf16)
    head_blocks = exchange(
        lambda i: lax.dynamic_index_in_dim(grad_heads, i, 0, keepdims=False), "s"
    )
    grad_heads = in_order(head_blocks, "s", token(grad_w_gate)).reshape(seq, cols)
    grad_w_up = dot("krd,krf->kdf", rows_in, after(grad_up, grad_heads)).astype(bf16)
    up_done = grad_w_up
    grad_w_down, grad_w_gate, grad_w_up = [
        scatter_expert(grad) for grad in (grad_w_down, grad_w_gate, grad_w_up)
    ]
    low_blocks = gather_near(after(grad_low, grad_heads), "s")
    down_ready = swap(grad_w_down, "z")
    grad_q, grad_k, grad_v, q_inner, k_inner, gain_q_grad, gain_k_grad = attend_back(
        projected, shared, query, keyed, valued, after(grad_heads, up_done), log_total, heads
    )
    grad_attn_out = in_order(low_blocks, "s", token(grad_q)).reshape(seq, width)
    down_ready = after(down_ready, grad_q)
    q_inner = after(q_inner, down_ready, grad_attn_out)
    grad_w_out = dot("td,tc->dc", grad_attn_out, attended).astype(bf16)
    q_inner, k_inner = over_heads(q_inner[:, 0], k_inner[:, 0], grad_w_out)

    def norm_grad(grad, raw, mean, inner):
        factor = lax.rsqrt(mean + epsilon)
        return (factor * (grad - raw * factor * inner)).astype(bf16)

    grad_proj = jnp.concatenate(
        [
            norm_grad(grad_q, query_raw, q_mean, q_inner),
            norm_grad(grad_k, key_raw, k_mean, k_inner),
            grad_v,
        ],
        axis=1,
    )

    def back_half(weight):
        grad = dot("tc,dc->td", grad_proj, weight).astype(bf16)
        return exchange_sum(grad.reshape(seqs, own, width // 2), "s")

    grad_normed = whole_of(back_half(w_qkv), back_half(w_qkv_other), 1)
    grad_w_qkv = dot("td,tc->dc", normed_in, grad_proj).astype(bf16)
    summed = jnp.concatenate([sum_cores(grad_w_qkv), sum_cores(grad_w_out)], axis=1)
    summed = summed.astype(bf16).reshape(planes, part, 4 * cols)
    gate_ready = swap(grad_w_gate, "z")
    grad_attn = after(exchange_sum(summed, "z"), gate_ready).astype(bf16)
    up_ready = swap(after(grad_w_up, grad_attn), "z")
    grad_in_norm, gain_in_grad = norm_back(inputs, gain_in, grad_normed)
    grad_tokens = to_outer(grad_resid + grad_in_norm)

    def widen(local):
        full = jnp.zeros((width,), f32)
        return to_inner(lax.dynamic_update_slice_in_dim(full, local, rank * cols, 0))

    gains = jnp.stack([gain_in_grad, gain_mid_grad, widen(gain_q_grad[0]), widen(gain_k_grad[0])])
    for axis in ("z", "c", "s", "o"):
        gains = sum(gather_near(gains, axis))
    row = (lax.axis_index(("c", "o", "z")) * seqs + rank) * rows_dev
    grad_gains = lax.dynamic_slice_in_dim(gains, row, rows_dev, 1).T

    got = exchange_by_rank(grad_attn.reshape(seqs, rows_dev, 4 * cols), "s")
    got = in_order(got, "s").astype(f32)
    grad_attn = jnp.concatenate(
        [got[s, :, i * cols : (i + 1) * cols] for i in range(4) for s in range(seqs)], axis=1
    )
    grad_expert = jnp.concatenate([gate_ready, up_ready, down_ready], axis=2)
    grad_expert = grad_expert.astype(f32).transpose(1, 0, 2)
    return (
        to_outer(final_out).astype(bf16),
        loss_value,
        grad_tokens,
        grad_attn,
        grad_gains,
        grad_expert,
    )


def solution(mesh):
    fsdp, seqs = mesh.shape["fsdp"], mesh.shape["sp"]

    def whole(*arrays):
        planes = arrays[3].shape[1] // seqs
        outer = fsdp // (planes * CORES)
        inner = Mesh(mesh.devices.reshape(outer, planes, CORES, seqs), ("o", "z", "c", "s"))
        every = ("o", "z", "c", "s")
        rows = P(every, None)
        experts = P(("o", "z", "c"), "s", None)
        return jax.shard_map(
            shards,
            mesh=inner,
            in_specs=(
                rows,
                rows,
                rows,
                experts,
                rows,
                rows,
                P(("o", "z", "c")),
                P(every),
                rows,
                rows,
            ),
            out_specs=(rows, P(), rows, rows, rows, experts),
            check_vma=False,
        )(*arrays)

    return whole
```

```python
import functools

import jax
import jax.numpy as jnp
from jax import lax
from jax.experimental import pallas as pl
from jax.experimental.pallas import tpu as pltpu
from jax.sharding import Mesh, PartitionSpec as P

H = 16
HD = 128
TOP = 8
CORES = 2
PAD = 128

epsilon = 1e-05
masked = -1e30
f32 = jnp.float32
bf16 = jnp.bfloat16


def send(block, axis, step):
    size = lax.axis_size(axis)
    return lax.ppermute(block, axis, [(i, i ^ step) for i in range(size)])


def gather_near(block, axis):
    return [block] + [send(block, axis, k) for k in range(1, lax.axis_size(axis))]


def in_order(blocks, axis, start=0):
    rank = lax.axis_index(axis)
    if len(blocks) == 1:
        return blocks[0][None]
    stacked = jnp.zeros((len(blocks),) + blocks[0].shape, blocks[0].dtype)
    for k, block in enumerate(blocks):
        stacked = lax.dynamic_update_index_in_dim(stacked, block, (rank ^ k) + start, 0)
    return stacked


def collect(block, axis):
    return in_order(gather_near(block, axis), axis)


def exchange(piece_for, axis, start=0):
    rank, size = lax.axis_index(axis) + start, lax.axis_size(axis)
    return [piece_for(rank)] + [send(piece_for(rank ^ k), axis, k) for k in range(1, size)]


def swap(pieces, axis):
    return lax.all_to_all(pieces, axis, split_axis=0, concat_axis=0, tiled=True)


def exchange_by_rank(pieces, axis):
    return exchange(lambda i: lax.dynamic_index_in_dim(pieces, i, 0, keepdims=False), axis)


def exchange_sum(pieces, axis):
    got = exchange_by_rank(pieces, axis)
    return sum(piece.astype(f32) for piece in got)


def token(*values):
    firsts = [value[(slice(0, 1),) * value.ndim].reshape(()).astype(f32) for value in values]
    total = sum(firsts)
    return (total != total).astype(jnp.int32)


def after(value, *others):
    return value + token(*others).astype(value.dtype)


def rms_factor(values):
    return lax.rsqrt(jnp.mean(values * values, axis=-1, keepdims=True) + epsilon)


def norm_back(values, gain_vec, grad_in):
    factor = rms_factor(values)
    normed = values * factor
    gain_grad = jnp.sum(grad_in * normed, axis=0)
    inner = grad_in * gain_vec
    grad = factor * (inner - normed * jnp.mean(inner * normed, axis=-1, keepdims=True))
    return grad, gain_grad


def rope_tables(rows):
    inverse = 10000.0 ** (-(jnp.arange(HD // 2).astype(f32) * 2.0 / HD))
    angles = jnp.arange(rows).astype(f32)[:, None] * inverse[None, :]
    cosine = jnp.concatenate([jnp.cos(angles), jnp.cos(angles)], axis=-1)
    sine = jnp.concatenate([-jnp.sin(angles), jnp.sin(angles)], axis=-1)
    return cosine, sine


def mm(left, right, dims):
    return lax.dot_general(left, right, (dims, ((), ())), preferred_element_type=f32)


def masked_scores(query, keyed, seg_col, seg_row, first, scale):
    scores = mm(query, keyed, ((1,), (1,))) * scale
    rows = first + lax.broadcasted_iota(jnp.int32, scores.shape, 0)
    allowed = (rows >= lax.broadcasted_iota(jnp.int32, scores.shape, 1)) & (seg_col == seg_row)
    return jnp.where(allowed, scores, masked)


def attend_kernel(
    block,
    q_raw,
    k_raw,
    v_raw,
    q_mean,
    k_mean,
    gain_q,
    gain_k,
    cosine,
    sine,
    seg_col,
    seg_row,
    out,
    q_out,
    k_out,
    v_out,
    log_total,
):
    def rope(raw, mean, gain):
        values = raw[...] * lax.rsqrt(mean[...] + epsilon) * gain[...]
        turned = pltpu.roll(values, HD // 2, 1)
        return (values * cosine[...] + turned * sine[...]).astype(bf16)

    q_out[...] = rope(q_raw, q_mean, gain_q)
    k_out[...] = rope(k_raw, k_mean, gain_k)
    v_out[...] = v_raw[...].astype(bf16)
    for first in range(0, out.shape[0], block):
        last = first + block
        scores = masked_scores(
            q_out[first:last],
            k_out[:last],
            seg_col[first:last],
            seg_row[:, :last],
            first,
            HD**-0.5,
        )
        top = jnp.max(scores, axis=-1, keepdims=True)
        exps = jnp.exp(scores - top)
        total = jnp.sum(exps, axis=-1, keepdims=True)
        weights = (exps * (1.0 / total)).astype(bf16)
        out[first:last] = mm(weights, v_out[:last], ((1,), (0,))).astype(bf16)
        log_total[0, first:last] = top + jnp.log(total)


def attend_back_kernel(
    block,
    q_raw,
    k_raw,
    q_mean,
    k_mean,
    gain_q,
    gain_k,
    cosine,
    sine,
    seg_col,
    seg_row,
    query,
    keyed,
    valued,
    grad,
    log_total,
    grad_q,
    grad_k,
    grad_v,
    q_inner,
    k_inner,
    gain_q_grad,
    gain_k_grad,
    sum_q,
    sum_k,
    sum_v,
):
    scale = HD**-0.5
    sum_k[...] = jnp.zeros_like(sum_k)
    sum_v[...] = jnp.zeros_like(sum_v)
    for first in range(0, query.shape[0], block):
        last = first + block
        q_block, g_block = query[first:last], grad[first:last]
        scores = masked_scores(
            q_block, keyed[:last], seg_col[first:last], seg_row[:, :last], first, scale
        )
        probs = jnp.exp(scores - log_total[0, first:last])
        sum_v[:last] += mm(probs.astype(bf16), g_block, ((0,), (0,)))
        grad_probs = mm(g_block, valued[:last], ((1,), (1,)))
        inner = jnp.sum(probs * grad_probs, axis=-1, keepdims=True)
        grad_scores = (probs * (grad_probs - inner)).astype(bf16)
        sum_q[first:last] = mm(grad_scores, keyed[:last], ((1,), (0,))) * scale
        sum_k[:last] += mm(grad_scores, q_block, ((0,), (0,))) * scale
    grad_v[...] = sum_v[...].astype(bf16)

    def undo(total, raw, mean, gain, inner_out, gain_out, grad_out):
        low = total[...].astype(bf16).astype(f32)
        back = low * cosine[...] + pltpu.roll(low * sine[...], HD // 2, 1)
        normed = raw[...] * lax.rsqrt(mean[...] + epsilon)
        gain_out[...] = jnp.sum(back * normed, axis=0, keepdims=True)
        back = back * gain[...]
        grad_out[...] = back
        inner = jnp.sum(back * normed, axis=-1, keepdims=True)

        @pl.when(pl.program_id(0) == 0)
        def _():
            inner_out[...] = inner

        @pl.when(pl.program_id(0) > 0)
        def _():
            inner_out[...] += inner

    undo(sum_q, q_raw, q_mean, gain_q, q_inner, gain_q_grad, grad_q)
    undo(sum_k, k_raw, k_mean, gain_k, k_inner, gain_k_grad, grad_k)


def head_specs(seq, heads):
    column = pl.BlockSpec((seq, 1), lambda h: (0, 0))
    gain = pl.BlockSpec((1, HD), lambda h: (0, h))
    table = pl.BlockSpec((seq, HD), lambda h: (0, 0))
    return [column, column, gain, gain, table, table, column, pl.BlockSpec((1, seq), lambda h: (0, 0))]


def raw_spec(seq, heads, which):
    return pl.BlockSpec((seq, HD), lambda h: (0, which * heads + h))


def attend(projected, shared, heads):
    seq = projected.shape[0]
    block = min(256, seq)
    head = pl.BlockSpec((seq, HD), lambda h: (0, h))
    low = jax.ShapeDtypeStruct((seq, heads * HD), bf16)
    return pl.pallas_call(
        functools.partial(attend_kernel, block),
        grid=(heads,),
        in_specs=[raw_spec(seq, heads, i) for i in range(3)] + head_specs(seq, heads),
        out_specs=[head] * 4 + [pl.BlockSpec((1, seq, 1), lambda h: (h, 0, 0))],
        out_shape=[low] * 4 + [jax.ShapeDtypeStruct((heads, seq, 1), f32)],
        compiler_params=pltpu.CompilerParams(vmem_limit_bytes=48 * 2**20),
        cost_estimate=pl.CostEstimate(flops=10**6, bytes_accessed=10**5, transcendentals=0),
    )(projected, projected, projected, *shared)


def attend_back(projected, shared, query, keyed, valued, grad, log_total, heads):
    seq = projected.shape[0]
    block = min(256, seq)
    head = pl.BlockSpec((seq, HD), lambda h: (0, h))
    column = pl.BlockSpec((seq, 1), lambda h: (0, 0))
    gain = pl.BlockSpec((1, HD), lambda h: (0, h))
    wide = jax.ShapeDtypeStruct((seq, heads * HD), f32)
    return pl.pallas_call(
        functools.partial(attend_back_kernel, block),
        grid=(heads,),
        in_specs=[raw_spec(seq, heads, i) for i in range(2)]
        + head_specs(seq, heads)
        + [head] * 4
        + [pl.BlockSpec((1, seq, 1), lambda h: (h, 0, 0))],
        out_specs=[head] * 3 + [column] * 2 + [gain] * 2,
        out_shape=[wide, wide, jax.ShapeDtypeStruct((seq, heads * HD), bf16)]
        + [jax.ShapeDtypeStruct((seq, 1), f32)] * 2
        + [jax.ShapeDtypeStruct((1, heads * HD), f32)] * 2,
        scratch_shapes=[pltpu.VMEM((seq, HD), f32)] * 3,
        compiler_params=pltpu.CompilerParams(vmem_limit_bytes=48 * 2**20),
        cost_estimate=pl.CostEstimate(flops=10**6, bytes_accessed=10**5, transcendentals=0),
    )(projected, projected, *shared, query, keyed, valued, grad, log_total)


def slot_choice(place, slots):
    return lax.broadcasted_iota(jnp.int32, (slots, place.shape[1]), 0) == place


def slot_weight(place, gate, slots):
    return jnp.sum(jnp.where(slot_choice(place, slots), gate, 0.0), axis=1, keepdims=True)


def spans_of(count, slots):
    return [(b, slice(b * slots, (b + 1) * slots)) for b in range(count)]


def add_tokens(place, b, slots, out, sum_tokens, partial):
    expert = pl.program_id(0)
    back = mm(slot_choice(place[0, b], slots).astype(bf16), out, ((0,), (0,)))

    @pl.when(expert == 0)
    def _():
        sum_tokens[b] = back

    @pl.when(expert > 0)
    def _():
        sum_tokens[b] += back

    @pl.when(expert == pl.num_programs(0) - 1)
    def _():
        partial[b][...] = sum_tokens[b].astype(bf16)


def hidden_kernel(count, slots, place, *refs):
    blocks, w_gate, w_up = refs[:count], refs[count], refs[count + 1]
    rows, activated, gate_pre, up_pre = refs[-4:]
    for b, span in spans_of(count, slots):
        choice = slot_choice(place[0, b], slots).astype(bf16)
        rows[0, 0, span] = mm(choice, blocks[b][...], ((1,), (0,))).astype(bf16)
    rows_in = rows[0, 0]
    g = mm(rows_in, w_gate[0], ((1,), (0,)))
    u = mm(rows_in, w_up[0], ((1,), (0,)))
    gate_pre[0], up_pre[0] = g.astype(bf16), u.astype(bf16)
    activated[0, 0] = (g * jax.nn.sigmoid(g) * u).astype(bf16)


def out_kernel(count, slots, place, gate, activated, w_down, *refs):
    partial, sum_tokens = refs[:-1], refs[-1]
    result = mm(activated[0, 0], w_down[0], ((1,), (1,)))
    for b, span in spans_of(count, slots):
        out = (result[span] * slot_weight(place[0, b], gate[0, b], slots)).astype(bf16)
        add_tokens(place, b, slots, out, sum_tokens, partial)


def expert_back_kernel(count, slots, place, gate, *refs):
    blocks, (w_gate, w_up, w_down) = refs[:count], refs[count : count + 3]
    gate_pre, up_pre = refs[count + 3 : count + 5]
    grad_rows, grad_gate, grad_up = refs[-4 - count : -1 - count]
    partial, sum_tokens = refs[-1 - count : -1], refs[-1]
    for b, span in spans_of(count, slots):
        choice = slot_choice(place[0, b], slots).astype(bf16)
        weight = slot_weight(place[0, b], gate[0, b], slots)
        picked = mm(choice, blocks[b][...], ((1,), (0,)))
        grad_rows[0, 0, span] = (picked * weight).astype(bf16)
    grad_act = mm(grad_rows[0, 0], w_down[0], ((1,), (0,)))
    g, u = gate_pre[0].astype(f32), up_pre[0].astype(f32)
    sigmoid = jax.nn.sigmoid(g)
    dg = (grad_act * u * sigmoid * (1.0 + g * (1.0 - sigmoid))).astype(bf16)
    du = (grad_act * g * sigmoid).astype(bf16)
    grad_gate[0, 0], grad_up[0, 0] = dg, du
    result = mm(dg, w_gate[0], ((1,), (1,))) + mm(du, w_up[0], ((1,), (1,)))
    result = result.astype(bf16)
    for b, span in spans_of(count, slots):
        add_tokens(place, b, slots, result[span], sum_tokens, partial)


class Experts:
    def __init__(self, group, slots, place, gate, blocks, weights):
        self.group, self.slots, self.place, self.gate = group, slots, place, gate
        self.experts, self.width, self.hidden = weights[0].shape
        self.count, self.own = len(blocks), blocks[0].shape[0]
        self.rows = self.count * slots
        group_of = lambda e: (e, group, 0, 0)
        self.table = pl.BlockSpec((1, self.count, 1, self.own), group_of)
        self.tokens = pl.BlockSpec((self.own, self.width), lambda e: (0, 0))
        self.weight = pl.BlockSpec((1, self.width, self.hidden), lambda e: (e, 0, 0))
        self.local = pl.BlockSpec((1, self.rows, self.hidden), lambda e: (e, 0, 0))
        self.wide = pl.BlockSpec((1, 1, self.rows, self.width), group_of)
        self.narrow = pl.BlockSpec((1, 1, self.rows, self.hidden), group_of)
        self.sums = pltpu.VMEM((self.count, self.own, self.width), f32)

    def shape(self, spec):
        rows, experts = self.rows, self.experts
        shapes = [
            (self.tokens, (self.own, self.width)),
            (self.local, (experts, rows, self.hidden)),
            (self.wide, (experts, 2, rows, self.width)),
            (self.narrow, (experts, 2, rows, self.hidden)),
        ]
        [shape] = [shape for known, shape in shapes if known is spec]
        return jax.ShapeDtypeStruct(shape, bf16)

    def run(self, kernel, ins, outs, scratch, prior=()):
        specs = [spec for spec, _ in ins] + [pl.BlockSpec(memory_space=pl.ANY)] * len(prior)
        return pl.pallas_call(
            functools.partial(kernel, self.count, self.slots),
            grid=(self.experts,),
            in_specs=specs,
            out_specs=outs,
            out_shape=[self.shape(spec) for spec in outs],
            scratch_shapes=scratch,
            input_output_aliases={len(ins) + i: i for i in range(len(prior))},
            compiler_params=pltpu.CompilerParams(vmem_limit_bytes=58 * 2**20),
            cost_estimate=pl.CostEstimate(
                flops=self.experts * self.rows * self.width * self.hidden * 4,
                bytes_accessed=self.experts * self.width * self.hidden * 6,
                transcendentals=self.experts * self.rows * self.hidden,
            ),
        )(*[array for _, array in ins], *prior)

    def to_hidden(self, blocks, w_gate, w_up, prior):
        ins = [(self.table, self.place)] + [(self.tokens, block) for block in blocks]
        ins += [(self.weight, w_gate), (self.weight, w_up)]
        outs = [self.wide, self.narrow, self.local, self.local]
        return self.run(hidden_kernel, ins, outs, [], prior)

    def to_tokens(self, activated, w_down):
        ins = [(self.table, self.place), (self.table, self.gate)]
        ins += [(self.narrow, activated), (self.weight, w_down)]
        return self.run(out_kernel, ins, [self.tokens] * self.count, [self.sums])

    def backward(self, blocks, weights, pres, prior):
        ins = [(self.table, self.place), (self.table, self.gate)]
        ins += [(self.tokens, block) for block in blocks]
        ins += [(self.weight, weight) for weight in weights]
        ins += [(self.local, pre) for pre in pres]
        outs = [self.wide, self.narrow, self.narrow] + [self.tokens] * self.count
        return self.run(expert_back_kernel, ins, outs, [self.sums], prior)


def dot(spec, left, right):
    return jnp.einsum(spec, left, right, preferred_element_type=f32)


def shards(
    tokens,
    w_attn,
    norm_gains,
    w_expert,
    gate_weights,
    routes,
    segment,
    valid_mask,
    teacher,
    cotangent,
):
    outer, planes, seqs = lax.axis_size("o"), lax.axis_size("z"), lax.axis_size("s")
    plane, rank = lax.axis_index("z"), lax.axis_index("s")
    own, width = tokens.shape
    rows_dev = w_attn.shape[0]
    seq = own * seqs
    heads = H // seqs
    cols = heads * HD
    hidden = w_expert.shape[2] // 3
    part = w_expert.shape[0]
    capacity = own * TOP * 17 // (16 * planes * seqs)
    scale = HD ** (-0.5)

    def to_inner(v):
        lead = v.shape[:-1]
        v = v.reshape(lead + (outer * planes, CORES, part))
        return jnp.swapaxes(v, -3, -2).reshape(lead + (width,))

    def to_outer(v):
        lead = v.shape[:-1]
        v = v.reshape(lead + (CORES, outer * planes, part))
        return jnp.swapaxes(v, -3, -2).reshape(lead + (width,))

    first_core = lax.axis_index("c") == 0

    def halves(v):
        low, high = v[..., : width // 2], v[..., width // 2 :]
        return jnp.where(first_core, low, high), jnp.where(first_core, high, low)

    def whole_of(mine, other, axis):
        low, high = jnp.where(first_core, mine, other), jnp.where(first_core, other, mine)
        return jnp.concatenate([low, high], axis=axis)

    def stack_rows(blocks, start=0):
        rows = in_order(blocks, "z", start)
        return collect(rows, "o").reshape((width // 2,) + rows.shape[2:])

    def sum_cores(grad):
        count = grad.shape[1]
        grad = exchange_sum(grad.reshape(CORES, width // 2, count), "c")
        if outer > 1:
            grad = exchange_sum(grad.astype(bf16).reshape(outer, planes * part, count), "o")
        return grad

    def gather_sum(value):
        for axis in ("z", "s", "c", "o"):
            value = sum(gather_near(jnp.broadcast_to(value, (8, PAD)), axis))[0, 0]
        return value

    by_expert = lax.optimization_barrier(w_expert.transpose(1, 0, 2))

    def expert_chunk(i, start=0):
        def piece_for(owner):
            return lax.dynamic_slice(by_expert, (owner, 0, i * hidden), (1, part, hidden))[0]

        return exchange(piece_for, "z", start)

    def gather_plane(ready):
        chunk = ready.reshape(planes * part, hidden)
        chunk = lax.all_gather(chunk, ("s", "c", "o"), axis=0, tiled=True)
        return chunk.reshape(seqs, width, hidden)

    count = jnp.sum(valid_mask).astype(jnp.int32)
    digits = jnp.stack([count // 128, count % 128]).astype(bf16)
    extra = jnp.concatenate(
        [
            norm_gains,
            jnp.broadcast_to(digits[None], (rows_dev, 2)),
            jnp.zeros((rows_dev, PAD - 6), bf16),
        ],
        axis=1,
    )

    routed = jnp.stack(
        gather_near(jnp.concatenate([routes.astype(f32), gate_weights], axis=1), "z")
    )
    route_all, gate_all = routed[..., :TOP].astype(jnp.int32), routed[..., TOP:]
    expert_ids = jnp.arange(seqs) * planes + plane
    match = route_all[:, :, None, :] == expert_ids[None, None, :, None]
    used = jnp.any(match, axis=-1)
    gate_of = jnp.sum(jnp.where(match, gate_all[:, :, None, :], 0.0), axis=-1)
    before = (jnp.arange(own)[:, None] > jnp.arange(own)[None, :]).astype(bf16)
    place = dot("tu,buk->btk", before, used.astype(bf16)).astype(jnp.int32)
    place = jnp.where(used, place, -1)
    slots = -(-capacity // 16) * 16
    place = place.transpose(2, 0, 1)[:, :, None, :]
    gate_of = gate_of.transpose(2, 0, 1)[:, :, None, :]

    groups = [[k for k in range(planes) if k % 2 == odd] for odd in range(2)]

    def by_group(table):
        return jnp.concatenate([table[:, k : k + 1] for group in groups for k in group], axis=1)

    place, gate_of = by_group(place), by_group(gate_of)

    inputs = to_inner(tokens)
    column_rows, extra_rows = rows_dev * 4 * cols // width, rows_dev * PAD // width
    extra = jnp.pad(extra.reshape(extra_rows, width), ((0, -extra_rows % 8), (0, 0)))

    def message_to(owner):
        picked = [
            lax.dynamic_slice_in_dim(w_attn, i * width + owner * cols, cols, 1) for i in range(4)
        ]
        picked = jnp.concatenate(picked, axis=1).reshape(column_rows, width)
        return jnp.concatenate([inputs, picked, extra], axis=0)

    messages = exchange(message_to, "s")
    gate_blocks = expert_chunk(0)
    up_blocks = expert_chunk(1, token(*gate_blocks))
    last = own + column_rows
    columns = [
        jnp.concatenate(
            [
                message[own:last].reshape(rows_dev, 4 * cols),
                message[last : last + extra_rows].reshape(rows_dev, PAD),
            ],
            axis=1,
        )
        for message in messages
    ]
    mine = in_order(columns, "s").reshape(part, 4 * cols + PAD)
    seq_tokens = in_order([message[:own] for message in messages], "s")
    seq_tokens = seq_tokens.reshape(seq, width).astype(f32)
    inputs = inputs.astype(f32)
    gate_ready = in_order(gate_blocks, "z", token(mine))
    w_gate = gather_plane(gate_ready)
    up_ready = in_order(up_blocks, "z", token(seq_tokens, place, gate_of))
    w_up = gather_plane(up_ready)
    in_blocks = gather_near(after(mine, up_ready), "z")
    seq_factor = rms_factor(seq_tokens)
    w_in = stack_rows(in_blocks, token(seq_factor))
    w_in_other = send(w_in, "c", 1)

    side = whole_of(w_in[:, 4 * cols :], w_in_other[:, 4 * cols :], 0)[:, :6].astype(f32).T
    gain_in, gain_mid = side[0], side[1]
    gain_q = lax.dynamic_slice_in_dim(to_outer(side[2]), rank * cols, cols, 0)
    gain_k = lax.dynamic_slice_in_dim(to_outer(side[3]), rank * cols, cols, 0)
    total_count = jnp.sum(side[4, ::rows_dev]) * 128.0 + jnp.sum(side[5, ::rows_dev])


    def near_planes(block):
        near = [block] + [None] * (planes - 1)
        for k in groups[0][1:]:
            near[k] = send(block, "z", k)
        later = after(block, *[near[k] for k in groups[0][1:]])
        for k in groups[1]:
            near[k] = send(later, "z", k)
        return [[near[k] for k in group] for group in groups]

    def send_back(first, second):
        got = [first[0]] + [send(first[i], "z", k) for i, k in enumerate(groups[0]) if k]
        base = after(total(got), second[0])
        second = [after(part, base) for part in second]
        return second[0], [base] + [send(second[i], "z", k) for i, k in enumerate(groups[1])]

    def total(pieces):
        return sum(piece.astype(f32) for piece in pieces)

    normed_in = (seq_tokens * seq_factor * gain_in).astype(bf16)
    normed_mine, normed_other = halves(normed_in)
    w_qkv, w_qkv_other = w_in[:, : 3 * cols], w_in_other[:, : 3 * cols]
    w_out = whole_of(w_in[:, 3 * cols : 4 * cols], w_in_other[:, 3 * cols : 4 * cols], 0)
    projected = jnp.dot(normed_mine, w_qkv, preferred_element_type=f32) + jnp.dot(
        normed_other, w_qkv_other, preferred_element_type=f32
    )
    query_raw = projected[:, :cols]
    key_raw = projected[:, cols : 2 * cols]

    def over_heads(first, second, *others):
        pairs = gather_near(jnp.stack([first, second]), "s")
        if others:
            pairs[0] = after(pairs[0], *others)
        pair = sum(pairs) / width
        return pair[0][:, None], pair[1][:, None]

    q_mean, k_mean = over_heads(
        jnp.sum(query_raw * query_raw, axis=-1), jnp.sum(key_raw * key_raw, axis=-1)
    )
    cosine, sine = rope_tables(seq)
    shared = [
        after(q_mean, w_gate, w_out),
        k_mean,
        gain_q[None],
        gain_k[None],
        cosine,
        sine,
        segment[:, None],
        segment[None],
    ]
    attended, query, keyed, valued, log_total = attend(projected, shared, heads)
    down_blocks = expert_chunk(2, token(attended))
    attn_out = dot("tc,dc->td", attended, w_out).astype(bf16)
    got = exchange_sum(attn_out.reshape(seqs, own, width), "s")
    residual = inputs + got
    down_ready = in_order(down_blocks, "z", token(residual))
    residual = after(residual, down_ready)
    w_down = gather_plane(down_ready)

    normed_mid = (residual * rms_factor(residual) * gain_mid).astype(bf16)
    expert_weights = (w_gate, w_up, w_down)
    blocks = near_planes(normed_mid)
    work = [Experts(i, slots, place, gate_of, blocks[i], expert_weights) for i in range(2)]
    rows_in, activated, *pres = work[0].to_hidden(blocks[0], w_gate, w_up, ())
    first = work[0].to_tokens(activated, w_down)
    pres = [pres]
    blocks[1][0] = after(blocks[1][0], first[0])
    rows_in, activated, *last = work[1].to_hidden(
        blocks[1], w_gate, w_up, (rows_in, activated)
    )
    pres.append(last)
    second = work[1].to_tokens(activated, w_down)
    final_out = residual + total(send_back(first, second)[1])
    rows_in, activated = [v.reshape(seqs, -1, v.shape[-1]) for v in (rows_in, activated)]

    w_out_all = lax.all_gather(after(w_out, w_up), "s", axis=0)
    valid_f = valid_mask.astype(f32)[:, None]
    difference = final_out - to_inner(teacher).astype(f32)
    squared = jnp.sum(valid_f * difference * difference)
    squared = gather_sum(squared)
    loss_value = squared / (total_count * width)
    grad_out = (
        to_inner(cotangent).astype(f32) + 2.0 / (total_count * width) * valid_f * difference
    )

    def scatter_expert(grad):
        grad = grad.reshape(seqs * width, hidden)
        grad = lax.psum_scatter(grad, ("s", "c", "o"), scatter_dimension=0, tiled=True)
        return grad.reshape(planes, part, hidden)

    blocks = near_planes(grad_out.astype(bf16))
    *grads, first, last = work[0].backward(blocks[0], expert_weights, pres[0], ())
    partial = [(first, last)]
    blocks[1][0] = after(blocks[1][0], first)
    *grads, first, last = work[1].backward(blocks[1], expert_weights, pres[1], grads)
    partial.append((first, last))
    back_last, back_pieces = send_back(*partial)
    grad_rows, grad_gate, grad_up = [v.reshape(seqs, -1, v.shape[-1]) for v in grads]
    grad_w_down = dot("krd,krf->kdf", grad_rows, after(activated, back_last)).astype(bf16)
    back_pieces[0] = after(back_pieces[0], grad_w_down)
    grad_mid = total(back_pieces)
    grad_w_gate = dot("krd,krf->kdf", rows_in, after(grad_gate, grad_mid)).astype(bf16)
    grad_resid_norm, gain_mid_grad = norm_back(residual, gain_mid, grad_mid)
    grad_resid = grad_out + grad_resid_norm

    grad_low = grad_resid.astype(bf16)
    grad_heads = dot("td,sdc->stc", grad_low, w_out_all).astype(bf16)
    head_blocks = exchange(
        lambda i: lax.dynamic_index_in_dim(grad_heads, i, 0, keepdims=False), "s"
    )
    grad_heads = in_order(head_blocks, "s", token(grad_w_gate)).reshape(seq, cols)
    grad_w_up = dot("krd,krf->kdf", rows_in, after(grad_up, grad_heads)).astype(bf16)
    up_done = grad_w_up
    grad_w_down, grad_w_gate, grad_w_up = [
        scatter_expert(grad) for grad in (grad_w_down, grad_w_gate, grad_w_up)
    ]
    low_blocks = gather_near(after(grad_low, grad_heads), "s")
    down_ready = swap(grad_w_down, "z")
    grad_q, grad_k, grad_v, q_inner, k_inner, gain_q_grad, gain_k_grad = attend_back(
        projected, shared, query, keyed, valued, after(grad_heads, up_done), log_total, heads
    )
    grad_attn_out = in_order(low_blocks, "s", token(grad_q)).reshape(seq, width)
    down_ready = after(down_ready, grad_q)
    q_inner = after(q_inner, down_ready, grad_attn_out)
    grad_w_out = dot("td,tc->dc", grad_attn_out, attended).astype(bf16)
    q_inner, k_inner = over_heads(q_inner[:, 0], k_inner[:, 0], grad_w_out)

    def norm_grad(grad, raw, mean, inner):
        factor = lax.rsqrt(mean + epsilon)
        return (factor * (grad - raw * factor * inner)).astype(bf16)

    grad_proj = jnp.concatenate(
        [
            norm_grad(grad_q, query_raw, q_mean, q_inner),
            norm_grad(grad_k, key_raw, k_mean, k_inner),
            grad_v,
        ],
        axis=1,
    )

    def back_half(weight):
        grad = dot("tc,dc->td", grad_proj, weight).astype(bf16)
        return exchange_sum(grad.reshape(seqs, own, width // 2), "s")

    grad_normed = whole_of(back_half(w_qkv), back_half(w_qkv_other), 1)
    grad_w_qkv = dot("td,tc->dc", normed_in, grad_proj).astype(bf16)
    summed = jnp.concatenate([sum_cores(grad_w_qkv), sum_cores(grad_w_out)], axis=1)
    summed = summed.astype(bf16).reshape(planes, part, 4 * cols)
    gate_ready = swap(grad_w_gate, "z")
    grad_attn = after(exchange_sum(summed, "z"), gate_ready).astype(bf16)
    up_ready = swap(after(grad_w_up, grad_attn), "z")
    grad_in_norm, gain_in_grad = norm_back(inputs, gain_in, grad_normed)
    grad_tokens = to_outer(grad_resid + grad_in_norm)

    def widen(local):
        full = jnp.zeros((width,), f32)
        return to_inner(lax.dynamic_update_slice_in_dim(full, local, rank * cols, 0))

    gains = jnp.stack([gain_in_grad, gain_mid_grad, widen(gain_q_grad[0]), widen(gain_k_grad[0])])
    gains = after(gains, grad_attn)
    for axis in ("z", "c", "s", "o"):
        gains = sum(gather_near(gains, axis))
    row = (lax.axis_index(("c", "o", "z")) * seqs + rank) * rows_dev
    grad_gains = lax.dynamic_slice_in_dim(gains, row, rows_dev, 1).T

    got = exchange_by_rank(grad_attn.reshape(seqs, rows_dev, 4 * cols), "s")
    got = in_order(got, "s").astype(f32)
    grad_attn = jnp.concatenate(
        [got[s, :, i * cols : (i + 1) * cols] for i in range(4) for s in range(seqs)], axis=1
    )
    grad_expert = jnp.concatenate([gate_ready, up_ready, down_ready], axis=2)
    grad_expert = grad_expert.astype(f32).transpose(1, 0, 2)
    return (
        to_outer(final_out).astype(bf16),
        loss_value,
        grad_tokens,
        grad_attn,
        grad_gains,
        grad_expert,
    )


def solution(mesh):
    fsdp, seqs = mesh.shape["fsdp"], mesh.shape["sp"]

    def whole(*arrays):
        planes = arrays[3].shape[1] // seqs
        outer = fsdp // (planes * CORES)
        inner = Mesh(mesh.devices.reshape(outer, planes, CORES, seqs), ("o", "z", "c", "s"))
        every = ("o", "z", "c", "s")
        rows = P(every, None)
        experts = P(("o", "z", "c"), "s", None)
        return jax.shard_map(
            shards,
            mesh=inner,
            in_specs=(
                rows,
                rows,
                rows,
                experts,
                rows,
                rows,
                P(("o", "z", "c")),
                P(every),
                rows,
                rows,
            ),
            out_specs=(rows, P(), rows, rows, rows, experts),
            check_vma=False,
        )(*arrays)

    return whole
```

```python
import functools

import jax
import jax.numpy as jnp
from jax import lax
from jax.experimental import pallas as pl
from jax.experimental.pallas import tpu as pltpu
from jax.sharding import Mesh, PartitionSpec as P

H = 16
HD = 128
TOP = 8
CORES = 2
PAD = 128

epsilon = 1e-05
masked = -1e30
f32 = jnp.float32
bf16 = jnp.bfloat16


def send(block, axis, step):
    size = lax.axis_size(axis)
    return lax.ppermute(block, axis, [(i, i ^ step) for i in range(size)])


def gather_near(block, axis):
    return [block] + [send(block, axis, k) for k in range(1, lax.axis_size(axis))]


def in_order(blocks, axis, start=0):
    rank = lax.axis_index(axis)
    if len(blocks) == 1:
        return blocks[0][None]
    stacked = jnp.zeros((len(blocks),) + blocks[0].shape, blocks[0].dtype)
    for k, block in enumerate(blocks):
        stacked = lax.dynamic_update_index_in_dim(stacked, block, (rank ^ k) + start, 0)
    return stacked


def collect(block, axis):
    return in_order(gather_near(block, axis), axis)


def exchange(piece_for, axis, start=0):
    rank, size = lax.axis_index(axis) + start, lax.axis_size(axis)
    return [piece_for(rank)] + [send(piece_for(rank ^ k), axis, k) for k in range(1, size)]


def swap(pieces, axis):
    return lax.all_to_all(pieces, axis, split_axis=0, concat_axis=0, tiled=True)


def exchange_by_rank(pieces, axis):
    return exchange(lambda i: lax.dynamic_index_in_dim(pieces, i, 0, keepdims=False), axis)


def exchange_sum(pieces, axis):
    got = exchange_by_rank(pieces, axis)
    return sum(piece.astype(f32) for piece in got)


def token(*values):
    firsts = [value[(slice(0, 1),) * value.ndim].reshape(()).astype(f32) for value in values]
    total = sum(firsts)
    return (total != total).astype(jnp.int32)


def after(value, *others):
    return value + token(*others).astype(value.dtype)


def rms_factor(values):
    return lax.rsqrt(jnp.mean(values * values, axis=-1, keepdims=True) + epsilon)


def norm_back(values, gain_vec, grad_in):
    factor = rms_factor(values)
    normed = values * factor
    gain_grad = jnp.sum(grad_in * normed, axis=0)
    inner = grad_in * gain_vec
    grad = factor * (inner - normed * jnp.mean(inner * normed, axis=-1, keepdims=True))
    return grad, gain_grad


def rope_tables(rows):
    inverse = 10000.0 ** (-(jnp.arange(HD // 2).astype(f32) * 2.0 / HD))
    angles = jnp.arange(rows).astype(f32)[:, None] * inverse[None, :]
    cosine = jnp.concatenate([jnp.cos(angles), jnp.cos(angles)], axis=-1)
    sine = jnp.concatenate([-jnp.sin(angles), jnp.sin(angles)], axis=-1)
    return cosine, sine


def mm(left, right, dims):
    return lax.dot_general(left, right, (dims, ((), ())), preferred_element_type=f32)


def masked_scores(query, keyed, seg_col, seg_row, first, scale):
    scores = mm(query, keyed, ((1,), (1,))) * scale
    rows = first + lax.broadcasted_iota(jnp.int32, scores.shape, 0)
    allowed = (rows >= lax.broadcasted_iota(jnp.int32, scores.shape, 1)) & (seg_col == seg_row)
    return jnp.where(allowed, scores, masked)


def attend_kernel(
    block,
    q_raw,
    k_raw,
    v_raw,
    q_mean,
    k_mean,
    gain_q,
    gain_k,
    cosine,
    sine,
    seg_col,
    seg_row,
    out,
    q_out,
    k_out,
    v_out,
    log_total,
):
    def rope(raw, mean, gain):
        values = raw[...] * lax.rsqrt(mean[...] + epsilon) * gain[...]
        turned = pltpu.roll(values, HD // 2, 1)
        return (values * cosine[...] + turned * sine[...]).astype(bf16)

    q_out[...] = rope(q_raw, q_mean, gain_q)
    k_out[...] = rope(k_raw, k_mean, gain_k)
    v_out[...] = v_raw[...].astype(bf16)
    for first in range(0, out.shape[0], block):
        last = first + block
        scores = masked_scores(
            q_out[first:last],
            k_out[:last],
            seg_col[first:last],
            seg_row[:, :last],
            first,
            HD**-0.5,
        )
        top = jnp.max(scores, axis=-1, keepdims=True)
        exps = jnp.exp(scores - top)
        total = jnp.sum(exps, axis=-1, keepdims=True)
        weights = (exps * (1.0 / total)).astype(bf16)
        out[first:last] = mm(weights, v_out[:last], ((1,), (0,))).astype(bf16)
        log_total[0, first:last] = top + jnp.log(total)


def attend_back_kernel(
    block,
    q_raw,
    k_raw,
    q_mean,
    k_mean,
    gain_q,
    gain_k,
    cosine,
    sine,
    seg_col,
    seg_row,
    query,
    keyed,
    valued,
    grad,
    log_total,
    grad_q,
    grad_k,
    grad_v,
    q_inner,
    k_inner,
    gain_q_grad,
    gain_k_grad,
    sum_q,
    sum_k,
    sum_v,
):
    scale = HD**-0.5
    sum_k[...] = jnp.zeros_like(sum_k)
    sum_v[...] = jnp.zeros_like(sum_v)
    for first in range(0, query.shape[0], block):
        last = first + block
        q_block, g_block = query[first:last], grad[first:last]
        scores = masked_scores(
            q_block, keyed[:last], seg_col[first:last], seg_row[:, :last], first, scale
        )
        probs = jnp.exp(scores - log_total[0, first:last])
        sum_v[:last] += mm(probs.astype(bf16), g_block, ((0,), (0,)))
        grad_probs = mm(g_block, valued[:last], ((1,), (1,)))
        inner = jnp.sum(probs * grad_probs, axis=-1, keepdims=True)
        grad_scores = (probs * (grad_probs - inner)).astype(bf16)
        sum_q[first:last] = mm(grad_scores, keyed[:last], ((1,), (0,))) * scale
        sum_k[:last] += mm(grad_scores, q_block, ((0,), (0,))) * scale
    grad_v[...] = sum_v[...].astype(bf16)

    def undo(total, raw, mean, gain, inner_out, gain_out, grad_out):
        low = total[...].astype(bf16).astype(f32)
        back = low * cosine[...] + pltpu.roll(low * sine[...], HD // 2, 1)
        normed = raw[...] * lax.rsqrt(mean[...] + epsilon)
        gain_out[...] = jnp.sum(back * normed, axis=0, keepdims=True)
        back = back * gain[...]
        grad_out[...] = back
        inner = jnp.sum(back * normed, axis=-1, keepdims=True)

        @pl.when(pl.program_id(0) == 0)
        def _():
            inner_out[...] = inner

        @pl.when(pl.program_id(0) > 0)
        def _():
            inner_out[...] += inner

    undo(sum_q, q_raw, q_mean, gain_q, q_inner, gain_q_grad, grad_q)
    undo(sum_k, k_raw, k_mean, gain_k, k_inner, gain_k_grad, grad_k)


def head_specs(seq, heads):
    column = pl.BlockSpec((seq, 1), lambda h: (0, 0))
    gain = pl.BlockSpec((1, HD), lambda h: (0, h))
    table = pl.BlockSpec((seq, HD), lambda h: (0, 0))
    return [column, column, gain, gain, table, table, column, pl.BlockSpec((1, seq), lambda h: (0, 0))]


def raw_spec(seq, heads, which):
    return pl.BlockSpec((seq, HD), lambda h: (0, which * heads + h))


def attend(projected, shared, heads):
    seq = projected.shape[0]
    block = min(256, seq)
    head = pl.BlockSpec((seq, HD), lambda h: (0, h))
    low = jax.ShapeDtypeStruct((seq, heads * HD), bf16)
    return pl.pallas_call(
        functools.partial(attend_kernel, block),
        grid=(heads,),
        in_specs=[raw_spec(seq, heads, i) for i in range(3)] + head_specs(seq, heads),
        out_specs=[head] * 4 + [pl.BlockSpec((1, seq, 1), lambda h: (h, 0, 0))],
        out_shape=[low] * 4 + [jax.ShapeDtypeStruct((heads, seq, 1), f32)],
        compiler_params=pltpu.CompilerParams(vmem_limit_bytes=48 * 2**20),
        cost_estimate=pl.CostEstimate(flops=10**6, bytes_accessed=10**5, transcendentals=0),
    )(projected, projected, projected, *shared)


def attend_back(projected, shared, query, keyed, valued, grad, log_total, heads):
    seq = projected.shape[0]
    block = min(256, seq)
    head = pl.BlockSpec((seq, HD), lambda h: (0, h))
    column = pl.BlockSpec((seq, 1), lambda h: (0, 0))
    gain = pl.BlockSpec((1, HD), lambda h: (0, h))
    wide = jax.ShapeDtypeStruct((seq, heads * HD), f32)
    return pl.pallas_call(
        functools.partial(attend_back_kernel, block),
        grid=(heads,),
        in_specs=[raw_spec(seq, heads, i) for i in range(2)]
        + head_specs(seq, heads)
        + [head] * 4
        + [pl.BlockSpec((1, seq, 1), lambda h: (h, 0, 0))],
        out_specs=[head] * 3 + [column] * 2 + [gain] * 2,
        out_shape=[wide, wide, jax.ShapeDtypeStruct((seq, heads * HD), bf16)]
        + [jax.ShapeDtypeStruct((seq, 1), f32)] * 2
        + [jax.ShapeDtypeStruct((1, heads * HD), f32)] * 2,
        scratch_shapes=[pltpu.VMEM((seq, HD), f32)] * 3,
        compiler_params=pltpu.CompilerParams(vmem_limit_bytes=48 * 2**20),
        cost_estimate=pl.CostEstimate(flops=10**6, bytes_accessed=10**5, transcendentals=0),
    )(projected, projected, *shared, query, keyed, valued, grad, log_total)


def slot_choice(place, slots):
    return lax.broadcasted_iota(jnp.int32, (slots, place.shape[1]), 0) == place


def slot_weight(place, gate, slots):
    return jnp.sum(jnp.where(slot_choice(place, slots), gate, 0.0), axis=1, keepdims=True)


def spans_of(count, slots):
    return [(b, slice(b * slots, (b + 1) * slots)) for b in range(count)]


def add_tokens(place, b, slots, out, sum_tokens, partial):
    expert = pl.program_id(0)
    back = mm(slot_choice(place[0, b], slots).astype(bf16), out, ((0,), (0,)))

    @pl.when(expert == 0)
    def _():
        sum_tokens[b] = back

    @pl.when(expert > 0)
    def _():
        sum_tokens[b] += back

    @pl.when(expert == pl.num_programs(0) - 1)
    def _():
        partial[b][...] = sum_tokens[b].astype(bf16)


def hidden_kernel(count, slots, place, *refs):
    blocks, w_gate, w_up = refs[:count], refs[count], refs[count + 1]
    rows, activated, gate_pre, up_pre = refs[-4:]
    for b, span in spans_of(count, slots):
        choice = slot_choice(place[0, b], slots).astype(bf16)
        rows[0, 0, span] = mm(choice, blocks[b][...], ((1,), (0,))).astype(bf16)
    rows_in = rows[0, 0]
    g = mm(rows_in, w_gate[0], ((1,), (0,)))
    u = mm(rows_in, w_up[0], ((1,), (0,)))
    gate_pre[0], up_pre[0] = g.astype(bf16), u.astype(bf16)
    activated[0, 0] = (g * jax.nn.sigmoid(g) * u).astype(bf16)


def out_kernel(count, slots, place, gate, activated, w_down, *refs):
    partial, sum_tokens = refs[:-1], refs[-1]
    result = mm(activated[0, 0], w_down[0], ((1,), (1,)))
    for b, span in spans_of(count, slots):
        out = (result[span] * slot_weight(place[0, b], gate[0, b], slots)).astype(bf16)
        add_tokens(place, b, slots, out, sum_tokens, partial)


def expert_back_kernel(count, slots, place, gate, *refs):
    blocks, (w_gate, w_up, w_down) = refs[:count], refs[count : count + 3]
    gate_pre, up_pre = refs[count + 3 : count + 5]
    grad_rows, grad_gate, grad_up = refs[-4 - count : -1 - count]
    partial, sum_tokens = refs[-1 - count : -1], refs[-1]
    for b, span in spans_of(count, slots):
        choice = slot_choice(place[0, b], slots).astype(bf16)
        weight = slot_weight(place[0, b], gate[0, b], slots)
        picked = mm(choice, blocks[b][...], ((1,), (0,)))
        grad_rows[0, 0, span] = (picked * weight).astype(bf16)
    grad_act = mm(grad_rows[0, 0], w_down[0], ((1,), (0,)))
    g, u = gate_pre[0].astype(f32), up_pre[0].astype(f32)
    sigmoid = jax.nn.sigmoid(g)
    dg = (grad_act * u * sigmoid * (1.0 + g * (1.0 - sigmoid))).astype(bf16)
    du = (grad_act * g * sigmoid).astype(bf16)
    grad_gate[0, 0], grad_up[0, 0] = dg, du
    result = mm(dg, w_gate[0], ((1,), (1,))) + mm(du, w_up[0], ((1,), (1,)))
    result = result.astype(bf16)
    for b, span in spans_of(count, slots):
        add_tokens(place, b, slots, result[span], sum_tokens, partial)


class Experts:
    def __init__(self, group, slots, place, gate, blocks, weights):
        self.group, self.slots, self.place, self.gate = group, slots, place, gate
        self.experts, self.width, self.hidden = weights[0].shape
        self.count, self.own = len(blocks), blocks[0].shape[0]
        self.rows = self.count * slots
        group_of = lambda e: (e, group, 0, 0)
        self.table = pl.BlockSpec((1, self.count, 1, self.own), group_of)
        self.tokens = pl.BlockSpec((self.own, self.width), lambda e: (0, 0))
        self.weight = pl.BlockSpec((1, self.width, self.hidden), lambda e: (e, 0, 0))
        self.local = pl.BlockSpec((1, self.rows, self.hidden), lambda e: (e, 0, 0))
        self.wide = pl.BlockSpec((1, 1, self.rows, self.width), group_of)
        self.narrow = pl.BlockSpec((1, 1, self.rows, self.hidden), group_of)
        self.sums = pltpu.VMEM((self.count, self.own, self.width), f32)

    def shape(self, spec):
        rows, experts = self.rows, self.experts
        shapes = [
            (self.tokens, (self.own, self.width)),
            (self.local, (experts, rows, self.hidden)),
            (self.wide, (experts, 2, rows, self.width)),
            (self.narrow, (experts, 2, rows, self.hidden)),
        ]
        [shape] = [shape for known, shape in shapes if known is spec]
        return jax.ShapeDtypeStruct(shape, bf16)

    def run(self, kernel, ins, outs, scratch, prior=()):
        specs = [spec for spec, _ in ins] + [pl.BlockSpec(memory_space=pl.ANY)] * len(prior)
        return pl.pallas_call(
            functools.partial(kernel, self.count, self.slots),
            grid=(self.experts,),
            in_specs=specs,
            out_specs=outs,
            out_shape=[self.shape(spec) for spec in outs],
            scratch_shapes=scratch,
            input_output_aliases={len(ins) + i: i for i in range(len(prior))},
            compiler_params=pltpu.CompilerParams(vmem_limit_bytes=58 * 2**20),
            cost_estimate=pl.CostEstimate(
                flops=self.experts * self.rows * self.width * self.hidden * 4,
                bytes_accessed=self.experts * self.width * self.hidden * 6,
                transcendentals=self.experts * self.rows * self.hidden,
            ),
        )(*[array for _, array in ins], *prior)

    def to_hidden(self, blocks, w_gate, w_up, prior):
        ins = [(self.table, self.place)] + [(self.tokens, block) for block in blocks]
        ins += [(self.weight, w_gate), (self.weight, w_up)]
        outs = [self.wide, self.narrow, self.local, self.local]
        return self.run(hidden_kernel, ins, outs, [], prior)

    def to_tokens(self, activated, w_down):
        ins = [(self.table, self.place), (self.table, self.gate)]
        ins += [(self.narrow, activated), (self.weight, w_down)]
        return self.run(out_kernel, ins, [self.tokens] * self.count, [self.sums])

    def backward(self, blocks, weights, pres, prior):
        ins = [(self.table, self.place), (self.table, self.gate)]
        ins += [(self.tokens, block) for block in blocks]
        ins += [(self.weight, weight) for weight in weights]
        ins += [(self.local, pre) for pre in pres]
        outs = [self.wide, self.narrow, self.narrow] + [self.tokens] * self.count
        return self.run(expert_back_kernel, ins, outs, [self.sums], prior)


def dot(spec, left, right):
    return jnp.einsum(spec, left, right, preferred_element_type=f32)


def shards(
    tokens,
    w_attn,
    norm_gains,
    w_expert,
    gate_weights,
    routes,
    segment,
    valid_mask,
    teacher,
    cotangent,
):
    outer, planes, seqs = lax.axis_size("o"), lax.axis_size("z"), lax.axis_size("s")
    plane, rank = lax.axis_index("z"), lax.axis_index("s")
    own, width = tokens.shape
    rows_dev = w_attn.shape[0]
    seq = own * seqs
    heads = H // seqs
    cols = heads * HD
    hidden = w_expert.shape[2] // 3
    part = w_expert.shape[0]
    capacity = own * TOP * 17 // (16 * planes * seqs)
    scale = HD ** (-0.5)

    def to_inner(v):
        lead = v.shape[:-1]
        v = v.reshape(lead + (outer * planes, CORES, part))
        return jnp.swapaxes(v, -3, -2).reshape(lead + (width,))

    def to_outer(v):
        lead = v.shape[:-1]
        v = v.reshape(lead + (CORES, outer * planes, part))
        return jnp.swapaxes(v, -3, -2).reshape(lead + (width,))

    first_core = lax.axis_index("c") == 0

    def halves(v):
        low, high = v[..., : width // 2], v[..., width // 2 :]
        return jnp.where(first_core, low, high), jnp.where(first_core, high, low)

    def whole_of(mine, other, axis):
        low, high = jnp.where(first_core, mine, other), jnp.where(first_core, other, mine)
        return jnp.concatenate([low, high], axis=axis)

    def stack_rows(blocks, start=0):
        rows = in_order(blocks, "z", start)
        return collect(rows, "o").reshape((width // 2,) + rows.shape[2:])

    def sum_cores(grad):
        count = grad.shape[1]
        grad = exchange_sum(grad.reshape(CORES, width // 2, count), "c")
        if outer > 1:
            grad = exchange_sum(grad.astype(bf16).reshape(outer, planes * part, count), "o")
        return grad

    def gather_sum(value):
        for axis in ("z", "s", "c", "o"):
            value = sum(gather_near(jnp.broadcast_to(value, (8, PAD)), axis))[0, 0]
        return value

    by_expert = lax.optimization_barrier(w_expert.transpose(1, 0, 2))

    def expert_chunk(i, start=0):
        def piece_for(owner):
            return lax.dynamic_slice(by_expert, (owner, 0, i * hidden), (1, part, hidden))[0]

        return exchange(piece_for, "z", start)

    def gather_plane(ready):
        chunk = ready.reshape(planes * part, hidden)
        chunk = lax.all_gather(chunk, ("s", "c", "o"), axis=0, tiled=True)
        return chunk.reshape(seqs, width, hidden)

    count = jnp.sum(valid_mask).astype(jnp.int32)
    digits = jnp.stack([count // 128, count % 128]).astype(bf16)
    extra = jnp.concatenate(
        [
            norm_gains,
            jnp.broadcast_to(digits[None], (rows_dev, 2)),
            jnp.zeros((rows_dev, PAD - 6), bf16),
        ],
        axis=1,
    )

    routed = jnp.stack(
        gather_near(jnp.concatenate([routes.astype(f32), gate_weights], axis=1), "z")
    )
    route_all, gate_all = routed[..., :TOP].astype(jnp.int32), routed[..., TOP:]
    expert_ids = jnp.arange(seqs) * planes + plane
    match = route_all[:, :, None, :] == expert_ids[None, None, :, None]
    used = jnp.any(match, axis=-1)
    gate_of = jnp.sum(jnp.where(match, gate_all[:, :, None, :], 0.0), axis=-1)
    before = (jnp.arange(own)[:, None] > jnp.arange(own)[None, :]).astype(bf16)
    place = dot("tu,buk->btk", before, used.astype(bf16)).astype(jnp.int32)
    place = jnp.where(used, place, -1)
    slots = -(-capacity // 16) * 16
    place = place.transpose(2, 0, 1)[:, :, None, :]
    gate_of = gate_of.transpose(2, 0, 1)[:, :, None, :]

    groups = [[k for k in range(planes) if k % 2 == odd] for odd in range(2)]

    def by_group(table):
        return jnp.concatenate([table[:, k : k + 1] for group in groups for k in group], axis=1)

    place, gate_of = by_group(place), by_group(gate_of)

    inputs = to_inner(tokens)
    column_rows, extra_rows = rows_dev * 4 * cols // width, rows_dev * PAD // width
    extra = jnp.pad(extra.reshape(extra_rows, width), ((0, -extra_rows % 8), (0, 0)))

    def message_to(owner):
        picked = [
            lax.dynamic_slice_in_dim(w_attn, i * width + owner * cols, cols, 1) for i in range(4)
        ]
        picked = jnp.concatenate(picked, axis=1).reshape(column_rows, width)
        return jnp.concatenate([inputs, picked, extra], axis=0)

    messages = exchange(message_to, "s")
    gate_blocks = expert_chunk(0)
    up_blocks = expert_chunk(1, token(*gate_blocks))
    last = own + column_rows
    columns = [
        jnp.concatenate(
            [
                message[own:last].reshape(rows_dev, 4 * cols),
                message[last : last + extra_rows].reshape(rows_dev, PAD),
            ],
            axis=1,
        )
        for message in messages
    ]
    mine = in_order(columns, "s").reshape(part, 4 * cols + PAD)
    seq_tokens = in_order([message[:own] for message in messages], "s")
    seq_tokens = seq_tokens.reshape(seq, width).astype(f32)
    inputs = inputs.astype(f32)
    gate_ready = in_order(gate_blocks, "z", token(mine))
    w_gate = gather_plane(gate_ready)
    up_ready = in_order(up_blocks, "z", token(seq_tokens, place, gate_of))
    w_up = gather_plane(up_ready)
    in_blocks = gather_near(after(mine, up_ready), "z")
    seq_factor = rms_factor(seq_tokens)
    w_in = stack_rows(in_blocks, token(seq_factor))
    w_in_other = send(w_in, "c", 1)
    down_blocks = expert_chunk(2, token(w_in))

    side = whole_of(w_in[:, 4 * cols :], w_in_other[:, 4 * cols :], 0)[:, :6].astype(f32).T
    gain_in, gain_mid = side[0], side[1]
    gain_q = lax.dynamic_slice_in_dim(to_outer(side[2]), rank * cols, cols, 0)
    gain_k = lax.dynamic_slice_in_dim(to_outer(side[3]), rank * cols, cols, 0)
    total_count = jnp.sum(side[4, ::rows_dev]) * 128.0 + jnp.sum(side[5, ::rows_dev])


    def near_planes(block):
        near = [block] + [None] * (planes - 1)
        for k in groups[0][1:]:
            near[k] = send(block, "z", k)
        later = after(block, *[near[k] for k in groups[0][1:]])
        for k in groups[1]:
            near[k] = send(later, "z", k)
        return [[near[k] for k in group] for group in groups]

    def send_back(first, second):
        got = [first[0]] + [send(first[i], "z", k) for i, k in enumerate(groups[0]) if k]
        base = after(total(got), second[0])
        second = [after(part, base) for part in second]
        return second[0], [base] + [send(second[i], "z", k) for i, k in enumerate(groups[1])]

    def total(pieces):
        return sum(piece.astype(f32) for piece in pieces)

    normed_in = (seq_tokens * seq_factor * gain_in).astype(bf16)
    normed_mine, normed_other = halves(normed_in)
    w_qkv, w_qkv_other = w_in[:, : 3 * cols], w_in_other[:, : 3 * cols]
    w_out = whole_of(w_in[:, 3 * cols : 4 * cols], w_in_other[:, 3 * cols : 4 * cols], 0)
    projected = jnp.dot(normed_mine, w_qkv, preferred_element_type=f32) + jnp.dot(
        normed_other, w_qkv_other, preferred_element_type=f32
    )
    query_raw = projected[:, :cols]
    key_raw = projected[:, cols : 2 * cols]

    def over_heads(first, second, *others):
        pairs = gather_near(jnp.stack([first, second]), "s")
        if others:
            pairs[0] = after(pairs[0], *others)
        pair = sum(pairs) / width
        return pair[0][:, None], pair[1][:, None]

    q_mean, k_mean = over_heads(
        jnp.sum(query_raw * query_raw, axis=-1), jnp.sum(key_raw * key_raw, axis=-1)
    )
    cosine, sine = rope_tables(seq)
    shared = [
        after(q_mean, w_gate, w_out),
        k_mean,
        gain_q[None],
        gain_k[None],
        cosine,
        sine,
        segment[:, None],
        segment[None],
    ]
    attended, query, keyed, valued, log_total = attend(projected, shared, heads)
    down_ready = in_order(down_blocks, "z", token(attended))
    w_down = gather_plane(down_ready)
    attn_out = dot("tc,dc->td", after(attended, down_ready), w_out).astype(bf16)
    got = exchange_sum(attn_out.reshape(seqs, own, width), "s")
    residual = inputs + got

    normed_mid = (residual * rms_factor(residual) * gain_mid).astype(bf16)
    expert_weights = (w_gate, w_up, w_down)
    blocks = near_planes(normed_mid)
    work = [Experts(i, slots, place, gate_of, blocks[i], expert_weights) for i in range(2)]
    rows_in, activated, *pres = work[0].to_hidden(blocks[0], w_gate, w_up, ())
    first = work[0].to_tokens(activated, w_down)
    pres = [pres]
    blocks[1][0] = after(blocks[1][0], first[0])
    rows_in, activated, *last = work[1].to_hidden(
        blocks[1], w_gate, w_up, (rows_in, activated)
    )
    pres.append(last)
    second = work[1].to_tokens(activated, w_down)
    final_out = residual + total(send_back(first, second)[1])
    rows_in, activated = [v.reshape(seqs, -1, v.shape[-1]) for v in (rows_in, activated)]

    w_out_all = lax.all_gather(after(w_out, w_up), "s", axis=0)
    valid_f = valid_mask.astype(f32)[:, None]
    difference = final_out - to_inner(teacher).astype(f32)
    squared = jnp.sum(valid_f * difference * difference)
    grad_out = (
        to_inner(cotangent).astype(f32) + 2.0 / (total_count * width) * valid_f * difference
    )

    def scatter_expert(grad):
        grad = grad.reshape(seqs * width, hidden)
        grad = lax.psum_scatter(grad, ("s", "c", "o"), scatter_dimension=0, tiled=True)
        return grad.reshape(planes, part, hidden)

    blocks = near_planes(grad_out.astype(bf16))
    *grads, first, last = work[0].backward(blocks[0], expert_weights, pres[0], ())
    partial = [(first, last)]
    blocks[1][0] = after(blocks[1][0], first)
    *grads, first, last = work[1].backward(blocks[1], expert_weights, pres[1], grads)
    partial.append((first, last))
    back_last, back_pieces = send_back(*partial)
    grad_rows, grad_gate, grad_up = [v.reshape(seqs, -1, v.shape[-1]) for v in grads]
    grad_w_down = dot("krd,krf->kdf", grad_rows, after(activated, back_last)).astype(bf16)
    back_pieces[0] = after(back_pieces[0], grad_w_down)
    grad_mid = total(back_pieces)
    grad_w_gate = dot("krd,krf->kdf", rows_in, after(grad_gate, grad_mid)).astype(bf16)
    grad_resid_norm, gain_mid_grad = norm_back(residual, gain_mid, grad_mid)
    grad_resid = grad_out + grad_resid_norm

    grad_low = grad_resid.astype(bf16)
    grad_attn_out = swap(jnp.broadcast_to(grad_low[None], (seqs, own, width)), "s")
    grad_attn_out = grad_attn_out.reshape(seq, width)
    grad_heads = dot("td,sdc->stc", grad_low, w_out_all).astype(bf16)
    head_blocks = exchange(
        lambda i: lax.dynamic_index_in_dim(grad_heads, i, 0, keepdims=False), "s"
    )
    grad_heads = in_order(head_blocks, "s", token(grad_w_gate)).reshape(seq, cols)
    grad_w_up = dot("krd,krf->kdf", rows_in, after(grad_up, grad_heads)).astype(bf16)
    up_done = grad_w_up
    grad_w_down, grad_w_gate, grad_w_up = [
        scatter_expert(grad) for grad in (grad_w_down, grad_w_gate, grad_w_up)
    ]
    down_ready = swap(grad_w_down, "z")
    grad_q, grad_k, grad_v, q_inner, k_inner, gain_q_grad, gain_k_grad = attend_back(
        projected, shared, query, keyed, valued, after(grad_heads, up_done), log_total, heads
    )
    grad_w_out = dot("td,tc->dc", grad_attn_out, attended).astype(bf16)
    q_inner, k_inner = over_heads(q_inner[:, 0], k_inner[:, 0])

    def norm_grad(grad, raw, mean, inner):
        factor = lax.rsqrt(mean + epsilon)
        return (factor * (grad - raw * factor * inner)).astype(bf16)

    grad_proj = jnp.concatenate(
        [
            norm_grad(grad_q, query_raw, q_mean, q_inner),
            norm_grad(grad_k, key_raw, k_mean, k_inner),
            grad_v,
        ],
        axis=1,
    )

    def back_half(weight):
        grad = dot("tc,dc->td", grad_proj, weight).astype(bf16)
        return exchange_sum(grad.reshape(seqs, own, width // 2), "s")

    grad_w_qkv = dot("td,tc->dc", normed_in, grad_proj).astype(bf16)
    summed = jnp.concatenate([sum_cores(grad_w_qkv), sum_cores(grad_w_out)], axis=1)
    summed = summed.astype(bf16).reshape(planes, part, 4 * cols)
    gate_ready = swap(after(grad_w_gate, down_ready), "z")
    grad_proj = after(grad_proj, summed)
    grad_normed = whole_of(back_half(w_qkv), back_half(w_qkv_other), 1)
    grad_attn = jnp.sum(swap(summed, "z").astype(f32), axis=0).astype(bf16)
    up_ready = swap(after(grad_w_up, grad_attn, gate_ready), "z")
    grad_in_norm, gain_in_grad = norm_back(inputs, gain_in, grad_normed)
    grad_tokens = to_outer(grad_resid + grad_in_norm)

    def widen(local):
        full = jnp.zeros((width,), f32)
        return to_inner(lax.dynamic_update_slice_in_dim(full, local, rank * cols, 0))

    gains = jnp.stack([gain_in_grad, gain_mid_grad, widen(gain_q_grad[0]), widen(gain_k_grad[0])])
    gains = after(gains, grad_attn)
    loss_value = gather_sum(after(squared, grad_attn)) / (total_count * width)
    for axis in ("z", "c", "s", "o"):
        gains = sum(gather_near(gains, axis))
    row = (lax.axis_index(("c", "o", "z")) * seqs + rank) * rows_dev
    grad_gains = lax.dynamic_slice_in_dim(gains, row, rows_dev, 1).T

    got = exchange_by_rank(grad_attn.reshape(seqs, rows_dev, 4 * cols), "s")
    got = in_order(got, "s").astype(f32)
    grad_attn = jnp.concatenate(
        [got[s, :, i * cols : (i + 1) * cols] for i in range(4) for s in range(seqs)], axis=1
    )
    grad_expert = jnp.concatenate([gate_ready, up_ready, down_ready], axis=2)
    grad_expert = grad_expert.astype(f32).transpose(1, 0, 2)
    return (
        to_outer(final_out).astype(bf16),
        loss_value,
        grad_tokens,
        grad_attn,
        grad_gains,
        grad_expert,
    )


def solution(mesh):
    fsdp, seqs = mesh.shape["fsdp"], mesh.shape["sp"]

    def whole(*arrays):
        planes = arrays[3].shape[1] // seqs
        outer = fsdp // (planes * CORES)
        inner = Mesh(mesh.devices.reshape(outer, planes, CORES, seqs), ("o", "z", "c", "s"))
        every = ("o", "z", "c", "s")
        rows = P(every, None)
        experts = P(("o", "z", "c"), "s", None)
        return jax.shard_map(
            shards,
            mesh=inner,
            in_specs=(
                rows,
                rows,
                rows,
                experts,
                rows,
                rows,
                P(("o", "z", "c")),
                P(every),
                rows,
                rows,
            ),
            out_specs=(rows, P(), rows, rows, rows, experts),
            check_vma=False,
        )(*arrays)

    return whole
```

```python
import functools

import jax
import jax.numpy as jnp
from jax import lax
from jax.experimental import pallas as pl
from jax.experimental.pallas import tpu as pltpu
from jax.sharding import Mesh, PartitionSpec as P

H = 16
HD = 128
TOP = 8
CORES = 2
PAD = 128

epsilon = 1e-05
masked = -1e30
f32 = jnp.float32
bf16 = jnp.bfloat16


def send(block, axis, step):
    size = lax.axis_size(axis)
    return lax.ppermute(block, axis, [(i, i ^ step) for i in range(size)])


def gather_near(block, axis):
    return [block] + [send(block, axis, k) for k in range(1, lax.axis_size(axis))]


def in_order(blocks, axis, start=0):
    rank = lax.axis_index(axis)
    if len(blocks) == 1:
        return blocks[0][None]
    stacked = jnp.zeros((len(blocks),) + blocks[0].shape, blocks[0].dtype)
    for k, block in enumerate(blocks):
        stacked = lax.dynamic_update_index_in_dim(stacked, block, (rank ^ k) + start, 0)
    return stacked


def collect(block, axis):
    return in_order(gather_near(block, axis), axis)


def exchange(piece_for, axis, start=0):
    rank, size = lax.axis_index(axis) + start, lax.axis_size(axis)
    return [piece_for(rank)] + [send(piece_for(rank ^ k), axis, k) for k in range(1, size)]


def swap(pieces, axis):
    return lax.all_to_all(pieces, axis, split_axis=0, concat_axis=0, tiled=True)


def exchange_by_rank(pieces, axis):
    return exchange(lambda i: lax.dynamic_index_in_dim(pieces, i, 0, keepdims=False), axis)


def exchange_sum(pieces, axis):
    got = exchange_by_rank(pieces, axis)
    return sum(piece.astype(f32) for piece in got)


def token(*values):
    firsts = [value[(slice(0, 1),) * value.ndim].reshape(()).astype(f32) for value in values]
    total = sum(firsts)
    return (total != total).astype(jnp.int32)


def after(value, *others):
    return value + token(*others).astype(value.dtype)


def rms_factor(values):
    return lax.rsqrt(jnp.mean(values * values, axis=-1, keepdims=True) + epsilon)


def norm_back(values, gain_vec, grad_in):
    factor = rms_factor(values)
    normed = values * factor
    gain_grad = jnp.sum(grad_in * normed, axis=0)
    inner = grad_in * gain_vec
    grad = factor * (inner - normed * jnp.mean(inner * normed, axis=-1, keepdims=True))
    return grad, gain_grad


def rope_tables(rows):
    inverse = 10000.0 ** (-(jnp.arange(HD // 2).astype(f32) * 2.0 / HD))
    angles = jnp.arange(rows).astype(f32)[:, None] * inverse[None, :]
    cosine = jnp.concatenate([jnp.cos(angles), jnp.cos(angles)], axis=-1)
    sine = jnp.concatenate([-jnp.sin(angles), jnp.sin(angles)], axis=-1)
    return cosine, sine


def mm(left, right, dims):
    return lax.dot_general(left, right, (dims, ((), ())), preferred_element_type=f32)


def masked_scores(query, keyed, seg_col, seg_row, first, scale):
    scores = mm(query, keyed, ((1,), (1,))) * scale
    rows = first + lax.broadcasted_iota(jnp.int32, scores.shape, 0)
    allowed = (rows >= lax.broadcasted_iota(jnp.int32, scores.shape, 1)) & (seg_col == seg_row)
    return jnp.where(allowed, scores, masked)


def attend_kernel(
    block,
    q_raw,
    k_raw,
    v_raw,
    q_mean,
    k_mean,
    gain_q,
    gain_k,
    cosine,
    sine,
    seg_col,
    seg_row,
    out,
    q_out,
    k_out,
    v_out,
    log_total,
):
    def rope(raw, mean, gain):
        values = raw[...] * lax.rsqrt(mean[...] + epsilon) * gain[...]
        turned = pltpu.roll(values, HD // 2, 1)
        return (values * cosine[...] + turned * sine[...]).astype(bf16)

    q_out[...] = rope(q_raw, q_mean, gain_q)
    k_out[...] = rope(k_raw, k_mean, gain_k)
    v_out[...] = v_raw[...].astype(bf16)
    for first in range(0, out.shape[0], block):
        last = first + block
        scores = masked_scores(
            q_out[first:last],
            k_out[:last],
            seg_col[first:last],
            seg_row[:, :last],
            first,
            HD**-0.5,
        )
        top = jnp.max(scores, axis=-1, keepdims=True)
        exps = jnp.exp(scores - top)
        total = jnp.sum(exps, axis=-1, keepdims=True)
        weights = (exps * (1.0 / total)).astype(bf16)
        out[first:last] = mm(weights, v_out[:last], ((1,), (0,))).astype(bf16)
        log_total[0, first:last] = top + jnp.log(total)


def attend_back_kernel(
    block,
    q_raw,
    k_raw,
    q_mean,
    k_mean,
    gain_q,
    gain_k,
    cosine,
    sine,
    seg_col,
    seg_row,
    query,
    keyed,
    valued,
    grad,
    log_total,
    grad_q,
    grad_k,
    grad_v,
    q_inner,
    k_inner,
    gain_q_grad,
    gain_k_grad,
    sum_q,
    sum_k,
    sum_v,
):
    scale = HD**-0.5
    sum_k[...] = jnp.zeros_like(sum_k)
    sum_v[...] = jnp.zeros_like(sum_v)
    for first in range(0, query.shape[0], block):
        last = first + block
        q_block, g_block = query[first:last], grad[first:last]
        scores = masked_scores(
            q_block, keyed[:last], seg_col[first:last], seg_row[:, :last], first, scale
        )
        probs = jnp.exp(scores - log_total[0, first:last])
        sum_v[:last] += mm(probs.astype(bf16), g_block, ((0,), (0,)))
        grad_probs = mm(g_block, valued[:last], ((1,), (1,)))
        inner = jnp.sum(probs * grad_probs, axis=-1, keepdims=True)
        grad_scores = (probs * (grad_probs - inner)).astype(bf16)
        sum_q[first:last] = mm(grad_scores, keyed[:last], ((1,), (0,))) * scale
        sum_k[:last] += mm(grad_scores, q_block, ((0,), (0,))) * scale
    grad_v[...] = sum_v[...].astype(bf16)

    def undo(total, raw, mean, gain, inner_out, gain_out, grad_out):
        low = total[...].astype(bf16).astype(f32)
        back = low * cosine[...] + pltpu.roll(low * sine[...], HD // 2, 1)
        normed = raw[...] * lax.rsqrt(mean[...] + epsilon)
        gain_out[...] = jnp.sum(back * normed, axis=0, keepdims=True)
        back = back * gain[...]
        grad_out[...] = back
        inner = jnp.sum(back * normed, axis=-1, keepdims=True)

        @pl.when(pl.program_id(0) == 0)
        def _():
            inner_out[...] = inner

        @pl.when(pl.program_id(0) > 0)
        def _():
            inner_out[...] += inner

    undo(sum_q, q_raw, q_mean, gain_q, q_inner, gain_q_grad, grad_q)
    undo(sum_k, k_raw, k_mean, gain_k, k_inner, gain_k_grad, grad_k)


def head_specs(seq, heads):
    column = pl.BlockSpec((seq, 1), lambda h: (0, 0))
    gain = pl.BlockSpec((1, HD), lambda h: (0, h))
    table = pl.BlockSpec((seq, HD), lambda h: (0, 0))
    return [column, column, gain, gain, table, table, column, pl.BlockSpec((1, seq), lambda h: (0, 0))]


def raw_spec(seq, heads, which):
    return pl.BlockSpec((seq, HD), lambda h: (0, which * heads + h))


def attend(projected, shared, heads):
    seq = projected.shape[0]
    block = min(256, seq)
    head = pl.BlockSpec((seq, HD), lambda h: (0, h))
    low = jax.ShapeDtypeStruct((seq, heads * HD), bf16)
    return pl.pallas_call(
        functools.partial(attend_kernel, block),
        grid=(heads,),
        in_specs=[raw_spec(seq, heads, i) for i in range(3)] + head_specs(seq, heads),
        out_specs=[head] * 4 + [pl.BlockSpec((1, seq, 1), lambda h: (h, 0, 0))],
        out_shape=[low] * 4 + [jax.ShapeDtypeStruct((heads, seq, 1), f32)],
        compiler_params=pltpu.CompilerParams(vmem_limit_bytes=48 * 2**20),
        cost_estimate=pl.CostEstimate(flops=10**6, bytes_accessed=10**5, transcendentals=0),
    )(projected, projected, projected, *shared)


def attend_back(projected, shared, query, keyed, valued, grad, log_total, heads):
    seq = projected.shape[0]
    block = min(256, seq)
    head = pl.BlockSpec((seq, HD), lambda h: (0, h))
    column = pl.BlockSpec((seq, 1), lambda h: (0, 0))
    gain = pl.BlockSpec((1, HD), lambda h: (0, h))
    wide = jax.ShapeDtypeStruct((seq, heads * HD), f32)
    return pl.pallas_call(
        functools.partial(attend_back_kernel, block),
        grid=(heads,),
        in_specs=[raw_spec(seq, heads, i) for i in range(2)]
        + head_specs(seq, heads)
        + [head] * 4
        + [pl.BlockSpec((1, seq, 1), lambda h: (h, 0, 0))],
        out_specs=[head] * 3 + [column] * 2 + [gain] * 2,
        out_shape=[wide, wide, jax.ShapeDtypeStruct((seq, heads * HD), bf16)]
        + [jax.ShapeDtypeStruct((seq, 1), f32)] * 2
        + [jax.ShapeDtypeStruct((1, heads * HD), f32)] * 2,
        scratch_shapes=[pltpu.VMEM((seq, HD), f32)] * 3,
        compiler_params=pltpu.CompilerParams(vmem_limit_bytes=48 * 2**20),
        cost_estimate=pl.CostEstimate(flops=10**6, bytes_accessed=10**5, transcendentals=0),
    )(projected, projected, *shared, query, keyed, valued, grad, log_total)


def slot_choice(place, slots):
    return lax.broadcasted_iota(jnp.int32, (slots, place.shape[1]), 0) == place


def slot_weight(place, gate, slots):
    return jnp.sum(jnp.where(slot_choice(place, slots), gate, 0.0), axis=1, keepdims=True)


def spans_of(count, slots):
    return [(b, slice(b * slots, (b + 1) * slots)) for b in range(count)]


def add_tokens(place, b, slots, out, sum_tokens, partial):
    expert = pl.program_id(0)
    back = mm(slot_choice(place[0, b], slots).astype(bf16), out, ((0,), (0,)))

    @pl.when(expert == 0)
    def _():
        sum_tokens[b] = back

    @pl.when(expert > 0)
    def _():
        sum_tokens[b] += back

    @pl.when(expert == pl.num_programs(0) - 1)
    def _():
        partial[b][...] = sum_tokens[b].astype(bf16)


def hidden_kernel(count, slots, place, *refs):
    blocks, w_gate, w_up = refs[:count], refs[count], refs[count + 1]
    rows, activated, gate_pre, up_pre = refs[-4:]
    for b, span in spans_of(count, slots):
        choice = slot_choice(place[0, b], slots).astype(bf16)
        rows[0, 0, span] = mm(choice, blocks[b][...], ((1,), (0,))).astype(bf16)
    rows_in = rows[0, 0]
    g = mm(rows_in, w_gate[0], ((1,), (0,)))
    u = mm(rows_in, w_up[0], ((1,), (0,)))
    gate_pre[0], up_pre[0] = g.astype(bf16), u.astype(bf16)
    activated[0, 0] = (g * jax.nn.sigmoid(g) * u).astype(bf16)


def out_kernel(count, slots, place, gate, activated, w_down, *refs):
    partial, sum_tokens = refs[:-1], refs[-1]
    result = mm(activated[0, 0], w_down[0], ((1,), (1,)))
    for b, span in spans_of(count, slots):
        out = (result[span] * slot_weight(place[0, b], gate[0, b], slots)).astype(bf16)
        add_tokens(place, b, slots, out, sum_tokens, partial)


def expert_back_kernel(count, slots, place, gate, *refs):
    blocks, (w_gate, w_up, w_down) = refs[:count], refs[count : count + 3]
    gate_pre, up_pre = refs[count + 3 : count + 5]
    grad_rows, grad_gate, grad_up = refs[-4 - count : -1 - count]
    partial, sum_tokens = refs[-1 - count : -1], refs[-1]
    for b, span in spans_of(count, slots):
        choice = slot_choice(place[0, b], slots).astype(bf16)
        weight = slot_weight(place[0, b], gate[0, b], slots)
        picked = mm(choice, blocks[b][...], ((1,), (0,)))
        grad_rows[0, 0, span] = (picked * weight).astype(bf16)
    grad_act = mm(grad_rows[0, 0], w_down[0], ((1,), (0,)))
    g, u = gate_pre[0].astype(f32), up_pre[0].astype(f32)
    sigmoid = jax.nn.sigmoid(g)
    dg = (grad_act * u * sigmoid * (1.0 + g * (1.0 - sigmoid))).astype(bf16)
    du = (grad_act * g * sigmoid).astype(bf16)
    grad_gate[0, 0], grad_up[0, 0] = dg, du
    result = mm(dg, w_gate[0], ((1,), (1,))) + mm(du, w_up[0], ((1,), (1,)))
    result = result.astype(bf16)
    for b, span in spans_of(count, slots):
        add_tokens(place, b, slots, result[span], sum_tokens, partial)


class Experts:
    def __init__(self, group, slots, place, gate, blocks, weights):
        self.group, self.slots, self.place, self.gate = group, slots, place, gate
        self.experts, self.width, self.hidden = weights[0].shape
        self.count, self.own = len(blocks), blocks[0].shape[0]
        self.rows = self.count * slots
        group_of = lambda e: (e, group, 0, 0)
        self.table = pl.BlockSpec((1, self.count, 1, self.own), group_of)
        self.tokens = pl.BlockSpec((self.own, self.width), lambda e: (0, 0))
        self.weight = pl.BlockSpec((1, self.width, self.hidden), lambda e: (e, 0, 0))
        self.local = pl.BlockSpec((1, self.rows, self.hidden), lambda e: (e, 0, 0))
        self.wide = pl.BlockSpec((1, 1, self.rows, self.width), group_of)
        self.narrow = pl.BlockSpec((1, 1, self.rows, self.hidden), group_of)
        self.sums = pltpu.VMEM((self.count, self.own, self.width), f32)

    def shape(self, spec):
        rows, experts = self.rows, self.experts
        shapes = [
            (self.tokens, (self.own, self.width)),
            (self.local, (experts, rows, self.hidden)),
            (self.wide, (experts, 2, rows, self.width)),
            (self.narrow, (experts, 2, rows, self.hidden)),
        ]
        [shape] = [shape for known, shape in shapes if known is spec]
        return jax.ShapeDtypeStruct(shape, bf16)

    def run(self, kernel, ins, outs, scratch, prior=()):
        specs = [spec for spec, _ in ins] + [pl.BlockSpec(memory_space=pl.ANY)] * len(prior)
        return pl.pallas_call(
            functools.partial(kernel, self.count, self.slots),
            grid=(self.experts,),
            in_specs=specs,
            out_specs=outs,
            out_shape=[self.shape(spec) for spec in outs],
            scratch_shapes=scratch,
            input_output_aliases={len(ins) + i: i for i in range(len(prior))},
            compiler_params=pltpu.CompilerParams(vmem_limit_bytes=58 * 2**20),
            cost_estimate=pl.CostEstimate(
                flops=self.experts * self.rows * self.width * self.hidden * 4,
                bytes_accessed=self.experts * self.width * self.hidden * 6,
                transcendentals=self.experts * self.rows * self.hidden,
            ),
        )(*[array for _, array in ins], *prior)

    def to_hidden(self, blocks, w_gate, w_up, prior):
        ins = [(self.table, self.place)] + [(self.tokens, block) for block in blocks]
        ins += [(self.weight, w_gate), (self.weight, w_up)]
        outs = [self.wide, self.narrow, self.local, self.local]
        return self.run(hidden_kernel, ins, outs, [], prior)

    def to_tokens(self, activated, w_down):
        ins = [(self.table, self.place), (self.table, self.gate)]
        ins += [(self.narrow, activated), (self.weight, w_down)]
        return self.run(out_kernel, ins, [self.tokens] * self.count, [self.sums])

    def backward(self, blocks, weights, pres, prior):
        ins = [(self.table, self.place), (self.table, self.gate)]
        ins += [(self.tokens, block) for block in blocks]
        ins += [(self.weight, weight) for weight in weights]
        ins += [(self.local, pre) for pre in pres]
        outs = [self.wide, self.narrow, self.narrow] + [self.tokens] * self.count
        return self.run(expert_back_kernel, ins, outs, [self.sums], prior)


def dot(spec, left, right):
    return jnp.einsum(spec, left, right, preferred_element_type=f32)


def shards(
    tokens,
    w_attn,
    norm_gains,
    w_expert,
    gate_weights,
    routes,
    segment,
    valid_mask,
    teacher,
    cotangent,
):
    outer, planes, seqs = lax.axis_size("o"), lax.axis_size("z"), lax.axis_size("s")
    plane, rank = lax.axis_index("z"), lax.axis_index("s")
    own, width = tokens.shape
    rows_dev = w_attn.shape[0]
    seq = own * seqs
    heads = H // seqs
    cols = heads * HD
    hidden = w_expert.shape[2] // 3
    part = w_expert.shape[0]
    capacity = own * TOP * 17 // (16 * planes * seqs)
    scale = HD ** (-0.5)

    def to_inner(v):
        lead = v.shape[:-1]
        v = v.reshape(lead + (outer * planes, CORES, part))
        return jnp.swapaxes(v, -3, -2).reshape(lead + (width,))

    def to_outer(v):
        lead = v.shape[:-1]
        v = v.reshape(lead + (CORES, outer * planes, part))
        return jnp.swapaxes(v, -3, -2).reshape(lead + (width,))

    first_core = lax.axis_index("c") == 0

    def halves(v):
        low, high = v[..., : width // 2], v[..., width // 2 :]
        return jnp.where(first_core, low, high), jnp.where(first_core, high, low)

    def whole_of(mine, other, axis):
        low, high = jnp.where(first_core, mine, other), jnp.where(first_core, other, mine)
        return jnp.concatenate([low, high], axis=axis)

    def stack_rows(blocks, start=0):
        rows = in_order(blocks, "z", start)
        return collect(rows, "o").reshape((width // 2,) + rows.shape[2:])

    def sum_cores(grad):
        count = grad.shape[1]
        grad = exchange_sum(grad.reshape(CORES, width // 2, count), "c")
        if outer > 1:
            grad = exchange_sum(grad.astype(bf16).reshape(outer, planes * part, count), "o")
        return grad

    def gather_sum(value):
        for axis in ("z", "s", "c", "o"):
            value = sum(gather_near(jnp.broadcast_to(value, (8, PAD)), axis))[0, 0]
        return value

    by_expert = lax.optimization_barrier(w_expert.transpose(1, 0, 2))

    def expert_chunk(i, start=0):
        def piece_for(owner):
            return lax.dynamic_slice(by_expert, (owner, 0, i * hidden), (1, part, hidden))[0]

        return exchange(piece_for, "z", start)

    def gather_plane(ready):
        chunk = ready.reshape(planes * part, hidden)
        chunk = lax.all_gather(chunk, ("s", "c", "o"), axis=0, tiled=True)
        return chunk.reshape(seqs, width, hidden)

    count = jnp.sum(valid_mask).astype(jnp.int32)
    digits = jnp.stack([count // 128, count % 128]).astype(bf16)
    extra = jnp.concatenate(
        [
            norm_gains,
            jnp.broadcast_to(digits[None], (rows_dev, 2)),
            jnp.zeros((rows_dev, PAD - 6), bf16),
        ],
        axis=1,
    )

    routed = jnp.stack(
        gather_near(jnp.concatenate([routes.astype(f32), gate_weights], axis=1), "z")
    )
    route_all, gate_all = routed[..., :TOP].astype(jnp.int32), routed[..., TOP:]
    expert_ids = jnp.arange(seqs) * planes + plane
    match = route_all[:, :, None, :] == expert_ids[None, None, :, None]
    used = jnp.any(match, axis=-1)
    gate_of = jnp.sum(jnp.where(match, gate_all[:, :, None, :], 0.0), axis=-1)
    before = (jnp.arange(own)[:, None] > jnp.arange(own)[None, :]).astype(bf16)
    place = dot("tu,buk->btk", before, used.astype(bf16)).astype(jnp.int32)
    place = jnp.where(used, place, -1)
    slots = -(-capacity // 16) * 16
    place = place.transpose(2, 0, 1)[:, :, None, :]
    gate_of = gate_of.transpose(2, 0, 1)[:, :, None, :]

    groups = [[k for k in range(planes) if k % 2 == odd] for odd in range(2)]

    def by_group(table):
        return jnp.concatenate([table[:, k : k + 1] for group in groups for k in group], axis=1)

    place, gate_of = by_group(place), by_group(gate_of)

    inputs = to_inner(tokens)
    column_rows, extra_rows = rows_dev * 4 * cols // width, rows_dev * PAD // width
    extra = jnp.pad(extra.reshape(extra_rows, width), ((0, -extra_rows % 8), (0, 0)))

    def message_to(owner):
        picked = [
            lax.dynamic_slice_in_dim(w_attn, i * width + owner * cols, cols, 1) for i in range(4)
        ]
        picked = jnp.concatenate(picked, axis=1).reshape(column_rows, width)
        return jnp.concatenate([inputs, picked, extra], axis=0)

    messages = exchange(message_to, "s")
    gate_blocks = expert_chunk(0)
    up_blocks = expert_chunk(1, token(*gate_blocks))
    last = own + column_rows
    columns = [
        jnp.concatenate(
            [
                message[own:last].reshape(rows_dev, 4 * cols),
                message[last : last + extra_rows].reshape(rows_dev, PAD),
            ],
            axis=1,
        )
        for message in messages
    ]
    mine = in_order(columns, "s").reshape(part, 4 * cols + PAD)
    seq_tokens = in_order([message[:own] for message in messages], "s")
    seq_tokens = seq_tokens.reshape(seq, width).astype(f32)
    inputs = inputs.astype(f32)
    gate_ready = in_order(gate_blocks, "z", token(mine))
    w_gate = gather_plane(gate_ready)
    up_ready = in_order(up_blocks, "z", token(seq_tokens, place, gate_of))
    w_up = gather_plane(up_ready)
    in_blocks = gather_near(after(mine, up_ready), "z")
    seq_factor = rms_factor(seq_tokens)
    w_in = stack_rows(in_blocks, token(seq_factor, w_gate))
    w_in_other = send(w_in, "c", 1)
    down_blocks = expert_chunk(2, token(w_in))

    side = whole_of(w_in[:, 4 * cols :], w_in_other[:, 4 * cols :], 0)[:, :6].astype(f32).T
    gain_in, gain_mid = side[0], side[1]
    gain_q = lax.dynamic_slice_in_dim(to_outer(side[2]), rank * cols, cols, 0)
    gain_k = lax.dynamic_slice_in_dim(to_outer(side[3]), rank * cols, cols, 0)
    total_count = jnp.sum(side[4, ::rows_dev]) * 128.0 + jnp.sum(side[5, ::rows_dev])


    def near_planes(block):
        near = [block] + [None] * (planes - 1)
        for k in groups[0][1:]:
            near[k] = send(block, "z", k)
        later = after(block, *[near[k] for k in groups[0][1:]])
        for k in groups[1]:
            near[k] = send(later, "z", k)
        return [[near[k] for k in group] for group in groups]

    def send_back(first, second):
        got = [first[0]] + [send(first[i], "z", k) for i, k in enumerate(groups[0]) if k]
        base = after(total(got), second[0])
        second = [after(part, base) for part in second]
        return second[0], [base] + [send(second[i], "z", k) for i, k in enumerate(groups[1])]

    def total(pieces):
        return sum(piece.astype(f32) for piece in pieces)

    normed_in = (seq_tokens * seq_factor * gain_in).astype(bf16)
    normed_mine, normed_other = halves(normed_in)
    w_qkv, w_qkv_other = w_in[:, : 3 * cols], w_in_other[:, : 3 * cols]
    w_out = whole_of(w_in[:, 3 * cols : 4 * cols], w_in_other[:, 3 * cols : 4 * cols], 0)
    projected = jnp.dot(normed_mine, w_qkv, preferred_element_type=f32) + jnp.dot(
        normed_other, w_qkv_other, preferred_element_type=f32
    )
    query_raw = projected[:, :cols]
    key_raw = projected[:, cols : 2 * cols]

    def over_heads(first, second, *others):
        pairs = gather_near(jnp.stack([first, second]), "s")
        if others:
            pairs[0] = after(pairs[0], *others)
        pair = sum(pairs) / width
        return pair[0][:, None], pair[1][:, None]

    q_mean, k_mean = over_heads(
        jnp.sum(query_raw * query_raw, axis=-1), jnp.sum(key_raw * key_raw, axis=-1)
    )
    down_ready = in_order(down_blocks, "z", token(projected))
    w_down = gather_plane(down_ready)
    cosine, sine = rope_tables(seq)
    shared = [
        after(q_mean, w_out, down_ready),
        k_mean,
        gain_q[None],
        gain_k[None],
        cosine,
        sine,
        segment[:, None],
        segment[None],
    ]
    attended, query, keyed, valued, log_total = attend(projected, shared, heads)
    attn_out = dot("tc,dc->td", attended, w_out).astype(bf16)
    got = exchange_sum(attn_out.reshape(seqs, own, width), "s")
    residual = inputs + got

    normed_mid = (residual * rms_factor(residual) * gain_mid).astype(bf16)
    expert_weights = (w_gate, w_up, w_down)
    blocks = near_planes(normed_mid)
    work = [Experts(i, slots, place, gate_of, blocks[i], expert_weights) for i in range(2)]
    rows_in, activated, *pres = work[0].to_hidden(blocks[0], w_gate, w_up, ())
    first = work[0].to_tokens(activated, w_down)
    pres = [pres]
    blocks[1][0] = after(blocks[1][0], first[0])
    rows_in, activated, *last = work[1].to_hidden(
        blocks[1], w_gate, w_up, (rows_in, activated)
    )
    pres.append(last)
    second = work[1].to_tokens(activated, w_down)
    final_out = residual + total(send_back(first, second)[1])
    rows_in, activated = [v.reshape(seqs, -1, v.shape[-1]) for v in (rows_in, activated)]

    w_out_all = lax.all_gather(after(w_out, w_up), "s", axis=0)
    valid_f = valid_mask.astype(f32)[:, None]
    difference = final_out - to_inner(teacher).astype(f32)
    squared = jnp.sum(valid_f * difference * difference)
    grad_out = (
        to_inner(cotangent).astype(f32) + 2.0 / (total_count * width) * valid_f * difference
    )

    def scatter_expert(grad):
        grad = grad.reshape(seqs * width, hidden)
        grad = lax.psum_scatter(grad, ("s", "c", "o"), scatter_dimension=0, tiled=True)
        return grad.reshape(planes, part, hidden)

    blocks = near_planes(grad_out.astype(bf16))
    *grads, first, last = work[0].backward(blocks[0], expert_weights, pres[0], ())
    partial = [(first, last)]
    blocks[1][0] = after(blocks[1][0], first)
    *grads, first, last = work[1].backward(blocks[1], expert_weights, pres[1], grads)
    partial.append((first, last))
    back_last, back_pieces = send_back(*partial)
    grad_rows, grad_gate, grad_up = [v.reshape(seqs, -1, v.shape[-1]) for v in grads]
    grad_w_down = dot("krd,krf->kdf", grad_rows, after(activated, back_last)).astype(bf16)
    back_pieces[0] = after(back_pieces[0], grad_w_down)
    grad_mid = total(back_pieces)
    grad_w_gate = dot("krd,krf->kdf", rows_in, after(grad_gate, grad_mid)).astype(bf16)
    grad_resid_norm, gain_mid_grad = norm_back(residual, gain_mid, grad_mid)
    grad_resid = grad_out + grad_resid_norm

    grad_low = grad_resid.astype(bf16)
    grad_heads = dot("td,sdc->stc", grad_low, w_out_all).astype(bf16)
    head_blocks = exchange(
        lambda i: lax.dynamic_index_in_dim(grad_heads, i, 0, keepdims=False), "s"
    )
    grad_heads = in_order(head_blocks, "s", token(grad_w_gate)).reshape(seq, cols)
    grad_w_up = dot("krd,krf->kdf", rows_in, after(grad_up, grad_heads)).astype(bf16)
    up_done = grad_w_up
    grad_w_down, grad_w_gate, grad_w_up = [
        scatter_expert(grad) for grad in (grad_w_down, grad_w_gate, grad_w_up)
    ]
    low_blocks = gather_near(after(grad_low, grad_heads), "s")
    down_ready = swap(grad_w_down, "z")
    grad_q, grad_k, grad_v, q_inner, k_inner, gain_q_grad, gain_k_grad = attend_back(
        projected, shared, query, keyed, valued, after(grad_heads, up_done), log_total, heads
    )
    grad_attn_out = in_order(low_blocks, "s", token(grad_q)).reshape(seq, width)
    down_ready = after(down_ready, grad_q)
    q_inner = after(q_inner, down_ready, grad_attn_out)
    grad_w_out = dot("td,tc->dc", grad_attn_out, attended).astype(bf16)
    q_inner, k_inner = over_heads(q_inner[:, 0], k_inner[:, 0], grad_w_out)

    def norm_grad(grad, raw, mean, inner):
        factor = lax.rsqrt(mean + epsilon)
        return (factor * (grad - raw * factor * inner)).astype(bf16)

    grad_proj = jnp.concatenate(
        [
            norm_grad(grad_q, query_raw, q_mean, q_inner),
            norm_grad(grad_k, key_raw, k_mean, k_inner),
            grad_v,
        ],
        axis=1,
    )

    grad_w_qkv = dot("td,tc->dc", normed_in, grad_proj).astype(bf16)
    summed = jnp.concatenate([sum_cores(grad_w_qkv), sum_cores(grad_w_out)], axis=1)
    summed = summed.astype(bf16).reshape(planes, part, 4 * cols)
    gate_ready = swap(grad_w_gate, "z")
    late_proj = after(grad_proj, summed)
    grad_normed = jnp.concatenate(
        [dot("tc,dc->td", late_proj, weight).astype(bf16) for weight in (w_qkv, w_qkv_other)],
        axis=1,
    )
    grad_normed = exchange_sum(grad_normed.reshape(seqs, own, width), "s")
    grad_normed = whole_of(grad_normed[:, : width // 2], grad_normed[:, width // 2 :], 1)
    grad_attn = after(exchange_sum(summed, "z"), gate_ready).astype(bf16)
    up_ready = swap(after(grad_w_up, grad_attn), "z")
    grad_in_norm, gain_in_grad = norm_back(inputs, gain_in, grad_normed)
    grad_tokens = to_outer(grad_resid + grad_in_norm)

    def widen(local):
        full = jnp.zeros((width,), f32)
        return to_inner(lax.dynamic_update_slice_in_dim(full, local, rank * cols, 0))

    gains = jnp.stack([gain_in_grad, gain_mid_grad, widen(gain_q_grad[0]), widen(gain_k_grad[0])])
    gains = after(gains, grad_attn)
    loss_value = gather_sum(after(squared, grad_attn)) / (total_count * width)
    for axis in ("z", "c", "s", "o"):
        gains = sum(gather_near(gains, axis))
    row = (lax.axis_index(("c", "o", "z")) * seqs + rank) * rows_dev
    grad_gains = lax.dynamic_slice_in_dim(gains, row, rows_dev, 1).T

    got = exchange_by_rank(grad_attn.reshape(seqs, rows_dev, 4 * cols), "s")
    got = in_order(got, "s").astype(f32)
    grad_attn = jnp.concatenate(
        [got[s, :, i * cols : (i + 1) * cols] for i in range(4) for s in range(seqs)], axis=1
    )
    grad_expert = jnp.concatenate([gate_ready, up_ready, down_ready], axis=2)
    grad_expert = grad_expert.astype(f32).transpose(1, 0, 2)
    return (
        to_outer(final_out).astype(bf16),
        loss_value,
        grad_tokens,
        grad_attn,
        grad_gains,
        grad_expert,
    )


def solution(mesh):
    fsdp, seqs = mesh.shape["fsdp"], mesh.shape["sp"]

    def whole(*arrays):
        planes = arrays[3].shape[1] // seqs
        outer = fsdp // (planes * CORES)
        inner = Mesh(mesh.devices.reshape(outer, planes, CORES, seqs), ("o", "z", "c", "s"))
        every = ("o", "z", "c", "s")
        rows = P(every, None)
        experts = P(("o", "z", "c"), "s", None)
        return jax.shard_map(
            shards,
            mesh=inner,
            in_specs=(
                rows,
                rows,
                rows,
                experts,
                rows,
                rows,
                P(("o", "z", "c")),
                P(every),
                rows,
                rows,
            ),
            out_specs=(rows, P(), rows, rows, rows, experts),
            check_vma=False,
        )(*arrays)

    return whole
```

```python
import functools

import jax
import jax.numpy as jnp
from jax import lax
from jax.experimental import pallas as pl
from jax.experimental.pallas import tpu as pltpu
from jax.sharding import Mesh, PartitionSpec as P

H = 16
HD = 128
TOP = 8
CORES = 2
PAD = 128

epsilon = 1e-05
masked = -1e30
f32 = jnp.float32
bf16 = jnp.bfloat16


def send(block, axis, step):
    size = lax.axis_size(axis)
    return lax.ppermute(block, axis, [(i, i ^ step) for i in range(size)])


def gather_near(block, axis):
    return [block] + [send(block, axis, k) for k in range(1, lax.axis_size(axis))]


def in_order(blocks, axis, start=0):
    rank = lax.axis_index(axis)
    if len(blocks) == 1:
        return blocks[0][None]
    stacked = jnp.zeros((len(blocks),) + blocks[0].shape, blocks[0].dtype)
    for k, block in enumerate(blocks):
        stacked = lax.dynamic_update_index_in_dim(stacked, block, (rank ^ k) + start, 0)
    return stacked


def collect(block, axis):
    return in_order(gather_near(block, axis), axis)


def exchange(piece_for, axis, start=0):
    rank, size = lax.axis_index(axis) + start, lax.axis_size(axis)
    return [piece_for(rank)] + [send(piece_for(rank ^ k), axis, k) for k in range(1, size)]


def swap(pieces, axis):
    return lax.all_to_all(pieces, axis, split_axis=0, concat_axis=0, tiled=True)


def exchange_by_rank(pieces, axis):
    return exchange(lambda i: lax.dynamic_index_in_dim(pieces, i, 0, keepdims=False), axis)


def exchange_sum(pieces, axis):
    got = exchange_by_rank(pieces, axis)
    return sum(piece.astype(f32) for piece in got)


def token(*values):
    firsts = [value[(slice(0, 1),) * value.ndim].reshape(()).astype(f32) for value in values]
    total = sum(firsts)
    return (total != total).astype(jnp.int32)


def after(value, *others):
    return value + token(*others).astype(value.dtype)


def rms_factor(values):
    return lax.rsqrt(jnp.mean(values * values, axis=-1, keepdims=True) + epsilon)


def norm_back(values, gain_vec, grad_in):
    factor = rms_factor(values)
    normed = values * factor
    gain_grad = jnp.sum(grad_in * normed, axis=0)
    inner = grad_in * gain_vec
    grad = factor * (inner - normed * jnp.mean(inner * normed, axis=-1, keepdims=True))
    return grad, gain_grad


def rope_tables(rows):
    inverse = 10000.0 ** (-(jnp.arange(HD // 2).astype(f32) * 2.0 / HD))
    angles = jnp.arange(rows).astype(f32)[:, None] * inverse[None, :]
    cosine = jnp.concatenate([jnp.cos(angles), jnp.cos(angles)], axis=-1)
    sine = jnp.concatenate([-jnp.sin(angles), jnp.sin(angles)], axis=-1)
    return cosine, sine


def mm(left, right, dims):
    return lax.dot_general(left, right, (dims, ((), ())), preferred_element_type=f32)


def masked_scores(query, keyed, seg_col, seg_row, first, scale):
    scores = mm(query, keyed, ((1,), (1,))) * scale
    rows = first + lax.broadcasted_iota(jnp.int32, scores.shape, 0)
    allowed = (rows >= lax.broadcasted_iota(jnp.int32, scores.shape, 1)) & (seg_col == seg_row)
    return jnp.where(allowed, scores, masked)


def attend_kernel(
    block,
    q_raw,
    k_raw,
    v_raw,
    q_mean,
    k_mean,
    gain_q,
    gain_k,
    cosine,
    sine,
    seg_col,
    seg_row,
    out,
    q_out,
    k_out,
    v_out,
    log_total,
):
    def rope(raw, mean, gain):
        values = raw[...] * lax.rsqrt(mean[...] + epsilon) * gain[...]
        turned = pltpu.roll(values, HD // 2, 1)
        return (values * cosine[...] + turned * sine[...]).astype(bf16)

    q_out[...] = rope(q_raw, q_mean, gain_q)
    k_out[...] = rope(k_raw, k_mean, gain_k)
    v_out[...] = v_raw[...].astype(bf16)
    for first in range(0, out.shape[0], block):
        last = first + block
        scores = masked_scores(
            q_out[first:last],
            k_out[:last],
            seg_col[first:last],
            seg_row[:, :last],
            first,
            HD**-0.5,
        )
        top = jnp.max(scores, axis=-1, keepdims=True)
        exps = jnp.exp(scores - top)
        total = jnp.sum(exps, axis=-1, keepdims=True)
        weights = (exps * (1.0 / total)).astype(bf16)
        out[first:last] = mm(weights, v_out[:last], ((1,), (0,))).astype(bf16)
        log_total[0, first:last] = top + jnp.log(total)


def attend_back_kernel(
    block,
    q_raw,
    k_raw,
    q_mean,
    k_mean,
    gain_q,
    gain_k,
    cosine,
    sine,
    seg_col,
    seg_row,
    query,
    keyed,
    valued,
    grad,
    log_total,
    grad_q,
    grad_k,
    grad_v,
    q_inner,
    k_inner,
    gain_q_grad,
    gain_k_grad,
    sum_q,
    sum_k,
    sum_v,
):
    scale = HD**-0.5
    sum_k[...] = jnp.zeros_like(sum_k)
    sum_v[...] = jnp.zeros_like(sum_v)
    for first in range(0, query.shape[0], block):
        last = first + block
        q_block, g_block = query[first:last], grad[first:last]
        scores = masked_scores(
            q_block, keyed[:last], seg_col[first:last], seg_row[:, :last], first, scale
        )
        probs = jnp.exp(scores - log_total[0, first:last])
        sum_v[:last] += mm(probs.astype(bf16), g_block, ((0,), (0,)))
        grad_probs = mm(g_block, valued[:last], ((1,), (1,)))
        inner = jnp.sum(probs * grad_probs, axis=-1, keepdims=True)
        grad_scores = (probs * (grad_probs - inner)).astype(bf16)
        sum_q[first:last] = mm(grad_scores, keyed[:last], ((1,), (0,))) * scale
        sum_k[:last] += mm(grad_scores, q_block, ((0,), (0,))) * scale
    grad_v[...] = sum_v[...].astype(bf16)

    def undo(total, raw, mean, gain, inner_out, gain_out, grad_out):
        low = total[...].astype(bf16).astype(f32)
        back = low * cosine[...] + pltpu.roll(low * sine[...], HD // 2, 1)
        normed = raw[...] * lax.rsqrt(mean[...] + epsilon)
        gain_out[...] = jnp.sum(back * normed, axis=0, keepdims=True)
        back = back * gain[...]
        grad_out[...] = back
        inner = jnp.sum(back * normed, axis=-1, keepdims=True)

        @pl.when(pl.program_id(0) == 0)
        def _():
            inner_out[...] = inner

        @pl.when(pl.program_id(0) > 0)
        def _():
            inner_out[...] += inner

    undo(sum_q, q_raw, q_mean, gain_q, q_inner, gain_q_grad, grad_q)
    undo(sum_k, k_raw, k_mean, gain_k, k_inner, gain_k_grad, grad_k)


def head_specs(seq, heads):
    column = pl.BlockSpec((seq, 1), lambda h: (0, 0))
    gain = pl.BlockSpec((1, HD), lambda h: (0, h))
    table = pl.BlockSpec((seq, HD), lambda h: (0, 0))
    return [column, column, gain, gain, table, table, column, pl.BlockSpec((1, seq), lambda h: (0, 0))]


def raw_spec(seq, heads, which):
    return pl.BlockSpec((seq, HD), lambda h: (0, which * heads + h))


def attend(projected, shared, heads):
    seq = projected.shape[0]
    block = min(256, seq)
    head = pl.BlockSpec((seq, HD), lambda h: (0, h))
    low = jax.ShapeDtypeStruct((seq, heads * HD), bf16)
    return pl.pallas_call(
        functools.partial(attend_kernel, block),
        grid=(heads,),
        in_specs=[raw_spec(seq, heads, i) for i in range(3)] + head_specs(seq, heads),
        out_specs=[head] * 4 + [pl.BlockSpec((1, seq, 1), lambda h: (h, 0, 0))],
        out_shape=[low] * 4 + [jax.ShapeDtypeStruct((heads, seq, 1), f32)],
        compiler_params=pltpu.CompilerParams(vmem_limit_bytes=48 * 2**20),
        cost_estimate=pl.CostEstimate(flops=10**6, bytes_accessed=10**5, transcendentals=0),
    )(projected, projected, projected, *shared)


def attend_back(projected, shared, query, keyed, valued, grad, log_total, heads):
    seq = projected.shape[0]
    block = min(256, seq)
    head = pl.BlockSpec((seq, HD), lambda h: (0, h))
    column = pl.BlockSpec((seq, 1), lambda h: (0, 0))
    gain = pl.BlockSpec((1, HD), lambda h: (0, h))
    wide = jax.ShapeDtypeStruct((seq, heads * HD), f32)
    return pl.pallas_call(
        functools.partial(attend_back_kernel, block),
        grid=(heads,),
        in_specs=[raw_spec(seq, heads, i) for i in range(2)]
        + head_specs(seq, heads)
        + [head] * 4
        + [pl.BlockSpec((1, seq, 1), lambda h: (h, 0, 0))],
        out_specs=[head] * 3 + [column] * 2 + [gain] * 2,
        out_shape=[wide, wide, jax.ShapeDtypeStruct((seq, heads * HD), bf16)]
        + [jax.ShapeDtypeStruct((seq, 1), f32)] * 2
        + [jax.ShapeDtypeStruct((1, heads * HD), f32)] * 2,
        scratch_shapes=[pltpu.VMEM((seq, HD), f32)] * 3,
        compiler_params=pltpu.CompilerParams(vmem_limit_bytes=48 * 2**20),
        cost_estimate=pl.CostEstimate(flops=10**6, bytes_accessed=10**5, transcendentals=0),
    )(projected, projected, *shared, query, keyed, valued, grad, log_total)


def slot_choice(place, slots):
    return lax.broadcasted_iota(jnp.int32, (slots, place.shape[1]), 0) == place


def slot_weight(place, gate, slots):
    return jnp.sum(jnp.where(slot_choice(place, slots), gate, 0.0), axis=1, keepdims=True)


def spans_of(count, slots):
    return [(b, slice(b * slots, (b + 1) * slots)) for b in range(count)]


def add_tokens(place, b, slots, out, sum_tokens, partial):
    expert = pl.program_id(0)
    back = mm(slot_choice(place[0, b], slots).astype(bf16), out, ((0,), (0,)))

    @pl.when(expert == 0)
    def _():
        sum_tokens[b] = back

    @pl.when(expert > 0)
    def _():
        sum_tokens[b] += back

    @pl.when(expert == pl.num_programs(0) - 1)
    def _():
        partial[b][...] = sum_tokens[b].astype(bf16)


def hidden_kernel(count, slots, place, *refs):
    blocks, w_gate, w_up = refs[:count], refs[count], refs[count + 1]
    rows, activated, gate_pre, up_pre = refs[-4:]
    for b, span in spans_of(count, slots):
        choice = slot_choice(place[0, b], slots).astype(bf16)
        rows[0, 0, span] = mm(choice, blocks[b][...], ((1,), (0,))).astype(bf16)
    rows_in = rows[0, 0]
    g = mm(rows_in, w_gate[0], ((1,), (0,)))
    u = mm(rows_in, w_up[0], ((1,), (0,)))
    gate_pre[0], up_pre[0] = g.astype(bf16), u.astype(bf16)
    activated[0, 0] = (g * jax.nn.sigmoid(g) * u).astype(bf16)


def out_kernel(count, slots, place, gate, activated, w_down, *refs):
    partial, sum_tokens = refs[:-1], refs[-1]
    result = mm(activated[0, 0], w_down[0], ((1,), (1,)))
    for b, span in spans_of(count, slots):
        out = (result[span] * slot_weight(place[0, b], gate[0, b], slots)).astype(bf16)
        add_tokens(place, b, slots, out, sum_tokens, partial)


def expert_back_kernel(count, slots, place, gate, *refs):
    blocks, (w_gate, w_up, w_down) = refs[:count], refs[count : count + 3]
    gate_pre, up_pre = refs[count + 3 : count + 5]
    grad_rows, grad_gate, grad_up = refs[-4 - count : -1 - count]
    partial, sum_tokens = refs[-1 - count : -1], refs[-1]
    for b, span in spans_of(count, slots):
        choice = slot_choice(place[0, b], slots).astype(bf16)
        weight = slot_weight(place[0, b], gate[0, b], slots)
        picked = mm(choice, blocks[b][...], ((1,), (0,)))
        grad_rows[0, 0, span] = (picked * weight).astype(bf16)
    grad_act = mm(grad_rows[0, 0], w_down[0], ((1,), (0,)))
    g, u = gate_pre[0].astype(f32), up_pre[0].astype(f32)
    sigmoid = jax.nn.sigmoid(g)
    dg = (grad_act * u * sigmoid * (1.0 + g * (1.0 - sigmoid))).astype(bf16)
    du = (grad_act * g * sigmoid).astype(bf16)
    grad_gate[0, 0], grad_up[0, 0] = dg, du
    result = mm(dg, w_gate[0], ((1,), (1,))) + mm(du, w_up[0], ((1,), (1,)))
    result = result.astype(bf16)
    for b, span in spans_of(count, slots):
        add_tokens(place, b, slots, result[span], sum_tokens, partial)


class Experts:
    def __init__(self, group, slots, place, gate, blocks, weights):
        self.group, self.slots, self.place, self.gate = group, slots, place, gate
        self.experts, self.width, self.hidden = weights[0].shape
        self.count, self.own = len(blocks), blocks[0].shape[0]
        self.rows = self.count * slots
        group_of = lambda e: (e, group, 0, 0)
        self.table = pl.BlockSpec((1, self.count, 1, self.own), group_of)
        self.tokens = pl.BlockSpec((self.own, self.width), lambda e: (0, 0))
        self.weight = pl.BlockSpec((1, self.width, self.hidden), lambda e: (e, 0, 0))
        self.local = pl.BlockSpec((1, self.rows, self.hidden), lambda e: (e, 0, 0))
        self.wide = pl.BlockSpec((1, 1, self.rows, self.width), group_of)
        self.narrow = pl.BlockSpec((1, 1, self.rows, self.hidden), group_of)
        self.sums = pltpu.VMEM((self.count, self.own, self.width), f32)

    def shape(self, spec):
        rows, experts = self.rows, self.experts
        shapes = [
            (self.tokens, (self.own, self.width)),
            (self.local, (experts, rows, self.hidden)),
            (self.wide, (experts, 2, rows, self.width)),
            (self.narrow, (experts, 2, rows, self.hidden)),
        ]
        [shape] = [shape for known, shape in shapes if known is spec]
        return jax.ShapeDtypeStruct(shape, bf16)

    def run(self, kernel, ins, outs, scratch, prior=()):
        specs = [spec for spec, _ in ins] + [pl.BlockSpec(memory_space=pl.ANY)] * len(prior)
        return pl.pallas_call(
            functools.partial(kernel, self.count, self.slots),
            grid=(self.experts,),
            in_specs=specs,
            out_specs=outs,
            out_shape=[self.shape(spec) for spec in outs],
            scratch_shapes=scratch,
            input_output_aliases={len(ins) + i: i for i in range(len(prior))},
            compiler_params=pltpu.CompilerParams(vmem_limit_bytes=58 * 2**20),
            cost_estimate=pl.CostEstimate(
                flops=self.experts * self.rows * self.width * self.hidden * 4,
                bytes_accessed=self.experts * self.width * self.hidden * 6,
                transcendentals=self.experts * self.rows * self.hidden,
            ),
        )(*[array for _, array in ins], *prior)

    def to_hidden(self, blocks, w_gate, w_up, prior):
        ins = [(self.table, self.place)] + [(self.tokens, block) for block in blocks]
        ins += [(self.weight, w_gate), (self.weight, w_up)]
        outs = [self.wide, self.narrow, self.local, self.local]
        return self.run(hidden_kernel, ins, outs, [], prior)

    def to_tokens(self, activated, w_down):
        ins = [(self.table, self.place), (self.table, self.gate)]
        ins += [(self.narrow, activated), (self.weight, w_down)]
        return self.run(out_kernel, ins, [self.tokens] * self.count, [self.sums])

    def backward(self, blocks, weights, pres, prior):
        ins = [(self.table, self.place), (self.table, self.gate)]
        ins += [(self.tokens, block) for block in blocks]
        ins += [(self.weight, weight) for weight in weights]
        ins += [(self.local, pre) for pre in pres]
        outs = [self.wide, self.narrow, self.narrow] + [self.tokens] * self.count
        return self.run(expert_back_kernel, ins, outs, [self.sums], prior)


def dot(spec, left, right):
    return jnp.einsum(spec, left, right, preferred_element_type=f32)


def shards(
    tokens,
    w_attn,
    norm_gains,
    w_expert,
    gate_weights,
    routes,
    segment,
    valid_mask,
    teacher,
    cotangent,
):
    outer, planes, seqs = lax.axis_size("o"), lax.axis_size("z"), lax.axis_size("s")
    plane, rank = lax.axis_index("z"), lax.axis_index("s")
    own, width = tokens.shape
    rows_dev = w_attn.shape[0]
    seq = own * seqs
    heads = H // seqs
    cols = heads * HD
    hidden = w_expert.shape[2] // 3
    part = w_expert.shape[0]
    capacity = own * TOP * 17 // (16 * planes * seqs)
    scale = HD ** (-0.5)

    def to_inner(v):
        lead = v.shape[:-1]
        v = v.reshape(lead + (outer * planes, CORES, part))
        return jnp.swapaxes(v, -3, -2).reshape(lead + (width,))

    def to_outer(v):
        lead = v.shape[:-1]
        v = v.reshape(lead + (CORES, outer * planes, part))
        return jnp.swapaxes(v, -3, -2).reshape(lead + (width,))

    first_core = lax.axis_index("c") == 0

    def halves(v):
        low, high = v[..., : width // 2], v[..., width // 2 :]
        return jnp.where(first_core, low, high), jnp.where(first_core, high, low)

    def whole_of(mine, other, axis):
        low, high = jnp.where(first_core, mine, other), jnp.where(first_core, other, mine)
        return jnp.concatenate([low, high], axis=axis)

    def stack_rows(blocks, start=0):
        rows = in_order(blocks, "z", start)
        return collect(rows, "o").reshape((width // 2,) + rows.shape[2:])

    def sum_cores(grad):
        count = grad.shape[1]
        grad = exchange_sum(grad.reshape(CORES, width // 2, count), "c")
        if outer > 1:
            grad = exchange_sum(grad.astype(bf16).reshape(outer, planes * part, count), "o")
        return grad

    def gather_sum(value):
        for axis in ("z", "s", "c", "o"):
            value = sum(gather_near(jnp.broadcast_to(value, (8, PAD)), axis))[0, 0]
        return value

    by_expert = lax.optimization_barrier(w_expert.transpose(1, 0, 2))

    def expert_chunk(i, start=0):
        def piece_for(owner):
            return lax.dynamic_slice(by_expert, (owner, 0, i * hidden), (1, part, hidden))[0]

        return exchange(piece_for, "z", start)

    def gather_plane(ready):
        chunk = ready.reshape(planes * part, hidden)
        chunk = lax.all_gather(chunk, ("s", "c", "o"), axis=0, tiled=True)
        return chunk.reshape(seqs, width, hidden)

    count = jnp.sum(valid_mask).astype(jnp.int32)
    digits = jnp.stack([count // 128, count % 128]).astype(bf16)
    extra = jnp.concatenate(
        [
            norm_gains,
            jnp.broadcast_to(digits[None], (rows_dev, 2)),
            jnp.zeros((rows_dev, PAD - 6), bf16),
        ],
        axis=1,
    )

    routed = jnp.stack(
        gather_near(jnp.concatenate([routes.astype(f32), gate_weights], axis=1), "z")
    )
    route_all, gate_all = routed[..., :TOP].astype(jnp.int32), routed[..., TOP:]
    expert_ids = jnp.arange(seqs) * planes + plane
    match = route_all[:, :, None, :] == expert_ids[None, None, :, None]
    used = jnp.any(match, axis=-1)
    gate_of = jnp.sum(jnp.where(match, gate_all[:, :, None, :], 0.0), axis=-1)
    before = (jnp.arange(own)[:, None] > jnp.arange(own)[None, :]).astype(bf16)
    place = dot("tu,buk->btk", before, used.astype(bf16)).astype(jnp.int32)
    place = jnp.where(used, place, -1)
    slots = -(-capacity // 16) * 16
    place = place.transpose(2, 0, 1)[:, :, None, :]
    gate_of = gate_of.transpose(2, 0, 1)[:, :, None, :]

    groups = [[k for k in range(planes) if k % 2 == odd] for odd in range(2)]

    def by_group(table):
        return jnp.concatenate([table[:, k : k + 1] for group in groups for k in group], axis=1)

    place, gate_of = by_group(place), by_group(gate_of)

    inputs = to_inner(tokens)
    column_rows, extra_rows = rows_dev * 4 * cols // width, rows_dev * PAD // width
    extra = jnp.pad(extra.reshape(extra_rows, width), ((0, -extra_rows % 8), (0, 0)))

    def message_to(owner):
        picked = [
            lax.dynamic_slice_in_dim(w_attn, i * width + owner * cols, cols, 1) for i in range(4)
        ]
        picked = jnp.concatenate(picked, axis=1).reshape(column_rows, width)
        return jnp.concatenate([inputs, picked, extra], axis=0)

    messages = exchange(message_to, "s")
    gate_blocks = expert_chunk(0)
    up_blocks = expert_chunk(1, token(*gate_blocks))
    last = own + column_rows
    columns = [
        jnp.concatenate(
            [
                message[own:last].reshape(rows_dev, 4 * cols),
                message[last : last + extra_rows].reshape(rows_dev, PAD),
            ],
            axis=1,
        )
        for message in messages
    ]
    mine = in_order(columns, "s").reshape(part, 4 * cols + PAD)
    seq_tokens = in_order([message[:own] for message in messages], "s")
    seq_tokens = seq_tokens.reshape(seq, width).astype(f32)
    inputs = inputs.astype(f32)
    gate_ready = in_order(gate_blocks, "z", token(mine))
    w_gate = gather_plane(gate_ready)
    up_ready = in_order(up_blocks, "z", token(seq_tokens, place, gate_of))
    w_up = gather_plane(up_ready)
    in_blocks = gather_near(after(mine, up_ready), "z")
    seq_factor = rms_factor(seq_tokens)
    w_in = stack_rows(in_blocks, token(seq_factor))
    w_in_other = send(w_in, "c", 1)

    side = whole_of(w_in[:, 4 * cols :], w_in_other[:, 4 * cols :], 0)[:, :6].astype(f32).T
    gain_in, gain_mid = side[0], side[1]
    gain_q = lax.dynamic_slice_in_dim(to_outer(side[2]), rank * cols, cols, 0)
    gain_k = lax.dynamic_slice_in_dim(to_outer(side[3]), rank * cols, cols, 0)
    total_count = jnp.sum(side[4, ::rows_dev]) * 128.0 + jnp.sum(side[5, ::rows_dev])


    def near_planes(block):
        near = [block] + [None] * (planes - 1)
        for k in groups[0][1:]:
            near[k] = send(block, "z", k)
        later = after(block, *[near[k] for k in groups[0][1:]])
        for k in groups[1]:
            near[k] = send(later, "z", k)
        return [[near[k] for k in group] for group in groups]

    def send_back(first, second):
        got = [first[0]] + [send(first[i], "z", k) for i, k in enumerate(groups[0]) if k]
        base = after(total(got), second[0])
        second = [after(part, base) for part in second]
        return second[0], [base] + [send(second[i], "z", k) for i, k in enumerate(groups[1])]

    def total(pieces):
        return sum(piece.astype(f32) for piece in pieces)

    normed_in = (seq_tokens * seq_factor * gain_in).astype(bf16)
    normed_mine, normed_other = halves(normed_in)
    w_qkv, w_qkv_other = w_in[:, : 3 * cols], w_in_other[:, : 3 * cols]
    w_out = whole_of(w_in[:, 3 * cols : 4 * cols], w_in_other[:, 3 * cols : 4 * cols], 0)
    projected = jnp.dot(normed_mine, w_qkv, preferred_element_type=f32) + jnp.dot(
        normed_other, w_qkv_other, preferred_element_type=f32
    )
    query_raw = projected[:, :cols]
    key_raw = projected[:, cols : 2 * cols]

    def over_heads(first, second, *others):
        pairs = gather_near(jnp.stack([first, second]), "s")
        if others:
            pairs[0] = after(pairs[0], *others)
        pair = sum(pairs) / width
        return pair[0][:, None], pair[1][:, None]

    q_mean, k_mean = over_heads(
        jnp.sum(query_raw * query_raw, axis=-1), jnp.sum(key_raw * key_raw, axis=-1)
    )
    cosine, sine = rope_tables(seq)
    shared = [
        after(q_mean, w_gate, w_out),
        k_mean,
        gain_q[None],
        gain_k[None],
        cosine,
        sine,
        segment[:, None],
        segment[None],
    ]
    attended, query, keyed, valued, log_total = attend(projected, shared, heads)
    start = token(attended)
    down_blocks = exchange(
        lambda owner: lax.dynamic_slice(
            w_expert, (0, owner, 2 * hidden), (part, 1, hidden)
        )[:, 0],
        "z",
        start,
    )
    attn_out = dot("tc,dc->td", attended, w_out).astype(bf16)
    got = exchange_sum(attn_out.reshape(seqs, own, width), "s")
    residual = inputs + got
    down_ready = in_order(down_blocks, "z", token(residual))
    residual = after(residual, down_ready)
    w_down = gather_plane(down_ready)

    normed_mid = (residual * rms_factor(residual) * gain_mid).astype(bf16)
    expert_weights = (w_gate, w_up, w_down)
    blocks = near_planes(normed_mid)
    work = [Experts(i, slots, place, gate_of, blocks[i], expert_weights) for i in range(2)]
    rows_in, activated, *pres = work[0].to_hidden(blocks[0], w_gate, w_up, ())
    first = work[0].to_tokens(activated, w_down)
    pres = [pres]
    blocks[1][0] = after(blocks[1][0], first[0])
    rows_in, activated, *last = work[1].to_hidden(
        blocks[1], w_gate, w_up, (rows_in, activated)
    )
    pres.append(last)
    second = work[1].to_tokens(activated, w_down)
    final_out = residual + total(send_back(first, second)[1])
    rows_in, activated = [v.reshape(seqs, -1, v.shape[-1]) for v in (rows_in, activated)]

    w_out_all = lax.all_gather(after(w_out, w_up), "s", axis=0)
    valid_f = valid_mask.astype(f32)[:, None]
    difference = final_out - to_inner(teacher).astype(f32)
    squared = jnp.sum(valid_f * difference * difference)
    grad_out = (
        to_inner(cotangent).astype(f32) + 2.0 / (total_count * width) * valid_f * difference
    )

    def scatter_expert(grad):
        grad = grad.reshape(seqs * width, hidden)
        grad = lax.psum_scatter(grad, ("s", "c", "o"), scatter_dimension=0, tiled=True)
        return grad.reshape(planes, part, hidden)

    blocks = near_planes(grad_out.astype(bf16))
    *grads, first, last = work[0].backward(blocks[0], expert_weights, pres[0], ())
    partial = [(first, last)]
    blocks[1][0] = after(blocks[1][0], first)
    *grads, first, last = work[1].backward(blocks[1], expert_weights, pres[1], grads)
    partial.append((first, last))
    back_last, back_pieces = send_back(*partial)
    grad_rows, grad_gate, grad_up = [v.reshape(seqs, -1, v.shape[-1]) for v in grads]
    grad_w_down = dot("krd,krf->kdf", grad_rows, after(activated, back_last)).astype(bf16)
    back_pieces[0] = after(back_pieces[0], grad_w_down)
    grad_mid = total(back_pieces)
    grad_w_gate = dot("krd,krf->kdf", rows_in, after(grad_gate, grad_mid)).astype(bf16)
    grad_resid_norm, gain_mid_grad = norm_back(residual, gain_mid, grad_mid)
    grad_resid = grad_out + grad_resid_norm

    grad_low = grad_resid.astype(bf16)
    grad_heads = dot("td,sdc->stc", grad_low, w_out_all).astype(bf16)
    head_blocks = exchange(
        lambda i: lax.dynamic_index_in_dim(grad_heads, i, 0, keepdims=False), "s"
    )
    grad_heads = in_order(head_blocks, "s", token(grad_w_gate)).reshape(seq, cols)
    grad_w_up = dot("krd,krf->kdf", rows_in, after(grad_up, grad_heads)).astype(bf16)
    up_done = grad_w_up
    grad_w_down, grad_w_gate, grad_w_up = [
        scatter_expert(grad) for grad in (grad_w_down, grad_w_gate, grad_w_up)
    ]
    low_blocks = gather_near(after(grad_low, grad_heads), "s")
    down_ready = swap(grad_w_down, "z")
    grad_q, grad_k, grad_v, q_inner, k_inner, gain_q_grad, gain_k_grad = attend_back(
        projected, shared, query, keyed, valued, after(grad_heads, up_done), log_total, heads
    )
    grad_attn_out = in_order(low_blocks, "s", token(grad_q)).reshape(seq, width)
    down_ready = after(down_ready, grad_q)
    q_inner = after(q_inner, down_ready, grad_attn_out)
    grad_w_out = dot("td,tc->dc", grad_attn_out, attended).astype(bf16)
    q_inner, k_inner = over_heads(q_inner[:, 0], k_inner[:, 0], grad_w_out)

    def norm_grad(grad, raw, mean, inner):
        factor = lax.rsqrt(mean + epsilon)
        return (factor * (grad - raw * factor * inner)).astype(bf16)

    grad_proj = jnp.concatenate(
        [
            norm_grad(grad_q, query_raw, q_mean, q_inner),
            norm_grad(grad_k, key_raw, k_mean, k_inner),
            grad_v,
        ],
        axis=1,
    )

    grad_w_qkv = dot("td,tc->dc", normed_in, grad_proj).astype(bf16)
    summed = jnp.concatenate([sum_cores(grad_w_qkv), sum_cores(grad_w_out)], axis=1)
    summed = summed.astype(bf16).reshape(planes, part, 4 * cols)
    gate_ready = swap(grad_w_gate, "z")
    late_proj = after(grad_proj, summed)
    grad_normed = jnp.concatenate(
        [dot("tc,dc->td", late_proj, weight).astype(bf16) for weight in (w_qkv, w_qkv_other)],
        axis=1,
    )
    grad_normed = exchange_sum(grad_normed.reshape(seqs, own, width), "s")
    grad_normed = whole_of(grad_normed[:, : width // 2], grad_normed[:, width // 2 :], 1)
    row_blocks = exchange_by_rank(summed, "z")
    grad_attn = after(total(row_blocks), gate_ready).astype(bf16)
    up_ready = swap(after(grad_w_up, row_blocks[1]), "z")
    grad_in_norm, gain_in_grad = norm_back(inputs, gain_in, grad_normed)
    grad_tokens = to_outer(grad_resid + grad_in_norm)

    def widen(local):
        full = jnp.zeros((width,), f32)
        return to_inner(lax.dynamic_update_slice_in_dim(full, local, rank * cols, 0))

    gains = jnp.stack([gain_in_grad, gain_mid_grad, widen(gain_q_grad[0]), widen(gain_k_grad[0])])
    gains = after(gains, grad_attn)
    loss_value = gather_sum(after(squared, grad_attn)) / (total_count * width)
    for axis in ("z", "c", "s", "o"):
        gains = sum(gather_near(gains, axis))
    row = (lax.axis_index(("c", "o", "z")) * seqs + rank) * rows_dev
    grad_gains = lax.dynamic_slice_in_dim(gains, row, rows_dev, 1).T

    got = exchange_by_rank(grad_attn.reshape(seqs, rows_dev, 4 * cols), "s")
    got = in_order(got, "s").astype(f32)
    grad_attn = jnp.concatenate(
        [got[s, :, i * cols : (i + 1) * cols] for i in range(4) for s in range(seqs)], axis=1
    )
    grad_expert = jnp.concatenate([gate_ready, up_ready, down_ready], axis=2)
    grad_expert = grad_expert.astype(f32).transpose(1, 0, 2)
    return (
        to_outer(final_out).astype(bf16),
        loss_value,
        grad_tokens,
        grad_attn,
        grad_gains,
        grad_expert,
    )


def solution(mesh):
    fsdp, seqs = mesh.shape["fsdp"], mesh.shape["sp"]

    def whole(*arrays):
        planes = arrays[3].shape[1] // seqs
        outer = fsdp // (planes * CORES)
        inner = Mesh(mesh.devices.reshape(outer, planes, CORES, seqs), ("o", "z", "c", "s"))
        every = ("o", "z", "c", "s")
        rows = P(every, None)
        experts = P(("o", "z", "c"), "s", None)
        return jax.shard_map(
            shards,
            mesh=inner,
            in_specs=(
                rows,
                rows,
                rows,
                experts,
                rows,
                rows,
                P(("o", "z", "c")),
                P(every),
                rows,
                rows,
            ),
            out_specs=(rows, P(), rows, rows, rows, experts),
            check_vma=False,
        )(*arrays)

    return whole
```

```python
import functools

import jax
import jax.numpy as jnp
from jax import lax
from jax.experimental import pallas as pl
from jax.experimental.pallas import tpu as pltpu
from jax.sharding import Mesh, PartitionSpec as P

H = 16
HD = 128
TOP = 8
CORES = 2
PAD = 128

epsilon = 1e-05
masked = -1e30
f32 = jnp.float32
bf16 = jnp.bfloat16


def send(block, axis, step):
    size = lax.axis_size(axis)
    return lax.ppermute(block, axis, [(i, i ^ step) for i in range(size)])


def gather_near(block, axis):
    return [block] + [send(block, axis, k) for k in range(1, lax.axis_size(axis))]


def in_order(blocks, axis, start=0):
    rank = lax.axis_index(axis)
    if len(blocks) == 1:
        return blocks[0][None]
    stacked = jnp.zeros((len(blocks),) + blocks[0].shape, blocks[0].dtype)
    for k, block in enumerate(blocks):
        stacked = lax.dynamic_update_index_in_dim(stacked, block, (rank ^ k) + start, 0)
    return stacked


def collect(block, axis):
    return in_order(gather_near(block, axis), axis)


def exchange(piece_for, axis, start=0):
    rank, size = lax.axis_index(axis) + start, lax.axis_size(axis)
    return [piece_for(rank)] + [send(piece_for(rank ^ k), axis, k) for k in range(1, size)]


def swap(pieces, axis):
    return lax.all_to_all(pieces, axis, split_axis=0, concat_axis=0, tiled=True)


def exchange_by_rank(pieces, axis):
    return exchange(lambda i: lax.dynamic_index_in_dim(pieces, i, 0, keepdims=False), axis)


def exchange_sum(pieces, axis):
    got = exchange_by_rank(pieces, axis)
    return sum(piece.astype(f32) for piece in got)


def token(*values):
    firsts = [value[(slice(0, 1),) * value.ndim].reshape(()).astype(f32) for value in values]
    total = sum(firsts)
    return (total != total).astype(jnp.int32)


def after(value, *others):
    return value + token(*others).astype(value.dtype)


def rms_factor(values):
    return lax.rsqrt(jnp.mean(values * values, axis=-1, keepdims=True) + epsilon)


def norm_back(values, gain_vec, grad_in):
    factor = rms_factor(values)
    normed = values * factor
    gain_grad = jnp.sum(grad_in * normed, axis=0)
    inner = grad_in * gain_vec
    grad = factor * (inner - normed * jnp.mean(inner * normed, axis=-1, keepdims=True))
    return grad, gain_grad


def rope_tables(rows):
    inverse = 10000.0 ** (-(jnp.arange(HD // 2).astype(f32) * 2.0 / HD))
    angles = jnp.arange(rows).astype(f32)[:, None] * inverse[None, :]
    cosine = jnp.concatenate([jnp.cos(angles), jnp.cos(angles)], axis=-1)
    sine = jnp.concatenate([-jnp.sin(angles), jnp.sin(angles)], axis=-1)
    return cosine, sine


def mm(left, right, dims):
    return lax.dot_general(left, right, (dims, ((), ())), preferred_element_type=f32)


def masked_scores(query, keyed, seg_col, seg_row, first, scale):
    scores = mm(query, keyed, ((1,), (1,))) * scale
    rows = first + lax.broadcasted_iota(jnp.int32, scores.shape, 0)
    allowed = (rows >= lax.broadcasted_iota(jnp.int32, scores.shape, 1)) & (seg_col == seg_row)
    return jnp.where(allowed, scores, masked)


def attend_kernel(
    block,
    q_raw,
    k_raw,
    v_raw,
    q_mean,
    k_mean,
    gain_q,
    gain_k,
    cosine,
    sine,
    seg_col,
    seg_row,
    out,
    q_out,
    k_out,
    v_out,
    log_total,
):
    def rope(raw, mean, gain):
        values = raw[...] * lax.rsqrt(mean[...] + epsilon) * gain[...]
        turned = pltpu.roll(values, HD // 2, 1)
        return (values * cosine[...] + turned * sine[...]).astype(bf16)

    q_out[...] = rope(q_raw, q_mean, gain_q)
    k_out[...] = rope(k_raw, k_mean, gain_k)
    v_out[...] = v_raw[...].astype(bf16)
    for first in range(0, out.shape[0], block):
        last = first + block
        scores = masked_scores(
            q_out[first:last],
            k_out[:last],
            seg_col[first:last],
            seg_row[:, :last],
            first,
            HD**-0.5,
        )
        top = jnp.max(scores, axis=-1, keepdims=True)
        exps = jnp.exp(scores - top)
        total = jnp.sum(exps, axis=-1, keepdims=True)
        weights = (exps * (1.0 / total)).astype(bf16)
        out[first:last] = mm(weights, v_out[:last], ((1,), (0,))).astype(bf16)
        log_total[0, first:last] = top + jnp.log(total)


def attend_back_kernel(
    block,
    q_raw,
    k_raw,
    q_mean,
    k_mean,
    gain_q,
    gain_k,
    cosine,
    sine,
    seg_col,
    seg_row,
    query,
    keyed,
    valued,
    grad,
    log_total,
    grad_q,
    grad_k,
    grad_v,
    q_inner,
    k_inner,
    gain_q_grad,
    gain_k_grad,
    sum_q,
    sum_k,
    sum_v,
):
    scale = HD**-0.5
    sum_k[...] = jnp.zeros_like(sum_k)
    sum_v[...] = jnp.zeros_like(sum_v)
    for first in range(0, query.shape[0], block):
        last = first + block
        q_block, g_block = query[first:last], grad[first:last]
        scores = masked_scores(
            q_block, keyed[:last], seg_col[first:last], seg_row[:, :last], first, scale
        )
        probs = jnp.exp(scores - log_total[0, first:last])
        sum_v[:last] += mm(probs.astype(bf16), g_block, ((0,), (0,)))
        grad_probs = mm(g_block, valued[:last], ((1,), (1,)))
        inner = jnp.sum(probs * grad_probs, axis=-1, keepdims=True)
        grad_scores = (probs * (grad_probs - inner)).astype(bf16)
        sum_q[first:last] = mm(grad_scores, keyed[:last], ((1,), (0,))) * scale
        sum_k[:last] += mm(grad_scores, q_block, ((0,), (0,))) * scale
    grad_v[...] = sum_v[...].astype(bf16)

    def undo(total, raw, mean, gain, inner_out, gain_out, grad_out):
        low = total[...].astype(bf16).astype(f32)
        back = low * cosine[...] + pltpu.roll(low * sine[...], HD // 2, 1)
        normed = raw[...] * lax.rsqrt(mean[...] + epsilon)
        gain_out[...] = jnp.sum(back * normed, axis=0, keepdims=True)
        back = back * gain[...]
        grad_out[...] = back
        inner = jnp.sum(back * normed, axis=-1, keepdims=True)

        @pl.when(pl.program_id(0) == 0)
        def _():
            inner_out[...] = inner

        @pl.when(pl.program_id(0) > 0)
        def _():
            inner_out[...] += inner

    undo(sum_q, q_raw, q_mean, gain_q, q_inner, gain_q_grad, grad_q)
    undo(sum_k, k_raw, k_mean, gain_k, k_inner, gain_k_grad, grad_k)


def head_specs(seq, heads):
    column = pl.BlockSpec((seq, 1), lambda h: (0, 0))
    gain = pl.BlockSpec((1, HD), lambda h: (0, h))
    table = pl.BlockSpec((seq, HD), lambda h: (0, 0))
    return [column, column, gain, gain, table, table, column, pl.BlockSpec((1, seq), lambda h: (0, 0))]


def raw_spec(seq, heads, which):
    return pl.BlockSpec((seq, HD), lambda h: (0, which * heads + h))


def attend(projected, shared, heads):
    seq = projected.shape[0]
    block = min(256, seq)
    head = pl.BlockSpec((seq, HD), lambda h: (0, h))
    low = jax.ShapeDtypeStruct((seq, heads * HD), bf16)
    return pl.pallas_call(
        functools.partial(attend_kernel, block),
        grid=(heads,),
        in_specs=[raw_spec(seq, heads, i) for i in range(3)] + head_specs(seq, heads),
        out_specs=[head] * 4 + [pl.BlockSpec((1, seq, 1), lambda h: (h, 0, 0))],
        out_shape=[low] * 4 + [jax.ShapeDtypeStruct((heads, seq, 1), f32)],
        compiler_params=pltpu.CompilerParams(vmem_limit_bytes=48 * 2**20),
        cost_estimate=pl.CostEstimate(flops=10**6, bytes_accessed=10**5, transcendentals=0),
    )(projected, projected, projected, *shared)


def attend_back(projected, shared, query, keyed, valued, grad, log_total, heads):
    seq = projected.shape[0]
    block = min(256, seq)
    head = pl.BlockSpec((seq, HD), lambda h: (0, h))
    column = pl.BlockSpec((seq, 1), lambda h: (0, 0))
    gain = pl.BlockSpec((1, HD), lambda h: (0, h))
    wide = jax.ShapeDtypeStruct((seq, heads * HD), f32)
    return pl.pallas_call(
        functools.partial(attend_back_kernel, block),
        grid=(heads,),
        in_specs=[raw_spec(seq, heads, i) for i in range(2)]
        + head_specs(seq, heads)
        + [head] * 4
        + [pl.BlockSpec((1, seq, 1), lambda h: (h, 0, 0))],
        out_specs=[head] * 3 + [column] * 2 + [gain] * 2,
        out_shape=[wide, wide, jax.ShapeDtypeStruct((seq, heads * HD), bf16)]
        + [jax.ShapeDtypeStruct((seq, 1), f32)] * 2
        + [jax.ShapeDtypeStruct((1, heads * HD), f32)] * 2,
        scratch_shapes=[pltpu.VMEM((seq, HD), f32)] * 3,
        compiler_params=pltpu.CompilerParams(vmem_limit_bytes=48 * 2**20),
        cost_estimate=pl.CostEstimate(flops=10**6, bytes_accessed=10**5, transcendentals=0),
    )(projected, projected, *shared, query, keyed, valued, grad, log_total)


def slot_choice(place, slots):
    return lax.broadcasted_iota(jnp.int32, (slots, place.shape[1]), 0) == place


def slot_weight(place, gate, slots):
    return jnp.sum(jnp.where(slot_choice(place, slots), gate, 0.0), axis=1, keepdims=True)


def spans_of(count, slots):
    return [(b, slice(b * slots, (b + 1) * slots)) for b in range(count)]


def add_tokens(place, b, slots, out, sum_tokens, partial):
    expert = pl.program_id(0)
    back = mm(slot_choice(place[0, b], slots).astype(bf16), out, ((0,), (0,)))

    @pl.when(expert == 0)
    def _():
        sum_tokens[b] = back

    @pl.when(expert > 0)
    def _():
        sum_tokens[b] += back

    @pl.when(expert == pl.num_programs(0) - 1)
    def _():
        partial[b][...] = sum_tokens[b].astype(bf16)


def hidden_kernel(count, slots, place, *refs):
    blocks, w_gate, w_up = refs[:count], refs[count], refs[count + 1]
    rows, activated, gate_pre, up_pre = refs[-4:]
    for b, span in spans_of(count, slots):
        choice = slot_choice(place[0, b], slots).astype(bf16)
        rows[0, 0, span] = mm(choice, blocks[b][...], ((1,), (0,))).astype(bf16)
    rows_in = rows[0, 0]
    g = mm(rows_in, w_gate[0], ((1,), (0,)))
    u = mm(rows_in, w_up[0], ((1,), (0,)))
    gate_pre[0], up_pre[0] = g.astype(bf16), u.astype(bf16)
    activated[0, 0] = (g * jax.nn.sigmoid(g) * u).astype(bf16)


def out_kernel(count, slots, place, gate, activated, w_down, *refs):
    partial, sum_tokens = refs[:-1], refs[-1]
    result = mm(activated[0, 0], w_down[0], ((1,), (1,)))
    for b, span in spans_of(count, slots):
        out = (result[span] * slot_weight(place[0, b], gate[0, b], slots)).astype(bf16)
        add_tokens(place, b, slots, out, sum_tokens, partial)


def expert_back_kernel(count, slots, place, gate, *refs):
    blocks, (w_gate, w_up, w_down) = refs[:count], refs[count : count + 3]
    gate_pre, up_pre = refs[count + 3 : count + 5]
    grad_rows, grad_gate, grad_up = refs[-4 - count : -1 - count]
    partial, sum_tokens = refs[-1 - count : -1], refs[-1]
    for b, span in spans_of(count, slots):
        choice = slot_choice(place[0, b], slots).astype(bf16)
        weight = slot_weight(place[0, b], gate[0, b], slots)
        picked = mm(choice, blocks[b][...], ((1,), (0,)))
        grad_rows[0, 0, span] = (picked * weight).astype(bf16)
    grad_act = mm(grad_rows[0, 0], w_down[0], ((1,), (0,)))
    g, u = gate_pre[0].astype(f32), up_pre[0].astype(f32)
    sigmoid = jax.nn.sigmoid(g)
    dg = (grad_act * u * sigmoid * (1.0 + g * (1.0 - sigmoid))).astype(bf16)
    du = (grad_act * g * sigmoid).astype(bf16)
    grad_gate[0, 0], grad_up[0, 0] = dg, du
    result = mm(dg, w_gate[0], ((1,), (1,))) + mm(du, w_up[0], ((1,), (1,)))
    result = result.astype(bf16)
    for b, span in spans_of(count, slots):
        add_tokens(place, b, slots, result[span], sum_tokens, partial)


class Experts:
    def __init__(self, group, slots, place, gate, blocks, weights):
        self.group, self.slots, self.place, self.gate = group, slots, place, gate
        self.experts, self.width, self.hidden = weights[0].shape
        self.count, self.own = len(blocks), blocks[0].shape[0]
        self.rows = self.count * slots
        group_of = lambda e: (e, group, 0, 0)
        self.table = pl.BlockSpec((1, self.count, 1, self.own), group_of)
        self.tokens = pl.BlockSpec((self.own, self.width), lambda e: (0, 0))
        self.weight = pl.BlockSpec((1, self.width, self.hidden), lambda e: (e, 0, 0))
        self.local = pl.BlockSpec((1, self.rows, self.hidden), lambda e: (e, 0, 0))
        self.wide = pl.BlockSpec((1, 1, self.rows, self.width), group_of)
        self.narrow = pl.BlockSpec((1, 1, self.rows, self.hidden), group_of)
        self.sums = pltpu.VMEM((self.count, self.own, self.width), f32)

    def shape(self, spec):
        rows, experts = self.rows, self.experts
        shapes = [
            (self.tokens, (self.own, self.width)),
            (self.local, (experts, rows, self.hidden)),
            (self.wide, (experts, 2, rows, self.width)),
            (self.narrow, (experts, 2, rows, self.hidden)),
        ]
        [shape] = [shape for known, shape in shapes if known is spec]
        return jax.ShapeDtypeStruct(shape, bf16)

    def run(self, kernel, ins, outs, scratch, prior=()):
        specs = [spec for spec, _ in ins] + [pl.BlockSpec(memory_space=pl.ANY)] * len(prior)
        return pl.pallas_call(
            functools.partial(kernel, self.count, self.slots),
            grid=(self.experts,),
            in_specs=specs,
            out_specs=outs,
            out_shape=[self.shape(spec) for spec in outs],
            scratch_shapes=scratch,
            input_output_aliases={len(ins) + i: i for i in range(len(prior))},
            compiler_params=pltpu.CompilerParams(vmem_limit_bytes=58 * 2**20),
            cost_estimate=pl.CostEstimate(
                flops=self.experts * self.rows * self.width * self.hidden * 4,
                bytes_accessed=self.experts * self.width * self.hidden * 6,
                transcendentals=self.experts * self.rows * self.hidden,
            ),
        )(*[array for _, array in ins], *prior)

    def to_hidden(self, blocks, w_gate, w_up, prior):
        ins = [(self.table, self.place)] + [(self.tokens, block) for block in blocks]
        ins += [(self.weight, w_gate), (self.weight, w_up)]
        outs = [self.wide, self.narrow, self.local, self.local]
        return self.run(hidden_kernel, ins, outs, [], prior)

    def to_tokens(self, activated, w_down):
        ins = [(self.table, self.place), (self.table, self.gate)]
        ins += [(self.narrow, activated), (self.weight, w_down)]
        return self.run(out_kernel, ins, [self.tokens] * self.count, [self.sums])

    def backward(self, blocks, weights, pres, prior):
        ins = [(self.table, self.place), (self.table, self.gate)]
        ins += [(self.tokens, block) for block in blocks]
        ins += [(self.weight, weight) for weight in weights]
        ins += [(self.local, pre) for pre in pres]
        outs = [self.wide, self.narrow, self.narrow] + [self.tokens] * self.count
        return self.run(expert_back_kernel, ins, outs, [self.sums], prior)


def dot(spec, left, right):
    return jnp.einsum(spec, left, right, preferred_element_type=f32)


def shards(
    tokens,
    w_attn,
    norm_gains,
    w_expert,
    gate_weights,
    routes,
    segment,
    valid_mask,
    teacher,
    cotangent,
):
    outer, planes, seqs = lax.axis_size("o"), lax.axis_size("z"), lax.axis_size("s")
    plane, rank = lax.axis_index("z"), lax.axis_index("s")
    own, width = tokens.shape
    rows_dev = w_attn.shape[0]
    seq = own * seqs
    heads = H // seqs
    cols = heads * HD
    hidden = w_expert.shape[2] // 3
    part = w_expert.shape[0]
    capacity = own * TOP * 17 // (16 * planes * seqs)
    scale = HD ** (-0.5)

    def to_inner(v):
        lead = v.shape[:-1]
        v = v.reshape(lead + (outer * planes, CORES, part))
        return jnp.swapaxes(v, -3, -2).reshape(lead + (width,))

    def to_outer(v):
        lead = v.shape[:-1]
        v = v.reshape(lead + (CORES, outer * planes, part))
        return jnp.swapaxes(v, -3, -2).reshape(lead + (width,))

    first_core = lax.axis_index("c") == 0

    def halves(v):
        low, high = v[..., : width // 2], v[..., width // 2 :]
        return jnp.where(first_core, low, high), jnp.where(first_core, high, low)

    def whole_of(mine, other, axis):
        low, high = jnp.where(first_core, mine, other), jnp.where(first_core, other, mine)
        return jnp.concatenate([low, high], axis=axis)

    def stack_rows(blocks, start=0):
        rows = in_order(blocks, "z", start)
        return collect(rows, "o").reshape((width // 2,) + rows.shape[2:])

    def sum_cores(grad):
        count = grad.shape[1]
        grad = exchange_sum(grad.reshape(CORES, width // 2, count), "c")
        if outer > 1:
            grad = exchange_sum(grad.astype(bf16).reshape(outer, planes * part, count), "o")
        return grad

    def gather_sum(value):
        for axis in ("z", "s", "c", "o"):
            value = sum(gather_near(jnp.broadcast_to(value, (8, PAD)), axis))[0, 0]
        return value

    by_expert = lax.optimization_barrier(w_expert.transpose(1, 0, 2))

    def expert_chunk(i, start=0):
        def piece_for(owner):
            return lax.dynamic_slice(by_expert, (owner, 0, i * hidden), (1, part, hidden))[0]

        return exchange(piece_for, "z", start)

    def gather_plane(ready):
        chunk = ready.reshape(planes * part, hidden)
        chunk = lax.all_gather(chunk, ("s", "c", "o"), axis=0, tiled=True)
        return chunk.reshape(seqs, width, hidden)

    count = jnp.sum(valid_mask).astype(jnp.int32)
    digits = jnp.stack([count // 128, count % 128]).astype(bf16)
    extra = jnp.concatenate(
        [
            norm_gains,
            jnp.broadcast_to(digits[None], (rows_dev, 2)),
            jnp.zeros((rows_dev, PAD - 6), bf16),
        ],
        axis=1,
    )

    routed = jnp.stack(
        gather_near(jnp.concatenate([routes.astype(f32), gate_weights], axis=1), "z")
    )
    route_all, gate_all = routed[..., :TOP].astype(jnp.int32), routed[..., TOP:]
    expert_ids = jnp.arange(seqs) * planes + plane
    match = route_all[:, :, None, :] == expert_ids[None, None, :, None]
    used = jnp.any(match, axis=-1)
    gate_of = jnp.sum(jnp.where(match, gate_all[:, :, None, :], 0.0), axis=-1)
    before = (jnp.arange(own)[:, None] > jnp.arange(own)[None, :]).astype(bf16)
    place = dot("tu,buk->btk", before, used.astype(bf16)).astype(jnp.int32)
    place = jnp.where(used, place, -1)
    slots = -(-capacity // 16) * 16
    place = place.transpose(2, 0, 1)[:, :, None, :]
    gate_of = gate_of.transpose(2, 0, 1)[:, :, None, :]

    groups = [[k for k in range(planes) if k % 2 == odd] for odd in range(2)]

    def by_group(table):
        return jnp.concatenate([table[:, k : k + 1] for group in groups for k in group], axis=1)

    place, gate_of = by_group(place), by_group(gate_of)

    inputs = to_inner(tokens)
    column_rows, extra_rows = rows_dev * 4 * cols // width, rows_dev * PAD // width
    extra = jnp.pad(extra.reshape(extra_rows, width), ((0, -extra_rows % 8), (0, 0)))

    def message_to(owner):
        picked = [
            lax.dynamic_slice_in_dim(w_attn, i * width + owner * cols, cols, 1) for i in range(4)
        ]
        picked = jnp.concatenate(picked, axis=1).reshape(column_rows, width)
        return jnp.concatenate([inputs, picked, extra], axis=0)

    messages = exchange(message_to, "s")
    gate_blocks = expert_chunk(0)
    up_blocks = expert_chunk(1, token(*gate_blocks))
    last = own + column_rows
    columns = [
        jnp.concatenate(
            [
                message[own:last].reshape(rows_dev, 4 * cols),
                message[last : last + extra_rows].reshape(rows_dev, PAD),
            ],
            axis=1,
        )
        for message in messages
    ]
    mine = in_order(columns, "s").reshape(part, 4 * cols + PAD)
    seq_tokens = in_order([message[:own] for message in messages], "s")
    seq_tokens = seq_tokens.reshape(seq, width).astype(f32)
    inputs = inputs.astype(f32)
    gate_ready = in_order(gate_blocks, "z", token(mine))
    w_gate = gather_plane(gate_ready)
    up_ready = in_order(up_blocks, "z", token(seq_tokens, place, gate_of))
    w_up = gather_plane(up_ready)
    in_blocks = gather_near(after(mine, up_ready), "z")
    seq_factor = rms_factor(seq_tokens)
    w_in = stack_rows(in_blocks, token(seq_factor))
    w_in_other = send(w_in, "c", 1)

    side = whole_of(w_in[:, 4 * cols :], w_in_other[:, 4 * cols :], 0)[:, :6].astype(f32).T
    gain_in, gain_mid = side[0], side[1]
    gain_q = lax.dynamic_slice_in_dim(to_outer(side[2]), rank * cols, cols, 0)
    gain_k = lax.dynamic_slice_in_dim(to_outer(side[3]), rank * cols, cols, 0)
    total_count = jnp.sum(side[4, ::rows_dev]) * 128.0 + jnp.sum(side[5, ::rows_dev])


    def near_planes(block):
        near = [block] + [None] * (planes - 1)
        for k in groups[0][1:]:
            near[k] = send(block, "z", k)
        later = after(block, *[near[k] for k in groups[0][1:]])
        for k in groups[1]:
            near[k] = send(later, "z", k)
        return [[near[k] for k in group] for group in groups]

    def send_back(first, second):
        got = [first[0]] + [send(first[i], "z", k) for i, k in enumerate(groups[0]) if k]
        base = after(total(got), second[0])
        second = [after(part, base) for part in second]
        return second[0], [base] + [send(second[i], "z", k) for i, k in enumerate(groups[1])]

    def total(pieces):
        return sum(piece.astype(f32) for piece in pieces)

    normed_in = (seq_tokens * seq_factor * gain_in).astype(bf16)
    normed_mine, normed_other = halves(normed_in)
    w_qkv, w_qkv_other = w_in[:, : 3 * cols], w_in_other[:, : 3 * cols]
    w_out = whole_of(w_in[:, 3 * cols : 4 * cols], w_in_other[:, 3 * cols : 4 * cols], 0)
    projected = jnp.dot(normed_mine, w_qkv, preferred_element_type=f32) + jnp.dot(
        normed_other, w_qkv_other, preferred_element_type=f32
    )
    query_raw = projected[:, :cols]
    key_raw = projected[:, cols : 2 * cols]

    def over_heads(first, second, *others):
        pairs = gather_near(jnp.stack([first, second]), "s")
        if others:
            pairs[0] = after(pairs[0], *others)
        pair = sum(pairs) / width
        return pair[0][:, None], pair[1][:, None]

    q_mean, k_mean = over_heads(
        jnp.sum(query_raw * query_raw, axis=-1), jnp.sum(key_raw * key_raw, axis=-1)
    )
    cosine, sine = rope_tables(seq)
    shared = [
        after(q_mean, w_gate, w_out),
        k_mean,
        gain_q[None],
        gain_k[None],
        cosine,
        sine,
        segment[:, None],
        segment[None],
    ]
    attended, query, keyed, valued, log_total = attend(projected, shared, heads)
    start = token(attended)
    down_blocks = exchange(
        lambda owner: lax.dynamic_slice(
            w_expert, (0, owner, 2 * hidden), (part, 1, hidden)
        )[:, 0],
        "z",
        start,
    )
    attn_out = dot("tc,dc->td", attended, w_out).astype(bf16)
    got = exchange_sum(attn_out.reshape(seqs, own, width), "s")
    residual = inputs + got
    down_ready = in_order(down_blocks, "z", token(residual))
    residual = after(residual, down_ready)
    w_down = gather_plane(down_ready)

    normed_mid = (residual * rms_factor(residual) * gain_mid).astype(bf16)
    expert_weights = (w_gate, w_up, w_down)
    blocks = near_planes(normed_mid)
    work = [Experts(i, slots, place, gate_of, blocks[i], expert_weights) for i in range(2)]
    rows_in, activated, *pres = work[0].to_hidden(blocks[0], w_gate, w_up, ())
    first = work[0].to_tokens(activated, w_down)
    pres = [pres]
    blocks[1][0] = after(blocks[1][0], first[0])
    rows_in, activated, *last = work[1].to_hidden(
        blocks[1], w_gate, w_up, (rows_in, activated)
    )
    pres.append(last)
    second = work[1].to_tokens(activated, w_down)
    final_out = residual + total(send_back(first, second)[1])
    rows_in, activated = [v.reshape(seqs, -1, v.shape[-1]) for v in (rows_in, activated)]

    w_out_all = lax.all_gather(after(w_out, w_up), "s", axis=0)
    valid_f = valid_mask.astype(f32)[:, None]
    difference = final_out - to_inner(teacher).astype(f32)
    squared = jnp.sum(valid_f * difference * difference)
    grad_out = (
        to_inner(cotangent).astype(f32) + 2.0 / (total_count * width) * valid_f * difference
    )

    def scatter_expert(grad):
        grad = grad.reshape(seqs * width, hidden)
        grad = lax.psum_scatter(grad, ("s", "c", "o"), scatter_dimension=0, tiled=True)
        return grad.reshape(planes, part, hidden)

    blocks = near_planes(grad_out.astype(bf16))
    *grads, first, last = work[0].backward(blocks[0], expert_weights, pres[0], ())
    partial = [(first, last)]
    blocks[1][0] = after(blocks[1][0], first)
    *grads, first, last = work[1].backward(blocks[1], expert_weights, pres[1], grads)
    partial.append((first, last))
    back_last, back_pieces = send_back(*partial)
    grad_rows, grad_gate, grad_up = [v.reshape(seqs, -1, v.shape[-1]) for v in grads]
    grad_w_down = dot("krd,krf->kdf", grad_rows, after(activated, back_last)).astype(bf16)
    back_pieces[0] = after(back_pieces[0], grad_w_down)
    grad_mid = total(back_pieces)
    grad_w_gate = dot("krd,krf->kdf", rows_in, after(grad_gate, grad_mid)).astype(bf16)
    grad_resid_norm, gain_mid_grad = norm_back(residual, gain_mid, grad_mid)
    grad_resid = grad_out + grad_resid_norm

    grad_low = grad_resid.astype(bf16)
    grad_heads = dot("td,sdc->stc", grad_low, w_out_all).astype(bf16)
    head_blocks = exchange(
        lambda i: lax.dynamic_index_in_dim(grad_heads, i, 0, keepdims=False), "s"
    )
    grad_heads = in_order(head_blocks, "s", token(grad_w_gate)).reshape(seq, cols)
    grad_w_up = dot("krd,krf->kdf", rows_in, after(grad_up, grad_heads)).astype(bf16)
    up_done = grad_w_up
    grad_w_down, grad_w_gate, grad_w_up = [
        scatter_expert(grad) for grad in (grad_w_down, grad_w_gate, grad_w_up)
    ]
    low_blocks = gather_near(after(grad_low, grad_heads), "s")
    down_ready = swap(grad_w_down, "z")
    grad_q, grad_k, grad_v, q_inner, k_inner, gain_q_grad, gain_k_grad = attend_back(
        projected, shared, query, keyed, valued, after(grad_heads, up_done), log_total, heads
    )
    grad_attn_out = in_order(low_blocks, "s", token(grad_q)).reshape(seq, width)
    down_ready = after(down_ready, grad_q)
    q_inner = after(q_inner, down_ready, grad_attn_out)
    grad_w_out = dot("td,tc->dc", grad_attn_out, attended).astype(bf16)
    q_inner, k_inner = over_heads(q_inner[:, 0], k_inner[:, 0], grad_w_out)

    def norm_grad(grad, raw, mean, inner):
        factor = lax.rsqrt(mean + epsilon)
        return (factor * (grad - raw * factor * inner)).astype(bf16)

    grad_proj = jnp.concatenate(
        [
            norm_grad(grad_q, query_raw, q_mean, q_inner),
            norm_grad(grad_k, key_raw, k_mean, k_inner),
            grad_v,
        ],
        axis=1,
    )

    grad_w_qkv = dot("td,tc->dc", normed_in, grad_proj).astype(bf16)
    summed = jnp.concatenate([sum_cores(grad_w_qkv), sum_cores(grad_w_out)], axis=1)
    summed = summed.astype(bf16).reshape(planes, part, 4 * cols)
    gate_ready = swap(grad_w_gate, "z")
    late_proj = after(grad_proj, summed)
    grad_normed = jnp.concatenate(
        [dot("tc,dc->td", late_proj, weight).astype(bf16) for weight in (w_qkv, w_qkv_other)],
        axis=1,
    )
    normed_blocks = exchange_by_rank(grad_normed.reshape(seqs, own, width), "s")
    row_blocks = exchange_by_rank(summed, "z")
    grad_attn = after(total(row_blocks), gate_ready).astype(bf16)
    grad_w_up = after(grad_w_up, grad_attn)
    up_ready = swap(grad_w_up, "z")
    normed_blocks[0] = after(normed_blocks[0], grad_w_up)
    grad_normed = total(normed_blocks)
    grad_normed = whole_of(grad_normed[:, : width // 2], grad_normed[:, width // 2 :], 1)
    grad_in_norm, gain_in_grad = norm_back(inputs, gain_in, grad_normed)
    grad_tokens = to_outer(grad_resid + grad_in_norm)

    def widen(local):
        full = jnp.zeros((width,), f32)
        return to_inner(lax.dynamic_update_slice_in_dim(full, local, rank * cols, 0))

    gains = jnp.stack([gain_in_grad, gain_mid_grad, widen(gain_q_grad[0]), widen(gain_k_grad[0])])
    gains = after(gains, grad_w_up)
    loss_value = gather_sum(after(squared, grad_w_up)) / (total_count * width)
    for axis in ("z", "c", "s", "o"):
        gains = sum(gather_near(gains, axis))
    row = (lax.axis_index(("c", "o", "z")) * seqs + rank) * rows_dev
    grad_gains = lax.dynamic_slice_in_dim(gains, row, rows_dev, 1).T

    got = exchange_by_rank(grad_attn.reshape(seqs, rows_dev, 4 * cols), "s")
    got = in_order(got, "s").astype(f32)
    grad_attn = jnp.concatenate(
        [got[s, :, i * cols : (i + 1) * cols] for i in range(4) for s in range(seqs)], axis=1
    )
    grad_expert = jnp.concatenate([gate_ready, up_ready, down_ready], axis=2)
    grad_expert = grad_expert.astype(f32).transpose(1, 0, 2)
    return (
        to_outer(final_out).astype(bf16),
        loss_value,
        grad_tokens,
        grad_attn,
        grad_gains,
        grad_expert,
    )


def solution(mesh):
    fsdp, seqs = mesh.shape["fsdp"], mesh.shape["sp"]

    def whole(*arrays):
        planes = arrays[3].shape[1] // seqs
        outer = fsdp // (planes * CORES)
        inner = Mesh(mesh.devices.reshape(outer, planes, CORES, seqs), ("o", "z", "c", "s"))
        every = ("o", "z", "c", "s")
        rows = P(every, None)
        experts = P(("o", "z", "c"), "s", None)
        return jax.shard_map(
            shards,
            mesh=inner,
            in_specs=(
                rows,
                rows,
                rows,
                experts,
                rows,
                rows,
                P(("o", "z", "c")),
                P(every),
                rows,
                rows,
            ),
            out_specs=(rows, P(), rows, rows, rows, experts),
            check_vma=False,
        )(*arrays)

    return whole
```

```python
import functools

import jax
import jax.numpy as jnp
from jax import lax
from jax.experimental import pallas as pl
from jax.experimental.pallas import tpu as pltpu
from jax.sharding import Mesh, PartitionSpec as P

H = 16
HD = 128
TOP = 8
CORES = 2
PAD = 128

epsilon = 1e-05
masked = -1e30
f32 = jnp.float32
bf16 = jnp.bfloat16


def send(block, axis, step):
    size = lax.axis_size(axis)
    return lax.ppermute(block, axis, [(i, i ^ step) for i in range(size)])


def gather_near(block, axis):
    return [block] + [send(block, axis, k) for k in range(1, lax.axis_size(axis))]


def in_order(blocks, axis, start=0):
    rank = lax.axis_index(axis)
    if len(blocks) == 1:
        return blocks[0][None]
    stacked = jnp.zeros((len(blocks),) + blocks[0].shape, blocks[0].dtype)
    for k, block in enumerate(blocks):
        stacked = lax.dynamic_update_index_in_dim(stacked, block, (rank ^ k) + start, 0)
    return stacked


def collect(block, axis):
    return in_order(gather_near(block, axis), axis)


def exchange(piece_for, axis, start=0):
    rank, size = lax.axis_index(axis) + start, lax.axis_size(axis)
    return [piece_for(rank)] + [send(piece_for(rank ^ k), axis, k) for k in range(1, size)]


def swap(pieces, axis):
    return lax.all_to_all(pieces, axis, split_axis=0, concat_axis=0, tiled=True)


def exchange_by_rank(pieces, axis):
    return exchange(lambda i: lax.dynamic_index_in_dim(pieces, i, 0, keepdims=False), axis)


def exchange_sum(pieces, axis):
    got = exchange_by_rank(pieces, axis)
    return sum(piece.astype(f32) for piece in got)


def token(*values):
    firsts = [value[(slice(0, 1),) * value.ndim].reshape(()).astype(f32) for value in values]
    total = sum(firsts)
    return (total != total).astype(jnp.int32)


def after(value, *others):
    return value + token(*others).astype(value.dtype)


def rms_factor(values):
    return lax.rsqrt(jnp.mean(values * values, axis=-1, keepdims=True) + epsilon)


def norm_back(values, gain_vec, grad_in):
    factor = rms_factor(values)
    normed = values * factor
    gain_grad = jnp.sum(grad_in * normed, axis=0)
    inner = grad_in * gain_vec
    grad = factor * (inner - normed * jnp.mean(inner * normed, axis=-1, keepdims=True))
    return grad, gain_grad


def rope_tables(rows):
    inverse = 10000.0 ** (-(jnp.arange(HD // 2).astype(f32) * 2.0 / HD))
    angles = jnp.arange(rows).astype(f32)[:, None] * inverse[None, :]
    cosine = jnp.concatenate([jnp.cos(angles), jnp.cos(angles)], axis=-1)
    sine = jnp.concatenate([-jnp.sin(angles), jnp.sin(angles)], axis=-1)
    return cosine, sine


def mm(left, right, dims):
    return lax.dot_general(left, right, (dims, ((), ())), preferred_element_type=f32)


def masked_scores(query, keyed, seg_col, seg_row, first, scale):
    scores = mm(query, keyed, ((1,), (1,))) * scale
    rows = first + lax.broadcasted_iota(jnp.int32, scores.shape, 0)
    allowed = (rows >= lax.broadcasted_iota(jnp.int32, scores.shape, 1)) & (seg_col == seg_row)
    return jnp.where(allowed, scores, masked)


def attend_kernel(
    block,
    q_raw,
    k_raw,
    v_raw,
    q_mean,
    k_mean,
    gain_q,
    gain_k,
    cosine,
    sine,
    seg_col,
    seg_row,
    out,
    q_out,
    k_out,
    v_out,
    log_total,
):
    def rope(raw, mean, gain):
        values = raw[...] * lax.rsqrt(mean[...] + epsilon) * gain[...]
        turned = pltpu.roll(values, HD // 2, 1)
        return (values * cosine[...] + turned * sine[...]).astype(bf16)

    q_out[...] = rope(q_raw, q_mean, gain_q)
    k_out[...] = rope(k_raw, k_mean, gain_k)
    v_out[...] = v_raw[...].astype(bf16)
    for first in range(0, out.shape[0], block):
        last = first + block
        scores = masked_scores(
            q_out[first:last],
            k_out[:last],
            seg_col[first:last],
            seg_row[:, :last],
            first,
            HD**-0.5,
        )
        top = jnp.max(scores, axis=-1, keepdims=True)
        exps = jnp.exp(scores - top)
        total = jnp.sum(exps, axis=-1, keepdims=True)
        weights = (exps * (1.0 / total)).astype(bf16)
        out[first:last] = mm(weights, v_out[:last], ((1,), (0,))).astype(bf16)
        log_total[0, first:last] = top + jnp.log(total)


def attend_back_kernel(
    block,
    q_raw,
    k_raw,
    q_mean,
    k_mean,
    gain_q,
    gain_k,
    cosine,
    sine,
    seg_col,
    seg_row,
    query,
    keyed,
    valued,
    grad,
    log_total,
    grad_q,
    grad_k,
    grad_v,
    q_inner,
    k_inner,
    gain_q_grad,
    gain_k_grad,
    sum_q,
    sum_k,
    sum_v,
):
    scale = HD**-0.5
    sum_k[...] = jnp.zeros_like(sum_k)
    sum_v[...] = jnp.zeros_like(sum_v)
    for first in range(0, query.shape[0], block):
        last = first + block
        q_block, g_block = query[first:last], grad[first:last]
        scores = masked_scores(
            q_block, keyed[:last], seg_col[first:last], seg_row[:, :last], first, scale
        )
        probs = jnp.exp(scores - log_total[0, first:last])
        sum_v[:last] += mm(probs.astype(bf16), g_block, ((0,), (0,)))
        grad_probs = mm(g_block, valued[:last], ((1,), (1,)))
        inner = jnp.sum(probs * grad_probs, axis=-1, keepdims=True)
        grad_scores = (probs * (grad_probs - inner)).astype(bf16)
        sum_q[first:last] = mm(grad_scores, keyed[:last], ((1,), (0,))) * scale
        sum_k[:last] += mm(grad_scores, q_block, ((0,), (0,))) * scale
    grad_v[...] = sum_v[...].astype(bf16)

    def undo(total, raw, mean, gain, inner_out, gain_out, grad_out):
        low = total[...].astype(bf16).astype(f32)
        back = low * cosine[...] + pltpu.roll(low * sine[...], HD // 2, 1)
        normed = raw[...] * lax.rsqrt(mean[...] + epsilon)
        gain_out[...] = jnp.sum(back * normed, axis=0, keepdims=True)
        back = back * gain[...]
        grad_out[...] = back
        inner = jnp.sum(back * normed, axis=-1, keepdims=True)

        @pl.when(pl.program_id(0) == 0)
        def _():
            inner_out[...] = inner

        @pl.when(pl.program_id(0) > 0)
        def _():
            inner_out[...] += inner

    undo(sum_q, q_raw, q_mean, gain_q, q_inner, gain_q_grad, grad_q)
    undo(sum_k, k_raw, k_mean, gain_k, k_inner, gain_k_grad, grad_k)


def head_specs(seq, heads):
    column = pl.BlockSpec((seq, 1), lambda h: (0, 0))
    gain = pl.BlockSpec((1, HD), lambda h: (0, h))
    table = pl.BlockSpec((seq, HD), lambda h: (0, 0))
    return [column, column, gain, gain, table, table, column, pl.BlockSpec((1, seq), lambda h: (0, 0))]


def raw_spec(seq, heads, which):
    return pl.BlockSpec((seq, HD), lambda h: (0, which * heads + h))


def attend(projected, shared, heads):
    seq = projected.shape[0]
    block = min(256, seq)
    head = pl.BlockSpec((seq, HD), lambda h: (0, h))
    low = jax.ShapeDtypeStruct((seq, heads * HD), bf16)
    return pl.pallas_call(
        functools.partial(attend_kernel, block),
        grid=(heads,),
        in_specs=[raw_spec(seq, heads, i) for i in range(3)] + head_specs(seq, heads),
        out_specs=[head] * 4 + [pl.BlockSpec((1, seq, 1), lambda h: (h, 0, 0))],
        out_shape=[low] * 4 + [jax.ShapeDtypeStruct((heads, seq, 1), f32)],
        compiler_params=pltpu.CompilerParams(vmem_limit_bytes=48 * 2**20),
        cost_estimate=pl.CostEstimate(flops=10**6, bytes_accessed=10**5, transcendentals=0),
    )(projected, projected, projected, *shared)


def attend_back(projected, shared, query, keyed, valued, grad, log_total, heads):
    seq = projected.shape[0]
    block = min(256, seq)
    head = pl.BlockSpec((seq, HD), lambda h: (0, h))
    column = pl.BlockSpec((seq, 1), lambda h: (0, 0))
    gain = pl.BlockSpec((1, HD), lambda h: (0, h))
    wide = jax.ShapeDtypeStruct((seq, heads * HD), f32)
    return pl.pallas_call(
        functools.partial(attend_back_kernel, block),
        grid=(heads,),
        in_specs=[raw_spec(seq, heads, i) for i in range(2)]
        + head_specs(seq, heads)
        + [head] * 4
        + [pl.BlockSpec((1, seq, 1), lambda h: (h, 0, 0))],
        out_specs=[head] * 3 + [column] * 2 + [gain] * 2,
        out_shape=[wide, wide, jax.ShapeDtypeStruct((seq, heads * HD), bf16)]
        + [jax.ShapeDtypeStruct((seq, 1), f32)] * 2
        + [jax.ShapeDtypeStruct((1, heads * HD), f32)] * 2,
        scratch_shapes=[pltpu.VMEM((seq, HD), f32)] * 3,
        compiler_params=pltpu.CompilerParams(vmem_limit_bytes=48 * 2**20),
        cost_estimate=pl.CostEstimate(flops=10**6, bytes_accessed=10**5, transcendentals=0),
    )(projected, projected, *shared, query, keyed, valued, grad, log_total)


def slot_choice(place, slots):
    return lax.broadcasted_iota(jnp.int32, (slots, place.shape[1]), 0) == place


def slot_weight(place, gate, slots):
    return jnp.sum(jnp.where(slot_choice(place, slots), gate, 0.0), axis=1, keepdims=True)


def spans_of(count, slots):
    return [(b, slice(b * slots, (b + 1) * slots)) for b in range(count)]


def add_tokens(place, b, slots, out, sum_tokens, partial):
    expert = pl.program_id(0)
    back = mm(slot_choice(place[0, b], slots).astype(bf16), out, ((0,), (0,)))

    @pl.when(expert == 0)
    def _():
        sum_tokens[b] = back

    @pl.when(expert > 0)
    def _():
        sum_tokens[b] += back

    @pl.when(expert == pl.num_programs(0) - 1)
    def _():
        partial[b][...] = sum_tokens[b].astype(bf16)


def hidden_kernel(count, slots, place, *refs):
    blocks, w_gate, w_up = refs[:count], refs[count], refs[count + 1]
    rows, activated, gate_pre, up_pre = refs[-4:]
    for b, span in spans_of(count, slots):
        choice = slot_choice(place[0, b], slots).astype(bf16)
        rows[0, 0, span] = mm(choice, blocks[b][...], ((1,), (0,))).astype(bf16)
    rows_in = rows[0, 0]
    g = mm(rows_in, w_gate[0], ((1,), (0,)))
    u = mm(rows_in, w_up[0], ((1,), (0,)))
    gate_pre[0], up_pre[0] = g.astype(bf16), u.astype(bf16)
    activated[0, 0] = (g * jax.nn.sigmoid(g) * u).astype(bf16)


def out_kernel(count, slots, place, gate, activated, w_down, *refs):
    partial, sum_tokens = refs[:-1], refs[-1]
    result = mm(activated[0, 0], w_down[0], ((1,), (1,)))
    for b, span in spans_of(count, slots):
        out = (result[span] * slot_weight(place[0, b], gate[0, b], slots)).astype(bf16)
        add_tokens(place, b, slots, out, sum_tokens, partial)


def expert_back_kernel(count, slots, place, gate, *refs):
    blocks, (w_gate, w_up, w_down) = refs[:count], refs[count : count + 3]
    gate_pre, up_pre = refs[count + 3 : count + 5]
    grad_rows, grad_gate, grad_up = refs[-4 - count : -1 - count]
    partial, sum_tokens = refs[-1 - count : -1], refs[-1]
    for b, span in spans_of(count, slots):
        choice = slot_choice(place[0, b], slots).astype(bf16)
        weight = slot_weight(place[0, b], gate[0, b], slots)
        picked = mm(choice, blocks[b][...], ((1,), (0,)))
        grad_rows[0, 0, span] = (picked * weight).astype(bf16)
    grad_act = mm(grad_rows[0, 0], w_down[0], ((1,), (0,)))
    g, u = gate_pre[0].astype(f32), up_pre[0].astype(f32)
    sigmoid = jax.nn.sigmoid(g)
    dg = (grad_act * u * sigmoid * (1.0 + g * (1.0 - sigmoid))).astype(bf16)
    du = (grad_act * g * sigmoid).astype(bf16)
    grad_gate[0, 0], grad_up[0, 0] = dg, du
    result = mm(dg, w_gate[0], ((1,), (1,))) + mm(du, w_up[0], ((1,), (1,)))
    result = result.astype(bf16)
    for b, span in spans_of(count, slots):
        add_tokens(place, b, slots, result[span], sum_tokens, partial)


class Experts:
    def __init__(self, group, slots, place, gate, blocks, weights):
        self.group, self.slots, self.place, self.gate = group, slots, place, gate
        self.experts, self.width, self.hidden = weights[0].shape
        self.count, self.own = len(blocks), blocks[0].shape[0]
        self.rows = self.count * slots
        group_of = lambda e: (e, group, 0, 0)
        self.table = pl.BlockSpec((1, self.count, 1, self.own), group_of)
        self.tokens = pl.BlockSpec((self.own, self.width), lambda e: (0, 0))
        self.weight = pl.BlockSpec((1, self.width, self.hidden), lambda e: (e, 0, 0))
        self.local = pl.BlockSpec((1, self.rows, self.hidden), lambda e: (e, 0, 0))
        self.wide = pl.BlockSpec((1, 1, self.rows, self.width), group_of)
        self.narrow = pl.BlockSpec((1, 1, self.rows, self.hidden), group_of)
        self.sums = pltpu.VMEM((self.count, self.own, self.width), f32)

    def shape(self, spec):
        rows, experts = self.rows, self.experts
        shapes = [
            (self.tokens, (self.own, self.width)),
            (self.local, (experts, rows, self.hidden)),
            (self.wide, (experts, 2, rows, self.width)),
            (self.narrow, (experts, 2, rows, self.hidden)),
        ]
        [shape] = [shape for known, shape in shapes if known is spec]
        return jax.ShapeDtypeStruct(shape, bf16)

    def run(self, kernel, ins, outs, scratch, prior=()):
        specs = [spec for spec, _ in ins] + [pl.BlockSpec(memory_space=pl.ANY)] * len(prior)
        return pl.pallas_call(
            functools.partial(kernel, self.count, self.slots),
            grid=(self.experts,),
            in_specs=specs,
            out_specs=outs,
            out_shape=[self.shape(spec) for spec in outs],
            scratch_shapes=scratch,
            input_output_aliases={len(ins) + i: i for i in range(len(prior))},
            compiler_params=pltpu.CompilerParams(vmem_limit_bytes=58 * 2**20),
            cost_estimate=pl.CostEstimate(
                flops=self.experts * self.rows * self.width * self.hidden * 4,
                bytes_accessed=self.experts * self.width * self.hidden * 6,
                transcendentals=self.experts * self.rows * self.hidden,
            ),
        )(*[array for _, array in ins], *prior)

    def to_hidden(self, blocks, w_gate, w_up, prior):
        ins = [(self.table, self.place)] + [(self.tokens, block) for block in blocks]
        ins += [(self.weight, w_gate), (self.weight, w_up)]
        outs = [self.wide, self.narrow, self.local, self.local]
        return self.run(hidden_kernel, ins, outs, [], prior)

    def to_tokens(self, activated, w_down):
        ins = [(self.table, self.place), (self.table, self.gate)]
        ins += [(self.narrow, activated), (self.weight, w_down)]
        return self.run(out_kernel, ins, [self.tokens] * self.count, [self.sums])

    def backward(self, blocks, weights, pres, prior):
        ins = [(self.table, self.place), (self.table, self.gate)]
        ins += [(self.tokens, block) for block in blocks]
        ins += [(self.weight, weight) for weight in weights]
        ins += [(self.local, pre) for pre in pres]
        outs = [self.wide, self.narrow, self.narrow] + [self.tokens] * self.count
        return self.run(expert_back_kernel, ins, outs, [self.sums], prior)


def dot(spec, left, right):
    return jnp.einsum(spec, left, right, preferred_element_type=f32)


def shards(
    tokens,
    w_attn,
    norm_gains,
    w_expert,
    gate_weights,
    routes,
    segment,
    valid_mask,
    teacher,
    cotangent,
):
    outer, planes, seqs = lax.axis_size("o"), lax.axis_size("z"), lax.axis_size("s")
    plane, rank = lax.axis_index("z"), lax.axis_index("s")
    own, width = tokens.shape
    rows_dev = w_attn.shape[0]
    seq = own * seqs
    heads = H // seqs
    cols = heads * HD
    hidden = w_expert.shape[2] // 3
    part = w_expert.shape[0]
    capacity = own * TOP * 17 // (16 * planes * seqs)
    scale = HD ** (-0.5)

    def to_inner(v):
        lead = v.shape[:-1]
        v = v.reshape(lead + (outer * planes, CORES, part))
        return jnp.swapaxes(v, -3, -2).reshape(lead + (width,))

    def to_outer(v):
        lead = v.shape[:-1]
        v = v.reshape(lead + (CORES, outer * planes, part))
        return jnp.swapaxes(v, -3, -2).reshape(lead + (width,))

    first_core = lax.axis_index("c") == 0

    def halves(v):
        low, high = v[..., : width // 2], v[..., width // 2 :]
        return jnp.where(first_core, low, high), jnp.where(first_core, high, low)

    def whole_of(mine, other, axis):
        low, high = jnp.where(first_core, mine, other), jnp.where(first_core, other, mine)
        return jnp.concatenate([low, high], axis=axis)

    def stack_rows(blocks, start=0):
        rows = in_order(blocks, "z", start)
        return collect(rows, "o").reshape((width // 2,) + rows.shape[2:])

    def sum_cores(grad):
        count = grad.shape[1]
        grad = exchange_sum(grad.reshape(CORES, width // 2, count), "c")
        if outer > 1:
            grad = exchange_sum(grad.astype(bf16).reshape(outer, planes * part, count), "o")
        return grad

    def gather_sum(value):
        for axis in ("z", "s", "c", "o"):
            value = sum(gather_near(jnp.broadcast_to(value, (8, PAD)), axis))[0, 0]
        return value

    by_expert = lax.optimization_barrier(w_expert.transpose(1, 0, 2))

    def expert_chunk(i, start=0):
        def piece_for(owner):
            return lax.dynamic_slice(by_expert, (owner, 0, i * hidden), (1, part, hidden))[0]

        return exchange(piece_for, "z", start)

    def gather_plane(ready):
        chunk = ready.reshape(planes * part, hidden)
        chunk = lax.all_gather(chunk, ("s", "c", "o"), axis=0, tiled=True)
        return chunk.reshape(seqs, width, hidden)

    count = jnp.sum(valid_mask).astype(jnp.int32)
    digits = jnp.stack([count // 128, count % 128]).astype(bf16)
    extra = jnp.concatenate(
        [
            norm_gains,
            jnp.broadcast_to(digits[None], (rows_dev, 2)),
            jnp.zeros((rows_dev, PAD - 6), bf16),
        ],
        axis=1,
    )

    routed = jnp.stack(
        gather_near(jnp.concatenate([routes.astype(f32), gate_weights], axis=1), "z")
    )
    route_all, gate_all = routed[..., :TOP].astype(jnp.int32), routed[..., TOP:]
    expert_ids = jnp.arange(seqs) * planes + plane
    match = route_all[:, :, None, :] == expert_ids[None, None, :, None]
    used = jnp.any(match, axis=-1)
    gate_of = jnp.sum(jnp.where(match, gate_all[:, :, None, :], 0.0), axis=-1)
    before = (jnp.arange(own)[:, None] > jnp.arange(own)[None, :]).astype(bf16)
    place = dot("tu,buk->btk", before, used.astype(bf16)).astype(jnp.int32)
    place = jnp.where(used, place, -1)
    slots = -(-capacity // 16) * 16
    place = place.transpose(2, 0, 1)[:, :, None, :]
    gate_of = gate_of.transpose(2, 0, 1)[:, :, None, :]

    groups = [[k for k in range(planes) if k % 2 == odd] for odd in range(2)]

    def by_group(table):
        return jnp.concatenate([table[:, k : k + 1] for group in groups for k in group], axis=1)

    place, gate_of = by_group(place), by_group(gate_of)

    inputs = to_inner(tokens)
    column_rows, extra_rows = rows_dev * 4 * cols // width, rows_dev * PAD // width
    extra = jnp.pad(extra.reshape(extra_rows, width), ((0, -extra_rows % 8), (0, 0)))

    def message_to(owner):
        picked = [
            lax.dynamic_slice_in_dim(w_attn, i * width + owner * cols, cols, 1) for i in range(4)
        ]
        picked = jnp.concatenate(picked, axis=1).reshape(column_rows, width)
        return jnp.concatenate([inputs, picked, extra], axis=0)

    messages = exchange(message_to, "s")
    gate_blocks = expert_chunk(0)
    up_blocks = expert_chunk(1, token(*gate_blocks))
    last = own + column_rows
    columns = [
        jnp.concatenate(
            [
                message[own:last].reshape(rows_dev, 4 * cols),
                message[last : last + extra_rows].reshape(rows_dev, PAD),
            ],
            axis=1,
        )
        for message in messages
    ]
    mine = in_order(columns, "s").reshape(part, 4 * cols + PAD)
    inputs = inputs.astype(f32)
    gate_ready = in_order(gate_blocks, "z", token(*messages))
    w_gate = gather_plane(gate_ready)
    up_ready = in_order(up_blocks, "z", token(gate_ready, mine))
    w_up = gather_plane(up_ready)
    in_blocks = gather_near(after(mine, up_ready), "z")
    seq_tokens = in_order([message[:own] for message in messages], "s", token(up_ready))
    seq_tokens = seq_tokens.reshape(seq, width).astype(f32)
    seq_factor = rms_factor(seq_tokens)
    w_in = stack_rows(in_blocks, token(seq_factor))
    w_in_other = send(w_in, "c", 1)

    side = whole_of(w_in[:, 4 * cols :], w_in_other[:, 4 * cols :], 0)[:, :6].astype(f32).T
    gain_in, gain_mid = side[0], side[1]
    gain_q = lax.dynamic_slice_in_dim(to_outer(side[2]), rank * cols, cols, 0)
    gain_k = lax.dynamic_slice_in_dim(to_outer(side[3]), rank * cols, cols, 0)
    total_count = jnp.sum(side[4, ::rows_dev]) * 128.0 + jnp.sum(side[5, ::rows_dev])


    def near_planes(block):
        near = [block] + [None] * (planes - 1)
        for k in groups[0][1:]:
            near[k] = send(block, "z", k)
        later = after(block, *[near[k] for k in groups[0][1:]])
        for k in groups[1]:
            near[k] = send(later, "z", k)
        return [[near[k] for k in group] for group in groups]

    def send_back(first, second):
        got = [first[0]] + [send(first[i], "z", k) for i, k in enumerate(groups[0]) if k]
        base = after(total(got), second[0])
        second = [after(part, base) for part in second]
        return second[0], [base] + [send(second[i], "z", k) for i, k in enumerate(groups[1])]

    def total(pieces):
        return sum(piece.astype(f32) for piece in pieces)

    normed_in = (seq_tokens * seq_factor * gain_in).astype(bf16)
    normed_mine, normed_other = halves(normed_in)
    w_qkv, w_qkv_other = w_in[:, : 3 * cols], w_in_other[:, : 3 * cols]
    w_out = whole_of(w_in[:, 3 * cols : 4 * cols], w_in_other[:, 3 * cols : 4 * cols], 0)
    projected = jnp.dot(normed_mine, w_qkv, preferred_element_type=f32) + jnp.dot(
        normed_other, w_qkv_other, preferred_element_type=f32
    )
    query_raw = projected[:, :cols]
    key_raw = projected[:, cols : 2 * cols]

    def over_heads(first, second, *others):
        pairs = gather_near(jnp.stack([first, second]), "s")
        if others:
            pairs[0] = after(pairs[0], *others)
        pair = sum(pairs) / width
        return pair[0][:, None], pair[1][:, None]

    q_mean, k_mean = over_heads(
        jnp.sum(query_raw * query_raw, axis=-1), jnp.sum(key_raw * key_raw, axis=-1)
    )
    cosine, sine = rope_tables(seq)
    shared = [
        after(q_mean, w_gate, w_out),
        k_mean,
        gain_q[None],
        gain_k[None],
        cosine,
        sine,
        segment[:, None],
        segment[None],
    ]
    attended, query, keyed, valued, log_total = attend(projected, shared, heads)
    start = token(attended)
    down_blocks = exchange(
        lambda owner: lax.dynamic_slice(
            w_expert, (0, owner, 2 * hidden), (part, 1, hidden)
        )[:, 0],
        "z",
        start,
    )
    attn_out = dot("tc,dc->td", attended, w_out).astype(bf16)
    got = exchange_sum(attn_out.reshape(seqs, own, width), "s")
    residual = inputs + got
    down_ready = in_order(down_blocks, "z", token(residual))
    residual = after(residual, down_ready)
    w_down = gather_plane(down_ready)

    normed_mid = (residual * rms_factor(residual) * gain_mid).astype(bf16)
    expert_weights = (w_gate, w_up, w_down)
    blocks = near_planes(normed_mid)
    work = [Experts(i, slots, place, gate_of, blocks[i], expert_weights) for i in range(2)]
    rows_in, activated, *pres = work[0].to_hidden(blocks[0], w_gate, w_up, ())
    first = work[0].to_tokens(activated, w_down)
    pres = [pres]
    blocks[1][0] = after(blocks[1][0], first[0])
    rows_in, activated, *last = work[1].to_hidden(
        blocks[1], w_gate, w_up, (rows_in, activated)
    )
    pres.append(last)
    second = work[1].to_tokens(activated, w_down)
    final_out = residual + total(send_back(first, second)[1])
    rows_in, activated = [v.reshape(seqs, -1, v.shape[-1]) for v in (rows_in, activated)]

    w_out_all = lax.all_gather(after(w_out, w_up), "s", axis=0)
    valid_f = valid_mask.astype(f32)[:, None]
    difference = final_out - to_inner(teacher).astype(f32)
    squared = jnp.sum(valid_f * difference * difference)
    grad_out = (
        to_inner(cotangent).astype(f32) + 2.0 / (total_count * width) * valid_f * difference
    )

    def scatter_expert(grad):
        grad = grad.reshape(seqs * width, hidden)
        grad = lax.psum_scatter(grad, ("s", "c", "o"), scatter_dimension=0, tiled=True)
        return grad.reshape(planes, part, hidden)

    blocks = near_planes(grad_out.astype(bf16))
    *grads, first, last = work[0].backward(blocks[0], expert_weights, pres[0], ())
    partial = [(first, last)]
    blocks[1][0] = after(blocks[1][0], first)
    *grads, first, last = work[1].backward(blocks[1], expert_weights, pres[1], grads)
    partial.append((first, last))
    back_last, back_pieces = send_back(*partial)
    grad_rows, grad_gate, grad_up = [v.reshape(seqs, -1, v.shape[-1]) for v in grads]
    grad_w_down = dot("krd,krf->kdf", grad_rows, after(activated, back_last)).astype(bf16)
    back_pieces[0] = after(back_pieces[0], grad_w_down)
    grad_mid = total(back_pieces)
    grad_w_gate = dot("krd,krf->kdf", rows_in, after(grad_gate, grad_mid)).astype(bf16)
    grad_resid_norm, gain_mid_grad = norm_back(residual, gain_mid, grad_mid)
    grad_resid = grad_out + grad_resid_norm

    grad_low = grad_resid.astype(bf16)
    grad_heads = dot("td,sdc->stc", grad_low, w_out_all).astype(bf16)
    head_blocks = exchange(
        lambda i: lax.dynamic_index_in_dim(grad_heads, i, 0, keepdims=False), "s"
    )
    grad_heads = in_order(head_blocks, "s", token(grad_w_gate)).reshape(seq, cols)
    grad_w_up = dot("krd,krf->kdf", rows_in, after(grad_up, grad_heads)).astype(bf16)
    up_done = grad_w_up
    grad_w_down, grad_w_gate, grad_w_up = [
        scatter_expert(grad) for grad in (grad_w_down, grad_w_gate, grad_w_up)
    ]
    low_blocks = gather_near(after(grad_low, grad_heads), "s")
    down_ready = swap(grad_w_down, "z")
    grad_q, grad_k, grad_v, q_inner, k_inner, gain_q_grad, gain_k_grad = attend_back(
        projected, shared, query, keyed, valued, after(grad_heads, up_done), log_total, heads
    )
    grad_attn_out = in_order(low_blocks, "s", token(grad_q)).reshape(seq, width)
    down_ready = after(down_ready, grad_q)
    q_inner = after(q_inner, down_ready, grad_attn_out)
    grad_w_out = dot("td,tc->dc", grad_attn_out, attended).astype(bf16)
    q_inner, k_inner = over_heads(q_inner[:, 0], k_inner[:, 0], grad_w_out)

    def norm_grad(grad, raw, mean, inner):
        factor = lax.rsqrt(mean + epsilon)
        return (factor * (grad - raw * factor * inner)).astype(bf16)

    grad_proj = jnp.concatenate(
        [
            norm_grad(grad_q, query_raw, q_mean, q_inner),
            norm_grad(grad_k, key_raw, k_mean, k_inner),
            grad_v,
        ],
        axis=1,
    )

    grad_w_qkv = dot("td,tc->dc", normed_in, grad_proj).astype(bf16)
    summed = jnp.concatenate([sum_cores(grad_w_qkv), sum_cores(grad_w_out)], axis=1)
    summed = summed.astype(bf16).reshape(planes, part, 4 * cols)
    gate_ready = swap(grad_w_gate, "z")
    late_proj = after(grad_proj, summed)
    grad_normed = jnp.concatenate(
        [dot("tc,dc->td", late_proj, weight).astype(bf16) for weight in (w_qkv, w_qkv_other)],
        axis=1,
    )
    grad_normed = exchange_sum(grad_normed.reshape(seqs, own, width), "s")
    grad_normed = whole_of(grad_normed[:, : width // 2], grad_normed[:, width // 2 :], 1)
    row_blocks = exchange_by_rank(summed, "z")
    grad_attn = after(total(row_blocks), gate_ready).astype(bf16)
    up_ready = swap(after(grad_w_up, row_blocks[1]), "z")
    grad_in_norm, gain_in_grad = norm_back(inputs, gain_in, grad_normed)
    grad_tokens = to_outer(grad_resid + grad_in_norm)

    def widen(local):
        full = jnp.zeros((width,), f32)
        return to_inner(lax.dynamic_update_slice_in_dim(full, local, rank * cols, 0))

    gains = jnp.stack([gain_in_grad, gain_mid_grad, widen(gain_q_grad[0]), widen(gain_k_grad[0])])
    gains = after(gains, grad_attn)
    loss_value = gather_sum(after(squared, grad_attn)) / (total_count * width)
    for axis in ("z", "c", "s", "o"):
        gains = sum(gather_near(gains, axis))
    row = (lax.axis_index(("c", "o", "z")) * seqs + rank) * rows_dev
    grad_gains = lax.dynamic_slice_in_dim(gains, row, rows_dev, 1).T

    got = exchange_by_rank(grad_attn.reshape(seqs, rows_dev, 4 * cols), "s")
    got = in_order(got, "s").astype(f32)
    grad_attn = jnp.concatenate(
        [got[s, :, i * cols : (i + 1) * cols] for i in range(4) for s in range(seqs)], axis=1
    )
    grad_expert = jnp.concatenate([gate_ready, up_ready, down_ready], axis=2)
    grad_expert = grad_expert.astype(f32).transpose(1, 0, 2)
    return (
        to_outer(final_out).astype(bf16),
        loss_value,
        grad_tokens,
        grad_attn,
        grad_gains,
        grad_expert,
    )


def solution(mesh):
    fsdp, seqs = mesh.shape["fsdp"], mesh.shape["sp"]

    def whole(*arrays):
        planes = arrays[3].shape[1] // seqs
        outer = fsdp // (planes * CORES)
        inner = Mesh(mesh.devices.reshape(outer, planes, CORES, seqs), ("o", "z", "c", "s"))
        every = ("o", "z", "c", "s")
        rows = P(every, None)
        experts = P(("o", "z", "c"), "s", None)
        return jax.shard_map(
            shards,
            mesh=inner,
            in_specs=(
                rows,
                rows,
                rows,
                experts,
                rows,
                rows,
                P(("o", "z", "c")),
                P(every),
                rows,
                rows,
            ),
            out_specs=(rows, P(), rows, rows, rows, experts),
            check_vma=False,
        )(*arrays)

    return whole
```

```python
import functools

import jax
import jax.numpy as jnp
from jax import lax
from jax.experimental import pallas as pl
from jax.experimental.pallas import tpu as pltpu
from jax.sharding import Mesh, PartitionSpec as P

H = 16
HD = 128
TOP = 8
CORES = 2
PAD = 128

epsilon = 1e-05
masked = -1e30
f32 = jnp.float32
bf16 = jnp.bfloat16


def send(block, axis, step):
    size = lax.axis_size(axis)
    return lax.ppermute(block, axis, [(i, i ^ step) for i in range(size)])


def gather_near(block, axis):
    return [block] + [send(block, axis, k) for k in range(1, lax.axis_size(axis))]


def in_order(blocks, axis, start=0):
    rank = lax.axis_index(axis)
    if len(blocks) == 1:
        return blocks[0][None]
    stacked = jnp.zeros((len(blocks),) + blocks[0].shape, blocks[0].dtype)
    for k, block in enumerate(blocks):
        stacked = lax.dynamic_update_index_in_dim(stacked, block, (rank ^ k) + start, 0)
    return stacked


def collect(block, axis):
    return in_order(gather_near(block, axis), axis)


def exchange(piece_for, axis, start=0):
    rank, size = lax.axis_index(axis) + start, lax.axis_size(axis)
    return [piece_for(rank)] + [send(piece_for(rank ^ k), axis, k) for k in range(1, size)]


def swap(pieces, axis):
    return lax.all_to_all(pieces, axis, split_axis=0, concat_axis=0, tiled=True)


def exchange_by_rank(pieces, axis):
    return exchange(lambda i: lax.dynamic_index_in_dim(pieces, i, 0, keepdims=False), axis)


def exchange_sum(pieces, axis):
    got = exchange_by_rank(pieces, axis)
    return sum(piece.astype(f32) for piece in got)


def token(*values):
    firsts = [value[(slice(0, 1),) * value.ndim].reshape(()).astype(f32) for value in values]
    total = sum(firsts)
    return (total != total).astype(jnp.int32)


def after(value, *others):
    return value + token(*others).astype(value.dtype)


def rms_factor(values):
    return lax.rsqrt(jnp.mean(values * values, axis=-1, keepdims=True) + epsilon)


def norm_back(values, gain_vec, grad_in):
    factor = rms_factor(values)
    normed = values * factor
    gain_grad = jnp.sum(grad_in * normed, axis=0)
    inner = grad_in * gain_vec
    grad = factor * (inner - normed * jnp.mean(inner * normed, axis=-1, keepdims=True))
    return grad, gain_grad


def rope_tables(rows):
    inverse = 10000.0 ** (-(jnp.arange(HD // 2).astype(f32) * 2.0 / HD))
    angles = jnp.arange(rows).astype(f32)[:, None] * inverse[None, :]
    cosine = jnp.concatenate([jnp.cos(angles), jnp.cos(angles)], axis=-1)
    sine = jnp.concatenate([-jnp.sin(angles), jnp.sin(angles)], axis=-1)
    return cosine, sine


def mm(left, right, dims):
    return lax.dot_general(left, right, (dims, ((), ())), preferred_element_type=f32)


def masked_scores(query, keyed, seg_col, seg_row, first, scale):
    scores = mm(query, keyed, ((1,), (1,))) * scale
    rows = first + lax.broadcasted_iota(jnp.int32, scores.shape, 0)
    allowed = (rows >= lax.broadcasted_iota(jnp.int32, scores.shape, 1)) & (seg_col == seg_row)
    return jnp.where(allowed, scores, masked)


def attend_kernel(
    block,
    q_raw,
    k_raw,
    v_raw,
    q_mean,
    k_mean,
    gain_q,
    gain_k,
    cosine,
    sine,
    seg_col,
    seg_row,
    out,
    q_out,
    k_out,
    v_out,
    log_total,
):
    def rope(raw, mean, gain):
        values = raw[...] * lax.rsqrt(mean[...] + epsilon) * gain[...]
        turned = pltpu.roll(values, HD // 2, 1)
        return (values * cosine[...] + turned * sine[...]).astype(bf16)

    q_out[...] = rope(q_raw, q_mean, gain_q)
    k_out[...] = rope(k_raw, k_mean, gain_k)
    v_out[...] = v_raw[...].astype(bf16)
    for first in range(0, out.shape[0], block):
        last = first + block
        scores = masked_scores(
            q_out[first:last],
            k_out[:last],
            seg_col[first:last],
            seg_row[:, :last],
            first,
            HD**-0.5,
        )
        top = jnp.max(scores, axis=-1, keepdims=True)
        exps = jnp.exp(scores - top)
        total = jnp.sum(exps, axis=-1, keepdims=True)
        weights = (exps * (1.0 / total)).astype(bf16)
        out[first:last] = mm(weights, v_out[:last], ((1,), (0,))).astype(bf16)
        log_total[0, first:last] = top + jnp.log(total)


def attend_back_kernel(
    block,
    q_raw,
    k_raw,
    q_mean,
    k_mean,
    gain_q,
    gain_k,
    cosine,
    sine,
    seg_col,
    seg_row,
    query,
    keyed,
    valued,
    grad,
    log_total,
    grad_q,
    grad_k,
    grad_v,
    q_inner,
    k_inner,
    gain_q_grad,
    gain_k_grad,
    sum_q,
    sum_k,
    sum_v,
):
    scale = HD**-0.5
    sum_k[...] = jnp.zeros_like(sum_k)
    sum_v[...] = jnp.zeros_like(sum_v)
    for first in range(0, query.shape[0], block):
        last = first + block
        q_block, g_block = query[first:last], grad[first:last]
        scores = masked_scores(
            q_block, keyed[:last], seg_col[first:last], seg_row[:, :last], first, scale
        )
        probs = jnp.exp(scores - log_total[0, first:last])
        sum_v[:last] += mm(probs.astype(bf16), g_block, ((0,), (0,)))
        grad_probs = mm(g_block, valued[:last], ((1,), (1,)))
        inner = jnp.sum(probs * grad_probs, axis=-1, keepdims=True)
        grad_scores = (probs * (grad_probs - inner)).astype(bf16)
        sum_q[first:last] = mm(grad_scores, keyed[:last], ((1,), (0,))) * scale
        sum_k[:last] += mm(grad_scores, q_block, ((0,), (0,))) * scale
    grad_v[...] = sum_v[...].astype(bf16)

    def undo(total, raw, mean, gain, inner_out, gain_out, grad_out):
        low = total[...].astype(bf16).astype(f32)
        back = low * cosine[...] + pltpu.roll(low * sine[...], HD // 2, 1)
        normed = raw[...] * lax.rsqrt(mean[...] + epsilon)
        gain_out[...] = jnp.sum(back * normed, axis=0, keepdims=True)
        back = back * gain[...]
        grad_out[...] = back
        inner = jnp.sum(back * normed, axis=-1, keepdims=True)

        @pl.when(pl.program_id(0) == 0)
        def _():
            inner_out[...] = inner

        @pl.when(pl.program_id(0) > 0)
        def _():
            inner_out[...] += inner

    undo(sum_q, q_raw, q_mean, gain_q, q_inner, gain_q_grad, grad_q)
    undo(sum_k, k_raw, k_mean, gain_k, k_inner, gain_k_grad, grad_k)


def head_specs(seq, heads):
    column = pl.BlockSpec((seq, 1), lambda h: (0, 0))
    gain = pl.BlockSpec((1, HD), lambda h: (0, h))
    table = pl.BlockSpec((seq, HD), lambda h: (0, 0))
    return [column, column, gain, gain, table, table, column, pl.BlockSpec((1, seq), lambda h: (0, 0))]


def raw_spec(seq, heads, which):
    return pl.BlockSpec((seq, HD), lambda h: (0, which * heads + h))


def attend(projected, shared, heads):
    seq = projected.shape[0]
    block = min(256, seq)
    head = pl.BlockSpec((seq, HD), lambda h: (0, h))
    low = jax.ShapeDtypeStruct((seq, heads * HD), bf16)
    return pl.pallas_call(
        functools.partial(attend_kernel, block),
        grid=(heads,),
        in_specs=[raw_spec(seq, heads, i) for i in range(3)] + head_specs(seq, heads),
        out_specs=[head] * 4 + [pl.BlockSpec((1, seq, 1), lambda h: (h, 0, 0))],
        out_shape=[low] * 4 + [jax.ShapeDtypeStruct((heads, seq, 1), f32)],
        compiler_params=pltpu.CompilerParams(vmem_limit_bytes=48 * 2**20),
        cost_estimate=pl.CostEstimate(flops=10**6, bytes_accessed=10**5, transcendentals=0),
    )(projected, projected, projected, *shared)


def attend_back(projected, shared, query, keyed, valued, grad, log_total, heads):
    seq = projected.shape[0]
    block = min(256, seq)
    head = pl.BlockSpec((seq, HD), lambda h: (0, h))
    column = pl.BlockSpec((seq, 1), lambda h: (0, 0))
    gain = pl.BlockSpec((1, HD), lambda h: (0, h))
    wide = jax.ShapeDtypeStruct((seq, heads * HD), f32)
    return pl.pallas_call(
        functools.partial(attend_back_kernel, block),
        grid=(heads,),
        in_specs=[raw_spec(seq, heads, i) for i in range(2)]
        + head_specs(seq, heads)
        + [head] * 4
        + [pl.BlockSpec((1, seq, 1), lambda h: (h, 0, 0))],
        out_specs=[head] * 3 + [column] * 2 + [gain] * 2,
        out_shape=[wide, wide, jax.ShapeDtypeStruct((seq, heads * HD), bf16)]
        + [jax.ShapeDtypeStruct((seq, 1), f32)] * 2
        + [jax.ShapeDtypeStruct((1, heads * HD), f32)] * 2,
        scratch_shapes=[pltpu.VMEM((seq, HD), f32)] * 3,
        compiler_params=pltpu.CompilerParams(vmem_limit_bytes=48 * 2**20),
        cost_estimate=pl.CostEstimate(flops=10**6, bytes_accessed=10**5, transcendentals=0),
    )(projected, projected, *shared, query, keyed, valued, grad, log_total)


def slot_choice(place, slots):
    return lax.broadcasted_iota(jnp.int32, (slots, place.shape[1]), 0) == place


def slot_weight(place, gate, slots):
    return jnp.sum(jnp.where(slot_choice(place, slots), gate, 0.0), axis=1, keepdims=True)


def spans_of(count, slots):
    return [(b, slice(b * slots, (b + 1) * slots)) for b in range(count)]


def add_tokens(place, b, slots, out, sum_tokens, partial):
    expert = pl.program_id(0)
    back = mm(slot_choice(place[0, b], slots).astype(bf16), out, ((0,), (0,)))

    @pl.when(expert == 0)
    def _():
        sum_tokens[b] = back

    @pl.when(expert > 0)
    def _():
        sum_tokens[b] += back

    @pl.when(expert == pl.num_programs(0) - 1)
    def _():
        partial[b][...] = sum_tokens[b].astype(bf16)


def hidden_kernel(count, slots, place, *refs):
    blocks, w_gate, w_up = refs[:count], refs[count], refs[count + 1]
    rows, activated, gate_pre, up_pre = refs[-4:]
    for b, span in spans_of(count, slots):
        choice = slot_choice(place[0, b], slots).astype(bf16)
        rows[0, 0, span] = mm(choice, blocks[b][...], ((1,), (0,))).astype(bf16)
    rows_in = rows[0, 0]
    g = mm(rows_in, w_gate[0], ((1,), (0,)))
    u = mm(rows_in, w_up[0], ((1,), (0,)))
    gate_pre[0], up_pre[0] = g.astype(bf16), u.astype(bf16)
    activated[0, 0] = (g * jax.nn.sigmoid(g) * u).astype(bf16)


def out_kernel(count, slots, place, gate, activated, w_down, *refs):
    partial, sum_tokens = refs[:-1], refs[-1]
    result = mm(activated[0, 0], w_down[0], ((1,), (1,)))
    for b, span in spans_of(count, slots):
        out = (result[span] * slot_weight(place[0, b], gate[0, b], slots)).astype(bf16)
        add_tokens(place, b, slots, out, sum_tokens, partial)


def expert_back_kernel(count, slots, place, gate, *refs):
    blocks, (w_gate, w_up, w_down) = refs[:count], refs[count : count + 3]
    gate_pre, up_pre = refs[count + 3 : count + 5]
    grad_rows, grad_gate, grad_up = refs[-4 - count : -1 - count]
    partial, sum_tokens = refs[-1 - count : -1], refs[-1]
    for b, span in spans_of(count, slots):
        choice = slot_choice(place[0, b], slots).astype(bf16)
        weight = slot_weight(place[0, b], gate[0, b], slots)
        picked = mm(choice, blocks[b][...], ((1,), (0,)))
        grad_rows[0, 0, span] = (picked * weight).astype(bf16)
    grad_act = mm(grad_rows[0, 0], w_down[0], ((1,), (0,)))
    g, u = gate_pre[0].astype(f32), up_pre[0].astype(f32)
    sigmoid = jax.nn.sigmoid(g)
    dg = (grad_act * u * sigmoid * (1.0 + g * (1.0 - sigmoid))).astype(bf16)
    du = (grad_act * g * sigmoid).astype(bf16)
    grad_gate[0, 0], grad_up[0, 0] = dg, du
    result = mm(dg, w_gate[0], ((1,), (1,))) + mm(du, w_up[0], ((1,), (1,)))
    result = result.astype(bf16)
    for b, span in spans_of(count, slots):
        add_tokens(place, b, slots, result[span], sum_tokens, partial)


class Experts:
    def __init__(self, group, slots, place, gate, blocks, weights):
        self.group, self.slots, self.place, self.gate = group, slots, place, gate
        self.experts, self.width, self.hidden = weights[0].shape
        self.count, self.own = len(blocks), blocks[0].shape[0]
        self.rows = self.count * slots
        group_of = lambda e: (e, group, 0, 0)
        self.table = pl.BlockSpec((1, self.count, 1, self.own), group_of)
        self.tokens = pl.BlockSpec((self.own, self.width), lambda e: (0, 0))
        self.weight = pl.BlockSpec((1, self.width, self.hidden), lambda e: (e, 0, 0))
        self.local = pl.BlockSpec((1, self.rows, self.hidden), lambda e: (e, 0, 0))
        self.wide = pl.BlockSpec((1, 1, self.rows, self.width), group_of)
        self.narrow = pl.BlockSpec((1, 1, self.rows, self.hidden), group_of)
        self.sums = pltpu.VMEM((self.count, self.own, self.width), f32)

    def shape(self, spec):
        rows, experts = self.rows, self.experts
        shapes = [
            (self.tokens, (self.own, self.width)),
            (self.local, (experts, rows, self.hidden)),
            (self.wide, (experts, 2, rows, self.width)),
            (self.narrow, (experts, 2, rows, self.hidden)),
        ]
        [shape] = [shape for known, shape in shapes if known is spec]
        return jax.ShapeDtypeStruct(shape, bf16)

    def run(self, kernel, ins, outs, scratch, prior=()):
        specs = [spec for spec, _ in ins] + [pl.BlockSpec(memory_space=pl.ANY)] * len(prior)
        return pl.pallas_call(
            functools.partial(kernel, self.count, self.slots),
            grid=(self.experts,),
            in_specs=specs,
            out_specs=outs,
            out_shape=[self.shape(spec) for spec in outs],
            scratch_shapes=scratch,
            input_output_aliases={len(ins) + i: i for i in range(len(prior))},
            compiler_params=pltpu.CompilerParams(vmem_limit_bytes=58 * 2**20),
            cost_estimate=pl.CostEstimate(
                flops=self.experts * self.rows * self.width * self.hidden * 4,
                bytes_accessed=self.experts * self.width * self.hidden * 6,
                transcendentals=self.experts * self.rows * self.hidden,
            ),
        )(*[array for _, array in ins], *prior)

    def to_hidden(self, blocks, w_gate, w_up, prior):
        ins = [(self.table, self.place)] + [(self.tokens, block) for block in blocks]
        ins += [(self.weight, w_gate), (self.weight, w_up)]
        outs = [self.wide, self.narrow, self.local, self.local]
        return self.run(hidden_kernel, ins, outs, [], prior)

    def to_tokens(self, activated, w_down):
        ins = [(self.table, self.place), (self.table, self.gate)]
        ins += [(self.narrow, activated), (self.weight, w_down)]
        return self.run(out_kernel, ins, [self.tokens] * self.count, [self.sums])

    def backward(self, blocks, weights, pres, prior):
        ins = [(self.table, self.place), (self.table, self.gate)]
        ins += [(self.tokens, block) for block in blocks]
        ins += [(self.weight, weight) for weight in weights]
        ins += [(self.local, pre) for pre in pres]
        outs = [self.wide, self.narrow, self.narrow] + [self.tokens] * self.count
        return self.run(expert_back_kernel, ins, outs, [self.sums], prior)


def dot(spec, left, right):
    return jnp.einsum(spec, left, right, preferred_element_type=f32)


def shards(
    tokens,
    w_attn,
    norm_gains,
    w_expert,
    gate_weights,
    routes,
    segment,
    valid_mask,
    teacher,
    cotangent,
):
    outer, planes, seqs = lax.axis_size("o"), lax.axis_size("z"), lax.axis_size("s")
    plane, rank = lax.axis_index("z"), lax.axis_index("s")
    own, width = tokens.shape
    rows_dev = w_attn.shape[0]
    seq = own * seqs
    heads = H // seqs
    cols = heads * HD
    hidden = w_expert.shape[2] // 3
    part = w_expert.shape[0]
    capacity = own * TOP * 17 // (16 * planes * seqs)
    scale = HD ** (-0.5)

    def to_inner(v):
        lead = v.shape[:-1]
        v = v.reshape(lead + (outer * planes, CORES, part))
        return jnp.swapaxes(v, -3, -2).reshape(lead + (width,))

    def to_outer(v):
        lead = v.shape[:-1]
        v = v.reshape(lead + (CORES, outer * planes, part))
        return jnp.swapaxes(v, -3, -2).reshape(lead + (width,))

    first_core = lax.axis_index("c") == 0

    def halves(v):
        low, high = v[..., : width // 2], v[..., width // 2 :]
        return jnp.where(first_core, low, high), jnp.where(first_core, high, low)

    def whole_of(mine, other, axis):
        low, high = jnp.where(first_core, mine, other), jnp.where(first_core, other, mine)
        return jnp.concatenate([low, high], axis=axis)

    def stack_rows(blocks, start=0):
        rows = in_order(blocks, "z", start)
        return collect(rows, "o").reshape((width // 2,) + rows.shape[2:])

    def sum_cores(grad):
        count = grad.shape[1]
        grad = exchange_sum(grad.reshape(CORES, width // 2, count), "c")
        if outer > 1:
            grad = exchange_sum(grad.astype(bf16).reshape(outer, planes * part, count), "o")
        return grad

    def gather_sum(value):
        for axis in ("z", "s", "c", "o"):
            value = sum(gather_near(jnp.broadcast_to(value, (8, PAD)), axis))[0, 0]
        return value

    by_expert = lax.optimization_barrier(w_expert.transpose(1, 0, 2))

    def expert_chunk(i, start=0):
        def piece_for(owner):
            return lax.dynamic_slice(by_expert, (owner, 0, i * hidden), (1, part, hidden))[0]

        return exchange(piece_for, "z", start)

    def gather_plane(ready):
        chunk = ready.reshape(planes * part, hidden)
        chunk = lax.all_gather(chunk, ("s", "c", "o"), axis=0, tiled=True)
        return chunk.reshape(seqs, width, hidden)

    count = jnp.sum(valid_mask).astype(jnp.int32)
    digits = jnp.stack([count // 128, count % 128]).astype(bf16)
    extra = jnp.concatenate(
        [
            norm_gains,
            jnp.broadcast_to(digits[None], (rows_dev, 2)),
            jnp.zeros((rows_dev, PAD - 6), bf16),
        ],
        axis=1,
    )

    routed = jnp.stack(
        gather_near(jnp.concatenate([routes.astype(f32), gate_weights], axis=1), "z")
    )
    route_all, gate_all = routed[..., :TOP].astype(jnp.int32), routed[..., TOP:]
    expert_ids = jnp.arange(seqs) * planes + plane
    match = route_all[:, :, None, :] == expert_ids[None, None, :, None]
    used = jnp.any(match, axis=-1)
    gate_of = jnp.sum(jnp.where(match, gate_all[:, :, None, :], 0.0), axis=-1)
    before = (jnp.arange(own)[:, None] > jnp.arange(own)[None, :]).astype(bf16)
    place = dot("tu,buk->btk", before, used.astype(bf16)).astype(jnp.int32)
    place = jnp.where(used, place, -1)
    slots = -(-capacity // 16) * 16
    place = place.transpose(2, 0, 1)[:, :, None, :]
    gate_of = gate_of.transpose(2, 0, 1)[:, :, None, :]

    groups = [[k for k in range(planes) if k % 2 == odd] for odd in range(2)]

    def by_group(table):
        return jnp.concatenate([table[:, k : k + 1] for group in groups for k in group], axis=1)

    place, gate_of = by_group(place), by_group(gate_of)

    inputs = to_inner(tokens)
    column_rows, extra_rows = rows_dev * 4 * cols // width, rows_dev * PAD // width
    extra = jnp.pad(extra.reshape(extra_rows, width), ((0, -extra_rows % 8), (0, 0)))

    def message_to(owner):
        picked = [
            lax.dynamic_slice_in_dim(w_attn, i * width + owner * cols, cols, 1) for i in range(4)
        ]
        picked = jnp.concatenate(picked, axis=1).reshape(column_rows, width)
        return jnp.concatenate([inputs, picked, extra], axis=0)

    messages = exchange(message_to, "s")
    gate_blocks = expert_chunk(0)
    up_blocks = expert_chunk(1, token(*gate_blocks))
    last = own + column_rows
    columns = [
        jnp.concatenate(
            [
                message[own:last].reshape(rows_dev, 4 * cols),
                message[last : last + extra_rows].reshape(rows_dev, PAD),
            ],
            axis=1,
        )
        for message in messages
    ]
    mine = in_order(columns, "s").reshape(part, 4 * cols + PAD)
    inputs = inputs.astype(f32)
    gate_ready = in_order(gate_blocks, "z", token(*messages))
    w_gate = gather_plane(gate_ready)
    up_ready = in_order(up_blocks, "z", token(gate_ready, mine))
    w_up = gather_plane(up_ready)
    in_blocks = gather_near(after(mine, up_ready), "z")
    seq_tokens = in_order([message[:own] for message in messages], "s", token(up_ready))
    seq_tokens = seq_tokens.reshape(seq, width).astype(f32)
    seq_factor = rms_factor(seq_tokens)
    w_in = stack_rows(in_blocks, token(seq_factor))
    w_in_other = send(w_in, "c", 1)

    side = whole_of(w_in[:, 4 * cols :], w_in_other[:, 4 * cols :], 0)[:, :6].astype(f32).T
    gain_in, gain_mid = side[0], side[1]
    gain_q = lax.dynamic_slice_in_dim(to_outer(side[2]), rank * cols, cols, 0)
    gain_k = lax.dynamic_slice_in_dim(to_outer(side[3]), rank * cols, cols, 0)
    total_count = jnp.sum(side[4, ::rows_dev]) * 128.0 + jnp.sum(side[5, ::rows_dev])


    def near_planes(block):
        near = [block] + [None] * (planes - 1)
        for k in groups[0][1:]:
            near[k] = send(block, "z", k)
        later = after(block, *[near[k] for k in groups[0][1:]])
        for k in groups[1]:
            near[k] = send(later, "z", k)
        return [[near[k] for k in group] for group in groups]

    def send_back(first, second):
        got = [first[0]] + [send(first[i], "z", k) for i, k in enumerate(groups[0]) if k]
        base = after(total(got), second[0])
        second = [after(part, base) for part in second]
        return second[0], [base] + [send(second[i], "z", k) for i, k in enumerate(groups[1])]

    def total(pieces):
        return sum(piece.astype(f32) for piece in pieces)

    normed_in = (seq_tokens * seq_factor * gain_in).astype(bf16)
    normed_mine, normed_other = halves(normed_in)
    w_qkv, w_qkv_other = w_in[:, : 3 * cols], w_in_other[:, : 3 * cols]
    w_out = whole_of(w_in[:, 3 * cols : 4 * cols], w_in_other[:, 3 * cols : 4 * cols], 0)
    projected = jnp.dot(normed_mine, w_qkv, preferred_element_type=f32) + jnp.dot(
        normed_other, w_qkv_other, preferred_element_type=f32
    )
    query_raw = projected[:, :cols]
    key_raw = projected[:, cols : 2 * cols]

    def over_heads(first, second, *others):
        pairs = gather_near(jnp.stack([first, second]), "s")
        if others:
            pairs[0] = after(pairs[0], *others)
        pair = sum(pairs) / width
        return pair[0][:, None], pair[1][:, None]

    q_mean, k_mean = over_heads(
        jnp.sum(query_raw * query_raw, axis=-1), jnp.sum(key_raw * key_raw, axis=-1)
    )
    cosine, sine = rope_tables(seq)
    shared = [
        after(q_mean, w_gate, w_out),
        k_mean,
        gain_q[None],
        gain_k[None],
        cosine,
        sine,
        segment[:, None],
        segment[None],
    ]
    attended, query, keyed, valued, log_total = attend(projected, shared, heads)
    start = token(attended)
    down_blocks = exchange(
        lambda owner: lax.dynamic_slice(
            w_expert, (0, owner, 2 * hidden), (part, 1, hidden)
        )[:, 0],
        "z",
        start,
    )
    attn_out = dot("tc,dc->td", attended, w_out).astype(bf16)
    got = exchange_sum(attn_out.reshape(seqs, own, width), "s")
    residual = inputs + got
    down_ready = in_order(down_blocks, "z", token(residual))
    residual = after(residual, down_ready)
    w_down = gather_plane(down_ready)

    normed_mid = (residual * rms_factor(residual) * gain_mid).astype(bf16)
    expert_weights = (w_gate, w_up, w_down)
    blocks = near_planes(normed_mid)
    work = [Experts(i, slots, place, gate_of, blocks[i], expert_weights) for i in range(2)]
    rows_in, activated, *pres = work[0].to_hidden(blocks[0], w_gate, w_up, ())
    first = work[0].to_tokens(activated, w_down)
    pres = [pres]
    blocks[1][0] = after(blocks[1][0], first[0])
    rows_in, activated, *last = work[1].to_hidden(
        blocks[1], w_gate, w_up, (rows_in, activated)
    )
    pres.append(last)
    second = work[1].to_tokens(activated, w_down)
    final_out = residual + total(send_back(first, second)[1])
    rows_in, activated = [v.reshape(seqs, -1, v.shape[-1]) for v in (rows_in, activated)]

    w_out_all = lax.all_gather(after(w_out, w_up), "s", axis=0)
    valid_f = valid_mask.astype(f32)[:, None]
    difference = final_out - to_inner(teacher).astype(f32)
    squared = jnp.sum(valid_f * difference * difference)
    grad_out = (
        to_inner(cotangent).astype(f32) + 2.0 / (total_count * width) * valid_f * difference
    )

    def scatter_expert(grad):
        grad = grad.reshape(seqs * width, hidden)
        grad = lax.psum_scatter(grad, ("s", "c", "o"), scatter_dimension=0, tiled=True)
        return grad.reshape(planes, part, hidden)

    blocks = near_planes(grad_out.astype(bf16))
    *grads, first, last = work[0].backward(blocks[0], expert_weights, pres[0], ())
    partial = [(first, last)]
    blocks[1][0] = after(blocks[1][0], first)
    *grads, first, last = work[1].backward(blocks[1], expert_weights, pres[1], grads)
    partial.append((first, last))
    back_last, back_pieces = send_back(*partial)
    grad_rows, grad_gate, grad_up = [v.reshape(seqs, -1, v.shape[-1]) for v in grads]
    grad_w_down = dot("krd,krf->kdf", grad_rows, after(activated, back_last)).astype(bf16)
    back_pieces[0] = after(back_pieces[0], grad_w_down)
    grad_mid = total(back_pieces)
    grad_w_gate = dot("krd,krf->kdf", rows_in, after(grad_gate, grad_mid)).astype(bf16)
    grad_resid_norm, gain_mid_grad = norm_back(residual, gain_mid, grad_mid)
    grad_resid = grad_out + grad_resid_norm

    grad_low = grad_resid.astype(bf16)
    grad_heads = dot("td,sdc->stc", grad_low, w_out_all).astype(bf16)
    head_blocks = exchange(
        lambda i: lax.dynamic_index_in_dim(grad_heads, i, 0, keepdims=False), "s"
    )
    grad_heads = in_order(head_blocks, "s", token(grad_w_gate)).reshape(seq, cols)
    grad_w_up = dot("krd,krf->kdf", rows_in, after(grad_up, grad_heads)).astype(bf16)
    up_done = grad_w_up
    grad_w_down, grad_w_gate, grad_w_up = [
        scatter_expert(grad) for grad in (grad_w_down, grad_w_gate, grad_w_up)
    ]
    low_blocks = gather_near(after(grad_low, grad_heads), "s")
    down_ready = swap(grad_w_down, "z")
    grad_q, grad_k, grad_v, q_inner, k_inner, gain_q_grad, gain_k_grad = attend_back(
        projected, shared, query, keyed, valued, after(grad_heads, up_done), log_total, heads
    )
    grad_attn_out = in_order(low_blocks, "s", token(grad_q)).reshape(seq, width)
    down_ready = after(down_ready, grad_q)
    q_inner = after(q_inner, down_ready, grad_attn_out)
    grad_w_out = dot("td,tc->dc", grad_attn_out, attended).astype(bf16)
    q_inner, k_inner = over_heads(q_inner[:, 0], k_inner[:, 0], grad_w_out)

    def norm_grad(grad, raw, mean, inner):
        factor = lax.rsqrt(mean + epsilon)
        return (factor * (grad - raw * factor * inner)).astype(bf16)

    grad_proj = jnp.concatenate(
        [
            norm_grad(grad_q, query_raw, q_mean, q_inner),
            norm_grad(grad_k, key_raw, k_mean, k_inner),
            grad_v,
        ],
        axis=1,
    )

    grad_w_qkv = dot("td,tc->dc", normed_in, grad_proj).astype(bf16)
    summed = jnp.concatenate([sum_cores(grad_w_qkv), sum_cores(grad_w_out)], axis=1)
    summed = summed.astype(bf16).reshape(planes, part, 4 * cols)
    gate_ready = swap(grad_w_gate, "z")
    late_proj = after(grad_proj, summed)
    grad_normed = jnp.concatenate(
        [dot("tc,dc->td", late_proj, weight).astype(bf16) for weight in (w_qkv, w_qkv_other)],
        axis=1,
    )
    grad_normed = exchange_sum(grad_normed.reshape(seqs, own, width), "s")
    grad_normed = whole_of(grad_normed[:, : width // 2], grad_normed[:, width // 2 :], 1)
    row_blocks = exchange_by_rank(summed, "z")
    grad_attn = after(total(row_blocks), gate_ready).astype(bf16)
    up_ready = swap(after(grad_w_up, row_blocks[1]), "z")
    grad_in_norm, gain_in_grad = norm_back(inputs, gain_in, grad_normed)
    grad_tokens = to_outer(grad_resid + grad_in_norm)

    def widen(local):
        full = jnp.zeros((width,), f32)
        return to_inner(lax.dynamic_update_slice_in_dim(full, local, rank * cols, 0))

    gains = jnp.stack([gain_in_grad, gain_mid_grad, widen(gain_q_grad[0]), widen(gain_k_grad[0])])
    gains = after(gains, grad_attn)
    loss_value = gather_sum(after(squared, grad_attn)) / (total_count * width)
    for axis in ("z", "c", "s", "o"):
        gains = sum(gather_near(gains, axis))
    row = (lax.axis_index(("c", "o", "z")) * seqs + rank) * rows_dev
    grad_gains = lax.dynamic_slice_in_dim(gains, row, rows_dev, 1).T

    got = exchange_by_rank(grad_attn.reshape(seqs, rows_dev, 4 * cols), "s")
    got = in_order(got, "s").astype(f32)
    grad_attn = jnp.concatenate(
        [got[s, :, i * cols : (i + 1) * cols] for i in range(4) for s in range(seqs)], axis=1
    )
    grad_expert = jnp.concatenate([gate_ready, up_ready, down_ready], axis=2)
    grad_expert = lax.optimization_barrier(grad_expert.transpose(1, 0, 2)).astype(f32)
    return (
        to_outer(final_out).astype(bf16),
        loss_value,
        grad_tokens,
        grad_attn,
        grad_gains,
        grad_expert,
    )


def solution(mesh):
    fsdp, seqs = mesh.shape["fsdp"], mesh.shape["sp"]

    def whole(*arrays):
        planes = arrays[3].shape[1] // seqs
        outer = fsdp // (planes * CORES)
        inner = Mesh(mesh.devices.reshape(outer, planes, CORES, seqs), ("o", "z", "c", "s"))
        every = ("o", "z", "c", "s")
        rows = P(every, None)
        experts = P(("o", "z", "c"), "s", None)
        return jax.shard_map(
            shards,
            mesh=inner,
            in_specs=(
                rows,
                rows,
                rows,
                experts,
                rows,
                rows,
                P(("o", "z", "c")),
                P(every),
                rows,
                rows,
            ),
            out_specs=(rows, P(), rows, rows, rows, experts),
            check_vma=False,
        )(*arrays)

    return whole
```
